32 devices in a mesh: sweep: 2 (over y), wide: 4 (over z), narrow: 4 (over x, core).
Axes of the slice: x: 2, y: 2, z: 4, core: 2. Of those that a mesh axis runs over, the one named last changes fastest.
Arguments:
- fresh_coefs: bfloat16 [1024, 32, 128], P(('sweep', 'wide', 'narrow')), parts along dimension 0, may hold values from -1.5 to 1.5
- older_coefs: bfloat16 [8, 4, 8, 2, 32, 128], P(('sweep', 'wide'), 'narrow'), parts along dimension 0, may hold values from -1.5 to 1.5
- state: float32 [2, 131072], P(None, ('sweep', 'wide', 'narrow')), parts along dimension 1, may hold values from 0 to 1
- lesion: int32 [131072], P(('sweep', 'wide', 'narrow')), parts along dimension 0, may hold values 0 or 1
- stim_nodes: int32 [128], P('sweep'), parts along dimension 0, may hold values from 0 to 65535
- stim_wave: float32 [64], P('sweep'), parts along dimension 0, may hold values from -12 to 12
- read_blocks: int32 [4, 4, 4, 2], P('wide', 'narrow'), may hold values from -1 to 31, as said below
- tract_slot: int32 [4, 4, 96], P('wide', 'narrow'), may hold values from 0 to 7, as said below
- tract_target: int32 [4, 4, 96], P('wide', 'narrow'), may hold values from 0 to 127, as said below
- tract_delay: int32 [4, 4, 96], P('wide', 'narrow'), may hold values from 32 to 95
- tract_frac: float32 [4, 4, 96], P('wide', 'narrow'), may hold values from 0 to 1
- tract_weights: bfloat16 [4, 4, 96, 128, 128], P('wide', 'narrow'), may hold values from -0.3125 to 0.3125
Outputs:
- new_coefs: bfloat16 [1024, 32, 128], P(('sweep', 'wide', 'narrow')), parts along dimension 0
- final_state: float32 [2, 131072], P(None, ('sweep', 'wide', 'narrow')), parts along dimension 1
The draws below stay inside these ranges and needn't reach their ends.
There are 2 independent parts, one for each index of `sweep`. The reference program is written for one: setup_inputs(seed, part) draws one part's arguments, and reference() takes and returns one part's arrays. A program takes and returns all parts, laid end to end along the dimension named above; an argument that names none is the same for every part. Nothing has to cross between parts.
Inputs may be any that keep to these rules, and one draw needn't show every extreme that they name: `read_blocks`: entry [w, n, o, c] is a block of device (o, n) or -1 for an empty slot; the blocks named for one (w, n, o) are distinct and fill its first slots; some owner fills all 2 slots of every reader. `tract_slot`: each entry names a slot of its own device whose read_blocks entry is not -1. `tract_target`: the tiles of one device (w, n) name, for every narrow index p, exactly 12 distinct targets among p * 32 to (p + 1) * 32 - 1.
All inputs are finite; a program needn't handle non-finite values. No bound on the sum of `lesion` on one device may be relied on, other than what follows from the above.
Results may differ from the reference program's by a relative error of at most 0.003.
Values may be sent and summed in bfloat16 or wider, within the bound.
No kernel may reach another device: no remote copies, remote signals or barrier semaphores. Data moves between devices by JAX's collectives and lax.ppermute only.
A program may use at most 128 MiB of HBM per device.

```python
import math
import jax
import jax.numpy as jnp
from jax import lax

K = 32
STEPS = 32
BLK = 128
HSEG = 2
CAP = 2
NSTIM = 64
OWN_BLK = 32
TILES = 96
SLOTS = 8
PEER_TGT = 12
NBLK = 512
NODES = 65536
N_WIDE = 4
N_NARROW = 4


def read_table(key):
    hub_key, count_key, order_key = jax.random.split(key, 3)
    owners = jnp.arange(N_WIDE, dtype=jnp.int32)
    hubs = (jax.random.randint(hub_key, (N_WIDE,), 0, 4) == 0) | (owners == N_WIDE - 1)
    counts = jax.random.randint(count_key, (N_WIDE, N_NARROW, N_WIDE), 0, CAP + 1)
    counts = jnp.where(hubs[None, None, :], CAP, counts)
    scores = jax.random.randint(order_key, (N_WIDE, N_NARROW, N_WIDE, OWN_BLK), 0, 1 << 20) * OWN_BLK + jnp.arange(OWN_BLK, dtype=jnp.int32)
    order = jnp.argsort(scores, axis=-1, stable=True).astype(jnp.int32)[..., :CAP]
    places = jnp.arange(CAP, dtype=jnp.int32)
    return jnp.where(places < counts[..., None], order, -1).astype(jnp.int32)


def draw_read_blocks(key, part):
    return read_table(key)


def draw_tract_slot(key, part):
    table = read_table(key)
    key = jax.random.fold_in(key, 7)
    slot_total = N_WIDE * CAP
    live = (table >= 0).reshape(N_WIDE, N_NARROW, slot_total)
    positions = jnp.arange(slot_total, dtype=jnp.int32)
    ranked = jnp.argsort(jnp.where(live, positions, positions + slot_total), axis=-1, stable=True).astype(jnp.int32)
    live_count = jnp.sum(live.astype(jnp.int32), axis=-1, keepdims=True)
    picks = jax.random.randint(key, (N_WIDE, N_NARROW, TILES), 0, 1 << 20) % live_count
    picks = picks.at[..., 0].set(live_count[..., 0] - 1)
    return jnp.take_along_axis(ranked, picks, axis=-1).astype(jnp.int32)


def draw_tract_target(key, part):
    key = jax.random.fold_in(key, 11)
    order_key, dest_key, pick_key = jax.random.split(key, 3)
    scores = jax.random.randint(order_key, (N_WIDE, N_NARROW, N_NARROW, OWN_BLK), 0, 1 << 20) * OWN_BLK + jnp.arange(OWN_BLK, dtype=jnp.int32)
    chosen = jnp.argsort(scores, axis=-1, stable=True).astype(jnp.int32)[..., :PEER_TGT]
    tiles = jnp.arange(TILES, dtype=jnp.int32)
    fixed_dest = tiles // PEER_TGT
    fixed_pick = tiles % PEER_TGT
    rand_dest = jax.random.randint(dest_key, (N_WIDE, N_NARROW, TILES), 0, N_NARROW)
    rand_pick = jax.random.randint(pick_key, (N_WIDE, N_NARROW, TILES), 0, PEER_TGT)
    covered = tiles < PEER_TGT * N_NARROW
    dest = jnp.where(covered[None, None, :], fixed_dest[None, None, :], rand_dest).astype(jnp.int32)
    pick = jnp.where(covered[None, None, :], fixed_pick[None, None, :], rand_pick).astype(jnp.int32)
    per_dest = jnp.take_along_axis(chosen, dest[..., None], axis=2)
    local = jnp.take_along_axis(per_dest, pick[..., None], axis=-1)[..., 0]
    return (dest * OWN_BLK + local).astype(jnp.int32)


def plant(array, stream_key, smallest, high):
    shape = array.shape
    spot = [jax.random.randint(jax.random.fold_in(stream_key, axis), (), 0, shape[axis]) for axis in range(len(shape))]
    array = array.at[tuple(spot)].set(smallest)
    longest = shape.index(max(shape))
    spot[longest] = (spot[longest] + 1) % shape[longest]
    return array.at[tuple(spot)].set(high)


def level_of(stream_key, extent, cuts, least, largest):
    loudness = 1.0
    for dim, shards_of in cuts:
        draws = jax.random.uniform(jax.random.fold_in(jax.random.fold_in(stream_key, 6), dim), (shards_of,), jnp.float32, least / len(cuts), largest / len(cuts))
        loudness = loudness * jnp.repeat(jnp.exp(draws), extent[dim] // shards_of).reshape((-1,) + (1,) * (len(extent) - 1 - dim))
    return loudness


def bell_draw(stream_key, shape, deviation, bound, cuts=(), held_as=jnp.bfloat16):
    loudness = level_of(stream_key, shape, cuts, -0.22, 0.18) if cuts else 1.0
    array = jax.random.normal(stream_key, shape, jnp.float32) * deviation * loudness
    return jnp.minimum(jnp.maximum(array, -bound), bound).astype(held_as)


def setup_inputs(seed: int = 0, part: int = 0) -> dict:
    keys = jax.random.split(jax.random.key(seed), 13)
    part_keys = jax.random.split(jax.random.fold_in(keys[12], part), 13)
    return {
        "fresh_coefs": bell_draw(part_keys[0], (NBLK, K, BLK), 0.25, 1.5, ((0, 16),)),
        "older_coefs": bell_draw(part_keys[1], (N_WIDE, N_NARROW, SLOTS, HSEG, K, BLK), 0.25, 1.5, ((0, 4), (1, 4))),
        "state": jnp.clip(1.0 * jax.random.uniform(part_keys[2], (2, NODES), jnp.float32) ** level_of(part_keys[2], (2, NODES), ((1, 16),), -0.2, 0.2), 0.0, 1.0),
        "lesion": plant((jax.random.randint(part_keys[3], (NODES,), 0, 8) < 1).astype(jnp.int32), jax.random.fold_in(part_keys[3], 1), 0, 1),
        "stim_nodes": plant(jax.random.randint(part_keys[4], (NSTIM,), 0, NODES), jax.random.fold_in(part_keys[4], 1), 0, NODES - 1).astype(jnp.int32),
        "stim_wave": bell_draw(part_keys[5], (STEPS,), 2.0, 12.0, (), jnp.float32),
        "read_blocks": draw_read_blocks(jax.random.fold_in(keys[12], 71), part),
        "tract_slot": draw_tract_slot(jax.random.fold_in(keys[12], 71), part),
        "tract_target": draw_tract_target(jax.random.fold_in(keys[12], 71), part),
        "tract_delay": plant(jax.random.randint(keys[9], (N_WIDE, N_NARROW, TILES), STEPS, (HSEG + 1) * STEPS), jax.random.fold_in(keys[9], 1), STEPS, ((HSEG + 1) * STEPS) - 1).astype(jnp.int32),
        "tract_frac": jnp.clip(1.0 * jax.random.uniform(keys[10], (N_WIDE, N_NARROW, TILES), jnp.float32) ** level_of(keys[10], (N_WIDE, N_NARROW, TILES), ((0, 4), (1, 4)), -0.2, 0.2), 0.0, 1.0),
        "tract_weights": bell_draw(keys[11], (N_WIDE, N_NARROW, TILES, BLK, BLK), (BLK * TILES // OWN_BLK) ** -0.5, 0.3125, ((0, 4), (1, 4))),
    }


excite_rate = 0.1
inhibit_rate = 0.05
excite_excite = 1.5
inhibit_excite = 2.0
excite_inhibit = 2.0
inhibit_inhibit = 0.5
excite_offset = 0.5
inhibit_offset = 0.5
tract_gain = 2.0


def basis_table(coef_count, step_count):
    order = jnp.arange(coef_count, dtype=jnp.float32)[:, None]
    places = jnp.arange(step_count, dtype=jnp.float32)[None, :]
    angles = math.pi * (step_count - places - 0.5) / step_count
    return jnp.cos(order * angles)


def fit_table(coef_count, step_count):
    scales = jnp.where(jnp.arange(coef_count)[:, None] == 0, 1.0, 2.0) / step_count
    return basis_table(coef_count, step_count) * scales


def join_history(older_values, newest_values):
    slot_count = older_values.shape[0]
    earlier = older_values[:, ::-1].reshape(slot_count, HSEG * STEPS, older_values.shape[-1])
    return jnp.concatenate([earlier, newest_values], axis=1)


def delayed_inputs(history, slot_ids, delay_bins, fractions):
    history_length = history.shape[1]

    def one_tile(slot_id, delay_bin, fraction):
        source_rows = jnp.take(history, slot_id, axis=0)
        window = lax.dynamic_slice_in_dim(source_rows, (history_length - delay_bin - 1).astype(jnp.int32), STEPS + 1, 0)
        return ((1.0 - fraction) * window[1:] + fraction * window[:-1]).astype(jnp.bfloat16)

    return jax.vmap(one_tile)(slot_ids, delay_bins, fractions)


def integrate(state, forcing):
    def advance(current, inflow):
        excite, inhibit = current
        excite_next = excite + excite_rate * (-excite + jax.nn.sigmoid(excite_excite * excite - inhibit_excite * inhibit + inflow - excite_offset))
        inhibit_next = inhibit + inhibit_rate * (-inhibit + jax.nn.sigmoid(excite_inhibit * excite - inhibit_inhibit * inhibit - inhibit_offset))
        return (excite_next, inhibit_next), excite_next

    (excite, inhibit), samples = lax.scan(advance, (state[0], state[1]), forcing)
    return jnp.stack([excite, inhibit]), samples


def expand_segments(coefs, table):
    return jnp.einsum('...kn,km->...mn', coefs.astype(jnp.float32), table, precision=lax.Precision.HIGHEST)


def reference(fresh_coefs, older_coefs, state, lesion, stim_nodes, stim_wave, read_blocks, tract_slot, tract_target, tract_delay, tract_frac, tract_weights):
    table = lax.optimization_barrier(basis_table(K, STEPS).astype(jnp.bfloat16)).astype(jnp.float32)
    device_count = N_WIDE * N_NARROW
    target_count = OWN_BLK * N_NARROW
    owners_all = fresh_coefs.reshape(N_WIDE, N_NARROW, OWN_BLK, K, BLK)
    narrow_ids = jnp.tile(jnp.arange(N_NARROW, dtype=jnp.int32), N_WIDE)

    def device_partial(inputs):
        narrow_id, reads, older, slot_ids, targets, delay_bins, fractions, weights = inputs
        owned = jnp.take(owners_all, narrow_id, axis=1).reshape(N_WIDE * OWN_BLK, K, BLK)
        flat = (jnp.arange(N_WIDE, dtype=jnp.int32)[:, None] * OWN_BLK + jnp.maximum(reads, 0)).reshape(-1)
        newest = jnp.take(owned, flat, axis=0)
        history = join_history(expand_segments(older, table), expand_segments(newest, table))
        delayed = delayed_inputs(history, slot_ids, delay_bins, fractions)
        contrib = jnp.einsum('tjs,tqs->tjq', delayed.astype(jnp.float32), weights.astype(jnp.float32), precision=lax.Precision.HIGHEST)
        return jax.ops.segment_sum(contrib, targets, num_segments=target_count)

    partials = lax.map(device_partial, (
        narrow_ids,
        read_blocks.reshape(device_count, N_WIDE, CAP),
        older_coefs.reshape(device_count, SLOTS, HSEG, K, BLK),
        tract_slot.reshape(device_count, TILES),
        tract_target.reshape(device_count, TILES),
        tract_delay.reshape(device_count, TILES),
        tract_frac.reshape(device_count, TILES),
        tract_weights.reshape(device_count, TILES, BLK, BLK)))
    coupling = partials.reshape(N_WIDE, N_NARROW, target_count, STEPS, BLK).sum(axis=1).reshape(NBLK, STEPS, BLK)
    inflow = coupling.transpose(1, 0, 2).reshape(STEPS, NODES)
    counts = jnp.zeros((NODES,), jnp.float32).at[stim_nodes].add(1.0)
    forcing = tract_gain * inflow * (1.0 - lesion.astype(jnp.float32))[None, :] + stim_wave[:, None] * counts[None, :]
    final_state, samples = integrate(state, forcing)
    fitted = jnp.dot(fit_table(K, STEPS), samples, precision=lax.Precision.HIGHEST)
    new_coefs = fitted.reshape(K, NBLK, BLK).transpose(1, 0, 2).astype(jnp.bfloat16)
    return new_coefs, final_state
```

```python
import functools

import jax
import jax.numpy as jnp
import ml_dtypes
import numpy as np
from jax import lax
from jax.experimental import pallas as pl
from jax.experimental.pallas import tpu as pltpu
from jax.sharding import PartitionSpec as P

STEPS = 32
HSEG = 2
SEGS = HSEG + 1
LENGTH = SEGS * STEPS
GROUP = 4

excite_rate = 0.1
inhibit_rate = 0.05
excite_excite = 1.5
inhibit_excite = 2.0
excite_inhibit = 2.0
inhibit_inhibit = 0.5
excite_offset = 0.5
inhibit_offset = 0.5
tract_gain = 2.0

SMEM = pltpu.SMEM
VMEM = pltpu.VMEM
smem_spec = pl.BlockSpec(memory_space=SMEM)
vmem_spec = pl.BlockSpec(memory_space=VMEM)
any_spec = pl.BlockSpec(memory_space=pl.ANY)


def basis_table(coef_count, step_count):
    order = np.arange(coef_count, dtype=np.float32)[:, None]
    places = np.arange(step_count, dtype=np.float32)[None, :]
    angles = np.float32(np.pi) * (step_count - places - np.float32(0.5)) / np.float32(step_count)
    return np.cos((order * angles).astype(np.float64)).astype(np.float32)


def expand_table(coef_count):
    basis = basis_table(coef_count, STEPS).astype(ml_dtypes.bfloat16)
    table = np.zeros((LENGTH, SEGS * coef_count), ml_dtypes.bfloat16)
    for seg in range(SEGS):
        table[seg * STEPS : (seg + 1) * STEPS, seg * coef_count : (seg + 1) * coef_count] = basis.T
    return table


def fit_tables(coef_count):
    scales = np.where(np.arange(coef_count)[:, None] == 0, 1.0, 2.0) / STEPS
    fit = (basis_table(coef_count, STEPS) * scales).astype(np.float32)
    whole = np.zeros((GROUP * coef_count, GROUP * STEPS), np.float32)
    for g in range(GROUP):
        whole[g * coef_count : (g + 1) * coef_count, g * STEPS : (g + 1) * STEPS] = fit
    high = whole.astype(ml_dtypes.bfloat16)
    low = (whole - high.astype(np.float32)).astype(ml_dtypes.bfloat16)
    return high, low


def pick_kernel(place_ref, own_reads, *refs, capacity, peers):
    asked = (own_reads,) + refs[: peers - 1]
    fresh = refs[peers - 1]
    outs = refs[peers : 2 * peers]
    sems = refs[2 * peers]
    place = place_ref[0]
    copies = []
    for r in range(peers):
        for c in range(capacity):
            block = jnp.maximum(asked[r][c, place], 0)
            copy = pltpu.make_async_copy(fresh.at[block], outs[r].at[c], sems.at[r, c])
            copy.start()
            copies.append(copy)
    for copy in copies:
        copy.wait()


def list_kernel(target_ref, compact_ref, ids_ref, seen, counts, *, peers, own_blocks, peer_targets):
    tile_count = target_ref.shape[1]

    @pl.loop(0, peers * own_blocks)
    def _(g):
        seen[g] = -1

    for p in range(peers):
        counts[p] = 0

    @pl.loop(0, tile_count)
    def _(t):
        target = target_ref[0, t]
        known = seen[target]
        peer = target // own_blocks
        rank = counts[peer]
        number = jnp.where(known < 0, peer * peer_targets + rank, known)
        counts[peer] = rank + jnp.where(known < 0, 1, 0)
        seen[target] = number
        compact_ref[0, t] = number
        ids_ref[0, number] = target - peer * own_blocks


def tract_kernel(
    place_ref, slot_ref, delay_ref, frac_ref, compact_ref, table_ref, older_ref, weights_ref, *refs,
    wide_peers, narrow_peers, capacity, peer_targets, unroll,
):
    news = refs[:wide_peers]
    outs = refs[wide_peers : wide_peers + narrow_peers]
    hist, total = refs[wide_peers + narrow_peers :]
    tile_count = slot_ref.shape[1]
    wide_place = place_ref[0]
    narrow_place = place_ref[1]
    table = table_ref[...]
    for r in range(wide_peers):
        owner = wide_place ^ r
        for c in range(capacity):
            slot = owner * capacity + c
            segments = [older_ref[slot, h] for h in range(HSEG - 1, -1, -1)] + [news[r][c]]
            coefs = jnp.concatenate(segments, axis=0)
            values = jnp.dot(table, coefs, preferred_element_type=jnp.float32)
            hist[pl.ds(pl.multiple_of(slot * LENGTH, 8), LENGTH), :] = values
    total[...] = jnp.zeros_like(total)

    @pl.loop(0, tile_count // unroll)
    def _(step):
        sums = []
        for u in range(unroll):
            t = step * unroll + u
            fraction = frac_ref[0, t]
            start = slot_ref[0, t] * LENGTH + LENGTH - 1 - delay_ref[0, t]
            earlier = hist[pl.ds(start, STEPS), :]
            later = hist[pl.ds(start + 1, STEPS), :]
            delayed = ((1.0 - fraction) * later + fraction * earlier).astype(jnp.bfloat16)
            sums.append(
                lax.dot_general(
                    delayed, weights_ref[t], (((1,), (1,)), ((), ())),
                    preferred_element_type=jnp.float32,
                )
            )
        for u in range(unroll):
            t = step * unroll + u
            rows = pl.ds(pl.multiple_of(compact_ref[0, t] * STEPS, 8), STEPS)
            total[rows, :] += sums[u]

    span = peer_targets * STEPS
    for r in range(narrow_peers):
        first = pl.multiple_of((narrow_place ^ r) * span, 8)
        outs[r][...] = total[pl.ds(first, span), :].astype(jnp.bfloat16)


def window_kernel(
    place_ref, stim_ref, wave_ref, *refs, narrow_peers, own_blocks, peer_targets, coef_count
):
    ids = refs[:narrow_peers]
    sums = refs[narrow_peers : 2 * narrow_peers]
    state_ref, lesion_ref, high_ref, low_ref, coefs_out, state_out = refs[
        2 * narrow_peers : 2 * narrow_peers + 6
    ]
    inflow, samples, rates = refs[2 * narrow_peers + 6 :]
    block_rows = lesion_ref.shape[1]
    narrow_place = place_ref[1]
    first_node = (place_ref[0] * narrow_peers + narrow_place) * (own_blocks * block_rows)

    inflow[...] = jnp.zeros_like(inflow)
    for r in range(narrow_peers):
        for i in range(peer_targets):
            target = ids[r][0, narrow_place * peer_targets + i]
            rows = pl.ds(pl.multiple_of(target * STEPS, 8), STEPS)
            inflow[rows, :] += sums[r][i * STEPS : (i + 1) * STEPS, :].astype(jnp.float32)

    for b in range(own_blocks):
        piece = state_ref[:, b * block_rows : (b + 1) * block_rows]
        rates[0, b : b + 1, :] = piece[0:1, :]
        rates[1, b : b + 1, :] = piece[1:2, :]

    shape = (own_blocks, block_rows)
    nodes = (
        first_node
        + lax.broadcasted_iota(jnp.int32, shape, 0) * block_rows
        + lax.broadcasted_iota(jnp.int32, shape, 1)
    )
    counts = jnp.zeros(shape, jnp.float32)
    for n in range(stim_ref.shape[0]):
        counts = counts + jnp.where(nodes == stim_ref[n], 1.0, 0.0)
    gain = tract_gain * (1.0 - lesion_ref[...].astype(jnp.float32))
    excite = rates[0]
    inhibit = rates[1]
    for j in range(STEPS):
        arriving = inflow[pl.ds(j, own_blocks, stride=STEPS), :]
        forcing = gain * arriving + wave_ref[j] * counts
        excite_drive = excite_excite * excite - inhibit_excite * inhibit + forcing - excite_offset
        inhibit_drive = excite_inhibit * excite - inhibit_inhibit * inhibit - inhibit_offset
        excite, inhibit = (
            excite + excite_rate * (0.5 * jnp.tanh(0.5 * excite_drive) + 0.5 - excite),
            inhibit + inhibit_rate * (0.5 * jnp.tanh(0.5 * inhibit_drive) + 0.5 - inhibit),
        )
        samples[pl.ds(j, own_blocks, stride=STEPS), :] = excite
    rates[0] = excite
    rates[1] = inhibit
    for b in range(own_blocks):
        columns = slice(b * block_rows, (b + 1) * block_rows)
        state_out[0:1, columns] = rates[0, b : b + 1, :]
        state_out[1:2, columns] = rates[1, b : b + 1, :]

    high = high_ref[...]
    low = low_ref[...]
    rows = GROUP * STEPS
    for g in range(own_blocks // GROUP):
        part = samples[g * rows : (g + 1) * rows, :]
        part_high = part.astype(jnp.bfloat16)
        part_low = (part - part_high.astype(jnp.float32)).astype(jnp.bfloat16)
        fitted = (
            jnp.dot(high, part_high, preferred_element_type=jnp.float32)
            + jnp.dot(high, part_low, preferred_element_type=jnp.float32)
            + jnp.dot(low, part_high, preferred_element_type=jnp.float32)
        )
        coefs_out[g * GROUP : (g + 1) * GROUP] = fitted.astype(jnp.bfloat16).reshape(
            GROUP, coef_count, block_rows
        )


def local(
    fresh_coefs,
    older_coefs,
    state,
    lesion,
    stim_nodes,
    stim_wave,
    read_blocks,
    tract_slot,
    tract_target,
    tract_delay,
    tract_frac,
    tract_weights,
):
    wide_peers = lax.axis_size("wide")
    narrow_peers = lax.axis_size("narrow")
    own_blocks, coef_count, block_rows = fresh_coefs.shape
    capacity = read_blocks.shape[3]
    slot_count = wide_peers * capacity
    tile_count = tract_slot.shape[2]
    peer_targets = tile_count // (2 * narrow_peers)
    target_count = narrow_peers * own_blocks

    def swap(x, axis, peers, r):
        return lax.ppermute(x, axis, [(i, i ^ r) for i in range(peers)])

    place = jnp.stack([lax.axis_index("wide"), lax.axis_index("narrow")]).astype(jnp.int32)
    reads = read_blocks.reshape(wide_peers, capacity).T
    asked = [swap(reads, "wide", wide_peers, r) for r in range(1, wide_peers)]

    picked = pl.pallas_call(
        functools.partial(pick_kernel, capacity=capacity, peers=wide_peers),
        out_shape=[
            jax.ShapeDtypeStruct((capacity, coef_count, block_rows), jnp.bfloat16)
        ]
        * wide_peers,
        in_specs=[smem_spec] * (wide_peers + 1) + [any_spec],
        out_specs=[any_spec] * wide_peers,
        scratch_shapes=[pltpu.SemaphoreType.DMA((wide_peers, capacity))],
        name="pick_blocks",
    )(place, reads, *asked, fresh_coefs)

    compact, ids = pl.pallas_call(
        functools.partial(
            list_kernel, peers=narrow_peers, own_blocks=own_blocks, peer_targets=peer_targets
        ),
        out_shape=[
            jax.ShapeDtypeStruct((1, tile_count), jnp.int32),
            jax.ShapeDtypeStruct((1, narrow_peers * peer_targets), jnp.int32),
        ],
        in_specs=[smem_spec],
        out_specs=[smem_spec] * 2,
        scratch_shapes=[SMEM((target_count,), jnp.int32), SMEM((narrow_peers,), jnp.int32)],
        name="list_targets",
    )(tract_target.reshape(1, tile_count))
    ids_by_peer = [ids] + [swap(ids, "narrow", narrow_peers, r) for r in range(1, narrow_peers)]

    news = [picked[0]] + [
        swap(picked[r], "wide", wide_peers, r) for r in range(1, wide_peers)
    ]

    span = peer_targets * STEPS
    shares = pl.pallas_call(
        functools.partial(
            tract_kernel,
            wide_peers=wide_peers,
            narrow_peers=narrow_peers,
            capacity=capacity,
            peer_targets=peer_targets,
            unroll=16,
        ),
        out_shape=[jax.ShapeDtypeStruct((span, block_rows), jnp.bfloat16)] * narrow_peers,
        in_specs=[smem_spec] * 5 + [vmem_spec] * (3 + wide_peers),
        out_specs=[vmem_spec] * narrow_peers,
        scratch_shapes=[
            VMEM((slot_count * LENGTH, block_rows), jnp.float32),
            VMEM((narrow_peers * span, block_rows), jnp.float32),
        ],
        compiler_params=pltpu.CompilerParams(vmem_limit_bytes=24 << 20),
        name="tract_tiles",
    )(
        place,
        tract_slot.reshape(1, tile_count),
        tract_delay.reshape(1, tile_count),
        tract_frac.reshape(1, tile_count),
        compact,
        expand_table(coef_count),
        older_coefs.reshape(slot_count, HSEG, coef_count, block_rows),
        tract_weights.reshape(tile_count, block_rows, block_rows),
        *news,
    )
    sums = [shares[0]] + [
        swap(shares[r], "narrow", narrow_peers, r) for r in range(1, narrow_peers)
    ]

    high, low = fit_tables(coef_count)
    new_coefs, final_state = pl.pallas_call(
        functools.partial(
            window_kernel,
            narrow_peers=narrow_peers,
            own_blocks=own_blocks,
            peer_targets=peer_targets,
            coef_count=coef_count,
        ),
        out_shape=[
            jax.ShapeDtypeStruct(fresh_coefs.shape, jnp.bfloat16),
            jax.ShapeDtypeStruct(state.shape, jnp.float32),
        ],
        in_specs=[smem_spec] * (3 + narrow_peers) + [vmem_spec] * (narrow_peers + 4),
        out_specs=[vmem_spec] * 2,
        scratch_shapes=[
            VMEM((own_blocks * STEPS, block_rows), jnp.float32),
            VMEM((own_blocks * STEPS, block_rows), jnp.float32),
            VMEM((2, own_blocks, block_rows), jnp.float32),
        ],
        compiler_params=pltpu.CompilerParams(vmem_limit_bytes=24 << 20),
        name="window_steps",
    )(
        place,
        stim_nodes,
        stim_wave,
        *ids_by_peer,
        *sums,
        state,
        lesion.reshape(own_blocks, block_rows),
        high,
        low,
    )
    return new_coefs, final_state


def solution(mesh):
    in_specs = (
        P(("sweep", "wide", "narrow"), None, None),
        P(("sweep", "wide"), "narrow", None, None, None, None),
        P(None, ("sweep", "wide", "narrow")),
        P(("sweep", "wide", "narrow")),
        P("sweep"),
        P("sweep"),
        P("wide", "narrow", None, None),
        P("wide", "narrow", None),
        P("wide", "narrow", None),
        P("wide", "narrow", None),
        P("wide", "narrow", None),
        P("wide", "narrow", None, None, None),
    )
    out_specs = (P(("sweep", "wide", "narrow"), None, None), P(None, ("sweep", "wide", "narrow")))
    return jax.shard_map(local, mesh=mesh, in_specs=in_specs, out_specs=out_specs, check_vma=False)
```

```python
import functools
import math

import jax
import jax.numpy as jnp
import ml_dtypes
import numpy as np
from jax import lax
from jax.experimental import pallas as pl
from jax.experimental.pallas import tpu as pltpu
from jax.sharding import PartitionSpec as P

STEPS = 32
HSEG = 2
SEGS = HSEG + 1
LENGTH = SEGS * STEPS
GROUP = 4
HEAD = 16
UNROLL = 16

excite_rate = 0.1
inhibit_rate = 0.05
excite_excite = 1.5
inhibit_excite = 2.0
excite_inhibit = 2.0
inhibit_inhibit = 0.5
excite_offset = 0.5
inhibit_offset = 0.5
tract_gain = 2.0

SMEM = pltpu.SMEM
VMEM = pltpu.VMEM
smem_spec = pl.BlockSpec(memory_space=SMEM)
vmem_spec = pl.BlockSpec(memory_space=VMEM)
hbm_spec = pl.BlockSpec(memory_space=pltpu.HBM)


def basis_table(coef_count, step_count):
    order = np.arange(coef_count, dtype=np.float32)[:, None]
    places = np.arange(step_count, dtype=np.float32)[None, :]
    angles = np.float32(np.pi) * (step_count - places - np.float32(0.5)) / np.float32(step_count)
    return np.cos((order * angles).astype(np.float64)).astype(np.float32)


def expand_table(coef_count):
    basis = basis_table(coef_count, STEPS).astype(ml_dtypes.bfloat16)
    table = np.zeros((LENGTH, SEGS * coef_count), ml_dtypes.bfloat16)
    for seg in range(SEGS):
        table[seg * STEPS : (seg + 1) * STEPS, seg * coef_count : (seg + 1) * coef_count] = basis.T
    return table


def fit_tables(coef_count):
    scales = np.where(np.arange(coef_count)[:, None] == 0, 1.0, 2.0) / STEPS
    fit = (basis_table(coef_count, STEPS) * scales).astype(np.float32)
    whole = np.zeros((GROUP * coef_count, GROUP * STEPS), np.float32)
    for g in range(GROUP):
        whole[g * coef_count : (g + 1) * coef_count, g * STEPS : (g + 1) * STEPS] = fit
    high = whole.astype(ml_dtypes.bfloat16)
    low = (whole - high.astype(np.float32)).astype(ml_dtypes.bfloat16)
    return high, low


def steps_together(peer_targets):
    return 16 // math.gcd(16, peer_targets)


def lane_tables(peers, peer_targets, own_blocks):
    together = steps_together(peer_targets)
    width = together * peer_targets
    assert together * own_blocks <= 256 and peers * width <= HEAD * 128
    lane = np.arange(HEAD * 128)
    used = lane < peers * width
    within = lane % width
    rank = np.where(used, within % peer_targets, -5)
    offset = within // peer_targets * own_blocks + 1
    place = np.where(used, lane // width, -5)
    return np.stack([rank, offset, place]).astype(np.float32).reshape(3, HEAD, 128)


def pick_kernel(asked_ref, fresh_ref, out_ref, asked, asked_sem, sems, *, capacity, peers):
    asked_copy = pltpu.make_async_copy(asked_ref, asked, asked_sem)
    asked_copy.start()
    asked_copy.wait()
    copies = [
        pltpu.make_async_copy(
            fresh_ref.at[jnp.maximum(asked[reader, c], 0)],
            out_ref.at[reader, c],
            sems.at[reader, c],
        )
        for reader in range(peers)
        for c in range(capacity)
    ]
    for copy in copies:
        copy.start()
    for copy in copies:
        copy.wait()


def list_kernel(
    place_ref, target_ref, lanes_ref, rows_ref, head_ref, *, peers, own_blocks, peer_targets
):
    place = place_ref[1].astype(jnp.float32)
    shape = (own_blocks, 128)
    block = lax.broadcasted_iota(jnp.int32, shape, 0)
    peer = lax.broadcasted_iota(jnp.int32, shape, 1)
    number = peer * own_blocks + block
    present = number == target_ref[0, 0]
    for t in range(1, target_ref.shape[1]):
        present = present | (number == target_ref[0, t])
    below = (
        lax.broadcasted_iota(jnp.int32, (own_blocks, own_blocks), 0)
        > lax.broadcasted_iota(jnp.int32, (own_blocks, own_blocks), 1)
    ).astype(jnp.float32).astype(jnp.bfloat16)
    held = present.astype(jnp.float32)
    rank = jnp.dot(below, held.astype(jnp.bfloat16), preferred_element_type=jnp.float32)
    rows_ref[...] = peer * (peer_targets * STEPS) + rank.astype(jnp.int32)
    rank = jnp.where(present, rank, -1.0)
    block = block.astype(jnp.float32)
    for p in range(peers):
        column = jnp.broadcast_to(rank[:, p : p + 1], shape)
        head_ref[p] = jnp.zeros((HEAD, 128), jnp.float32)
        for h in range(pl.cdiv(peers * steps_together(peer_targets) * peer_targets, 128)):
            match = column == lanes_ref[0, h : h + 1, :]
            ids = jnp.sum(jnp.where(match, block, 0.0), axis=0, keepdims=True)
            mine = lanes_ref[2, h : h + 1, :] == place
            head_ref[p, h : h + 1, :] = jnp.where(mine, ids + lanes_ref[1, h : h + 1, :], 0.0)


def tract_kernel(
    slot_hbm, target_hbm, delay_hbm, frac_hbm, rows_ref, head_ref, table_ref, older_hbm,
    weights_hbm, news_ref, out_ref,
    slot, target, delay, frac, rows, older, weights, hist, total, small_sem, older_sem, sems,
    *, peers, own_blocks, peer_targets,
):
    tile_count = slot_hbm.shape[1]
    slot_count = older.shape[0]
    turns = tile_count // UNROLL
    copies = [
        pltpu.make_async_copy(source, into, small_sem.at[i])
        for i, (source, into) in enumerate(
            [(slot_hbm, slot), (target_hbm, target), (delay_hbm, delay), (frac_hbm, frac),
             (rows_ref, rows)]
        )
    ]
    older_copy = pltpu.make_async_copy(older_hbm, older, older_sem)
    older_copy.start()
    for copy in copies:
        copy.start()

    def weights_copy(turn):
        part = pl.ds(turn * UNROLL, UNROLL)
        return pltpu.make_async_copy(weights_hbm.at[part], weights.at[part], sems.at[turn])

    for turn in range(turns):
        weights_copy(turn).start()
    total[...] = jnp.zeros_like(total)
    older_copy.wait()
    table = table_ref[...]
    for s in range(slot_count):
        segments = [older[s, h] for h in range(HSEG - 1, -1, -1)] + [news_ref[s]]
        values = jnp.dot(
            table, jnp.concatenate(segments, axis=0), preferred_element_type=jnp.float32
        )
        hist[s * LENGTH : (s + 1) * LENGTH, :] = values
    for copy in copies:
        copy.wait()

    @pl.loop(0, turns)
    def _(turn):
        weights_copy(turn).wait()
        sums = []
        for u in range(UNROLL):
            t = turn * UNROLL + u
            fraction = frac[0, t]
            start = slot[0, t] * LENGTH + LENGTH - 1 - delay[0, t]
            earlier = hist[pl.ds(start, STEPS), :]
            later = hist[pl.ds(start + 1, STEPS), :]
            delayed = ((1.0 - fraction) * later + fraction * earlier).astype(jnp.bfloat16)
            sums.append(
                lax.dot_general(
                    delayed, weights[t], (((1,), (1,)), ((), ())),
                    preferred_element_type=jnp.float32,
                )
            )
        for u in range(UNROLL):
            aim = target[0, turn * UNROLL + u]
            first = rows[lax.rem(aim, own_blocks), lax.div(aim, own_blocks)]
            where = pl.ds(first, STEPS, stride=peer_targets)
            total[where, :] += sums[u]

    span = peer_targets * STEPS
    for p in range(peers):
        out_ref[p, :span, :] = total[p * span : (p + 1) * span, :].astype(jnp.bfloat16)
        out_ref[p, span:, :] = head_ref[p].astype(jnp.bfloat16)


def window_kernel(
    place_ref, stim_ref, wave_ref, shares_ref, state_ref, lesion_ref, high_ref, low_ref,
    coefs_out, state_out, samples, rates,
    *, peers, own_blocks, peer_targets, coef_count,
):
    block_rows = lesion_ref.shape[1]
    first_node = (place_ref[0] * peers + place_ref[1]) * (own_blocks * block_rows)
    together = steps_together(peer_targets)
    width = together * peer_targets
    span = peer_targets * STEPS

    head = shares_ref[0, span:, :].astype(jnp.float32)
    for p in range(1, peers):
        head = head + shares_ref[p, span:, :].astype(jnp.float32)
    row = lax.broadcasted_iota(jnp.int32, (together * own_blocks, 128), 0).astype(jnp.float32) + 1.0
    columns = peers * width
    scatter = jnp.concatenate(
        [
            jnp.where(row == head[h : h + 1, :], 1.0, 0.0).astype(jnp.bfloat16)
            for h in range(pl.cdiv(columns, 128))
        ],
        axis=1,
    )[:, :columns]

    for b in range(own_blocks):
        piece = state_ref[:, b * block_rows : (b + 1) * block_rows]
        rates[0, b : b + 1, :] = piece[0:1, :]
        rates[1, b : b + 1, :] = piece[1:2, :]

    shape = (own_blocks, block_rows)
    nodes = (
        first_node
        + lax.broadcasted_iota(jnp.int32, shape, 0) * block_rows
        + lax.broadcasted_iota(jnp.int32, shape, 1)
    )
    counts = jnp.zeros(shape, jnp.float32)
    for n in range(stim_ref.shape[0]):
        counts = counts + jnp.where(nodes == stim_ref[n], 1.0, 0.0)
    gain = tract_gain * (1.0 - lesion_ref[...].astype(jnp.float32))
    excite = rates[0]
    inhibit = rates[1]
    for g in range(STEPS // together):
        arrived = jnp.concatenate(
            [shares_ref[p, g * width : (g + 1) * width, :] for p in range(peers)], axis=0
        )
        inflow = jnp.dot(scatter, arrived, preferred_element_type=jnp.float32)
        for jj in range(together):
            j = g * together + jj
            forcing = gain * inflow[jj * own_blocks : (jj + 1) * own_blocks] + wave_ref[j] * counts
            excite_drive = (
                excite_excite * excite - inhibit_excite * inhibit + forcing - excite_offset
            )
            inhibit_drive = excite_inhibit * excite - inhibit_inhibit * inhibit - inhibit_offset
            excite, inhibit = (
                excite + excite_rate * (0.5 * jnp.tanh(0.5 * excite_drive) + 0.5 - excite),
                inhibit + inhibit_rate * (0.5 * jnp.tanh(0.5 * inhibit_drive) + 0.5 - inhibit),
            )
            samples[pl.ds(j, own_blocks, stride=STEPS), :] = excite
    rates[0] = excite
    rates[1] = inhibit
    for b in range(own_blocks):
        where = slice(b * block_rows, (b + 1) * block_rows)
        state_out[0:1, where] = rates[0, b : b + 1, :]
        state_out[1:2, where] = rates[1, b : b + 1, :]

    high = high_ref[...]
    low = low_ref[...]
    rows = GROUP * STEPS
    for g in range(own_blocks // GROUP):
        part = samples[g * rows : (g + 1) * rows, :]
        part_high = part.astype(jnp.bfloat16)
        part_low = (part - part_high.astype(jnp.float32)).astype(jnp.bfloat16)
        fitted = (
            jnp.dot(high, part_high, preferred_element_type=jnp.float32)
            + jnp.dot(high, part_low, preferred_element_type=jnp.float32)
            + jnp.dot(low, part_high, preferred_element_type=jnp.float32)
        )
        coefs_out[g * GROUP : (g + 1) * GROUP] = fitted.astype(jnp.bfloat16).reshape(
            GROUP, coef_count, block_rows
        )


def local(
    fresh_coefs,
    older_coefs,
    state,
    lesion,
    stim_nodes,
    stim_wave,
    read_blocks,
    tract_slot,
    tract_target,
    tract_delay,
    tract_frac,
    tract_weights,
):
    wide_peers = lax.axis_size("wide")
    peers = lax.axis_size("narrow")
    own_blocks, coef_count, block_rows = fresh_coefs.shape
    capacity = read_blocks.shape[3]
    slot_count = wide_peers * capacity
    tile_count = tract_slot.shape[2]
    peer_targets = tile_count // (2 * peers)
    share_rows = peer_targets * STEPS + HEAD

    place = jnp.stack([lax.axis_index("wide"), lax.axis_index("narrow")]).astype(jnp.int32)
    asked = lax.all_to_all(
        read_blocks.reshape(wide_peers, capacity), "wide", 0, 0, tiled=True
    )
    picked = pl.pallas_call(
        functools.partial(pick_kernel, capacity=capacity, peers=wide_peers),
        out_shape=jax.ShapeDtypeStruct(
            (wide_peers, capacity, coef_count, block_rows), jnp.bfloat16
        ),
        in_specs=[hbm_spec] * 2,
        out_specs=hbm_spec,
        scratch_shapes=[
            SMEM((wide_peers, capacity), jnp.int32),
            pltpu.SemaphoreType.DMA,
            pltpu.SemaphoreType.DMA((wide_peers, capacity)),
        ],
        compiler_params=pltpu.CompilerParams(vmem_limit_bytes=60 << 20),
        name="pick_blocks",
    )(asked, fresh_coefs)
    news = lax.all_to_all(picked, "wide", 0, 0, tiled=True)

    targets = tract_target.reshape(1, tile_count)
    rows, heads = pl.pallas_call(
        functools.partial(
            list_kernel, peers=peers, own_blocks=own_blocks, peer_targets=peer_targets
        ),
        out_shape=[
            jax.ShapeDtypeStruct((own_blocks, 128), jnp.int32),
            jax.ShapeDtypeStruct((peers, HEAD, 128), jnp.float32),
        ],
        in_specs=[smem_spec] * 2 + [vmem_spec],
        out_specs=[vmem_spec] * 2,
        compiler_params=pltpu.CompilerParams(vmem_limit_bytes=60 << 20),
        name="list_targets",
    )(place, targets, lane_tables(peers, peer_targets, own_blocks))

    shares = pl.pallas_call(
        functools.partial(
            tract_kernel, peers=peers, own_blocks=own_blocks, peer_targets=peer_targets
        ),
        out_shape=jax.ShapeDtypeStruct((peers, share_rows, block_rows), jnp.bfloat16),
        in_specs=[hbm_spec] * 5 + [vmem_spec] * 2 + [hbm_spec] * 2 + [vmem_spec],
        out_specs=vmem_spec,
        scratch_shapes=[
            SMEM((1, tile_count), jnp.int32),
            SMEM((1, tile_count), jnp.int32),
            SMEM((1, tile_count), jnp.int32),
            SMEM((1, tile_count), jnp.float32),
            SMEM((own_blocks, 128), jnp.int32),
            VMEM((slot_count, HSEG, coef_count, block_rows), jnp.bfloat16),
            VMEM((tile_count, block_rows, block_rows), jnp.bfloat16),
            VMEM((slot_count * LENGTH, block_rows), jnp.float32),
            VMEM((peers * peer_targets * STEPS, block_rows), jnp.float32),
            pltpu.SemaphoreType.DMA((5,)),
            pltpu.SemaphoreType.DMA,
            pltpu.SemaphoreType.DMA((tile_count // UNROLL,)),
        ],
        compiler_params=pltpu.CompilerParams(vmem_limit_bytes=60 << 20),
        name="tract_tiles",
    )(
        tract_slot.reshape(1, tile_count),
        targets,
        tract_delay.reshape(1, tile_count),
        tract_frac.reshape(1, tile_count),
        rows,
        heads,
        expand_table(coef_count),
        older_coefs.reshape(slot_count, HSEG, coef_count, block_rows),
        tract_weights.reshape(tile_count, block_rows, block_rows),
        news.reshape(slot_count, coef_count, block_rows),
    )
    arrived = lax.all_to_all(shares, "narrow", 0, 0, tiled=True)

    high, low = fit_tables(coef_count)
    new_coefs, final_state = pl.pallas_call(
        functools.partial(
            window_kernel,
            peers=peers,
            own_blocks=own_blocks,
            peer_targets=peer_targets,
            coef_count=coef_count,
        ),
        out_shape=[
            jax.ShapeDtypeStruct(fresh_coefs.shape, jnp.bfloat16),
            jax.ShapeDtypeStruct(state.shape, jnp.float32),
        ],
        in_specs=[smem_spec] * 3 + [vmem_spec] * 5,
        out_specs=[vmem_spec] * 2,
        scratch_shapes=[
            VMEM((own_blocks * STEPS, block_rows), jnp.float32),
            VMEM((2, own_blocks, block_rows), jnp.float32),
        ],
        compiler_params=pltpu.CompilerParams(vmem_limit_bytes=16 << 20),
        name="window_steps",
    )(
        place,
        stim_nodes,
        stim_wave,
        arrived,
        state,
        lesion.reshape(own_blocks, block_rows),
        high,
        low,
    )
    return new_coefs, final_state


def solution(mesh):
    in_specs = (
        P(("sweep", "wide", "narrow"), None, None),
        P(("sweep", "wide"), "narrow", None, None, None, None),
        P(None, ("sweep", "wide", "narrow")),
        P(("sweep", "wide", "narrow")),
        P("sweep"),
        P("sweep"),
        P("wide", "narrow", None, None),
        P("wide", "narrow", None),
        P("wide", "narrow", None),
        P("wide", "narrow", None),
        P("wide", "narrow", None),
        P("wide", "narrow", None, None, None),
    )
    out_specs = (P(("sweep", "wide", "narrow"), None, None), P(None, ("sweep", "wide", "narrow")))
    return jax.shard_map(local, mesh=mesh, in_specs=in_specs, out_specs=out_specs, check_vma=False)
```

```python
import functools
import math

import jax
import jax.numpy as jnp
import ml_dtypes
import numpy as np
from jax import lax
from jax.experimental import pallas as pl
from jax.experimental.pallas import tpu as pltpu
from jax.sharding import PartitionSpec as P

STEPS = 32
HSEG = 2
SEGS = HSEG + 1
LENGTH = SEGS * STEPS
GROUP = 4
HEAD = 16
UNROLL = 16

excite_rate = 0.1
inhibit_rate = 0.05
excite_excite = 1.5
inhibit_excite = 2.0
excite_inhibit = 2.0
inhibit_inhibit = 0.5
excite_offset = 0.5
inhibit_offset = 0.5
tract_gain = 2.0

SMEM = pltpu.SMEM
VMEM = pltpu.VMEM
vmem_spec = pl.BlockSpec(memory_space=VMEM)
hbm_spec = pl.BlockSpec(memory_space=pltpu.HBM)


def basis_table(coef_count, step_count):
    order = np.arange(coef_count, dtype=np.float32)[:, None]
    places = np.arange(step_count, dtype=np.float32)[None, :]
    angles = np.float32(np.pi) * (step_count - places - np.float32(0.5)) / np.float32(step_count)
    return np.cos((order * angles).astype(np.float64)).astype(np.float32)


def expand_table(coef_count):
    basis = basis_table(coef_count, STEPS).astype(ml_dtypes.bfloat16)
    table = np.zeros((LENGTH, SEGS * coef_count), ml_dtypes.bfloat16)
    for seg in range(SEGS):
        table[seg * STEPS : (seg + 1) * STEPS, seg * coef_count : (seg + 1) * coef_count] = basis.T
    return table


def fit_tables(coef_count):
    scales = np.where(np.arange(coef_count)[:, None] == 0, 1.0, 2.0) / STEPS
    fit = (basis_table(coef_count, STEPS) * scales).astype(np.float32)
    whole = np.zeros((GROUP * coef_count, GROUP * STEPS), np.float32)
    for g in range(GROUP):
        whole[g * coef_count : (g + 1) * coef_count, g * STEPS : (g + 1) * STEPS] = fit
    high = whole.astype(ml_dtypes.bfloat16)
    low = (whole - high.astype(np.float32)).astype(ml_dtypes.bfloat16)
    return high, low


def steps_together(peer_targets):
    return 16 // math.gcd(16, peer_targets)


def lane_tables(peers, peer_targets, own_blocks):
    together = steps_together(peer_targets)
    width = together * peer_targets
    assert together * own_blocks <= 256 and peers * width <= HEAD * 128
    lane = np.arange(HEAD * 128)
    used = lane < peers * width
    within = lane % width
    rank = np.where(used, within % peer_targets, -5)
    offset = within // peer_targets * own_blocks + 1
    place = np.where(used, lane // width, -5)
    return np.stack([rank, offset, place]).astype(np.float32).reshape(3, HEAD, 128)


def ready_kernel(
    fresh_ref, state_ref, lesion_ref, stim_ref, wave_ref, fresh_out, ready_out, sem,
    *, peers, own_blocks,
):
    copy = pltpu.make_async_copy(fresh_ref, fresh_out, sem)
    copy.start()
    block_rows = lesion_ref.shape[1]
    place = lax.axis_index("wide") * peers + lax.axis_index("narrow")
    for b in range(own_blocks):
        piece = state_ref[:, b * block_rows : (b + 1) * block_rows]
        ready_out[b : b + 1, :] = piece[0:1, :]
        ready_out[own_blocks + b : own_blocks + b + 1, :] = piece[1:2, :]
    ready_out[2 * own_blocks : 3 * own_blocks, :] = tract_gain * (
        1.0 - lesion_ref[...].astype(jnp.float32)
    )
    stim_count = stim_ref.shape[1]
    nodes = stim_ref[...] - place * (own_blocks * block_rows)
    blocks = lax.shift_right_arithmetic(nodes, block_rows.bit_length() - 1)
    offsets = nodes & (block_rows - 1)
    in_block = lax.broadcasted_iota(jnp.int32, (own_blocks, stim_count), 0) == blocks
    at_offset = lax.broadcasted_iota(jnp.int32, (block_rows, stim_count), 0) == offsets
    ready_out[3 * own_blocks : 4 * own_blocks, :] = lax.dot_general(
        in_block.astype(jnp.float32).astype(jnp.bfloat16),
        at_offset.astype(jnp.float32).astype(jnp.bfloat16),
        (((1,), (1,)), ((), ())),
        preferred_element_type=jnp.float32,
    )
    shape = (STEPS, STEPS)
    diagonal = lax.broadcasted_iota(jnp.int32, shape, 0) == lax.broadcasted_iota(jnp.int32, shape, 1)
    column = jnp.sum(jnp.where(diagonal, wave_ref[...], 0.0), axis=1, keepdims=True)
    ready_out[4 * own_blocks :, :] = jnp.broadcast_to(column, (STEPS, block_rows))
    copy.wait()


def pick_kernel(*refs, capacity, peers):
    tables = refs[: peers - 1]
    fresh = refs[peers - 1]
    outs = refs[peers : 2 * peers - 1]
    asked, sems = refs[2 * peers - 1 :]
    place = lax.axis_index("wide")
    copies = [pltpu.make_async_copy(tables[r], asked.at[r], sems.at[r]) for r in range(peers - 1)]
    for copy in copies:
        copy.start()
    for r in range(peers - 1):
        copies[r].wait()
        for c in range(capacity):
            outs[r][c] = fresh[jnp.maximum(asked[r, c, place], 0)]


def tiles_kernel(
    reads_ref, slot_ref, target_ref, delay_ref, lanes_ref, table_ref, older_ref, fresh_ref,
    weights_ref, weights_out, hist_out, tiles_out, head_out, reads, reads_sem, weights_sem,
    *, peers, own_blocks, peer_targets, capacity,
):
    copy = pltpu.make_async_copy(weights_ref, weights_out, weights_sem)
    copy.start()
    reads_copy = pltpu.make_async_copy(reads_ref, reads, reads_sem)
    reads_copy.start()
    tile_count = target_ref.shape[1]
    target_count = peers * own_blocks
    span = peer_targets * STEPS
    place = lax.axis_index("narrow")

    numbers = lax.broadcasted_iota(jnp.int32, (target_count, tile_count), 0)
    hits = (numbers == target_ref[...]).astype(jnp.float32)
    held = jnp.dot(
        hits.astype(jnp.bfloat16), jnp.ones((tile_count, 128), jnp.bfloat16),
        preferred_element_type=jnp.float32,
    )
    held = jnp.minimum(held, 1.0)
    shape = (own_blocks, own_blocks)
    below = (
        lax.broadcasted_iota(jnp.int32, shape, 0) > lax.broadcasted_iota(jnp.int32, shape, 1)
    ).astype(jnp.float32).astype(jnp.bfloat16)
    block = lax.broadcasted_iota(jnp.int32, (own_blocks, 128), 0).astype(jnp.float32)
    first = jnp.zeros((1, tile_count), jnp.float32)
    for p in range(peers):
        part = slice(p * own_blocks, (p + 1) * own_blocks)
        rank = jnp.dot(below, held[part].astype(jnp.bfloat16), preferred_element_type=jnp.float32)
        first = first + jnp.sum(
            hits[part] * (rank[:, :tile_count] + float(p * span)), axis=0, keepdims=True
        )
        rank = jnp.where(held[part] > 0.5, rank, -1.0)
        source = (place ^ p).astype(jnp.float32)
        head_out[p] = jnp.zeros((HEAD, 128), jnp.bfloat16)
        rows = []
        for h in range(pl.cdiv(peers * steps_together(peer_targets) * peer_targets, 128)):
            match = rank == lanes_ref[0, h : h + 1, :]
            ids = jnp.sum(jnp.where(match, block, 0.0), axis=0, keepdims=True)
            mine = lanes_ref[2, h : h + 1, :] == source
            rows.append(jnp.where(mine, ids + lanes_ref[1, h : h + 1, :], 0.0))
        rows.append(jnp.zeros((HEAD - len(rows), 128), jnp.float32))
        head_out[p] = jnp.concatenate(rows, axis=0).astype(jnp.bfloat16)
    tiles_out[0:1, :tile_count] = slot_ref[...] * LENGTH + (LENGTH - 1) - delay_ref[...]
    tiles_out[1:2, :tile_count] = first.astype(jnp.int32)

    table = table_ref[...]
    coef_count = older_ref.shape[2]
    earlier = HSEG * STEPS
    for s in range(older_ref.shape[0]):
        segments = [older_ref[s, h] for h in range(HSEG - 1, -1, -1)]
        hist_out[s * LENGTH : s * LENGTH + earlier, :] = jnp.dot(
            table[:earlier, : HSEG * coef_count], jnp.concatenate(segments, axis=0),
            preferred_element_type=jnp.float32,
        )
    reads_copy.wait()
    owner = lax.axis_index("wide")
    for c in range(capacity):
        rows = pl.ds(pl.multiple_of((owner * capacity + c) * LENGTH + earlier, 8), STEPS)
        hist_out[rows, :] = jnp.dot(
            table[:STEPS, :coef_count], fresh_ref[jnp.maximum(reads[c, owner], 0)],
            preferred_element_type=jnp.float32,
        )
    copy.wait()


def tract_kernel(
    tiles_ref, frac_ref, table_ref, hist_ref, weights, head_ref, *refs,
    wide_peers, peers, capacity, peer_targets,
):
    news = refs[: wide_peers - 1]
    outs = refs[wide_peers - 1 : wide_peers - 1 + peers]
    tiles, frac, hist, total, sems = refs[wide_peers - 1 + peers :]
    tile_count = frac_ref.shape[1]
    owner = lax.axis_index("wide")
    place = lax.axis_index("narrow")
    copies = [
        pltpu.make_async_copy(tiles_ref, tiles, sems.at[0]),
        pltpu.make_async_copy(frac_ref, frac, sems.at[1]),
    ]
    for copy in copies:
        copy.start()
    total[...] = jnp.zeros_like(total)
    hist[...] = hist_ref[...]
    coef_count = news[0].shape[1]
    table = table_ref[:STEPS, :coef_count]
    for r in range(1, wide_peers):
        for c in range(capacity):
            slot = (owner ^ r) * capacity + c
            rows = pl.ds(pl.multiple_of(slot * LENGTH + HSEG * STEPS, 8), STEPS)
            hist[rows, :] = jnp.dot(table, news[r - 1][c], preferred_element_type=jnp.float32)
    for copy in copies:
        copy.wait()

    @pl.loop(0, tile_count // UNROLL)
    def _(turn):
        sums = []
        for u in range(UNROLL):
            t = turn * UNROLL + u
            fraction = frac[0, t]
            start = tiles[0, t]
            earlier = hist[pl.ds(start, STEPS), :]
            later = hist[pl.ds(start + 1, STEPS), :]
            delayed = ((1.0 - fraction) * later + fraction * earlier).astype(jnp.bfloat16)
            sums.append(
                lax.dot_general(
                    delayed, weights[t], (((1,), (1,)), ((), ())),
                    preferred_element_type=jnp.float32,
                )
            )
        for u in range(UNROLL):
            where = pl.ds(tiles[1, turn * UNROLL + u], STEPS, stride=peer_targets)
            total[where, :] += sums[u]

    span = peer_targets * STEPS
    for r in range(peers):
        first = pl.multiple_of((place ^ r) * span, 8)
        outs[r][:span, :] = total[pl.ds(first, span), :].astype(jnp.bfloat16)
        outs[r][span:, :] = head_ref[place ^ r]


def window_kernel(*refs, peers, own_blocks, peer_targets, coef_count):
    shares = refs[:peers]
    ready_ref, high_ref, low_ref, coefs_out, state_out, samples, rates = refs[peers:]
    block_rows = ready_ref.shape[1]
    together = steps_together(peer_targets)
    width = together * peer_targets
    span = peer_targets * STEPS

    head = shares[0][span:, :].astype(jnp.float32)
    for r in range(1, peers):
        head = head + shares[r][span:, :].astype(jnp.float32)
    row = lax.broadcasted_iota(jnp.int32, (together * own_blocks, 128), 0).astype(jnp.float32) + 1.0
    columns = peers * width
    scatter = jnp.concatenate(
        [
            jnp.where(row == head[h : h + 1, :], 1.0, 0.0).astype(jnp.bfloat16)
            for h in range(pl.cdiv(columns, 128))
        ],
        axis=1,
    )[:, :columns]

    excite, inhibit, gain, counts = [
        ready_ref[i * own_blocks : (i + 1) * own_blocks, :] for i in range(4)
    ]
    for g in range(STEPS // together):
        arrived = jnp.concatenate(
            [shares[r][g * width : (g + 1) * width, :] for r in range(peers)], axis=0
        )
        inflow = jnp.dot(scatter, arrived, preferred_element_type=jnp.float32)
        for jj in range(together):
            j = g * together + jj
            wave = ready_ref[4 * own_blocks + j : 4 * own_blocks + j + 1, :]
            forcing = gain * inflow[jj * own_blocks : (jj + 1) * own_blocks] + wave * counts
            excite_drive = (
                excite_excite * excite - inhibit_excite * inhibit + forcing - excite_offset
            )
            inhibit_drive = excite_inhibit * excite - inhibit_inhibit * inhibit - inhibit_offset
            excite, inhibit = (
                excite + excite_rate * (0.5 * jnp.tanh(0.5 * excite_drive) + 0.5 - excite),
                inhibit + inhibit_rate * (0.5 * jnp.tanh(0.5 * inhibit_drive) + 0.5 - inhibit),
            )
            samples[pl.ds(j, own_blocks, stride=STEPS), :] = excite
    rates[0] = excite
    rates[1] = inhibit
    for b in range(own_blocks):
        where = slice(b * block_rows, (b + 1) * block_rows)
        state_out[0:1, where] = rates[0, b : b + 1, :]
        state_out[1:2, where] = rates[1, b : b + 1, :]

    high = high_ref[...]
    low = low_ref[...]
    rows = GROUP * STEPS
    for g in range(own_blocks // GROUP):
        part = samples[g * rows : (g + 1) * rows, :]
        part_high = part.astype(jnp.bfloat16)
        part_low = (part - part_high.astype(jnp.float32)).astype(jnp.bfloat16)
        fitted = (
            jnp.dot(high, part_high, preferred_element_type=jnp.float32)
            + jnp.dot(high, part_low, preferred_element_type=jnp.float32)
            + jnp.dot(low, part_high, preferred_element_type=jnp.float32)
        )
        coefs_out[g * GROUP : (g + 1) * GROUP] = fitted.astype(jnp.bfloat16).reshape(
            GROUP, coef_count, block_rows
        )


def far(x):
    return pltpu.with_memory_space_constraint(x, pltpu.HBM)


def params():
    return pltpu.CompilerParams(vmem_limit_bytes=20 << 20)


def local(
    fresh_coefs,
    older_coefs,
    state,
    lesion,
    stim_nodes,
    stim_wave,
    read_blocks,
    tract_slot,
    tract_target,
    tract_delay,
    tract_frac,
    tract_weights,
):
    wide_peers = lax.axis_size("wide")
    peers = lax.axis_size("narrow")
    own_blocks, coef_count, block_rows = fresh_coefs.shape
    capacity = read_blocks.shape[3]
    slot_count = wide_peers * capacity
    tile_count = tract_slot.shape[2]
    peer_targets = tile_count // (2 * peers)
    share_rows = peer_targets * STEPS + HEAD

    def swap(x, axis, r):
        return lax.ppermute(x, axis, [(i, i ^ r) for i in range(lax.axis_size(axis))])

    reads = read_blocks.reshape(wide_peers, capacity).T
    asked = [swap(reads, "wide", r) for r in range(1, wide_peers)]

    fresh, ready = pl.pallas_call(
        functools.partial(ready_kernel, peers=peers, own_blocks=own_blocks),
        out_shape=[
            pltpu.VMEM(fresh_coefs.shape, jnp.bfloat16),
            pltpu.VMEM((4 * own_blocks + STEPS, block_rows), jnp.float32),
        ],
        in_specs=[hbm_spec] + [vmem_spec] * 4,
        out_specs=[vmem_spec] * 2,
        scratch_shapes=[pltpu.SemaphoreType.DMA],
        compiler_params=params(),
        name="ready",
    )(
        far(fresh_coefs),
        far(state),
        far(lesion.reshape(own_blocks, block_rows)),
        far(stim_nodes.reshape(1, -1)),
        far(stim_wave.reshape(1, -1)),
    )

    picked = pl.pallas_call(
        functools.partial(pick_kernel, capacity=capacity, peers=wide_peers),
        out_shape=[pltpu.VMEM((capacity, coef_count, block_rows), jnp.bfloat16)]
        * (wide_peers - 1),
        in_specs=[vmem_spec] * wide_peers,
        out_specs=[vmem_spec] * (wide_peers - 1),
        scratch_shapes=[
            SMEM((wide_peers - 1, capacity, wide_peers), jnp.int32),
            pltpu.SemaphoreType.DMA((wide_peers - 1,)),
        ],
        compiler_params=params(),
        name="pick_blocks",
    )(*asked, fresh)
    news = [swap(picked[r - 1], "wide", r) for r in range(1, wide_peers)]

    table = expand_table(coef_count)
    weights, hist, tiles, heads = pl.pallas_call(
        functools.partial(
            tiles_kernel,
            peers=peers, own_blocks=own_blocks, peer_targets=peer_targets, capacity=capacity,
        ),
        out_shape=[
            pltpu.VMEM((tile_count, block_rows, block_rows), jnp.bfloat16),
            pltpu.VMEM((slot_count * LENGTH, block_rows), jnp.float32),
            pltpu.VMEM((8, 128), jnp.int32),
            pltpu.VMEM((peers, HEAD, 128), jnp.bfloat16),
        ],
        in_specs=[hbm_spec] + [vmem_spec] * 7 + [hbm_spec],
        out_specs=[vmem_spec] * 4,
        scratch_shapes=[
            SMEM((capacity, wide_peers), jnp.int32),
            pltpu.SemaphoreType.DMA,
            pltpu.SemaphoreType.DMA,
        ],
        compiler_params=params(),
        name="tile_tables",
    )(
        far(reads),
        far(tract_slot.reshape(1, tile_count)),
        far(tract_target.reshape(1, tile_count)),
        far(tract_delay.reshape(1, tile_count)),
        far(jnp.asarray(lane_tables(peers, peer_targets, own_blocks))),
        far(jnp.asarray(table)),
        far(older_coefs.reshape(slot_count, HSEG, coef_count, block_rows)),
        fresh,
        far(tract_weights.reshape(tile_count, block_rows, block_rows)),
    )

    shares = pl.pallas_call(
        functools.partial(
            tract_kernel,
            wide_peers=wide_peers, peers=peers, capacity=capacity, peer_targets=peer_targets,
        ),
        out_shape=[pltpu.VMEM((share_rows, block_rows), jnp.bfloat16)] * peers,
        in_specs=[vmem_spec, hbm_spec] + [vmem_spec] * (3 + wide_peers),
        out_specs=[vmem_spec] * peers,
        scratch_shapes=[
            SMEM((8, 128), jnp.int32),
            SMEM((1, tile_count), jnp.float32),
            VMEM((slot_count * LENGTH, block_rows), jnp.float32),
            VMEM((peers * peer_targets * STEPS, block_rows), jnp.float32),
            pltpu.SemaphoreType.DMA((2,)),
        ],
        compiler_params=params(),
        name="tract_tiles",
    )(
        tiles,
        far(tract_frac.reshape(1, tile_count)),
        far(jnp.asarray(table)),
        hist,
        weights,
        heads,
        *news,
    )
    arrived = [shares[0]] + [swap(shares[r], "narrow", r) for r in range(1, peers)]

    high, low = fit_tables(coef_count)
    new_coefs, final_state = pl.pallas_call(
        functools.partial(
            window_kernel,
            peers=peers, own_blocks=own_blocks, peer_targets=peer_targets, coef_count=coef_count,
        ),
        out_shape=[
            jax.ShapeDtypeStruct(fresh_coefs.shape, jnp.bfloat16),
            jax.ShapeDtypeStruct(state.shape, jnp.float32),
        ],
        in_specs=[vmem_spec] * (peers + 3),
        out_specs=[vmem_spec] * 2,
        scratch_shapes=[
            VMEM((own_blocks * STEPS, block_rows), jnp.float32),
            VMEM((2, own_blocks, block_rows), jnp.float32),
        ],
        compiler_params=params(),
        name="window_steps",
    )(*arrived, ready, high, low)
    return new_coefs, final_state


def solution(mesh):
    in_specs = (
        P(("sweep", "wide", "narrow"), None, None),
        P(("sweep", "wide"), "narrow", None, None, None, None),
        P(None, ("sweep", "wide", "narrow")),
        P(("sweep", "wide", "narrow")),
        P("sweep"),
        P("sweep"),
        P("wide", "narrow", None, None),
        P("wide", "narrow", None),
        P("wide", "narrow", None),
        P("wide", "narrow", None),
        P("wide", "narrow", None),
        P("wide", "narrow", None, None, None),
    )
    out_specs = (P(("sweep", "wide", "narrow"), None, None), P(None, ("sweep", "wide", "narrow")))
    return jax.shard_map(local, mesh=mesh, in_specs=in_specs, out_specs=out_specs, check_vma=False)
```

```python
import functools
import math

import jax
import jax.numpy as jnp
import ml_dtypes
import numpy as np
from jax import lax
from jax.experimental import pallas as pl
from jax.experimental.pallas import tpu as pltpu
from jax.sharding import PartitionSpec as P

STEPS = 32
HSEG = 2
SEGS = HSEG + 1
LENGTH = SEGS * STEPS
GROUP = 4
HEAD = 16
UNROLL = 8

excite_rate = 0.1
inhibit_rate = 0.05
excite_excite = 1.5
inhibit_excite = 2.0
excite_inhibit = 2.0
inhibit_inhibit = 0.5
excite_offset = 0.5
inhibit_offset = 0.5
tract_gain = 2.0

SMEM = pltpu.SMEM
VMEM = pltpu.VMEM
vmem_spec = pl.BlockSpec(memory_space=VMEM)
hbm_spec = pl.BlockSpec(memory_space=pltpu.HBM)


def basis_table(coef_count, step_count):
    order = np.arange(coef_count, dtype=np.float32)[:, None]
    places = np.arange(step_count, dtype=np.float32)[None, :]
    angles = np.float32(np.pi) * (step_count - places - np.float32(0.5)) / np.float32(step_count)
    return np.cos((order * angles).astype(np.float64)).astype(np.float32)


def expand_table(coef_count):
    basis = basis_table(coef_count, STEPS).astype(ml_dtypes.bfloat16)
    table = np.zeros((LENGTH, SEGS * coef_count), ml_dtypes.bfloat16)
    for seg in range(SEGS):
        table[seg * STEPS : (seg + 1) * STEPS, seg * coef_count : (seg + 1) * coef_count] = basis.T
    return table


def fit_tables(coef_count):
    scales = np.where(np.arange(coef_count)[:, None] == 0, 1.0, 2.0) / STEPS
    fit = (basis_table(coef_count, STEPS) * scales).astype(np.float32)
    whole = np.zeros((GROUP * coef_count, GROUP * STEPS), np.float32)
    for g in range(GROUP):
        whole[g * coef_count : (g + 1) * coef_count, g * STEPS : (g + 1) * STEPS] = fit
    high = whole.astype(ml_dtypes.bfloat16)
    low = (whole - high.astype(np.float32)).astype(ml_dtypes.bfloat16)
    return high, low


TOGETHER = 8


def lane_tables(peers, peer_targets, own_blocks):
    width = TOGETHER * peer_targets
    assert TOGETHER * own_blocks <= 256 and peers * width <= HEAD * 128
    lane = np.arange(HEAD * 128)
    used = lane < peers * width
    within = lane % width
    rank = np.where(used, within // TOGETHER, -5)
    offset = within % TOGETHER * own_blocks + 1
    place = np.where(used, lane // width, -5)
    return np.stack([rank, offset, place]).astype(np.float32).reshape(3, HEAD, 128)


def prepare_kernel(
    weights_hbm, fresh_hbm, reads_hbm, state_hbm, lesion_hbm, stim_hbm, wave_hbm, slot_hbm,
    target_hbm, delay_hbm, frac_hbm, lanes_hbm, table_hbm, older_hbm,
    weights_out, fresh_out, ready_out, hist_out, tiles_out, fracs_out, head_out,
    reads, state, lesion, stim, wave, slot, target, delay, frac, lanes, table, older, sems,
    *, peers, own_blocks, peer_targets, capacity,
):
    pairs = [
        (fresh_hbm, fresh_out), (reads_hbm, reads), (target_hbm, target), (slot_hbm, slot),
        (delay_hbm, delay), (frac_hbm, frac), (lanes_hbm, lanes), (table_hbm, table),
        (older_hbm, older), (state_hbm, state), (lesion_hbm, lesion), (stim_hbm, stim),
        (wave_hbm, wave), (weights_hbm, weights_out),
    ]
    copies = [
        pltpu.make_async_copy(source, into, sems.at[i]) for i, (source, into) in enumerate(pairs)
    ]
    for copy in copies:
        copy.start()
    for copy in copies[2:7]:
        copy.wait()
    place = lax.axis_index("narrow")
    owner = lax.axis_index("wide")
    tile_count = target.shape[1]
    target_count = peers * own_blocks

    numbers = lax.broadcasted_iota(jnp.int32, (target_count, tile_count), 0)
    hits = jnp.where(numbers == target[...], 1.0, 0.0)
    held = jnp.dot(
        hits.astype(jnp.bfloat16), jnp.ones((tile_count, 128), jnp.bfloat16),
        preferred_element_type=jnp.float32,
    )
    held = jnp.minimum(held, 1.0)
    shape = (own_blocks, own_blocks)
    below = jnp.where(
        lax.broadcasted_iota(jnp.int32, shape, 0) > lax.broadcasted_iota(jnp.int32, shape, 1),
        1.0, 0.0,
    ).astype(jnp.bfloat16)
    block = lax.broadcasted_iota(jnp.int32, (own_blocks, 128), 0).astype(jnp.float32)
    ranks = jnp.zeros((1, tile_count), jnp.float32)
    head_rows = pl.cdiv(peers * TOGETHER * peer_targets, 128)
    for p in range(peers):
        part = slice(p * own_blocks, (p + 1) * own_blocks)
        rank = jnp.dot(below, held[part].astype(jnp.bfloat16), preferred_element_type=jnp.float32)
        ranks = ranks + jnp.sum(hits[part] * rank[:, :tile_count], axis=0, keepdims=True)
        rank = jnp.where(held[part] > 0.5, rank, -1.0)
        source = (place ^ p).astype(jnp.float32)
        rows = []
        for h in range(head_rows):
            match = rank == lanes[0, h : h + 1, :]
            ids = jnp.sum(jnp.where(match, block, 0.0), axis=0, keepdims=True)
            mine = lanes[2, h : h + 1, :] == source
            rows.append(jnp.where(mine, ids + lanes[1, h : h + 1, :], 0.0))
        rows.append(jnp.zeros((HEAD - head_rows, 128), jnp.float32))
        head_out[p] = jnp.concatenate(rows, axis=0).astype(jnp.bfloat16)

    across = jnp.zeros((1, tile_count), jnp.int32)
    for p in range(1, peers):
        across = across + jnp.where(target[...] >= p * own_blocks, 1, 0)
    key_row = ((peers - 1) - (across ^ place)).astype(jnp.float32)
    shape = (tile_count, tile_count)
    down = lax.broadcasted_iota(jnp.int32, shape, 0)
    along = lax.broadcasted_iota(jnp.int32, shape, 1)
    key = jnp.sum(jnp.where(down == along, key_row, 0.0), axis=1, keepdims=True)
    ahead = (key_row < key) | ((key_row == key) & (along < down))
    position = jnp.sum(jnp.where(ahead, 1.0, 0.0), axis=1, keepdims=True)
    lane = lax.broadcasted_iota(jnp.int32, (tile_count, 128), 1).astype(jnp.float32)
    chosen = jnp.where(position == lane, 1.0, 0.0)
    starts = (slot[...] * LENGTH + (LENGTH - 1) - delay[...]).astype(jnp.float32)
    index = lax.broadcasted_iota(jnp.int32, (1, tile_count), 1).astype(jnp.float32)
    facts = jnp.concatenate(
        [index, starts, (key_row * peer_targets + ranks) * TOGETHER, frac[...], jnp.zeros((4, tile_count), jnp.float32)],
        axis=0,
    )
    ordered = jnp.dot(
        facts, chosen, precision=lax.Precision.HIGHEST, preferred_element_type=jnp.float32
    )
    fracs_out[...] = ordered
    tiles_out[...] = (ordered + 0.5).astype(jnp.int32)
    tiles_out[3:4, :] = jnp.sum(
        jnp.where(key < lane, 1.0, 0.0), axis=0, keepdims=True
    ).astype(jnp.int32)

    for copy in copies[7:9]:
        copy.wait()
    coef_count = older.shape[2]
    earlier = HSEG * STEPS
    for s in range(older.shape[0]):
        segments = [older[s, h] for h in range(HSEG - 1, -1, -1)]
        hist_out[s * LENGTH : s * LENGTH + earlier, :] = jnp.dot(
            table[:earlier, : HSEG * coef_count], jnp.concatenate(segments, axis=0),
            preferred_element_type=jnp.float32,
        )
        hist_out[s * LENGTH + earlier : (s + 1) * LENGTH, :] = jnp.zeros(
            (STEPS, hist_out.shape[1]), jnp.float32
        )
    for copy in copies[:2]:
        copy.wait()
    for c in range(capacity):
        rows = pl.ds(pl.multiple_of((owner * capacity + c) * LENGTH + earlier, 8), STEPS)
        hist_out[rows, :] = jnp.dot(
            table[:STEPS, :coef_count], fresh_out[jnp.maximum(reads[c, owner], 0)],
            preferred_element_type=jnp.float32,
        )

    for copy in copies[9:13]:
        copy.wait()
    block_rows = lesion.shape[1]
    for b in range(own_blocks):
        piece = state[:, b * block_rows : (b + 1) * block_rows]
        ready_out[b : b + 1, :] = piece[0:1, :]
        ready_out[own_blocks + b : own_blocks + b + 1, :] = piece[1:2, :]
    ready_out[2 * own_blocks : 3 * own_blocks, :] = tract_gain * (
        1.0 - lesion[...].astype(jnp.float32)
    )
    stim_count = stim.shape[1]
    nodes = stim[...] - (owner * peers + place) * (own_blocks * block_rows)
    blocks = lax.shift_right_arithmetic(nodes, block_rows.bit_length() - 1)
    offsets = nodes & (block_rows - 1)
    in_block = lax.broadcasted_iota(jnp.int32, (own_blocks, stim_count), 0) == blocks
    at_offset = lax.broadcasted_iota(jnp.int32, (block_rows, stim_count), 0) == offsets
    ready_out[3 * own_blocks : 4 * own_blocks, :] = lax.dot_general(
        jnp.where(in_block, 1.0, 0.0).astype(jnp.bfloat16),
        jnp.where(at_offset, 1.0, 0.0).astype(jnp.bfloat16),
        (((1,), (1,)), ((), ())),
        preferred_element_type=jnp.float32,
    )
    shape = (STEPS, STEPS)
    diagonal = lax.broadcasted_iota(jnp.int32, shape, 0) == lax.broadcasted_iota(jnp.int32, shape, 1)
    column = jnp.sum(jnp.where(diagonal, wave[...], 0.0), axis=1, keepdims=True)
    ready_out[4 * own_blocks :, :] = jnp.broadcast_to(column, (STEPS, block_rows))
    copies[13].wait()


def pick_kernel(*refs, capacity, peers):
    tables = refs[: peers - 1]
    fresh = refs[peers - 1]
    outs = refs[peers : 2 * peers - 1]
    asked, sems = refs[2 * peers - 1 :]
    place = lax.axis_index("wide")
    copies = [pltpu.make_async_copy(tables[r], asked.at[r], sems.at[r]) for r in range(peers - 1)]
    for copy in copies:
        copy.start()
    for r in range(peers - 1):
        copies[r].wait()
        for c in range(capacity):
            outs[r][c] = fresh[jnp.maximum(asked[r, c, place], 0)]


def tract_kernel(
    tiles_ref, fracs_ref, table_ref, head_ref, weights, hist_ref, *refs,
    parts, wide_peers, peers, capacity, peer_targets,
):
    place = lax.axis_index("narrow")
    owner = lax.axis_index("wide")
    tiles, fracs, total, sems = refs[-4:]
    if parts[0] == 0:
        news = refs[: wide_peers - 1]
        outs = refs[wide_peers - 1 : -5]
        hist = refs[-5]
        hist[...] = hist_ref[...]
    else:
        news = []
        outs = refs[:-4]
        hist = hist_ref
    copies = [
        pltpu.make_async_copy(tiles_ref, tiles, sems.at[0]),
        pltpu.make_async_copy(fracs_ref, fracs, sems.at[1]),
    ]
    for copy in copies:
        copy.start()
    total[...] = jnp.zeros_like(total)
    for i, block in enumerate(news):
        table = table_ref[:STEPS, : block.shape[1]]
        for c in range(capacity):
            slot = (owner ^ (wide_peers - 1 - i)) * capacity + c
            rows = pl.ds(pl.multiple_of(slot * LENGTH + HSEG * STEPS, 8), STEPS)
            hist[rows, :] = jnp.dot(table, block[c], preferred_element_type=jnp.float32)
    for copy in copies:
        copy.wait()
    begin = tiles[3, parts[0]]
    end = tiles[3, parts[-1] + 1]
    spare = len(parts) * peer_targets * TOGETHER
    pitch = spare + TOGETHER

    @pl.loop(0, lax.div(end - begin + (UNROLL - 1), UNROLL))
    def _(turn):
        sums = []
        for u in range(UNROLL):
            t = begin + turn * UNROLL + u
            fraction = fracs[3, t]
            start = tiles[1, t]
            earlier = hist[pl.ds(start, STEPS), :]
            later = hist[pl.ds(start + 1, STEPS), :]
            delayed = ((1.0 - fraction) * later + fraction * earlier).astype(jnp.bfloat16)
            sums.append(
                lax.dot_general(
                    delayed, weights[tiles[0, t]], (((1,), (1,)), ((), ())),
                    preferred_element_type=jnp.float32,
                )
            )
        for u in range(UNROLL):
            t = begin + turn * UNROLL + u
            first = jnp.where(t < end, tiles[2, t] - parts[0] * peer_targets * TOGETHER, spare)
            for g in range(STEPS // TOGETHER):
                rows = pl.ds(pl.multiple_of(g * pitch + first, 8), TOGETHER)
                total[rows, :] += sums[u][g * TOGETHER : (g + 1) * TOGETHER]

    span = peer_targets * TOGETHER
    for i, part in enumerate(parts):
        for g in range(STEPS // TOGETHER):
            first = g * pitch + i * span
            outs[i][g * span : (g + 1) * span, :] = total[first : first + span, :].astype(
                jnp.bfloat16
            )
        outs[i][peer_targets * STEPS :, :] = head_ref[place ^ (peers - 1 - part)]


def window_kernel(*refs, peers, own_blocks, peer_targets, coef_count):
    shares = refs[:peers][::-1]
    ready_ref, high_ref, low_ref, coefs_out, state_out, samples, rates = refs[peers:]
    block_rows = ready_ref.shape[1]
    width = TOGETHER * peer_targets
    span = peer_targets * STEPS

    head = shares[0][span:, :].astype(jnp.float32)
    for r in range(1, peers):
        head = head + shares[r][span:, :].astype(jnp.float32)
    row = lax.broadcasted_iota(jnp.int32, (TOGETHER * own_blocks, 128), 0).astype(jnp.float32) + 1.0
    columns = peers * width
    scatter = jnp.concatenate(
        [
            jnp.where(row == head[h : h + 1, :], 1.0, 0.0).astype(jnp.bfloat16)
            for h in range(pl.cdiv(columns, 128))
        ],
        axis=1,
    )[:, :columns]

    excite, inhibit, gain, counts = [
        ready_ref[i * own_blocks : (i + 1) * own_blocks, :] for i in range(4)
    ]
    for pair in range(0, STEPS // TOGETHER, 2):
        arrived = jnp.concatenate(
            [
                jnp.concatenate(
                    [shares[r][g * width : (g + 1) * width, :] for r in range(peers)], axis=0
                )
                for g in (pair, pair + 1)
            ],
            axis=1,
        )
        inflow = jnp.dot(scatter, arrived, preferred_element_type=jnp.float32)
        for jj in range(2 * TOGETHER):
            j = pair * TOGETHER + jj
            wave = ready_ref[4 * own_blocks + j : 4 * own_blocks + j + 1, :]
            first = jj % TOGETHER * own_blocks
            left = jj // TOGETHER * block_rows
            forcing = (
                gain * inflow[first : first + own_blocks, left : left + block_rows] + wave * counts
            )
            excite_drive = (
                excite_excite * excite - inhibit_excite * inhibit + forcing - excite_offset
            )
            inhibit_drive = excite_inhibit * excite - inhibit_inhibit * inhibit - inhibit_offset
            excite, inhibit = (
                excite + excite_rate * (0.5 * jnp.tanh(0.5 * excite_drive) + 0.5 - excite),
                inhibit + inhibit_rate * (0.5 * jnp.tanh(0.5 * inhibit_drive) + 0.5 - inhibit),
            )
            samples[pl.ds(j, own_blocks, stride=STEPS), :] = excite
    rates[0] = excite
    rates[1] = inhibit
    for b in range(own_blocks):
        where = slice(b * block_rows, (b + 1) * block_rows)
        state_out[0:1, where] = rates[0, b : b + 1, :]
        state_out[1:2, where] = rates[1, b : b + 1, :]

    high = high_ref[...]
    low = low_ref[...]
    rows = GROUP * STEPS
    for g in range(own_blocks // GROUP):
        part = samples[g * rows : (g + 1) * rows, :]
        part_high = part.astype(jnp.bfloat16)
        part_low = (part - part_high.astype(jnp.float32)).astype(jnp.bfloat16)
        fitted = (
            jnp.dot(high, part_high, preferred_element_type=jnp.float32)
            + jnp.dot(high, part_low, preferred_element_type=jnp.float32)
            + jnp.dot(low, part_high, preferred_element_type=jnp.float32)
        )
        coefs_out[g * GROUP : (g + 1) * GROUP] = fitted.astype(jnp.bfloat16).reshape(
            GROUP, coef_count, block_rows
        )


def far(x):
    return pltpu.with_memory_space_constraint(x, pltpu.HBM)


def params():
    return pltpu.CompilerParams(vmem_limit_bytes=20 << 20)


def local(
    fresh_coefs,
    older_coefs,
    state,
    lesion,
    stim_nodes,
    stim_wave,
    read_blocks,
    tract_slot,
    tract_target,
    tract_delay,
    tract_frac,
    tract_weights,
):
    wide_peers = lax.axis_size("wide")
    peers = lax.axis_size("narrow")
    own_blocks, coef_count, block_rows = fresh_coefs.shape
    capacity = read_blocks.shape[3]
    slot_count = wide_peers * capacity
    tile_count = tract_slot.shape[2]
    peer_targets = tile_count // (2 * peers)
    share_rows = peer_targets * STEPS + HEAD

    def swap(x, axis, r):
        return lax.ppermute(x, axis, [(i, i ^ r) for i in range(lax.axis_size(axis))])

    reads = read_blocks.reshape(wide_peers, capacity).T
    asked = [swap(reads, "wide", r) for r in range(1, wide_peers)]

    vmem_inputs = [
        VMEM(state.shape, jnp.float32),
        VMEM((own_blocks, block_rows), jnp.int32),
        VMEM((1, stim_nodes.shape[0]), jnp.int32),
        VMEM((1, STEPS), jnp.float32),
        VMEM((1, tile_count), jnp.int32),
        VMEM((1, tile_count), jnp.int32),
        VMEM((1, tile_count), jnp.int32),
        VMEM((1, tile_count), jnp.float32),
        VMEM((3, HEAD, 128), jnp.float32),
        VMEM((LENGTH, SEGS * coef_count), jnp.bfloat16),
        VMEM((slot_count, HSEG, coef_count, block_rows), jnp.bfloat16),
    ]
    table = far(jnp.asarray(expand_table(coef_count)))
    weights, fresh, ready, hist, tiles, fracs, heads = pl.pallas_call(
        functools.partial(
            prepare_kernel,
            peers=peers, own_blocks=own_blocks, peer_targets=peer_targets, capacity=capacity,
        ),
        out_shape=[
            pltpu.VMEM((tile_count, block_rows, block_rows), jnp.bfloat16),
            pltpu.VMEM(fresh_coefs.shape, jnp.bfloat16),
            pltpu.VMEM((4 * own_blocks + STEPS, block_rows), jnp.float32),
            pltpu.VMEM((slot_count * LENGTH, block_rows), jnp.float32),
            pltpu.VMEM((8, 128), jnp.int32),
            pltpu.VMEM((8, 128), jnp.float32),
            pltpu.VMEM((peers, HEAD, 128), jnp.bfloat16),
        ],
        in_specs=[hbm_spec] * 14,
        out_specs=[vmem_spec] * 7,
        scratch_shapes=[
            SMEM((capacity, wide_peers), jnp.int32),
            *vmem_inputs,
            pltpu.SemaphoreType.DMA((14,)),
        ],
        compiler_params=params(),
        name="prepare",
    )(
        far(tract_weights.reshape(tile_count, block_rows, block_rows)),
        far(fresh_coefs),
        far(reads),
        far(state),
        far(lesion.reshape(own_blocks, block_rows)),
        far(stim_nodes.reshape(1, -1)),
        far(stim_wave.reshape(1, -1)),
        far(tract_slot.reshape(1, tile_count)),
        far(tract_target.reshape(1, tile_count)),
        far(tract_delay.reshape(1, tile_count)),
        far(tract_frac.reshape(1, tile_count)),
        far(jnp.asarray(lane_tables(peers, peer_targets, own_blocks))),
        table,
        far(older_coefs.reshape(slot_count, HSEG, coef_count, block_rows)),
    )

    picked = pl.pallas_call(
        functools.partial(pick_kernel, capacity=capacity, peers=wide_peers),
        out_shape=[pltpu.VMEM((capacity, coef_count, block_rows), jnp.bfloat16)]
        * (wide_peers - 1),
        in_specs=[vmem_spec] * wide_peers,
        out_specs=[vmem_spec] * (wide_peers - 1),
        scratch_shapes=[
            SMEM((wide_peers - 1, capacity, wide_peers), jnp.int32),
            pltpu.SemaphoreType.DMA((wide_peers - 1,)),
        ],
        compiler_params=params(),
        name="pick_blocks",
    )(*asked, fresh)
    news = [swap(picked[r - 1], "wide", r) for r in range(wide_peers - 1, 0, -1)]

    shares = [None] * peers
    half = (peers + 1) // 2
    for parts in (range(half), range(half, peers)):
        blocks = news if parts[0] == 0 else []
        result = pl.pallas_call(
            functools.partial(
                tract_kernel,
                parts=parts, wide_peers=wide_peers, peers=peers, capacity=capacity,
                peer_targets=peer_targets,
            ),
            out_shape=[pltpu.VMEM((share_rows, block_rows), jnp.bfloat16)] * len(parts)
            + ([pltpu.VMEM(hist.shape, jnp.float32)] if parts[0] == 0 else []),
            in_specs=[vmem_spec] * (6 + len(blocks)),
            out_specs=[vmem_spec] * (len(parts) + (parts[0] == 0)),
            scratch_shapes=[
                SMEM((8, 128), jnp.int32),
                SMEM((8, 128), jnp.float32),
                VMEM(((len(parts) * peer_targets + 1) * STEPS, block_rows), jnp.float32),
                pltpu.SemaphoreType.DMA((2,)),
            ],
            compiler_params=params(),
            name=f"tract_tiles_{parts[0]}",
        )(tiles, fracs, table, heads, weights, hist, *blocks)
        if parts[0] == 0:
            hist = result[-1]
        for i, part in enumerate(parts):
            shares[peers - 1 - part] = result[i]
    arrived = [shares[0]] + [swap(shares[r], "narrow", r) for r in range(1, peers)]

    high, low = fit_tables(coef_count)
    new_coefs, final_state = pl.pallas_call(
        functools.partial(
            window_kernel,
            peers=peers, own_blocks=own_blocks, peer_targets=peer_targets, coef_count=coef_count,
        ),
        out_shape=[
            jax.ShapeDtypeStruct(fresh_coefs.shape, jnp.bfloat16),
            jax.ShapeDtypeStruct(state.shape, jnp.float32),
        ],
        in_specs=[vmem_spec] * (peers + 3),
        out_specs=[vmem_spec] * 2,
        scratch_shapes=[
            VMEM((own_blocks * STEPS, block_rows), jnp.float32),
            VMEM((2, own_blocks, block_rows), jnp.float32),
        ],
        compiler_params=params(),
        name="window_steps",
    )(*arrived[::-1], ready, high, low)
    return new_coefs, final_state


def solution(mesh):
    in_specs = (
        P(("sweep", "wide", "narrow"), None, None),
        P(("sweep", "wide"), "narrow", None, None, None, None),
        P(None, ("sweep", "wide", "narrow")),
        P(("sweep", "wide", "narrow")),
        P("sweep"),
        P("sweep"),
        P("wide", "narrow", None, None),
        P("wide", "narrow", None),
        P("wide", "narrow", None),
        P("wide", "narrow", None),
        P("wide", "narrow", None),
        P("wide", "narrow", None, None, None),
    )
    out_specs = (P(("sweep", "wide", "narrow"), None, None), P(None, ("sweep", "wide", "narrow")))
    return jax.shard_map(local, mesh=mesh, in_specs=in_specs, out_specs=out_specs, check_vma=False)
```

```python
import functools
import math

import jax
import jax.numpy as jnp
import ml_dtypes
import numpy as np
from jax import lax
from jax.experimental import pallas as pl
from jax.experimental.pallas import tpu as pltpu
from jax.sharding import PartitionSpec as P

STEPS = 32
HSEG = 2
SEGS = HSEG + 1
LENGTH = SEGS * STEPS
GROUP = 4
HEAD = 16
UNROLL = 16

excite_rate = 0.1
inhibit_rate = 0.05
excite_excite = 1.5
inhibit_excite = 2.0
excite_inhibit = 2.0
inhibit_inhibit = 0.5
excite_offset = 0.5
inhibit_offset = 0.5
tract_gain = 2.0

SMEM = pltpu.SMEM
VMEM = pltpu.VMEM
vmem_spec = pl.BlockSpec(memory_space=VMEM)
hbm_spec = pl.BlockSpec(memory_space=pltpu.HBM)


def basis_table(coef_count, step_count):
    order = np.arange(coef_count, dtype=np.float32)[:, None]
    places = np.arange(step_count, dtype=np.float32)[None, :]
    angles = np.float32(np.pi) * (step_count - places - np.float32(0.5)) / np.float32(step_count)
    return np.cos((order * angles).astype(np.float64)).astype(np.float32)


def expand_table(coef_count):
    basis = basis_table(coef_count, STEPS).astype(ml_dtypes.bfloat16)
    table = np.zeros((LENGTH, SEGS * coef_count), ml_dtypes.bfloat16)
    for seg in range(SEGS):
        table[seg * STEPS : (seg + 1) * STEPS, seg * coef_count : (seg + 1) * coef_count] = basis.T
    return table


def fit_tables(coef_count):
    scales = np.where(np.arange(coef_count)[:, None] == 0, 1.0, 2.0) / STEPS
    fit = (basis_table(coef_count, STEPS) * scales).astype(np.float32)
    whole = np.zeros((GROUP * coef_count, GROUP * STEPS), np.float32)
    for g in range(GROUP):
        whole[g * coef_count : (g + 1) * coef_count, g * STEPS : (g + 1) * STEPS] = fit
    high = whole.astype(ml_dtypes.bfloat16)
    low = (whole - high.astype(np.float32)).astype(ml_dtypes.bfloat16)
    return high, low


TOGETHER = 8


def lane_tables(peers, peer_targets, own_blocks):
    width = TOGETHER * peer_targets
    assert TOGETHER * own_blocks <= 256 and peers * width <= HEAD * 128
    lane = np.arange(HEAD * 128)
    used = lane < peers * width
    within = lane % width
    rank = np.where(used, within // TOGETHER, -5)
    offset = within % TOGETHER * own_blocks + 1
    place = np.where(used, lane // width, -5)
    return np.stack([rank, offset, place]).astype(np.float32).reshape(3, HEAD, 128)


def fresh_kernel(fresh_hbm, fresh_out, sem):
    copy = pltpu.make_async_copy(fresh_hbm, fresh_out, sem)
    copy.start()
    copy.wait()


def prepare_kernel(
    fresh_ref, weights_hbm, reads_hbm, state_hbm, lesion_hbm, stim_hbm, wave_hbm, slot_hbm,
    target_hbm, delay_hbm, frac_hbm, lanes_hbm, table_hbm, older_hbm,
    weights_out, ready_out, hist_out, tiles_out, fracs_out, head_out,
    reads, state, lesion, stim, wave, slot, target, delay, frac, lanes, table, older, sems,
    *, peers, own_blocks, peer_targets, capacity,
):
    pairs = [
        (weights_hbm, weights_out), (reads_hbm, reads), (target_hbm, target), (slot_hbm, slot),
        (delay_hbm, delay), (frac_hbm, frac), (lanes_hbm, lanes), (table_hbm, table),
        (older_hbm, older), (state_hbm, state), (lesion_hbm, lesion), (stim_hbm, stim),
        (wave_hbm, wave),
    ]
    copies = [
        pltpu.make_async_copy(source, into, sems.at[i]) for i, (source, into) in enumerate(pairs)
    ]
    for copy in copies:
        copy.start()
    for copy in copies[2:7]:
        copy.wait()
    place = lax.axis_index("narrow")
    owner = lax.axis_index("wide")
    tile_count = target.shape[1]
    target_count = peers * own_blocks

    numbers = lax.broadcasted_iota(jnp.int32, (target_count, tile_count), 0)
    hits = jnp.where(numbers == target[...], 1.0, 0.0)
    held = jnp.dot(
        hits.astype(jnp.bfloat16), jnp.ones((tile_count, 128), jnp.bfloat16),
        preferred_element_type=jnp.float32,
    )
    held = jnp.minimum(held, 1.0)
    shape = (own_blocks, own_blocks)
    below = jnp.where(
        lax.broadcasted_iota(jnp.int32, shape, 0) > lax.broadcasted_iota(jnp.int32, shape, 1),
        1.0, 0.0,
    ).astype(jnp.bfloat16)
    block = lax.broadcasted_iota(jnp.int32, (own_blocks, 128), 0).astype(jnp.float32)
    ranks = jnp.zeros((1, tile_count), jnp.float32)
    head_rows = pl.cdiv(peers * TOGETHER * peer_targets, 128)
    for p in range(peers):
        part = slice(p * own_blocks, (p + 1) * own_blocks)
        rank = jnp.dot(below, held[part].astype(jnp.bfloat16), preferred_element_type=jnp.float32)
        ranks = ranks + jnp.sum(hits[part] * rank[:, :tile_count], axis=0, keepdims=True)
        rank = jnp.where(held[part] > 0.5, rank, -1.0)
        source = (place ^ p).astype(jnp.float32)
        rows = []
        for h in range(head_rows):
            match = rank == lanes[0, h : h + 1, :]
            ids = jnp.sum(jnp.where(match, block, 0.0), axis=0, keepdims=True)
            mine = lanes[2, h : h + 1, :] == source
            rows.append(jnp.where(mine, ids + lanes[1, h : h + 1, :], 0.0))
        rows.append(jnp.zeros((HEAD - head_rows, 128), jnp.float32))
        head_out[p] = jnp.concatenate(rows, axis=0).astype(jnp.bfloat16)

    across = jnp.zeros((1, tile_count), jnp.int32)
    for p in range(1, peers):
        across = across + jnp.where(target[...] >= p * own_blocks, 1, 0)
    key_row = ((peers - 1) - (across ^ place)).astype(jnp.float32)
    shape = (tile_count, tile_count)
    down = lax.broadcasted_iota(jnp.int32, shape, 0)
    along = lax.broadcasted_iota(jnp.int32, shape, 1)
    key = jnp.sum(jnp.where(down == along, key_row, 0.0), axis=1, keepdims=True)
    ahead = (key_row < key) | ((key_row == key) & (along < down))
    position = jnp.sum(jnp.where(ahead, 1.0, 0.0), axis=1, keepdims=True)
    lane = lax.broadcasted_iota(jnp.int32, (tile_count, 128), 1).astype(jnp.float32)
    chosen = jnp.where(position == lane, 1.0, 0.0)
    starts = (slot[...] * LENGTH + (LENGTH - 1) - delay[...]).astype(jnp.float32)
    index = lax.broadcasted_iota(jnp.int32, (1, tile_count), 1).astype(jnp.float32)
    facts = jnp.concatenate(
        [index, starts, (key_row * peer_targets + ranks) * TOGETHER, frac[...], jnp.zeros((4, tile_count), jnp.float32)],
        axis=0,
    )
    ordered = jnp.dot(
        facts, chosen, precision=lax.Precision.HIGHEST, preferred_element_type=jnp.float32
    )
    fracs_out[...] = ordered
    tiles_out[...] = (ordered + 0.5).astype(jnp.int32)
    tiles_out[3:4, :] = jnp.sum(
        jnp.where(key < lane, 1.0, 0.0), axis=0, keepdims=True
    ).astype(jnp.int32)

    for copy in copies[7:9]:
        copy.wait()
    coef_count = older.shape[2]
    earlier = HSEG * STEPS
    for s in range(older.shape[0]):
        segments = [older[s, h] for h in range(HSEG - 1, -1, -1)]
        hist_out[s * LENGTH : s * LENGTH + earlier, :] = jnp.dot(
            table[:earlier, : HSEG * coef_count], jnp.concatenate(segments, axis=0),
            preferred_element_type=jnp.float32,
        )
        hist_out[s * LENGTH + earlier : (s + 1) * LENGTH, :] = jnp.zeros(
            (STEPS, hist_out.shape[1]), jnp.float32
        )
    copies[1].wait()
    for c in range(capacity):
        rows = pl.ds(pl.multiple_of((owner * capacity + c) * LENGTH + earlier, 8), STEPS)
        hist_out[rows, :] = jnp.dot(
            table[:STEPS, :coef_count], fresh_ref[jnp.maximum(reads[c, owner], 0)],
            preferred_element_type=jnp.float32,
        )

    for copy in copies[9:13]:
        copy.wait()
    block_rows = lesion.shape[1]
    for b in range(own_blocks):
        piece = state[:, b * block_rows : (b + 1) * block_rows]
        ready_out[b : b + 1, :] = piece[0:1, :]
        ready_out[own_blocks + b : own_blocks + b + 1, :] = piece[1:2, :]
    ready_out[2 * own_blocks : 3 * own_blocks, :] = tract_gain * (
        1.0 - lesion[...].astype(jnp.float32)
    )
    stim_count = stim.shape[1]
    nodes = stim[...] - (owner * peers + place) * (own_blocks * block_rows)
    blocks = lax.shift_right_arithmetic(nodes, block_rows.bit_length() - 1)
    offsets = nodes & (block_rows - 1)
    in_block = lax.broadcasted_iota(jnp.int32, (own_blocks, stim_count), 0) == blocks
    at_offset = lax.broadcasted_iota(jnp.int32, (block_rows, stim_count), 0) == offsets
    ready_out[3 * own_blocks : 4 * own_blocks, :] = lax.dot_general(
        jnp.where(in_block, 1.0, 0.0).astype(jnp.bfloat16),
        jnp.where(at_offset, 1.0, 0.0).astype(jnp.bfloat16),
        (((1,), (1,)), ((), ())),
        preferred_element_type=jnp.float32,
    )
    shape = (STEPS, STEPS)
    diagonal = lax.broadcasted_iota(jnp.int32, shape, 0) == lax.broadcasted_iota(jnp.int32, shape, 1)
    column = jnp.sum(jnp.where(diagonal, wave[...], 0.0), axis=1, keepdims=True)
    ready_out[4 * own_blocks :, :] = jnp.broadcast_to(column, (STEPS, block_rows))
    copies[0].wait()


def pick_kernel(*refs, capacity, peers, plan):
    tables = refs[: peers - 1]
    fresh = refs[peers - 1]
    outs = refs[peers : peers + len(plan)]
    asked, sems = refs[peers + len(plan) :]
    place = lax.axis_index("wide")
    copies = [pltpu.make_async_copy(tables[r], asked.at[r], sems.at[r]) for r in range(peers - 1)]
    for copy in copies:
        copy.start()
    for copy in copies:
        copy.wait()
    for out, distances in zip(outs, plan):
        for i, distance in enumerate(distances):
            for c in range(capacity):
                block = jnp.maximum(asked[distance - 1, c, place], 0)
                out[i * capacity + c] = fresh[block]


def forward_kernel(*refs, capacity, sources, plan):
    for out, places in zip(refs[sources + 1 :], plan):
        for i, (source, place) in enumerate(places):
            out[i * capacity : (i + 1) * capacity] = refs[source][
                place * capacity : (place + 1) * capacity
            ]


def tract_kernel(
    tiles_ref, fracs_ref, table_ref, head_ref, weights, hist_ref, *refs,
    parts, plan, peers, capacity, peer_targets,
):
    place = lax.axis_index("narrow")
    owner = lax.axis_index("wide")
    tiles, fracs, total, sems = refs[-4:]
    if parts[0] == 0:
        outs = refs[-5 - len(parts) : -5]
        hist = refs[-5]
        hist[...] = hist_ref[...]
    else:
        outs = refs[-4 - len(parts) : -4]
        hist = hist_ref
    copies = [
        pltpu.make_async_copy(tiles_ref, tiles, sems.at[0]),
        pltpu.make_async_copy(fracs_ref, fracs, sems.at[1]),
    ]
    for copy in copies:
        copy.start()
    total[...] = jnp.zeros_like(total)
    for source, first, distance in plan:
        block = refs[source]
        table = table_ref[:STEPS, : block.shape[1]]
        for c in range(capacity):
            slot = (owner ^ distance) * capacity + c
            rows = pl.ds(pl.multiple_of(slot * LENGTH + HSEG * STEPS, 8), STEPS)
            hist[rows, :] = jnp.dot(
                table, block[first * capacity + c], preferred_element_type=jnp.float32
            )
    for copy in copies:
        copy.wait()
    begin = tiles[3, parts[0]]
    end = tiles[3, parts[-1] + 1]
    spare = len(parts) * peer_targets * TOGETHER
    pitch = spare + TOGETHER

    @pl.loop(0, lax.div(end - begin + (UNROLL - 1), UNROLL))
    def _(turn):
        sums = []
        for u in range(UNROLL):
            t = begin + turn * UNROLL + u
            fraction = fracs[3, t]
            start = tiles[1, t]
            earlier = hist[pl.ds(start, STEPS), :]
            later = hist[pl.ds(start + 1, STEPS), :]
            delayed = ((1.0 - fraction) * later + fraction * earlier).astype(jnp.bfloat16)
            sums.append(
                lax.dot_general(
                    delayed, weights[tiles[0, t]], (((1,), (1,)), ((), ())),
                    preferred_element_type=jnp.float32,
                )
            )
        for u in range(UNROLL):
            t = begin + turn * UNROLL + u
            first = jnp.where(t < end, tiles[2, t] - parts[0] * peer_targets * TOGETHER, spare)
            for g in range(STEPS // TOGETHER):
                rows = pl.ds(pl.multiple_of(g * pitch + first, 8), TOGETHER)
                total[rows, :] += sums[u][g * TOGETHER : (g + 1) * TOGETHER]

    span = peer_targets * TOGETHER
    for i, part in enumerate(parts):
        for g in range(STEPS // TOGETHER):
            first = g * pitch + i * span
            outs[i][g * span : (g + 1) * span, :] = total[first : first + span, :].astype(
                jnp.bfloat16
            )
        outs[i][peer_targets * STEPS :, :] = head_ref[place ^ (peers - 1 - part)]


def window_kernel(*refs, peers, own_blocks, peer_targets, coef_count):
    shares = refs[:peers][::-1]
    ready_ref, high_ref, low_ref, coefs_out, state_out, samples, rates = refs[peers:]
    block_rows = ready_ref.shape[1]
    width = TOGETHER * peer_targets
    span = peer_targets * STEPS

    head = shares[0][span:, :].astype(jnp.float32)
    for r in range(1, peers):
        head = head + shares[r][span:, :].astype(jnp.float32)
    row = lax.broadcasted_iota(jnp.int32, (TOGETHER * own_blocks, 128), 0).astype(jnp.float32) + 1.0
    columns = peers * width
    scatter = jnp.concatenate(
        [
            jnp.where(row == head[h : h + 1, :], 1.0, 0.0).astype(jnp.bfloat16)
            for h in range(pl.cdiv(columns, 128))
        ],
        axis=1,
    )[:, :columns]

    excite, inhibit, gain, counts = [
        ready_ref[i * own_blocks : (i + 1) * own_blocks, :] for i in range(4)
    ]
    for pair in range(0, STEPS // TOGETHER, 2):
        arrived = jnp.concatenate(
            [
                jnp.concatenate(
                    [shares[r][g * width : (g + 1) * width, :] for r in range(peers)], axis=0
                )
                for g in (pair, pair + 1)
            ],
            axis=1,
        )
        inflow = jnp.dot(scatter, arrived, preferred_element_type=jnp.float32)
        for jj in range(2 * TOGETHER):
            j = pair * TOGETHER + jj
            wave = ready_ref[4 * own_blocks + j : 4 * own_blocks + j + 1, :]
            first = jj % TOGETHER * own_blocks
            left = jj // TOGETHER * block_rows
            forcing = (
                gain * inflow[first : first + own_blocks, left : left + block_rows] + wave * counts
            )
            excite_drive = (
                excite_excite * excite - inhibit_excite * inhibit + forcing - excite_offset
            )
            inhibit_drive = excite_inhibit * excite - inhibit_inhibit * inhibit - inhibit_offset
            excite, inhibit = (
                excite + excite_rate * (0.5 * jnp.tanh(0.5 * excite_drive) + 0.5 - excite),
                inhibit + inhibit_rate * (0.5 * jnp.tanh(0.5 * inhibit_drive) + 0.5 - inhibit),
            )
            samples[pl.ds(j, own_blocks, stride=STEPS), :] = excite
    rates[0] = excite
    rates[1] = inhibit
    for b in range(own_blocks):
        where = slice(b * block_rows, (b + 1) * block_rows)
        state_out[0:1, where] = rates[0, b : b + 1, :]
        state_out[1:2, where] = rates[1, b : b + 1, :]

    high = high_ref[...]
    low = low_ref[...]
    rows = GROUP * STEPS
    for g in range(own_blocks // GROUP):
        part = samples[g * rows : (g + 1) * rows, :]
        part_high = part.astype(jnp.bfloat16)
        part_low = (part - part_high.astype(jnp.float32)).astype(jnp.bfloat16)
        fitted = (
            jnp.dot(high, part_high, preferred_element_type=jnp.float32)
            + jnp.dot(high, part_low, preferred_element_type=jnp.float32)
            + jnp.dot(low, part_high, preferred_element_type=jnp.float32)
        )
        coefs_out[g * GROUP : (g + 1) * GROUP] = fitted.astype(jnp.bfloat16).reshape(
            GROUP, coef_count, block_rows
        )


def far(x):
    return pltpu.with_memory_space_constraint(x, pltpu.HBM)


def params():
    return pltpu.CompilerParams(vmem_limit_bytes=20 << 20)


def local(
    fresh_coefs,
    older_coefs,
    state,
    lesion,
    stim_nodes,
    stim_wave,
    read_blocks,
    tract_slot,
    tract_target,
    tract_delay,
    tract_frac,
    tract_weights,
):
    wide_peers = lax.axis_size("wide")
    peers = lax.axis_size("narrow")
    own_blocks, coef_count, block_rows = fresh_coefs.shape
    capacity = read_blocks.shape[3]
    slot_count = wide_peers * capacity
    tile_count = tract_slot.shape[2]
    peer_targets = tile_count // (2 * peers)
    share_rows = peer_targets * STEPS + HEAD

    def swap(x, axis, r):
        return lax.ppermute(x, axis, [(i, i ^ r) for i in range(lax.axis_size(axis))])

    reads = read_blocks.reshape(wide_peers, capacity).T
    bits = [1 << i for i in reversed(range(wide_peers.bit_length() - 1))]
    known = {0: reads}
    for bit in bits:
        known |= {distance ^ bit: swap(known[distance], "wide", bit) for distance in list(known)}

    fresh = pl.pallas_call(
        fresh_kernel,
        out_shape=pltpu.VMEM(fresh_coefs.shape, jnp.bfloat16),
        in_specs=[hbm_spec],
        out_specs=vmem_spec,
        scratch_shapes=[pltpu.SemaphoreType.DMA],
        compiler_params=params(),
        name="fresh_near",
    )(far(fresh_coefs))

    vmem_inputs = [
        VMEM(state.shape, jnp.float32),
        VMEM((own_blocks, block_rows), jnp.int32),
        VMEM((1, stim_nodes.shape[0]), jnp.int32),
        VMEM((1, STEPS), jnp.float32),
        VMEM((1, tile_count), jnp.int32),
        VMEM((1, tile_count), jnp.int32),
        VMEM((1, tile_count), jnp.int32),
        VMEM((1, tile_count), jnp.float32),
        VMEM((3, HEAD, 128), jnp.float32),
        VMEM((LENGTH, SEGS * coef_count), jnp.bfloat16),
        VMEM((slot_count, HSEG, coef_count, block_rows), jnp.bfloat16),
    ]
    table = far(jnp.asarray(expand_table(coef_count)))
    weights, ready, hist, tiles, fracs, heads = pl.pallas_call(
        functools.partial(
            prepare_kernel,
            peers=peers, own_blocks=own_blocks, peer_targets=peer_targets, capacity=capacity,
        ),
        out_shape=[
            pltpu.VMEM((tile_count, block_rows, block_rows), jnp.bfloat16),
            pltpu.VMEM((4 * own_blocks + STEPS, block_rows), jnp.float32),
            pltpu.VMEM((slot_count * LENGTH, block_rows), jnp.float32),
            pltpu.VMEM((8, 128), jnp.int32),
            pltpu.VMEM((8, 128), jnp.float32),
            pltpu.VMEM((peers, HEAD, 128), jnp.bfloat16),
        ],
        in_specs=[vmem_spec] + [hbm_spec] * 13,
        out_specs=[vmem_spec] * 6,
        scratch_shapes=[
            SMEM((capacity, wide_peers), jnp.int32),
            *vmem_inputs,
            pltpu.SemaphoreType.DMA((13,)),
        ],
        compiler_params=params(),
        name="prepare",
    )(
        fresh,
        far(tract_weights.reshape(tile_count, block_rows, block_rows)),
        far(reads),
        far(state),
        far(lesion.reshape(own_blocks, block_rows)),
        far(stim_nodes.reshape(1, -1)),
        far(stim_wave.reshape(1, -1)),
        far(tract_slot.reshape(1, tile_count)),
        far(tract_target.reshape(1, tile_count)),
        far(tract_delay.reshape(1, tile_count)),
        far(tract_frac.reshape(1, tile_count)),
        far(jnp.asarray(lane_tables(peers, peer_targets, own_blocks))),
        table,
        far(older_coefs.reshape(slot_count, HSEG, coef_count, block_rows)),
    )

    def stacked(count):
        return pltpu.VMEM((count * capacity, coef_count, block_rows), jnp.bfloat16)

    bit = bits[0]
    sent = [(0, d) for d in range(1, wide_peers) if d & bit]
    left = [(0, d) for d in range(1, wide_peers) if not d & bit]
    plan = [[d for _, d in items] for items in (sent, left) if items]
    payload, *rest = pl.pallas_call(
        functools.partial(pick_kernel, capacity=capacity, peers=wide_peers, plan=plan),
        out_shape=[stacked(len(items)) for items in plan],
        in_specs=[vmem_spec] * wide_peers,
        out_specs=[vmem_spec] * len(plan),
        scratch_shapes=[
            SMEM((wide_peers - 1, capacity, wide_peers), jnp.int32),
            pltpu.SemaphoreType.DMA((wide_peers - 1,)),
        ],
        compiler_params=params(),
        name="pick_blocks",
    )(*[known[d] for d in range(1, wide_peers)], fresh)
    news = [swap(payload, "wide", bit)]
    came = [(source ^ bit, d ^ bit) for source, d in sent]
    news_plan = [(0, i, source) for i, (source, d) in enumerate(came) if d == 0]
    for bit in bits[1:]:
        here = [(item, (0, i)) for i, item in enumerate(left)]
        here += [(item, (len(rest), i)) for i, item in enumerate(came) if item[1]]
        going = [x for x in here if x[0][1] & bit]
        staying = [x for x in here if not x[0][1] & bit]
        plan = [[place for _, place in items] for items in (going, staying) if items]
        payload, *rest = pl.pallas_call(
            functools.partial(
                forward_kernel, capacity=capacity, sources=len(rest) + 1, plan=plan
            ),
            out_shape=[stacked(len(places)) for places in plan],
            in_specs=[vmem_spec] * (len(rest) + 2),
            out_specs=[vmem_spec] * len(plan),
            compiler_params=params(),
            name=f"pass_on_{bit}",
        )(*rest, news[-1], tiles)
        news.append(swap(payload, "wide", bit))
        came = [(source ^ bit, d ^ bit) for (source, d), _ in going]
        left = [item for item, _ in staying]
        news_plan += [(len(news) - 1, i, source) for i, (source, d) in enumerate(came) if d == 0]

    shares = [None] * peers
    half = (peers + 1) // 2
    arrived = [None] * peers
    for parts in (range(half), range(half, peers)):
        far_call = parts[0] == 0
        others = news if far_call else [arrived[peers - 1]]
        result = pl.pallas_call(
            functools.partial(
                tract_kernel,
                parts=parts, plan=news_plan if far_call else [], peers=peers,
                capacity=capacity, peer_targets=peer_targets,
            ),
            out_shape=[pltpu.VMEM((share_rows, block_rows), jnp.bfloat16)] * len(parts)
            + ([pltpu.VMEM(hist.shape, jnp.float32)] if far_call else []),
            in_specs=[vmem_spec] * (6 + len(others)),
            out_specs=[vmem_spec] * (len(parts) + far_call),
            scratch_shapes=[
                SMEM((8, 128), jnp.int32),
                SMEM((8, 128), jnp.float32),
                VMEM(((len(parts) * peer_targets + 1) * STEPS, block_rows), jnp.float32),
                pltpu.SemaphoreType.DMA((2,)),
            ],
            compiler_params=params(),
            name="far_tiles" if far_call else "near_tiles",
        )(tiles, fracs, table, heads, weights, hist, *others)
        if far_call:
            hist = result[-1]
        for part, share in zip(parts, result):
            r = peers - 1 - part
            arrived[r] = swap(share, "narrow", r) if r else share

    high, low = fit_tables(coef_count)
    new_coefs, final_state = pl.pallas_call(
        functools.partial(
            window_kernel,
            peers=peers, own_blocks=own_blocks, peer_targets=peer_targets, coef_count=coef_count,
        ),
        out_shape=[
            jax.ShapeDtypeStruct(fresh_coefs.shape, jnp.bfloat16),
            jax.ShapeDtypeStruct(state.shape, jnp.float32),
        ],
        in_specs=[vmem_spec] * (peers + 3),
        out_specs=[vmem_spec] * 2,
        scratch_shapes=[
            VMEM((own_blocks * STEPS, block_rows), jnp.float32),
            VMEM((2, own_blocks, block_rows), jnp.float32),
        ],
        compiler_params=params(),
        name="window_steps",
    )(*arrived[::-1], ready, high, low)
    return new_coefs, final_state


def solution(mesh):
    in_specs = (
        P(("sweep", "wide", "narrow"), None, None),
        P(("sweep", "wide"), "narrow", None, None, None, None),
        P(None, ("sweep", "wide", "narrow")),
        P(("sweep", "wide", "narrow")),
        P("sweep"),
        P("sweep"),
        P("wide", "narrow", None, None),
        P("wide", "narrow", None),
        P("wide", "narrow", None),
        P("wide", "narrow", None),
        P("wide", "narrow", None),
        P("wide", "narrow", None, None, None),
    )
    out_specs = (P(("sweep", "wide", "narrow"), None, None), P(None, ("sweep", "wide", "narrow")))
    return jax.shard_map(local, mesh=mesh, in_specs=in_specs, out_specs=out_specs, check_vma=False)
```

```python
import functools
import math

import jax
import jax.numpy as jnp
import ml_dtypes
import numpy as np
from jax import lax
from jax.experimental import pallas as pl
from jax.experimental.pallas import tpu as pltpu
from jax.sharding import PartitionSpec as P

STEPS = 32
HSEG = 2
SEGS = HSEG + 1
LENGTH = SEGS * STEPS
GROUP = 4
HEAD = 16
UNROLL = 16

excite_rate = 0.1
inhibit_rate = 0.05
excite_excite = 1.5
inhibit_excite = 2.0
excite_inhibit = 2.0
inhibit_inhibit = 0.5
excite_offset = 0.5
inhibit_offset = 0.5
tract_gain = 2.0

SMEM = pltpu.SMEM
VMEM = pltpu.VMEM
vmem_spec = pl.BlockSpec(memory_space=VMEM)
hbm_spec = pl.BlockSpec(memory_space=pltpu.HBM)


def basis_table(coef_count, step_count):
    order = np.arange(coef_count, dtype=np.float32)[:, None]
    places = np.arange(step_count, dtype=np.float32)[None, :]
    angles = np.float32(np.pi) * (step_count - places - np.float32(0.5)) / np.float32(step_count)
    return np.cos((order * angles).astype(np.float64)).astype(np.float32)


def expand_table(coef_count):
    basis = basis_table(coef_count, STEPS).astype(ml_dtypes.bfloat16)
    table = np.zeros((LENGTH, SEGS * coef_count), ml_dtypes.bfloat16)
    for seg in range(SEGS):
        table[seg * STEPS : (seg + 1) * STEPS, seg * coef_count : (seg + 1) * coef_count] = basis.T
    return table


def fit_tables(coef_count):
    scales = np.where(np.arange(coef_count)[:, None] == 0, 1.0, 2.0) / STEPS
    fit = (basis_table(coef_count, STEPS) * scales).astype(np.float32)
    whole = np.zeros((GROUP * coef_count, GROUP * STEPS), np.float32)
    for g in range(GROUP):
        whole[g * coef_count : (g + 1) * coef_count, g * STEPS : (g + 1) * STEPS] = fit
    high = whole.astype(ml_dtypes.bfloat16)
    low = (whole - high.astype(np.float32)).astype(ml_dtypes.bfloat16)
    return high, low


TOGETHER = 8


def lane_tables(peers, peer_targets, own_blocks):
    width = TOGETHER * peer_targets
    assert TOGETHER * own_blocks <= 256 and peers * width <= HEAD * 128
    lane = np.arange(HEAD * 128)
    used = lane < peers * width
    within = lane % width
    rank = np.where(used, within // TOGETHER, -5)
    offset = within % TOGETHER * own_blocks + 1
    place = np.where(used, lane // width, -5)
    return np.stack([rank, offset, place]).astype(np.float32).reshape(3, HEAD, 128)


def prepare_kernel(
    fresh_hbm, reads_hbm, state_hbm, lesion_hbm, stim_hbm, wave_hbm, slot_hbm, target_hbm,
    delay_hbm, lanes_hbm, table_hbm, older_hbm,
    fresh_out, ready_out, hist_out, tiles_out, head_out,
    reads, state, lesion, stim, wave, slot, target, delay, lanes, table, older, sems,
    *, peers, own_blocks, peer_targets, capacity,
):
    pairs = [
        (fresh_hbm, fresh_out), (reads_hbm, reads), (target_hbm, target), (slot_hbm, slot),
        (delay_hbm, delay), (lanes_hbm, lanes), (table_hbm, table), (older_hbm, older),
        (state_hbm, state), (lesion_hbm, lesion), (stim_hbm, stim), (wave_hbm, wave),
    ]
    copies = [
        pltpu.make_async_copy(source, into, sems.at[i]) for i, (source, into) in enumerate(pairs)
    ]
    for copy in copies:
        copy.start()
    for copy in copies[2:6]:
        copy.wait()
    place = lax.axis_index("narrow")
    owner = lax.axis_index("wide")
    tile_count = target.shape[1]
    target_count = peers * own_blocks

    numbers = lax.broadcasted_iota(jnp.int32, (target_count, tile_count), 0)
    hits = jnp.where(numbers == target[...], 1.0, 0.0)
    held = jnp.dot(
        hits.astype(jnp.bfloat16), jnp.ones((tile_count, 128), jnp.bfloat16),
        preferred_element_type=jnp.float32,
    )
    held = jnp.minimum(held, 1.0)
    shape = (own_blocks, own_blocks)
    below = jnp.where(
        lax.broadcasted_iota(jnp.int32, shape, 0) > lax.broadcasted_iota(jnp.int32, shape, 1),
        1.0, 0.0,
    ).astype(jnp.bfloat16)
    block = lax.broadcasted_iota(jnp.int32, (own_blocks, 128), 0).astype(jnp.float32)
    ranks = jnp.zeros((1, tile_count), jnp.float32)
    head_rows = pl.cdiv(peers * TOGETHER * peer_targets, 128)
    for p in range(peers):
        part = slice(p * own_blocks, (p + 1) * own_blocks)
        rank = jnp.dot(below, held[part].astype(jnp.bfloat16), preferred_element_type=jnp.float32)
        ranks = ranks + jnp.sum(hits[part] * rank[:, :tile_count], axis=0, keepdims=True)
        rank = jnp.where(held[part] > 0.5, rank, -1.0)
        source = (place ^ p).astype(jnp.float32)
        rows = []
        for h in range(head_rows):
            match = rank == lanes[0, h : h + 1, :]
            ids = jnp.sum(jnp.where(match, block, 0.0), axis=0, keepdims=True)
            mine = lanes[2, h : h + 1, :] == source
            rows.append(jnp.where(mine, ids + lanes[1, h : h + 1, :], 0.0))
        rows.append(jnp.zeros((HEAD - head_rows, 128), jnp.float32))
        head_out[p] = jnp.concatenate(rows, axis=0).astype(jnp.bfloat16)

    across = jnp.zeros((1, tile_count), jnp.int32)
    for p in range(1, peers):
        across = across + jnp.where(target[...] >= p * own_blocks, 1, 0)
    tiles_out[0:1, :tile_count] = slot[...] * LENGTH + (LENGTH - 1) - delay[...]
    tiles_out[1:2, :tile_count] = (across * peer_targets + ranks.astype(jnp.int32)) * TOGETHER

    for copy in copies[6:8]:
        copy.wait()
    coef_count = older.shape[2]
    earlier = HSEG * STEPS
    for s in range(older.shape[0]):
        segments = [older[s, h] for h in range(HSEG - 1, -1, -1)]
        hist_out[s * LENGTH : s * LENGTH + earlier, :] = jnp.dot(
            table[:earlier, : HSEG * coef_count], jnp.concatenate(segments, axis=0),
            preferred_element_type=jnp.float32,
        )
        hist_out[s * LENGTH + earlier : (s + 1) * LENGTH, :] = jnp.zeros(
            (STEPS, hist_out.shape[1]), jnp.float32
        )
    for copy in copies[:2]:
        copy.wait()
    for c in range(capacity):
        rows = pl.ds(pl.multiple_of((owner * capacity + c) * LENGTH + earlier, 8), STEPS)
        hist_out[rows, :] = jnp.dot(
            table[:STEPS, :coef_count], fresh_out[jnp.maximum(reads[c, owner], 0)],
            preferred_element_type=jnp.float32,
        )

    for copy in copies[8:12]:
        copy.wait()
    block_rows = lesion.shape[1]
    for b in range(own_blocks):
        piece = state[:, b * block_rows : (b + 1) * block_rows]
        ready_out[b : b + 1, :] = piece[0:1, :]
        ready_out[own_blocks + b : own_blocks + b + 1, :] = piece[1:2, :]
    ready_out[2 * own_blocks : 3 * own_blocks, :] = tract_gain * (
        1.0 - lesion[...].astype(jnp.float32)
    )
    stim_count = stim.shape[1]
    nodes = stim[...] - (owner * peers + place) * (own_blocks * block_rows)
    blocks = lax.shift_right_arithmetic(nodes, block_rows.bit_length() - 1)
    offsets = nodes & (block_rows - 1)
    in_block = lax.broadcasted_iota(jnp.int32, (own_blocks, stim_count), 0) == blocks
    at_offset = lax.broadcasted_iota(jnp.int32, (block_rows, stim_count), 0) == offsets
    ready_out[3 * own_blocks : 4 * own_blocks, :] = lax.dot_general(
        jnp.where(in_block, 1.0, 0.0).astype(jnp.bfloat16),
        jnp.where(at_offset, 1.0, 0.0).astype(jnp.bfloat16),
        (((1,), (1,)), ((), ())),
        preferred_element_type=jnp.float32,
    )
    shape = (STEPS, STEPS)
    diagonal = lax.broadcasted_iota(jnp.int32, shape, 0) == lax.broadcasted_iota(jnp.int32, shape, 1)
    column = jnp.sum(jnp.where(diagonal, wave[...], 0.0), axis=1, keepdims=True)
    ready_out[4 * own_blocks :, :] = jnp.broadcast_to(column, (STEPS, block_rows))


def weights_kernel(weights_hbm, weights_out, sem):
    copy = pltpu.make_async_copy(weights_hbm, weights_out, sem)
    copy.start()
    copy.wait()


def pick_kernel(*refs, capacity, peers):
    tables = refs[: peers - 1]
    fresh = refs[peers - 1]
    outs = refs[peers : 2 * peers - 1]
    asked, sems = refs[2 * peers - 1 :]
    place = lax.axis_index("wide")
    copies = [pltpu.make_async_copy(tables[r], asked.at[r], sems.at[r]) for r in range(peers - 1)]
    for copy in copies:
        copy.start()
    for r in range(peers - 1):
        copies[r].wait()
        for c in range(capacity):
            outs[r][c] = fresh[jnp.maximum(asked[r, c, place], 0)]


def tract_kernel(
    frac_hbm, tiles_ref, table_ref, head_ref, weights, hist_ref, *refs,
    wide_peers, peers, capacity, peer_targets,
):
    news = refs[: wide_peers - 1]
    outs = refs[wide_peers - 1 : wide_peers - 1 + peers]
    tiles, frac, hist, total, sems = refs[wide_peers - 1 + peers :]
    place = lax.axis_index("narrow")
    owner = lax.axis_index("wide")
    copies = [
        pltpu.make_async_copy(tiles_ref, tiles, sems.at[0]),
        pltpu.make_async_copy(frac_hbm, frac, sems.at[1]),
    ]
    for copy in copies:
        copy.start()
    total[...] = jnp.zeros_like(total)
    hist[...] = hist_ref[...]
    for i, block in enumerate(news):
        table = table_ref[:STEPS, : block.shape[1]]
        for c in range(capacity):
            slot = (owner ^ (wide_peers - 1 - i)) * capacity + c
            rows = pl.ds(pl.multiple_of(slot * LENGTH + HSEG * STEPS, 8), STEPS)
            hist[rows, :] = jnp.dot(table, block[c], preferred_element_type=jnp.float32)
    for copy in copies:
        copy.wait()

    span = peer_targets * TOGETHER
    pitch = peers * span
    for turn in range(0, frac.shape[1], UNROLL):
        sums = []
        for t in range(turn, turn + UNROLL):
            fraction = frac[0, t]
            start = tiles[0, t]
            earlier = hist[pl.ds(start, STEPS), :]
            later = hist[pl.ds(start + 1, STEPS), :]
            delayed = ((1.0 - fraction) * later + fraction * earlier).astype(jnp.bfloat16)
            sums.append(
                lax.dot_general(
                    delayed, weights[t], (((1,), (1,)), ((), ())),
                    preferred_element_type=jnp.float32,
                )
            )
        for t in range(turn, turn + UNROLL):
            first = tiles[1, t]
            for g in range(STEPS // TOGETHER):
                rows = pl.ds(pl.multiple_of(first + g * pitch, 8), TOGETHER)
                total[rows, :] += sums[t - turn][g * TOGETHER : (g + 1) * TOGETHER]

    for r in range(peers):
        for g in range(STEPS // TOGETHER):
            first = pl.multiple_of(g * pitch + (place ^ r) * span, 8)
            outs[r][g * span : (g + 1) * span, :] = total[pl.ds(first, span), :].astype(
                jnp.bfloat16
            )
        outs[r][peer_targets * STEPS :, :] = head_ref[place ^ r]


def window_kernel(*refs, peers, own_blocks, peer_targets, coef_count):
    shares = dict(zip([*range(2, peers), 1, 0], refs))
    ready_ref, high_ref, low_ref, coefs_out, state_out, samples, rates = refs[peers:]
    block_rows = ready_ref.shape[1]
    width = TOGETHER * peer_targets
    span = peer_targets * STEPS

    head = shares[0][span:, :].astype(jnp.float32)
    for r in range(1, peers):
        head = head + shares[r][span:, :].astype(jnp.float32)
    row = lax.broadcasted_iota(jnp.int32, (TOGETHER * own_blocks, 128), 0).astype(jnp.float32) + 1.0
    columns = peers * width
    scatter = jnp.concatenate(
        [
            jnp.where(row == head[h : h + 1, :], 1.0, 0.0).astype(jnp.bfloat16)
            for h in range(pl.cdiv(columns, 128))
        ],
        axis=1,
    )[:, :columns]

    excite, inhibit, gain, counts = [
        ready_ref[i * own_blocks : (i + 1) * own_blocks, :] for i in range(4)
    ]
    for pair in range(0, STEPS // TOGETHER, 2):
        arrived = jnp.concatenate(
            [
                jnp.concatenate(
                    [shares[r][g * width : (g + 1) * width, :] for r in range(peers)], axis=0
                )
                for g in (pair, pair + 1)
            ],
            axis=1,
        )
        inflow = jnp.dot(scatter, arrived, preferred_element_type=jnp.float32)
        for jj in range(2 * TOGETHER):
            j = pair * TOGETHER + jj
            wave = ready_ref[4 * own_blocks + j : 4 * own_blocks + j + 1, :]
            first = jj % TOGETHER * own_blocks
            left = jj // TOGETHER * block_rows
            forcing = (
                gain * inflow[first : first + own_blocks, left : left + block_rows] + wave * counts
            )
            excite_drive = (
                excite_excite * excite - inhibit_excite * inhibit + forcing - excite_offset
            )
            inhibit_drive = excite_inhibit * excite - inhibit_inhibit * inhibit - inhibit_offset
            excite, inhibit = (
                excite + excite_rate * (0.5 * jnp.tanh(0.5 * excite_drive) + 0.5 - excite),
                inhibit + inhibit_rate * (0.5 * jnp.tanh(0.5 * inhibit_drive) + 0.5 - inhibit),
            )
            samples[pl.ds(j, own_blocks, stride=STEPS), :] = excite
    rates[0] = excite
    rates[1] = inhibit
    for b in range(own_blocks):
        where = slice(b * block_rows, (b + 1) * block_rows)
        state_out[0:1, where] = rates[0, b : b + 1, :]
        state_out[1:2, where] = rates[1, b : b + 1, :]

    high = high_ref[...]
    low = low_ref[...]
    rows = GROUP * STEPS
    for g in range(own_blocks // GROUP):
        part = samples[g * rows : (g + 1) * rows, :]
        part_high = part.astype(jnp.bfloat16)
        part_low = (part - part_high.astype(jnp.float32)).astype(jnp.bfloat16)
        fitted = (
            jnp.dot(high, part_high, preferred_element_type=jnp.float32)
            + jnp.dot(high, part_low, preferred_element_type=jnp.float32)
            + jnp.dot(low, part_high, preferred_element_type=jnp.float32)
        )
        coefs_out[g * GROUP : (g + 1) * GROUP] = fitted.astype(jnp.bfloat16).reshape(
            GROUP, coef_count, block_rows
        )


def far(x):
    return pltpu.with_memory_space_constraint(x, pltpu.HBM)


def params():
    return pltpu.CompilerParams(vmem_limit_bytes=20 << 20)


def local(
    fresh_coefs,
    older_coefs,
    state,
    lesion,
    stim_nodes,
    stim_wave,
    read_blocks,
    tract_slot,
    tract_target,
    tract_delay,
    tract_frac,
    tract_weights,
):
    wide_peers = lax.axis_size("wide")
    peers = lax.axis_size("narrow")
    own_blocks, coef_count, block_rows = fresh_coefs.shape
    capacity = read_blocks.shape[3]
    slot_count = wide_peers * capacity
    tile_count = tract_slot.shape[2]
    peer_targets = tile_count // (2 * peers)
    share_rows = peer_targets * STEPS + HEAD

    def swap(x, axis, r):
        return lax.ppermute(x, axis, [(i, i ^ r) for i in range(lax.axis_size(axis))])

    reads = read_blocks.reshape(wide_peers, capacity).T
    asked = [swap(reads, "wide", r) for r in range(1, wide_peers)]

    vmem_inputs = [
        VMEM(state.shape, jnp.float32),
        VMEM((own_blocks, block_rows), jnp.int32),
        VMEM((1, stim_nodes.shape[0]), jnp.int32),
        VMEM((1, STEPS), jnp.float32),
        VMEM((1, tile_count), jnp.int32),
        VMEM((1, tile_count), jnp.int32),
        VMEM((1, tile_count), jnp.int32),
        VMEM((3, HEAD, 128), jnp.float32),
        VMEM((LENGTH, SEGS * coef_count), jnp.bfloat16),
        VMEM((slot_count, HSEG, coef_count, block_rows), jnp.bfloat16),
    ]
    table = far(jnp.asarray(expand_table(coef_count)))
    fresh, ready, hist, tiles, heads = pl.pallas_call(
        functools.partial(
            prepare_kernel,
            peers=peers, own_blocks=own_blocks, peer_targets=peer_targets, capacity=capacity,
        ),
        out_shape=[
            pltpu.VMEM(fresh_coefs.shape, jnp.bfloat16),
            pltpu.VMEM((4 * own_blocks + STEPS, block_rows), jnp.float32),
            pltpu.VMEM((slot_count * LENGTH, block_rows), jnp.float32),
            pltpu.VMEM((8, 128), jnp.int32),
            pltpu.VMEM((peers, HEAD, 128), jnp.bfloat16),
        ],
        in_specs=[hbm_spec] * 12,
        out_specs=[vmem_spec] * 5,
        scratch_shapes=[
            SMEM((capacity, wide_peers), jnp.int32),
            *vmem_inputs,
            pltpu.SemaphoreType.DMA((12,)),
        ],
        compiler_params=params(),
        name="prepare",
    )(
        far(fresh_coefs),
        far(reads),
        far(state),
        far(lesion.reshape(own_blocks, block_rows)),
        far(stim_nodes.reshape(1, -1)),
        far(stim_wave.reshape(1, -1)),
        far(tract_slot.reshape(1, tile_count)),
        far(tract_target.reshape(1, tile_count)),
        far(tract_delay.reshape(1, tile_count)),
        far(jnp.asarray(lane_tables(peers, peer_targets, own_blocks))),
        table,
        far(older_coefs.reshape(slot_count, HSEG, coef_count, block_rows)),
    )

    picked = pl.pallas_call(
        functools.partial(pick_kernel, capacity=capacity, peers=wide_peers),
        out_shape=[pltpu.VMEM((capacity, coef_count, block_rows), jnp.bfloat16)]
        * (wide_peers - 1),
        in_specs=[vmem_spec] * wide_peers,
        out_specs=[vmem_spec] * (wide_peers - 1),
        scratch_shapes=[
            SMEM((wide_peers - 1, capacity, wide_peers), jnp.int32),
            pltpu.SemaphoreType.DMA((wide_peers - 1,)),
        ],
        compiler_params=params(),
        name="pick_blocks",
    )(*asked, fresh)
    news = [swap(picked[r - 1], "wide", r) for r in range(wide_peers - 1, 0, -1)]

    weights_shape = pltpu.VMEM((tile_count, block_rows, block_rows), jnp.bfloat16)
    weights = pl.pallas_call(
        weights_kernel,
        out_shape=weights_shape,
        in_specs=[hbm_spec],
        out_specs=vmem_spec,
        scratch_shapes=[pltpu.SemaphoreType.DMA],
        compiler_params=params(),
        name="weights_near",
    )(far(tract_weights.reshape(tile_count, block_rows, block_rows)))

    shares = pl.pallas_call(
        functools.partial(
            tract_kernel,
            wide_peers=wide_peers, peers=peers, capacity=capacity, peer_targets=peer_targets,
        ),
        out_shape=[pltpu.VMEM((share_rows, block_rows), jnp.bfloat16)] * peers,
        in_specs=[hbm_spec] + [vmem_spec] * (4 + wide_peers),
        out_specs=[vmem_spec] * peers,
        scratch_shapes=[
            SMEM((8, 128), jnp.int32),
            SMEM((1, tile_count), jnp.float32),
            VMEM((slot_count * LENGTH, block_rows), jnp.float32),
            VMEM((peers * peer_targets * STEPS, block_rows), jnp.float32),
            pltpu.SemaphoreType.DMA((2,)),
        ],
        compiler_params=params(),
        name="tract_tiles",
    )(far(tract_frac.reshape(1, tile_count)), tiles, table, heads, weights, hist, *news)
    order = [*range(2, peers), 1, 0]
    arrived = [swap(shares[r], "narrow", r) if r else shares[r] for r in order]

    high, low = fit_tables(coef_count)
    new_coefs, final_state = pl.pallas_call(
        functools.partial(
            window_kernel,
            peers=peers, own_blocks=own_blocks, peer_targets=peer_targets, coef_count=coef_count,
        ),
        out_shape=[
            jax.ShapeDtypeStruct(fresh_coefs.shape, jnp.bfloat16),
            jax.ShapeDtypeStruct(state.shape, jnp.float32),
        ],
        in_specs=[vmem_spec] * (peers + 3),
        out_specs=[vmem_spec] * 2,
        scratch_shapes=[
            VMEM((own_blocks * STEPS, block_rows), jnp.float32),
            VMEM((2, own_blocks, block_rows), jnp.float32),
        ],
        compiler_params=params(),
        name="window_steps",
    )(*arrived, ready, high, low)
    return new_coefs, final_state


def solution(mesh):
    in_specs = (
        P(("sweep", "wide", "narrow"), None, None),
        P(("sweep", "wide"), "narrow", None, None, None, None),
        P(None, ("sweep", "wide", "narrow")),
        P(("sweep", "wide", "narrow")),
        P("sweep"),
        P("sweep"),
        P("wide", "narrow", None, None),
        P("wide", "narrow", None),
        P("wide", "narrow", None),
        P("wide", "narrow", None),
        P("wide", "narrow", None),
        P("wide", "narrow", None, None, None),
    )
    out_specs = (P(("sweep", "wide", "narrow"), None, None), P(None, ("sweep", "wide", "narrow")))
    return jax.shard_map(local, mesh=mesh, in_specs=in_specs, out_specs=out_specs, check_vma=False)
```

```python
import functools
import math

import jax
import jax.numpy as jnp
import ml_dtypes
import numpy as np
from jax import lax
from jax.experimental import pallas as pl
from jax.experimental.pallas import tpu as pltpu
from jax.sharding import PartitionSpec as P

STEPS = 32
HSEG = 2
SEGS = HSEG + 1
LENGTH = SEGS * STEPS
GROUP = 4
HEAD = 16
CHUNKS = 8
UNROLL = 4

excite_rate = 0.1
inhibit_rate = 0.05
excite_excite = 1.5
inhibit_excite = 2.0
excite_inhibit = 2.0
inhibit_inhibit = 0.5
excite_offset = 0.5
inhibit_offset = 0.5
tract_gain = 2.0

SMEM = pltpu.SMEM
VMEM = pltpu.VMEM
vmem_spec = pl.BlockSpec(memory_space=VMEM)
hbm_spec = pl.BlockSpec(memory_space=pltpu.HBM)


def basis_table(coef_count, step_count):
    order = np.arange(coef_count, dtype=np.float32)[:, None]
    places = np.arange(step_count, dtype=np.float32)[None, :]
    angles = np.float32(np.pi) * (step_count - places - np.float32(0.5)) / np.float32(step_count)
    return np.cos((order * angles).astype(np.float64)).astype(np.float32)


def expand_table(coef_count):
    basis = basis_table(coef_count, STEPS).astype(ml_dtypes.bfloat16)
    table = np.zeros((LENGTH, SEGS * coef_count), ml_dtypes.bfloat16)
    for seg in range(SEGS):
        table[seg * STEPS : (seg + 1) * STEPS, seg * coef_count : (seg + 1) * coef_count] = basis.T
    return table


def fit_tables(coef_count):
    scales = np.where(np.arange(coef_count)[:, None] == 0, 1.0, 2.0) / STEPS
    fit = (basis_table(coef_count, STEPS) * scales).astype(np.float32)
    whole = np.zeros((GROUP * coef_count, GROUP * STEPS), np.float32)
    for g in range(GROUP):
        whole[g * coef_count : (g + 1) * coef_count, g * STEPS : (g + 1) * STEPS] = fit
    high = whole.astype(ml_dtypes.bfloat16)
    low = (whole - high.astype(np.float32)).astype(ml_dtypes.bfloat16)
    return high, low


TOGETHER = 8


def lane_tables(peers, peer_targets, own_blocks):
    width = TOGETHER * peer_targets
    assert TOGETHER * own_blocks <= 256 and peers * width <= HEAD * 128
    lane = np.arange(HEAD * 128)
    used = lane < peers * width
    within = lane % width
    rank = np.where(used, within // TOGETHER, -5)
    offset = within % TOGETHER * own_blocks + 1
    place = np.where(used, lane // width, -5)
    return np.stack([rank, offset, place]).astype(np.float32).reshape(3, HEAD, 128)


def prepare_kernel(
    fresh_ref, reads_hbm, state_hbm, lesion_hbm, stim_hbm, wave_hbm, slot_hbm, target_hbm,
    delay_hbm, lanes_hbm, table_hbm, older_hbm, weights_hbm,
    weights_out, ready_out, hist_out, tiles_out, head_out,
    reads, state, lesion, stim, wave, slot, target, delay, lanes, table, older, sems,
    *, peers, own_blocks, peer_targets, capacity,
):
    pairs = [
        (reads_hbm, reads), (target_hbm, target), (slot_hbm, slot),
        (delay_hbm, delay), (lanes_hbm, lanes), (table_hbm, table), (older_hbm, older),
        (state_hbm, state), (lesion_hbm, lesion), (stim_hbm, stim), (wave_hbm, wave),
    ]
    copies = [
        pltpu.make_async_copy(source, into, sems.at[i]) for i, (source, into) in enumerate(pairs)
    ]
    part = weights_hbm.shape[0] // CHUNKS
    for i in range(CHUNKS):
        rows = pl.ds(i * part, part)
        copies.append(
            pltpu.make_async_copy(
                weights_hbm.at[rows], weights_out.at[rows], sems.at[len(pairs) + i]
            )
        )
    for copy in copies:
        copy.start()
    for copy in copies[1:5]:
        copy.wait()
    place = lax.axis_index("narrow")
    owner = lax.axis_index("wide")
    tile_count = target.shape[1]
    target_count = peers * own_blocks

    numbers = lax.broadcasted_iota(jnp.int32, (target_count, tile_count), 0)
    hits = jnp.where(numbers == target[...], 1.0, 0.0)
    held = jnp.dot(
        hits.astype(jnp.bfloat16), jnp.ones((tile_count, 128), jnp.bfloat16),
        preferred_element_type=jnp.float32,
    )
    held = jnp.minimum(held, 1.0)
    shape = (own_blocks, own_blocks)
    below = jnp.where(
        lax.broadcasted_iota(jnp.int32, shape, 0) > lax.broadcasted_iota(jnp.int32, shape, 1),
        1.0, 0.0,
    ).astype(jnp.bfloat16)
    block = lax.broadcasted_iota(jnp.int32, (own_blocks, 128), 0).astype(jnp.float32)
    ranks = jnp.zeros((1, tile_count), jnp.float32)
    head_rows = pl.cdiv(peers * TOGETHER * peer_targets, 128)
    for p in range(peers):
        part = slice(p * own_blocks, (p + 1) * own_blocks)
        rank = jnp.dot(below, held[part].astype(jnp.bfloat16), preferred_element_type=jnp.float32)
        ranks = ranks + jnp.sum(hits[part] * rank[:, :tile_count], axis=0, keepdims=True)
        rank = jnp.where(held[part] > 0.5, rank, -1.0)
        source = (place ^ p).astype(jnp.float32)
        rows = []
        for h in range(head_rows):
            match = rank == lanes[0, h : h + 1, :]
            ids = jnp.sum(jnp.where(match, block, 0.0), axis=0, keepdims=True)
            mine = lanes[2, h : h + 1, :] == source
            rows.append(jnp.where(mine, ids + lanes[1, h : h + 1, :], 0.0))
        rows.append(jnp.zeros((HEAD - head_rows, 128), jnp.float32))
        head_out[p] = jnp.concatenate(rows, axis=0).astype(jnp.bfloat16)

    across = jnp.zeros((1, tile_count), jnp.int32)
    for p in range(1, peers):
        across = across + jnp.where(target[...] >= p * own_blocks, 1, 0)
    tiles_out[0:1, :tile_count] = slot[...] * LENGTH + (LENGTH - 1) - delay[...]
    tiles_out[1:2, :tile_count] = (across * peer_targets + ranks.astype(jnp.int32)) * TOGETHER

    for copy in copies[5:7]:
        copy.wait()
    coef_count = older.shape[2]
    earlier = HSEG * STEPS
    for s in range(older.shape[0]):
        segments = [older[s, h] for h in range(HSEG - 1, -1, -1)]
        hist_out[s * LENGTH : s * LENGTH + earlier, :] = jnp.dot(
            table[:earlier, : HSEG * coef_count], jnp.concatenate(segments, axis=0),
            preferred_element_type=jnp.float32,
        )
        hist_out[s * LENGTH + earlier : (s + 1) * LENGTH, :] = jnp.zeros(
            (STEPS, hist_out.shape[1]), jnp.float32
        )
    copies[0].wait()
    for c in range(capacity):
        rows = pl.ds(pl.multiple_of((owner * capacity + c) * LENGTH + earlier, 8), STEPS)
        hist_out[rows, :] = jnp.dot(
            table[:STEPS, :coef_count], fresh_ref[jnp.maximum(reads[c, owner], 0)],
            preferred_element_type=jnp.float32,
        )

    for copy in copies[7:11]:
        copy.wait()
    block_rows = lesion.shape[1]
    for b in range(own_blocks):
        piece = state[:, b * block_rows : (b + 1) * block_rows]
        ready_out[b : b + 1, :] = piece[0:1, :]
        ready_out[own_blocks + b : own_blocks + b + 1, :] = piece[1:2, :]
    ready_out[2 * own_blocks : 3 * own_blocks, :] = tract_gain * (
        1.0 - lesion[...].astype(jnp.float32)
    )
    stim_count = stim.shape[1]
    nodes = stim[...] - (owner * peers + place) * (own_blocks * block_rows)
    blocks = lax.shift_right_arithmetic(nodes, block_rows.bit_length() - 1)
    offsets = nodes & (block_rows - 1)
    in_block = lax.broadcasted_iota(jnp.int32, (own_blocks, stim_count), 0) == blocks
    at_offset = lax.broadcasted_iota(jnp.int32, (block_rows, stim_count), 0) == offsets
    ready_out[3 * own_blocks : 4 * own_blocks, :] = lax.dot_general(
        jnp.where(in_block, 1.0, 0.0).astype(jnp.bfloat16),
        jnp.where(at_offset, 1.0, 0.0).astype(jnp.bfloat16),
        (((1,), (1,)), ((), ())),
        preferred_element_type=jnp.float32,
    )
    shape = (STEPS, STEPS)
    diagonal = lax.broadcasted_iota(jnp.int32, shape, 0) == lax.broadcasted_iota(jnp.int32, shape, 1)
    column = jnp.sum(jnp.where(diagonal, wave[...], 0.0), axis=1, keepdims=True)
    ready_out[4 * own_blocks :, :] = jnp.broadcast_to(column, (STEPS, block_rows))
    for copy in copies[11:]:
        copy.wait()


def fresh_kernel(fresh_hbm, fresh_out, sem):
    copy = pltpu.make_async_copy(fresh_hbm, fresh_out, sem)
    copy.start()
    copy.wait()


def pick_kernel(*refs, capacity, peers, ways):
    tables = refs[: peers - 1]
    fresh = refs[peers - 1]
    outs = refs[peers : 2 * peers - 1]
    asked, sems = refs[2 * peers - 1 :]
    place = lax.axis_index("wide")
    copies = [pltpu.make_async_copy(tables[r], asked.at[r], sems.at[r]) for r in range(peers - 1)]
    for copy in copies:
        copy.start()
    for i, r in enumerate(ways):
        copies[i].wait()
        for c in range(capacity):
            outs[r - 1][c] = fresh[jnp.maximum(asked[i, c, place], 0)]


def tract_kernel(
    frac_hbm, tiles_ref, table_ref, head_ref, weights, hist_ref, *refs,
    wide_peers, peers, capacity, peer_targets,
):
    news = refs[: wide_peers - 1]
    outs = refs[wide_peers - 1 : wide_peers - 1 + peers]
    tiles, frac, hist, total, sems = refs[wide_peers - 1 + peers :]
    place = lax.axis_index("narrow")
    owner = lax.axis_index("wide")
    copies = [
        pltpu.make_async_copy(tiles_ref, tiles, sems.at[0]),
        pltpu.make_async_copy(frac_hbm, frac, sems.at[1]),
    ]
    for copy in copies:
        copy.start()
    total[...] = jnp.zeros_like(total)
    hist[...] = hist_ref[...]
    for i, block in enumerate(news):
        table = table_ref[:STEPS, : block.shape[1]]
        for c in range(capacity):
            slot = (owner ^ (wide_peers - 1 - i)) * capacity + c
            rows = pl.ds(pl.multiple_of(slot * LENGTH + HSEG * STEPS, 8), STEPS)
            hist[rows, :] = jnp.dot(table, block[c], preferred_element_type=jnp.float32)
    for copy in copies:
        copy.wait()

    span = peer_targets * TOGETHER
    pitch = peers * span
    for turn in range(0, frac.shape[1], UNROLL):
        sums = []
        for t in range(turn, turn + UNROLL):
            fraction = frac[0, t]
            start = tiles[0, t]
            earlier = hist[pl.ds(start, STEPS), :]
            later = hist[pl.ds(start + 1, STEPS), :]
            delayed = ((1.0 - fraction) * later + fraction * earlier).astype(jnp.bfloat16)
            sums.append(
                lax.dot_general(
                    delayed, weights[t], (((1,), (1,)), ((), ())),
                    preferred_element_type=jnp.float32,
                )
            )
        for t in range(turn, turn + UNROLL):
            first = tiles[1, t]
            for g in range(STEPS // TOGETHER):
                rows = pl.ds(pl.multiple_of(first + g * pitch, 8), TOGETHER)
                total[rows, :] += sums[t - turn][g * TOGETHER : (g + 1) * TOGETHER]

    for r in range(peers):
        for g in range(STEPS // TOGETHER):
            first = pl.multiple_of(g * pitch + (place ^ r) * span, 8)
            outs[r][g * span : (g + 1) * span, :] = total[pl.ds(first, span), :].astype(
                jnp.bfloat16
            )
        outs[r][peer_targets * STEPS :, :] = head_ref[place ^ r]


def window_kernel(*refs, peers, own_blocks, peer_targets, coef_count):
    shares = dict(zip([*range(2, peers), 1, 0], refs))
    (
        ready_ref, high_ref, low_ref, coefs_hbm, state_hbm, samples, rates, coefs, state, sems,
    ) = refs[peers:]
    block_rows = ready_ref.shape[1]
    width = TOGETHER * peer_targets
    span = peer_targets * STEPS

    head = shares[0][span:, :].astype(jnp.float32)
    for r in range(1, peers):
        head = head + shares[r][span:, :].astype(jnp.float32)
    row = lax.broadcasted_iota(jnp.int32, (TOGETHER * own_blocks, 128), 0).astype(jnp.float32) + 1.0
    columns = peers * width
    scatter = jnp.concatenate(
        [
            jnp.where(row == head[h : h + 1, :], 1.0, 0.0).astype(jnp.bfloat16)
            for h in range(pl.cdiv(columns, 128))
        ],
        axis=1,
    )[:, :columns]

    excite, inhibit, gain, counts = [
        ready_ref[i * own_blocks : (i + 1) * own_blocks, :] for i in range(4)
    ]
    a = excite_excite / 2
    gain = 0.5 * gain
    counts = 0.5 * counts
    carried = a * excite
    for pair in range(0, STEPS // TOGETHER, 2):
        arrived = jnp.concatenate(
            [
                jnp.concatenate(
                    [shares[r][g * width : (g + 1) * width, :] for r in range(peers)], axis=0
                )
                for g in (pair, pair + 1)
            ],
            axis=1,
        )
        inflow = jnp.dot(scatter, arrived, preferred_element_type=jnp.float32)
        for jj in range(2 * TOGETHER):
            j = pair * TOGETHER + jj
            wave = ready_ref[4 * own_blocks + j : 4 * own_blocks + j + 1, :]
            first = jj % TOGETHER * own_blocks
            left = jj // TOGETHER * block_rows
            half_forcing = gain * inflow[
                first : first + own_blocks, left : left + block_rows
            ] + (wave * counts - excite_offset / 2)
            inhibit_drive = (inhibit_inhibit / 2) * inhibit + inhibit_offset / 2
            excite_turn = jnp.tanh(carried + (half_forcing - (inhibit_excite / 2) * inhibit))
            inhibit_turn = jnp.tanh((excite_inhibit / 2 / a) * carried - inhibit_drive)
            carried = ((1 - excite_rate) * carried + a * excite_rate / 2) + (
                a * excite_rate / 2
            ) * excite_turn
            inhibit = ((1 - inhibit_rate) * inhibit + inhibit_rate / 2) + (
                inhibit_rate / 2
            ) * inhibit_turn
            samples[pl.ds(j, own_blocks, stride=STEPS), :] = carried * (1 / a)
    rates[0] = carried * (1 / a)
    rates[1] = inhibit
    for b in range(own_blocks):
        where = slice(b * block_rows, (b + 1) * block_rows)
        state[0:1, where] = rates[0, b : b + 1, :]
        state[1:2, where] = rates[1, b : b + 1, :]
    copies = [pltpu.make_async_copy(state, state_hbm, sems.at[0])]
    copies[0].start()

    high = high_ref[...]
    low = low_ref[...]
    rows = GROUP * STEPS
    for g in range(0, own_blocks // GROUP, 2):
        part = jnp.concatenate(
            [samples[g * rows : (g + 1) * rows, :], samples[(g + 1) * rows : (g + 2) * rows, :]],
            axis=1,
        )
        part_high = part.astype(jnp.bfloat16)
        part_low = (part - part_high.astype(jnp.float32)).astype(jnp.bfloat16)
        fitted = (
            jnp.dot(high, part_high, preferred_element_type=jnp.float32)
            + jnp.dot(high, part_low, preferred_element_type=jnp.float32)
            + jnp.dot(low, part_high, preferred_element_type=jnp.float32)
        ).astype(jnp.bfloat16)
        for i in range(2):
            coefs[(g + i) * GROUP : (g + i + 1) * GROUP] = fitted[
                :, i * block_rows : (i + 1) * block_rows
            ].reshape(GROUP, coef_count, block_rows)
        where = pl.ds(g * GROUP, 2 * GROUP)
        copies.append(
            pltpu.make_async_copy(coefs.at[where], coefs_hbm.at[where], sems.at[1 + g // 2])
        )
        copies[-1].start()
    for copy in copies:
        copy.wait()


def far(x):
    return pltpu.with_memory_space_constraint(x, pltpu.HBM)


def params():
    return pltpu.CompilerParams(vmem_limit_bytes=20 << 20)


def local(
    fresh_coefs,
    older_coefs,
    state,
    lesion,
    stim_nodes,
    stim_wave,
    read_blocks,
    tract_slot,
    tract_target,
    tract_delay,
    tract_frac,
    tract_weights,
):
    wide_peers = lax.axis_size("wide")
    peers = lax.axis_size("narrow")
    own_blocks, coef_count, block_rows = fresh_coefs.shape
    capacity = read_blocks.shape[3]
    slot_count = wide_peers * capacity
    tile_count = tract_slot.shape[2]
    peer_targets = tile_count // (2 * peers)
    share_rows = peer_targets * STEPS + HEAD

    def swap(x, axis, r):
        return lax.ppermute(x, axis, [(i, i ^ r) for i in range(lax.axis_size(axis))])

    reads = read_blocks.reshape(wide_peers, capacity).T
    ways = [1, *range(wide_peers - 1, 1, -1)]
    asked = [swap(reads, "wide", r) for r in ways]

    vmem_inputs = [
        VMEM(state.shape, jnp.float32),
        VMEM((own_blocks, block_rows), jnp.int32),
        VMEM((1, stim_nodes.shape[0]), jnp.int32),
        VMEM((1, STEPS), jnp.float32),
        VMEM((1, tile_count), jnp.int32),
        VMEM((1, tile_count), jnp.int32),
        VMEM((1, tile_count), jnp.int32),
        VMEM((3, HEAD, 128), jnp.float32),
        VMEM((LENGTH, SEGS * coef_count), jnp.bfloat16),
        VMEM((slot_count, HSEG, coef_count, block_rows), jnp.bfloat16),
    ]
    table = far(jnp.asarray(expand_table(coef_count)))
    fresh = pl.pallas_call(
        fresh_kernel,
        out_shape=pltpu.VMEM(fresh_coefs.shape, jnp.bfloat16),
        in_specs=[hbm_spec],
        out_specs=vmem_spec,
        scratch_shapes=[pltpu.SemaphoreType.DMA],
        compiler_params=params(),
        name="fresh_near",
    )(far(fresh_coefs))
    weights, ready, hist, tiles, heads = pl.pallas_call(
        functools.partial(
            prepare_kernel,
            peers=peers, own_blocks=own_blocks, peer_targets=peer_targets, capacity=capacity,
        ),
        out_shape=[
            pltpu.VMEM((tile_count, block_rows, block_rows), jnp.bfloat16),
            pltpu.VMEM((4 * own_blocks + STEPS, block_rows), jnp.float32),
            pltpu.VMEM((slot_count * LENGTH, block_rows), jnp.float32),
            pltpu.VMEM((8, 128), jnp.int32),
            pltpu.VMEM((peers, HEAD, 128), jnp.bfloat16),
        ],
        in_specs=[vmem_spec] + [hbm_spec] * 12,
        out_specs=[vmem_spec] * 5,
        scratch_shapes=[
            SMEM((capacity, wide_peers), jnp.int32),
            *vmem_inputs,
            pltpu.SemaphoreType.DMA((11 + CHUNKS,)),
        ],
        compiler_params=params(),
        name="prepare",
    )(
        fresh,
        far(reads),
        far(state),
        far(lesion.reshape(own_blocks, block_rows)),
        far(stim_nodes.reshape(1, -1)),
        far(stim_wave.reshape(1, -1)),
        far(tract_slot.reshape(1, tile_count)),
        far(tract_target.reshape(1, tile_count)),
        far(tract_delay.reshape(1, tile_count)),
        far(jnp.asarray(lane_tables(peers, peer_targets, own_blocks))),
        table,
        far(older_coefs.reshape(slot_count, HSEG, coef_count, block_rows)),
        far(tract_weights.reshape(tile_count, block_rows, block_rows)),
    )

    picked = pl.pallas_call(
        functools.partial(pick_kernel, capacity=capacity, peers=wide_peers, ways=ways),
        out_shape=[pltpu.VMEM((capacity, coef_count, block_rows), jnp.bfloat16)]
        * (wide_peers - 1),
        in_specs=[vmem_spec] * wide_peers,
        out_specs=[vmem_spec] * (wide_peers - 1),
        scratch_shapes=[
            SMEM((wide_peers - 1, capacity, wide_peers), jnp.int32),
            pltpu.SemaphoreType.DMA((wide_peers - 1,)),
        ],
        compiler_params=params(),
        name="pick_blocks",
    )(*asked, fresh)
    news = [swap(picked[r - 1], "wide", r) for r in range(wide_peers - 1, 0, -1)]

    shares = pl.pallas_call(
        functools.partial(
            tract_kernel,
            wide_peers=wide_peers, peers=peers, capacity=capacity, peer_targets=peer_targets,
        ),
        out_shape=[pltpu.VMEM((share_rows, block_rows), jnp.bfloat16)] * peers,
        in_specs=[hbm_spec] + [vmem_spec] * (4 + wide_peers),
        out_specs=[vmem_spec] * peers,
        scratch_shapes=[
            SMEM((8, 128), jnp.int32),
            SMEM((1, tile_count), jnp.float32),
            VMEM((slot_count * LENGTH, block_rows), jnp.float32),
            VMEM((peers * peer_targets * STEPS, block_rows), jnp.float32),
            pltpu.SemaphoreType.DMA((2,)),
        ],
        compiler_params=params(),
        name="tract_tiles",
    )(far(tract_frac.reshape(1, tile_count)), tiles, table, heads, weights, hist, *news)
    order = [*range(2, peers), 1, 0]
    arrived = [swap(shares[r], "narrow", r) if r else shares[r] for r in order]

    high, low = fit_tables(coef_count)
    new_coefs, final_state = pl.pallas_call(
        functools.partial(
            window_kernel,
            peers=peers, own_blocks=own_blocks, peer_targets=peer_targets, coef_count=coef_count,
        ),
        out_shape=[
            jax.ShapeDtypeStruct(fresh_coefs.shape, jnp.bfloat16),
            jax.ShapeDtypeStruct(state.shape, jnp.float32),
        ],
        in_specs=[vmem_spec] * (peers + 3),
        out_specs=[hbm_spec] * 2,
        scratch_shapes=[
            VMEM((own_blocks * STEPS, block_rows), jnp.float32),
            VMEM((2, own_blocks, block_rows), jnp.float32),
            VMEM(fresh_coefs.shape, jnp.bfloat16),
            VMEM(state.shape, jnp.float32),
            pltpu.SemaphoreType.DMA((1 + own_blocks // GROUP // 2,)),
        ],
        compiler_params=params(),
        name="window_steps",
    )(*arrived, ready, high, low)
    return new_coefs, final_state


def solution(mesh):
    in_specs = (
        P(("sweep", "wide", "narrow"), None, None),
        P(("sweep", "wide"), "narrow", None, None, None, None),
        P(None, ("sweep", "wide", "narrow")),
        P(("sweep", "wide", "narrow")),
        P("sweep"),
        P("sweep"),
        P("wide", "narrow", None, None),
        P("wide", "narrow", None),
        P("wide", "narrow", None),
        P("wide", "narrow", None),
        P("wide", "narrow", None),
        P("wide", "narrow", None, None, None),
    )
    out_specs = (P(("sweep", "wide", "narrow"), None, None), P(None, ("sweep", "wide", "narrow")))
    return jax.shard_map(local, mesh=mesh, in_specs=in_specs, out_specs=out_specs, check_vma=False)
```

```python
import functools
import math

import jax
import jax.numpy as jnp
import ml_dtypes
import numpy as np
from jax import lax
from jax.experimental import pallas as pl
from jax.experimental.pallas import tpu as pltpu
from jax.sharding import PartitionSpec as P

STEPS = 32
HSEG = 2
SEGS = HSEG + 1
LENGTH = SEGS * STEPS
GROUP = 4
HEAD = 16
PITCH = STEPS + 1
CHUNKS = 8
UNROLL = 4

excite_rate = 0.1
inhibit_rate = 0.05
excite_excite = 1.5
inhibit_excite = 2.0
excite_inhibit = 2.0
inhibit_inhibit = 0.5
excite_offset = 0.5
inhibit_offset = 0.5
tract_gain = 2.0

SMEM = pltpu.SMEM
VMEM = pltpu.VMEM
vmem_spec = pl.BlockSpec(memory_space=VMEM)
hbm_spec = pl.BlockSpec(memory_space=pltpu.HBM)


def basis_table(coef_count, step_count):
    order = np.arange(coef_count, dtype=np.float32)[:, None]
    places = np.arange(step_count, dtype=np.float32)[None, :]
    angles = np.float32(np.pi) * (step_count - places - np.float32(0.5)) / np.float32(step_count)
    return np.cos((order * angles).astype(np.float64)).astype(np.float32)


def expand_table(coef_count):
    basis = basis_table(coef_count, STEPS).astype(ml_dtypes.bfloat16)
    table = np.zeros((LENGTH, SEGS * coef_count), ml_dtypes.bfloat16)
    for seg in range(SEGS):
        table[seg * STEPS : (seg + 1) * STEPS, seg * coef_count : (seg + 1) * coef_count] = basis.T
    return table


def fit_tables(coef_count):
    scales = np.where(np.arange(coef_count)[:, None] == 0, 1.0, 2.0) / STEPS
    fit = (basis_table(coef_count, STEPS) * scales).astype(np.float32)
    whole = np.zeros((GROUP * coef_count, GROUP * STEPS), np.float32)
    for g in range(GROUP):
        whole[g * coef_count : (g + 1) * coef_count, g * STEPS : (g + 1) * STEPS] = fit
    high = whole.astype(ml_dtypes.bfloat16)
    low = (whole - high.astype(np.float32)).astype(ml_dtypes.bfloat16)
    return high, low


TOGETHER = 8


def lane_tables(peers, peer_targets, own_blocks):
    width = TOGETHER * peer_targets
    assert TOGETHER * own_blocks <= 256 and peers * width <= HEAD * 128
    lane = np.arange(HEAD * 128)
    used = lane < peers * width
    within = lane % width
    rank = np.where(used, within // TOGETHER, -5)
    offset = within % TOGETHER * own_blocks + 1
    place = np.where(used, lane // width, -5)
    return np.stack([rank, offset, place]).astype(np.float32).reshape(3, HEAD, 128)


def prepare_kernel(
    fresh_ref, reads_hbm, state_hbm, lesion_hbm, stim_hbm, wave_hbm, slot_hbm, target_hbm,
    delay_hbm, lanes_hbm, table_hbm, older_hbm, frac_hbm, weights_hbm,
    weights_out, ready_out, hist_out, tiles_out, fracs_out, head_out,
    reads, state, lesion, stim, wave, slot, target, delay, lanes, table, older, sems,
    *, peers, own_blocks, peer_targets, capacity,
):
    pairs = [
        (reads_hbm, reads), (target_hbm, target), (slot_hbm, slot),
        (delay_hbm, delay), (lanes_hbm, lanes), (table_hbm, table), (older_hbm, older),
        (state_hbm, state), (lesion_hbm, lesion), (stim_hbm, stim), (wave_hbm, wave),
        (frac_hbm, fracs_out),
    ]
    copies = [
        pltpu.make_async_copy(source, into, sems.at[i]) for i, (source, into) in enumerate(pairs)
    ]
    part = weights_hbm.shape[0] // CHUNKS
    for i in range(CHUNKS):
        rows = pl.ds(i * part, part)
        copies.append(
            pltpu.make_async_copy(
                weights_hbm.at[rows], weights_out.at[rows], sems.at[len(pairs) + i]
            )
        )
    for copy in copies:
        copy.start()
    for copy in copies[1:5]:
        copy.wait()
    place = lax.axis_index("narrow")
    owner = lax.axis_index("wide")
    tile_count = target.shape[1]
    target_count = peers * own_blocks

    numbers = lax.broadcasted_iota(jnp.int32, (target_count, tile_count), 0)
    hits = jnp.where(numbers == target[...], 1.0, 0.0)
    held = jnp.dot(
        hits.astype(jnp.bfloat16), jnp.ones((tile_count, 128), jnp.bfloat16),
        preferred_element_type=jnp.float32,
    )
    held = jnp.minimum(held, 1.0)
    shape = (own_blocks, own_blocks)
    below = jnp.where(
        lax.broadcasted_iota(jnp.int32, shape, 0) > lax.broadcasted_iota(jnp.int32, shape, 1),
        1.0, 0.0,
    ).astype(jnp.bfloat16)
    block = lax.broadcasted_iota(jnp.int32, (own_blocks, 128), 0).astype(jnp.float32)
    ranks = jnp.zeros((1, tile_count), jnp.float32)
    head_rows = pl.cdiv(peers * TOGETHER * peer_targets, 128)
    for p in range(peers):
        part = slice(p * own_blocks, (p + 1) * own_blocks)
        rank = jnp.dot(below, held[part].astype(jnp.bfloat16), preferred_element_type=jnp.float32)
        ranks = ranks + jnp.sum(hits[part] * rank[:, :tile_count], axis=0, keepdims=True)
        rank = jnp.where(held[part] > 0.5, rank, -1.0)
        source = (place ^ p).astype(jnp.float32)
        rows = []
        for h in range(head_rows):
            match = rank == lanes[0, h : h + 1, :]
            ids = jnp.sum(jnp.where(match, block, 0.0), axis=0, keepdims=True)
            mine = lanes[2, h : h + 1, :] == source
            rows.append(jnp.where(mine, ids + lanes[1, h : h + 1, :], 0.0))
        rows.append(jnp.zeros((HEAD - head_rows, 128), jnp.float32))
        head_out[p] = jnp.concatenate(rows, axis=0).astype(jnp.bfloat16)

    across = jnp.zeros((1, tile_count), jnp.int32)
    for p in range(1, peers):
        across = across + jnp.where(target[...] >= p * own_blocks, 1, 0)
    tiles_out[0:1, :tile_count] = slot[...] * LENGTH + (LENGTH - 1) - delay[...]
    tiles_out[1:2, :tile_count] = (across * peer_targets + ranks.astype(jnp.int32)) * TOGETHER

    for copy in copies[5:7]:
        copy.wait()
    coef_count = older.shape[2]
    earlier = HSEG * STEPS
    for s in range(older.shape[0]):
        segments = [older[s, h] for h in range(HSEG - 1, -1, -1)]
        hist_out[s * LENGTH : s * LENGTH + earlier, :] = jnp.dot(
            table[:earlier, : HSEG * coef_count], jnp.concatenate(segments, axis=0),
            preferred_element_type=jnp.float32,
        )
        hist_out[s * LENGTH + earlier : (s + 1) * LENGTH, :] = jnp.zeros(
            (STEPS, hist_out.shape[1]), jnp.float32
        )
    copies[0].wait()
    for c in range(capacity):
        rows = pl.ds(pl.multiple_of((owner * capacity + c) * LENGTH + earlier, 8), STEPS)
        hist_out[rows, :] = jnp.dot(
            table[:STEPS, :coef_count], fresh_ref[jnp.maximum(reads[c, owner], 0)],
            preferred_element_type=jnp.float32,
        )

    for copy in copies[7:11]:
        copy.wait()
    block_rows = lesion.shape[1]
    for b in range(own_blocks):
        piece = state[:, b * block_rows : (b + 1) * block_rows]
        ready_out[b : b + 1, :] = piece[0:1, :]
        ready_out[own_blocks + b : own_blocks + b + 1, :] = piece[1:2, :]
    ready_out[2 * own_blocks : 3 * own_blocks, :] = tract_gain * (
        1.0 - lesion[...].astype(jnp.float32)
    )
    stim_count = stim.shape[1]
    nodes = stim[...] - (owner * peers + place) * (own_blocks * block_rows)
    blocks = lax.shift_right_arithmetic(nodes, block_rows.bit_length() - 1)
    offsets = nodes & (block_rows - 1)
    in_block = lax.broadcasted_iota(jnp.int32, (own_blocks, stim_count), 0) == blocks
    at_offset = lax.broadcasted_iota(jnp.int32, (block_rows, stim_count), 0) == offsets
    ready_out[3 * own_blocks : 4 * own_blocks, :] = lax.dot_general(
        jnp.where(in_block, 1.0, 0.0).astype(jnp.bfloat16),
        jnp.where(at_offset, 1.0, 0.0).astype(jnp.bfloat16),
        (((1,), (1,)), ((), ())),
        preferred_element_type=jnp.float32,
    )
    shape = (STEPS, STEPS)
    diagonal = lax.broadcasted_iota(jnp.int32, shape, 0) == lax.broadcasted_iota(jnp.int32, shape, 1)
    column = jnp.sum(jnp.where(diagonal, wave[...], 0.0), axis=1, keepdims=True)
    ready_out[4 * own_blocks :, :] = jnp.broadcast_to(column, (STEPS, block_rows))
    for copy in copies[11:]:
        copy.wait()


def fresh_kernel(fresh_hbm, fresh_out, sem):
    copy = pltpu.make_async_copy(fresh_hbm, fresh_out, sem)
    copy.start()
    copy.wait()


def pick_kernel(*refs, capacity, peers, ways):
    tables = refs[: peers - 1]
    fresh = refs[peers - 1]
    outs = refs[peers : 2 * peers - 1]
    asked, sems = refs[2 * peers - 1 :]
    place = lax.axis_index("wide")
    copies = [pltpu.make_async_copy(tables[r], asked.at[r], sems.at[r]) for r in range(peers - 1)]
    for copy in copies:
        copy.start()
    for i, r in enumerate(ways):
        copies[i].wait()
        for c in range(capacity):
            outs[r - 1][c] = fresh[jnp.maximum(asked[i, c, place], 0)]


def tract_kernel(
    fracs_ref, tiles_ref, table_ref, head_ref, weights, hist_ref, *refs,
    wide_peers, peers, capacity, peer_targets,
):
    news = refs[: wide_peers - 1]
    outs = refs[wide_peers - 1 : wide_peers - 1 + peers]
    tiles, frac, hist, total, sems = refs[wide_peers - 1 + peers :]
    place = lax.axis_index("narrow")
    owner = lax.axis_index("wide")
    copies = [
        pltpu.make_async_copy(tiles_ref, tiles, sems.at[0]),
        pltpu.make_async_copy(fracs_ref, frac, sems.at[1]),
    ]
    for copy in copies:
        copy.start()
    total[...] = jnp.zeros_like(total)
    hist[...] = hist_ref[...]
    for i, block in enumerate(news):
        table = table_ref[:STEPS, : block.shape[1]]
        for c in range(capacity):
            slot = (owner ^ (wide_peers - 1 - i)) * capacity + c
            rows = pl.ds(pl.multiple_of(slot * LENGTH + HSEG * STEPS, 8), STEPS)
            hist[rows, :] = jnp.dot(table, block[c], preferred_element_type=jnp.float32)
    for copy in copies:
        copy.wait()

    span = peer_targets * TOGETHER
    pitch = peers * span
    block_rows = weights.shape[2]
    for turn in range(0, weights.shape[0], UNROLL):
        sums = []
        for t in range(turn, turn + UNROLL, 2):
            both = []
            for u in (t, t + 1):
                fraction = frac[0, u]
                start = tiles[0, u]
                earlier = hist[pl.ds(start, STEPS), :]
                later = hist[pl.ds(start + 1, STEPS), :]
                both.append(
                    ((1.0 - fraction) * later + fraction * earlier).astype(jnp.bfloat16)
                )
            product = lax.dot_general(
                jnp.concatenate(both, axis=0),
                weights[t : t + 2].reshape(2 * block_rows, block_rows),
                (((1,), (1,)), ((), ())),
                preferred_element_type=jnp.float32,
            )
            sums += [product[:STEPS, :block_rows], product[STEPS:, block_rows:]]
        for t in range(turn, turn + UNROLL):
            first = tiles[1, t]
            for g in range(STEPS // TOGETHER):
                rows = pl.ds(pl.multiple_of(first + g * pitch, 8), TOGETHER)
                total[rows, :] += sums[t - turn][g * TOGETHER : (g + 1) * TOGETHER]

    for r in range(peers):
        for g in range(STEPS // TOGETHER):
            first = pl.multiple_of(g * pitch + (place ^ r) * span, 8)
            outs[r][g * span : (g + 1) * span, :] = total[pl.ds(first, span), :].astype(
                jnp.bfloat16
            )
        outs[r][peer_targets * STEPS :, :] = head_ref[place ^ r]


def window_kernel(*refs, peers, own_blocks, peer_targets, coef_count):
    shares = dict(zip([*range(2, peers), 1, 0], refs))
    (
        ready_ref, high_ref, low_ref, coefs_hbm, state_hbm, samples, rates, coefs, state, sems,
    ) = refs[peers:]
    block_rows = ready_ref.shape[1]
    width = TOGETHER * peer_targets
    span = peer_targets * STEPS

    head = shares[0][span:, :].astype(jnp.float32)
    for r in range(1, peers):
        head = head + shares[r][span:, :].astype(jnp.float32)
    row = lax.broadcasted_iota(jnp.int32, (TOGETHER * own_blocks, 128), 0).astype(jnp.float32) + 1.0
    columns = peers * width
    scatter = jnp.concatenate(
        [
            jnp.where(row == head[h : h + 1, :], 1.0, 0.0).astype(jnp.bfloat16)
            for h in range(pl.cdiv(columns, 128))
        ],
        axis=1,
    )[:, :columns]

    excite, inhibit, gain, counts = [
        ready_ref[i * own_blocks : (i + 1) * own_blocks, :] for i in range(4)
    ]
    a = excite_excite / 2
    gain = 0.5 * gain
    counts = 0.5 * counts
    carried = a * excite
    for pair in range(0, STEPS // TOGETHER, 2):
        arrived = jnp.concatenate(
            [
                jnp.concatenate(
                    [shares[r][g * width : (g + 1) * width, :] for r in range(peers)], axis=0
                )
                for g in (pair, pair + 1)
            ],
            axis=1,
        )
        inflow = jnp.dot(scatter, arrived, preferred_element_type=jnp.float32)
        for jj in range(2 * TOGETHER):
            j = pair * TOGETHER + jj
            wave = ready_ref[4 * own_blocks + j : 4 * own_blocks + j + 1, :]
            first = jj % TOGETHER * own_blocks
            left = jj // TOGETHER * block_rows
            half_forcing = gain * inflow[
                first : first + own_blocks, left : left + block_rows
            ] + (wave * counts - excite_offset / 2)
            inhibit_drive = (inhibit_inhibit / 2) * inhibit + inhibit_offset / 2
            excite_turn = jnp.tanh(carried + (half_forcing - (inhibit_excite / 2) * inhibit))
            inhibit_turn = jnp.tanh((excite_inhibit / 2 / a) * carried - inhibit_drive)
            carried = ((1 - excite_rate) * carried + a * excite_rate / 2) + (
                a * excite_rate / 2
            ) * excite_turn
            inhibit = ((1 - inhibit_rate) * inhibit + inhibit_rate / 2) + (
                inhibit_rate / 2
            ) * inhibit_turn
            samples[pl.ds(j, own_blocks, stride=PITCH), :] = carried * (1 / a)
    rates[0] = carried * (1 / a)
    rates[1] = inhibit
    for b in range(own_blocks):
        where = slice(b * block_rows, (b + 1) * block_rows)
        state[0:1, where] = rates[0, b : b + 1, :]
        state[1:2, where] = rates[1, b : b + 1, :]
    copies = [pltpu.make_async_copy(state, state_hbm, sems.at[0])]
    copies[0].start()

    high = high_ref[...]
    low = low_ref[...]
    for g in range(0, own_blocks // GROUP, 2):
        part = jnp.concatenate(
            [
                jnp.concatenate(
                    [
                        samples[b * PITCH : b * PITCH + STEPS, :]
                        for b in range((g + i) * GROUP, (g + i + 1) * GROUP)
                    ],
                    axis=0,
                )
                for i in range(2)
            ],
            axis=1,
        )
        part_high = part.astype(jnp.bfloat16)
        part_low = (part - part_high.astype(jnp.float32)).astype(jnp.bfloat16)
        fitted = (
            jnp.dot(high, part_high, preferred_element_type=jnp.float32)
            + jnp.dot(high, part_low, preferred_element_type=jnp.float32)
            + jnp.dot(low, part_high, preferred_element_type=jnp.float32)
        ).astype(jnp.bfloat16)
        for i in range(2):
            coefs[(g + i) * GROUP : (g + i + 1) * GROUP] = fitted[
                :, i * block_rows : (i + 1) * block_rows
            ].reshape(GROUP, coef_count, block_rows)
        where = pl.ds(g * GROUP, 2 * GROUP)
        copies.append(
            pltpu.make_async_copy(coefs.at[where], coefs_hbm.at[where], sems.at[1 + g // 2])
        )
        copies[-1].start()
    for copy in copies:
        copy.wait()


def far(x):
    return pltpu.with_memory_space_constraint(x, pltpu.HBM)


def params():
    return pltpu.CompilerParams(vmem_limit_bytes=20 << 20)


def local(
    fresh_coefs,
    older_coefs,
    state,
    lesion,
    stim_nodes,
    stim_wave,
    read_blocks,
    tract_slot,
    tract_target,
    tract_delay,
    tract_frac,
    tract_weights,
):
    wide_peers = lax.axis_size("wide")
    peers = lax.axis_size("narrow")
    own_blocks, coef_count, block_rows = fresh_coefs.shape
    capacity = read_blocks.shape[3]
    slot_count = wide_peers * capacity
    tile_count = tract_slot.shape[2]
    peer_targets = tile_count // (2 * peers)
    share_rows = peer_targets * STEPS + HEAD

    def swap(x, axis, r):
        return lax.ppermute(x, axis, [(i, i ^ r) for i in range(lax.axis_size(axis))])

    reads = read_blocks.reshape(wide_peers, capacity).T
    ways = [1, *range(wide_peers - 1, 1, -1)]
    asked = [swap(reads, "wide", r) for r in ways]

    vmem_inputs = [
        VMEM(state.shape, jnp.float32),
        VMEM((own_blocks, block_rows), jnp.int32),
        VMEM((1, stim_nodes.shape[0]), jnp.int32),
        VMEM((1, STEPS), jnp.float32),
        VMEM((1, tile_count), jnp.int32),
        VMEM((1, tile_count), jnp.int32),
        VMEM((1, tile_count), jnp.int32),
        VMEM((3, HEAD, 128), jnp.float32),
        VMEM((LENGTH, SEGS * coef_count), jnp.bfloat16),
        VMEM((slot_count, HSEG, coef_count, block_rows), jnp.bfloat16),
    ]
    table = far(jnp.asarray(expand_table(coef_count)))
    fresh = pl.pallas_call(
        fresh_kernel,
        out_shape=pltpu.VMEM(fresh_coefs.shape, jnp.bfloat16),
        in_specs=[hbm_spec],
        out_specs=vmem_spec,
        scratch_shapes=[pltpu.SemaphoreType.DMA],
        compiler_params=params(),
        name="fresh_near",
    )(far(fresh_coefs))
    weights, ready, hist, tiles, fracs, heads = pl.pallas_call(
        functools.partial(
            prepare_kernel,
            peers=peers, own_blocks=own_blocks, peer_targets=peer_targets, capacity=capacity,
        ),
        out_shape=[
            pltpu.VMEM((tile_count, block_rows, block_rows), jnp.bfloat16),
            pltpu.VMEM((4 * own_blocks + STEPS, block_rows), jnp.float32),
            pltpu.VMEM((slot_count * LENGTH, block_rows), jnp.float32),
            pltpu.VMEM((8, 128), jnp.int32),
            pltpu.VMEM((1, tile_count), jnp.float32),
            pltpu.VMEM((peers, HEAD, 128), jnp.bfloat16),
        ],
        in_specs=[vmem_spec] + [hbm_spec] * 13,
        out_specs=[vmem_spec] * 6,
        scratch_shapes=[
            SMEM((capacity, wide_peers), jnp.int32),
            *vmem_inputs,
            pltpu.SemaphoreType.DMA((12 + CHUNKS,)),
        ],
        compiler_params=params(),
        name="prepare",
    )(
        fresh,
        far(reads),
        far(state),
        far(lesion.reshape(own_blocks, block_rows)),
        far(stim_nodes.reshape(1, -1)),
        far(stim_wave.reshape(1, -1)),
        far(tract_slot.reshape(1, tile_count)),
        far(tract_target.reshape(1, tile_count)),
        far(tract_delay.reshape(1, tile_count)),
        far(jnp.asarray(lane_tables(peers, peer_targets, own_blocks))),
        table,
        far(older_coefs.reshape(slot_count, HSEG, coef_count, block_rows)),
        far(tract_frac.reshape(1, tile_count)),
        far(tract_weights.reshape(tile_count, block_rows, block_rows)),
    )

    picked = pl.pallas_call(
        functools.partial(pick_kernel, capacity=capacity, peers=wide_peers, ways=ways),
        out_shape=[pltpu.VMEM((capacity, coef_count, block_rows), jnp.bfloat16)]
        * (wide_peers - 1),
        in_specs=[vmem_spec] * wide_peers,
        out_specs=[vmem_spec] * (wide_peers - 1),
        scratch_shapes=[
            SMEM((wide_peers - 1, capacity, wide_peers), jnp.int32),
            pltpu.SemaphoreType.DMA((wide_peers - 1,)),
        ],
        compiler_params=params(),
        name="pick_blocks",
    )(*asked, fresh)
    news = [swap(picked[r - 1], "wide", r) for r in range(wide_peers - 1, 0, -1)]

    shares = pl.pallas_call(
        functools.partial(
            tract_kernel,
            wide_peers=wide_peers, peers=peers, capacity=capacity, peer_targets=peer_targets,
        ),
        out_shape=[pltpu.VMEM((share_rows, block_rows), jnp.bfloat16)] * peers,
        in_specs=[vmem_spec] * (5 + wide_peers),
        out_specs=[vmem_spec] * peers,
        scratch_shapes=[
            SMEM((8, 128), jnp.int32),
            SMEM((1, tile_count), jnp.float32),
            VMEM((slot_count * LENGTH, block_rows), jnp.float32),
            VMEM((peers * peer_targets * STEPS, block_rows), jnp.float32),
            pltpu.SemaphoreType.DMA((2,)),
        ],
        compiler_params=params(),
        name="tract_tiles",
    )(fracs, tiles, table, heads, weights, hist, *news)
    order = [*range(2, peers), 1, 0]
    arrived = [swap(shares[r], "narrow", r) if r else shares[r] for r in order]

    high, low = fit_tables(coef_count)
    new_coefs, final_state = pl.pallas_call(
        functools.partial(
            window_kernel,
            peers=peers, own_blocks=own_blocks, peer_targets=peer_targets, coef_count=coef_count,
        ),
        out_shape=[
            jax.ShapeDtypeStruct(fresh_coefs.shape, jnp.bfloat16),
            jax.ShapeDtypeStruct(state.shape, jnp.float32),
        ],
        in_specs=[vmem_spec] * (peers + 3),
        out_specs=[hbm_spec] * 2,
        scratch_shapes=[
            VMEM((own_blocks * PITCH, block_rows), jnp.float32),
            VMEM((2, own_blocks, block_rows), jnp.float32),
            VMEM(fresh_coefs.shape, jnp.bfloat16),
            VMEM(state.shape, jnp.float32),
            pltpu.SemaphoreType.DMA((1 + own_blocks // GROUP // 2,)),
        ],
        compiler_params=params(),
        name="window_steps",
    )(*arrived, ready, high, low)
    return new_coefs, final_state


def solution(mesh):
    in_specs = (
        P(("sweep", "wide", "narrow"), None, None),
        P(("sweep", "wide"), "narrow", None, None, None, None),
        P(None, ("sweep", "wide", "narrow")),
        P(("sweep", "wide", "narrow")),
        P("sweep"),
        P("sweep"),
        P("wide", "narrow", None, None),
        P("wide", "narrow", None),
        P("wide", "narrow", None),
        P("wide", "narrow", None),
        P("wide", "narrow", None),
        P("wide", "narrow", None, None, None),
    )
    out_specs = (P(("sweep", "wide", "narrow"), None, None), P(None, ("sweep", "wide", "narrow")))
    return jax.shard_map(local, mesh=mesh, in_specs=in_specs, out_specs=out_specs, check_vma=False)
```

```python
import functools
import math

import jax
import jax.numpy as jnp
import ml_dtypes
import numpy as np
from jax import lax
from jax.experimental import pallas as pl
from jax.experimental.pallas import tpu as pltpu
from jax.sharding import PartitionSpec as P

STEPS = 32
HSEG = 2
SEGS = HSEG + 1
LENGTH = SEGS * STEPS
GROUP = 4
HEAD = 16
PITCH = STEPS + 1
CHUNKS = 8
UNROLL = 4

excite_rate = 0.1
inhibit_rate = 0.05
excite_excite = 1.5
inhibit_excite = 2.0
excite_inhibit = 2.0
inhibit_inhibit = 0.5
excite_offset = 0.5
inhibit_offset = 0.5
tract_gain = 2.0

SMEM = pltpu.SMEM
VMEM = pltpu.VMEM
vmem_spec = pl.BlockSpec(memory_space=VMEM)
hbm_spec = pl.BlockSpec(memory_space=pltpu.HBM)


def basis_table(coef_count, step_count):
    order = np.arange(coef_count, dtype=np.float32)[:, None]
    places = np.arange(step_count, dtype=np.float32)[None, :]
    angles = np.float32(np.pi) * (step_count - places - np.float32(0.5)) / np.float32(step_count)
    return np.cos((order * angles).astype(np.float64)).astype(np.float32)


def expand_table(coef_count):
    basis = basis_table(coef_count, STEPS).astype(ml_dtypes.bfloat16)
    table = np.zeros((LENGTH, SEGS * coef_count), ml_dtypes.bfloat16)
    for seg in range(SEGS):
        table[seg * STEPS : (seg + 1) * STEPS, seg * coef_count : (seg + 1) * coef_count] = basis.T
    return table


def fit_table(coef_count):
    scales = np.where(np.arange(coef_count)[:, None] == 0, 1.0, 2.0) / STEPS
    fit = (basis_table(coef_count, STEPS) * scales).astype(np.float32)
    whole = np.zeros((GROUP * coef_count, GROUP * STEPS), np.float32)
    for g in range(GROUP):
        whole[g * coef_count : (g + 1) * coef_count, g * STEPS : (g + 1) * STEPS] = fit
    high = whole.astype(ml_dtypes.bfloat16)
    low = (whole - high.astype(np.float32)).astype(ml_dtypes.bfloat16)
    return np.concatenate([high, high, low], axis=1)


TOGETHER = 8


def lane_tables(peers, peer_targets, own_blocks):
    width = TOGETHER * peer_targets
    assert TOGETHER * own_blocks <= 256 and peers * width <= HEAD * 128
    lane = np.arange(HEAD * 128)
    used = lane < peers * width
    within = lane % width
    rank = np.where(used, within // TOGETHER, -5)
    offset = within % TOGETHER * own_blocks + 1
    place = np.where(used, lane // width, -5)
    return np.stack([rank, offset, place]).astype(np.float32).reshape(3, HEAD, 128)


def prepare_kernel(
    fresh_ref, reads_hbm, state_hbm, lesion_hbm, stim_hbm, wave_hbm, slot_hbm, target_hbm,
    delay_hbm, lanes_hbm, table_hbm, older_hbm, frac_hbm, weights_hbm,
    weights_out, ready_out, hist_out, tiles_out, fracs_out, head_out,
    reads, state, lesion, stim, wave, slot, target, delay, lanes, table, older, sems,
    *, peers, own_blocks, peer_targets, capacity,
):
    pairs = [
        (reads_hbm, reads), (target_hbm, target), (slot_hbm, slot),
        (delay_hbm, delay), (lanes_hbm, lanes), (table_hbm, table), (older_hbm, older),
        (state_hbm, state), (lesion_hbm, lesion), (stim_hbm, stim), (wave_hbm, wave),
        (frac_hbm, fracs_out),
    ]
    copies = [
        pltpu.make_async_copy(source, into, sems.at[i]) for i, (source, into) in enumerate(pairs)
    ]
    part = weights_hbm.shape[0] // CHUNKS
    for i in range(CHUNKS):
        rows = pl.ds(i * part, part)
        copies.append(
            pltpu.make_async_copy(
                weights_hbm.at[rows], weights_out.at[rows], sems.at[len(pairs) + i]
            )
        )
    for copy in copies:
        copy.start()
    for copy in copies[1:5]:
        copy.wait()
    place = lax.axis_index("narrow")
    owner = lax.axis_index("wide")
    tile_count = target.shape[1]
    target_count = peers * own_blocks

    numbers = lax.broadcasted_iota(jnp.int32, (target_count, tile_count), 0)
    hits = jnp.where(numbers == target[...], 1.0, 0.0)
    held = jnp.dot(
        hits.astype(jnp.bfloat16), jnp.ones((tile_count, 128), jnp.bfloat16),
        preferred_element_type=jnp.float32,
    )
    held = jnp.minimum(held, 1.0)
    shape = (own_blocks, own_blocks)
    below = jnp.where(
        lax.broadcasted_iota(jnp.int32, shape, 0) > lax.broadcasted_iota(jnp.int32, shape, 1),
        1.0, 0.0,
    ).astype(jnp.bfloat16)
    block = lax.broadcasted_iota(jnp.int32, (own_blocks, 128), 0).astype(jnp.float32)
    ranks = jnp.zeros((1, tile_count), jnp.float32)
    head_rows = pl.cdiv(peers * TOGETHER * peer_targets, 128)
    for p in range(peers):
        part = slice(p * own_blocks, (p + 1) * own_blocks)
        rank = jnp.dot(below, held[part].astype(jnp.bfloat16), preferred_element_type=jnp.float32)
        ranks = ranks + jnp.sum(hits[part] * rank[:, :tile_count], axis=0, keepdims=True)
        rank = jnp.where(held[part] > 0.5, rank, -1.0)
        source = (place ^ p).astype(jnp.float32)
        rows = []
        for h in range(head_rows):
            match = rank == lanes[0, h : h + 1, :]
            ids = jnp.sum(jnp.where(match, block, 0.0), axis=0, keepdims=True)
            mine = lanes[2, h : h + 1, :] == source
            rows.append(jnp.where(mine, ids + lanes[1, h : h + 1, :], 0.0))
        rows.append(jnp.zeros((HEAD - head_rows, 128), jnp.float32))
        head_out[p] = jnp.concatenate(rows, axis=0).astype(jnp.bfloat16)

    across = jnp.zeros((1, tile_count), jnp.int32)
    for p in range(1, peers):
        across = across + jnp.where(target[...] >= p * own_blocks, 1, 0)
    tiles_out[0:1, :tile_count] = slot[...] * LENGTH + (LENGTH - 1) - delay[...]
    tiles_out[1:2, :tile_count] = (across * peer_targets + ranks.astype(jnp.int32)) * TOGETHER

    for copy in copies[5:7]:
        copy.wait()
    coef_count = older.shape[2]
    earlier = HSEG * STEPS
    for s in range(older.shape[0]):
        segments = [older[s, h] for h in range(HSEG - 1, -1, -1)]
        hist_out[s * LENGTH : s * LENGTH + earlier, :] = jnp.dot(
            table[:earlier, : HSEG * coef_count], jnp.concatenate(segments, axis=0),
            preferred_element_type=jnp.float32,
        )
        hist_out[s * LENGTH + earlier : (s + 1) * LENGTH, :] = jnp.zeros(
            (STEPS, hist_out.shape[1]), jnp.float32
        )
    copies[0].wait()
    for c in range(capacity):
        rows = pl.ds(pl.multiple_of((owner * capacity + c) * LENGTH + earlier, 8), STEPS)
        hist_out[rows, :] = jnp.dot(
            table[:STEPS, :coef_count], fresh_ref[jnp.maximum(reads[c, owner], 0)],
            preferred_element_type=jnp.float32,
        )

    for copy in copies[7:11]:
        copy.wait()
    block_rows = lesion.shape[1]
    for b in range(own_blocks):
        piece = state[:, b * block_rows : (b + 1) * block_rows]
        ready_out[b : b + 1, :] = piece[0:1, :]
        ready_out[own_blocks + b : own_blocks + b + 1, :] = piece[1:2, :]
    ready_out[2 * own_blocks : 3 * own_blocks, :] = tract_gain * (
        1.0 - lesion[...].astype(jnp.float32)
    )
    stim_count = stim.shape[1]
    nodes = stim[...] - (owner * peers + place) * (own_blocks * block_rows)
    blocks = lax.shift_right_arithmetic(nodes, block_rows.bit_length() - 1)
    offsets = nodes & (block_rows - 1)
    in_block = lax.broadcasted_iota(jnp.int32, (own_blocks, stim_count), 0) == blocks
    at_offset = lax.broadcasted_iota(jnp.int32, (block_rows, stim_count), 0) == offsets
    ready_out[3 * own_blocks : 4 * own_blocks, :] = lax.dot_general(
        jnp.where(in_block, 1.0, 0.0).astype(jnp.bfloat16),
        jnp.where(at_offset, 1.0, 0.0).astype(jnp.bfloat16),
        (((1,), (1,)), ((), ())),
        preferred_element_type=jnp.float32,
    )
    shape = (STEPS, STEPS)
    diagonal = lax.broadcasted_iota(jnp.int32, shape, 0) == lax.broadcasted_iota(jnp.int32, shape, 1)
    column = jnp.sum(jnp.where(diagonal, wave[...], 0.0), axis=1, keepdims=True)
    ready_out[4 * own_blocks :, :] = jnp.broadcast_to(column, (STEPS, block_rows))
    for copy in copies[11:]:
        copy.wait()


def fresh_kernel(fresh_hbm, fresh_out, sem):
    copy = pltpu.make_async_copy(fresh_hbm, fresh_out, sem)
    copy.start()
    copy.wait()


def pick_kernel(*refs, capacity, peers, ways):
    tables = refs[: peers - 1]
    fresh = refs[peers - 1]
    outs = refs[peers : 2 * peers - 1]
    asked, sems = refs[2 * peers - 1 :]
    place = lax.axis_index("wide")
    copies = [pltpu.make_async_copy(tables[r], asked.at[r], sems.at[r]) for r in range(peers - 1)]
    for copy in copies:
        copy.start()
    for i, r in enumerate(ways):
        copies[i].wait()
        for c in range(capacity):
            outs[r - 1][c] = fresh[jnp.maximum(asked[i, c, place], 0)]


def tract_kernel(
    fracs_ref, tiles_ref, table_ref, head_ref, weights, hist_ref, *refs,
    wide_peers, peers, capacity, peer_targets,
):
    news = refs[: wide_peers - 1]
    outs = refs[wide_peers - 1 : wide_peers - 1 + peers]
    tiles, frac, hist, total, sems = refs[wide_peers - 1 + peers :]
    place = lax.axis_index("narrow")
    owner = lax.axis_index("wide")
    copies = [
        pltpu.make_async_copy(tiles_ref, tiles, sems.at[0]),
        pltpu.make_async_copy(fracs_ref, frac, sems.at[1]),
    ]
    for copy in copies:
        copy.start()
    total[...] = jnp.zeros_like(total)
    hist[...] = hist_ref[...]
    for i, block in enumerate(news):
        table = table_ref[:STEPS, : block.shape[1]]
        for c in range(capacity):
            slot = (owner ^ (wide_peers - 1 - i)) * capacity + c
            rows = pl.ds(pl.multiple_of(slot * LENGTH + HSEG * STEPS, 8), STEPS)
            hist[rows, :] = jnp.dot(table, block[c], preferred_element_type=jnp.float32)
    for copy in copies:
        copy.wait()

    span = peer_targets * TOGETHER
    pitch = peers * span
    block_rows = weights.shape[2]
    for turn in range(0, weights.shape[0], UNROLL):
        rows = []
        for t in range(turn, turn + UNROLL):
            fraction = frac[0, t]
            start = tiles[0, t]
            earlier = hist[pl.ds(start, STEPS), :]
            later = hist[pl.ds(start + 1, STEPS), :]
            rows.append(((1.0 - fraction) * later + fraction * earlier).astype(jnp.bfloat16))
        none = jnp.zeros((2 * STEPS, block_rows), jnp.bfloat16)
        left = jnp.concatenate([*rows[:2], none], axis=0)
        right = jnp.concatenate([none, *rows[2:]], axis=0)
        product = lax.dot_general(
            jnp.concatenate([left, right], axis=1),
            jnp.concatenate(
                [
                    weights[t : t + 2].reshape(2 * block_rows, block_rows)
                    for t in (turn, turn + 2)
                ],
                axis=1,
            ),
            (((1,), (1,)), ((), ())),
            preferred_element_type=jnp.float32,
        )
        sums = [
            product[i * STEPS : (i + 1) * STEPS, i % 2 * block_rows : (i % 2 + 1) * block_rows]
            for i in range(UNROLL)
        ]
        for t in range(turn, turn + UNROLL):
            first = tiles[1, t]
            for g in range(STEPS // TOGETHER):
                rows = pl.ds(pl.multiple_of(first + g * pitch, 8), TOGETHER)
                total[rows, :] += sums[t - turn][g * TOGETHER : (g + 1) * TOGETHER]

    for r in range(peers):
        for g in range(STEPS // TOGETHER):
            first = pl.multiple_of(g * pitch + (place ^ r) * span, 8)
            outs[r][g * span : (g + 1) * span, :] = total[pl.ds(first, span), :].astype(
                jnp.bfloat16
            )
        outs[r][peer_targets * STEPS :, :] = head_ref[place ^ r]


def window_kernel(*refs, peers, own_blocks, peer_targets, coef_count):
    shares = dict(zip([*range(2, peers), 1, 0], refs))
    (
        ready_ref, fit_ref, coefs_hbm, state_hbm, samples, rates, coefs, state, sems,
    ) = refs[peers:]
    block_rows = ready_ref.shape[1]
    width = TOGETHER * peer_targets
    span = peer_targets * STEPS

    head = shares[0][span:, :].astype(jnp.float32)
    for r in range(1, peers):
        head = head + shares[r][span:, :].astype(jnp.float32)
    row = lax.broadcasted_iota(jnp.int32, (TOGETHER * own_blocks, 128), 0).astype(jnp.float32) + 1.0
    columns = peers * width
    scatter = jnp.concatenate(
        [
            jnp.where(row == head[h : h + 1, :], 1.0, 0.0).astype(jnp.bfloat16)
            for h in range(pl.cdiv(columns, 128))
        ],
        axis=1,
    )[:, :columns]

    excite, inhibit, gain, counts = [
        ready_ref[i * own_blocks : (i + 1) * own_blocks, :] for i in range(4)
    ]
    a = excite_excite / 2
    gain = 0.5 * gain
    counts = 0.5 * counts
    carried = a * excite
    for pair in range(0, STEPS // TOGETHER, 2):
        arrived = jnp.concatenate(
            [
                jnp.concatenate(
                    [shares[r][g * width : (g + 1) * width, :] for r in range(peers)], axis=0
                )
                for g in (pair, pair + 1)
            ],
            axis=1,
        )
        inflow = jnp.dot(scatter, arrived, preferred_element_type=jnp.float32)
        for jj in range(2 * TOGETHER):
            j = pair * TOGETHER + jj
            wave = ready_ref[4 * own_blocks + j : 4 * own_blocks + j + 1, :]
            first = jj % TOGETHER * own_blocks
            left = jj // TOGETHER * block_rows
            half_forcing = gain * inflow[
                first : first + own_blocks, left : left + block_rows
            ] + (wave * counts - excite_offset / 2)
            inhibit_drive = (inhibit_inhibit / 2) * inhibit + inhibit_offset / 2
            excite_turn = jnp.tanh(carried + (half_forcing - (inhibit_excite / 2) * inhibit))
            inhibit_turn = jnp.tanh((excite_inhibit / 2 / a) * carried - inhibit_drive)
            carried = ((1 - excite_rate) * carried + a * excite_rate / 2) + (
                a * excite_rate / 2
            ) * excite_turn
            inhibit = ((1 - inhibit_rate) * inhibit + inhibit_rate / 2) + (
                inhibit_rate / 2
            ) * inhibit_turn
            samples[pl.ds(j, own_blocks, stride=PITCH), :] = carried * (1 / a)
    rates[0] = carried * (1 / a)
    rates[1] = inhibit
    for b in range(own_blocks):
        where = slice(b * block_rows, (b + 1) * block_rows)
        state[0:1, where] = rates[0, b : b + 1, :]
        state[1:2, where] = rates[1, b : b + 1, :]
    copies = [pltpu.make_async_copy(state, state_hbm, sems.at[0])]
    copies[0].start()

    fit = fit_ref[...]
    for g in range(0, own_blocks // GROUP, 2):
        part = jnp.concatenate(
            [
                jnp.concatenate(
                    [
                        samples[b * PITCH : b * PITCH + STEPS, :]
                        for b in range((g + i) * GROUP, (g + i + 1) * GROUP)
                    ],
                    axis=0,
                )
                for i in range(2)
            ],
            axis=1,
        )
        part_high = part.astype(jnp.bfloat16)
        part_low = (part - part_high.astype(jnp.float32)).astype(jnp.bfloat16)
        fitted = jnp.dot(
            fit, jnp.concatenate([part_high, part_low, part_high], axis=0),
            preferred_element_type=jnp.float32,
        ).astype(jnp.bfloat16)
        for i in range(2):
            coefs[(g + i) * GROUP : (g + i + 1) * GROUP] = fitted[
                :, i * block_rows : (i + 1) * block_rows
            ].reshape(GROUP, coef_count, block_rows)
        where = pl.ds(g * GROUP, 2 * GROUP)
        copies.append(
            pltpu.make_async_copy(coefs.at[where], coefs_hbm.at[where], sems.at[1 + g // 2])
        )
        copies[-1].start()
    for copy in copies:
        copy.wait()


def far(x):
    return pltpu.with_memory_space_constraint(x, pltpu.HBM)


def params():
    return pltpu.CompilerParams(vmem_limit_bytes=20 << 20)


def local(
    fresh_coefs,
    older_coefs,
    state,
    lesion,
    stim_nodes,
    stim_wave,
    read_blocks,
    tract_slot,
    tract_target,
    tract_delay,
    tract_frac,
    tract_weights,
):
    wide_peers = lax.axis_size("wide")
    peers = lax.axis_size("narrow")
    own_blocks, coef_count, block_rows = fresh_coefs.shape
    capacity = read_blocks.shape[3]
    slot_count = wide_peers * capacity
    tile_count = tract_slot.shape[2]
    peer_targets = tile_count // (2 * peers)
    share_rows = peer_targets * STEPS + HEAD

    def swap(x, axis, r):
        return lax.ppermute(x, axis, [(i, i ^ r) for i in range(lax.axis_size(axis))])

    reads = read_blocks.reshape(wide_peers, capacity).T
    ways = [1, *range(wide_peers - 1, 1, -1)]
    asked = [swap(reads, "wide", r) for r in ways]

    vmem_inputs = [
        VMEM(state.shape, jnp.float32),
        VMEM((own_blocks, block_rows), jnp.int32),
        VMEM((1, stim_nodes.shape[0]), jnp.int32),
        VMEM((1, STEPS), jnp.float32),
        VMEM((1, tile_count), jnp.int32),
        VMEM((1, tile_count), jnp.int32),
        VMEM((1, tile_count), jnp.int32),
        VMEM((3, HEAD, 128), jnp.float32),
        VMEM((LENGTH, SEGS * coef_count), jnp.bfloat16),
        VMEM((slot_count, HSEG, coef_count, block_rows), jnp.bfloat16),
    ]
    table = far(jnp.asarray(expand_table(coef_count)))
    fresh = pl.pallas_call(
        fresh_kernel,
        out_shape=pltpu.VMEM(fresh_coefs.shape, jnp.bfloat16),
        in_specs=[hbm_spec],
        out_specs=vmem_spec,
        scratch_shapes=[pltpu.SemaphoreType.DMA],
        compiler_params=params(),
        name="fresh_near",
    )(far(fresh_coefs))
    weights, ready, hist, tiles, fracs, heads = pl.pallas_call(
        functools.partial(
            prepare_kernel,
            peers=peers, own_blocks=own_blocks, peer_targets=peer_targets, capacity=capacity,
        ),
        out_shape=[
            pltpu.VMEM((tile_count, block_rows, block_rows), jnp.bfloat16),
            pltpu.VMEM((4 * own_blocks + STEPS, block_rows), jnp.float32),
            pltpu.VMEM((slot_count * LENGTH, block_rows), jnp.float32),
            pltpu.VMEM((2, 128), jnp.int32),
            pltpu.VMEM((1, tile_count), jnp.float32),
            pltpu.VMEM((peers, HEAD, 128), jnp.bfloat16),
        ],
        in_specs=[vmem_spec] + [hbm_spec] * 13,
        out_specs=[vmem_spec] * 6,
        scratch_shapes=[
            SMEM((capacity, wide_peers), jnp.int32),
            *vmem_inputs,
            pltpu.SemaphoreType.DMA((12 + CHUNKS,)),
        ],
        compiler_params=params(),
        name="prepare",
    )(
        fresh,
        far(reads),
        far(state),
        far(lesion.reshape(own_blocks, block_rows)),
        far(stim_nodes.reshape(1, -1)),
        far(stim_wave.reshape(1, -1)),
        far(tract_slot.reshape(1, tile_count)),
        far(tract_target.reshape(1, tile_count)),
        far(tract_delay.reshape(1, tile_count)),
        far(jnp.asarray(lane_tables(peers, peer_targets, own_blocks))),
        table,
        far(older_coefs.reshape(slot_count, HSEG, coef_count, block_rows)),
        far(tract_frac.reshape(1, tile_count)),
        far(tract_weights.reshape(tile_count, block_rows, block_rows)),
    )

    picked = pl.pallas_call(
        functools.partial(pick_kernel, capacity=capacity, peers=wide_peers, ways=ways),
        out_shape=[pltpu.VMEM((capacity, coef_count, block_rows), jnp.bfloat16)]
        * (wide_peers - 1),
        in_specs=[vmem_spec] * wide_peers,
        out_specs=[vmem_spec] * (wide_peers - 1),
        scratch_shapes=[
            SMEM((wide_peers - 1, capacity, wide_peers), jnp.int32),
            pltpu.SemaphoreType.DMA((wide_peers - 1,)),
        ],
        compiler_params=params(),
        name="pick_blocks",
    )(*asked, fresh)
    news = [swap(picked[r - 1], "wide", r) for r in range(wide_peers - 1, 0, -1)]

    shares = pl.pallas_call(
        functools.partial(
            tract_kernel,
            wide_peers=wide_peers, peers=peers, capacity=capacity, peer_targets=peer_targets,
        ),
        out_shape=[pltpu.VMEM((share_rows, block_rows), jnp.bfloat16)] * peers,
        in_specs=[vmem_spec] * (5 + wide_peers),
        out_specs=[vmem_spec] * peers,
        scratch_shapes=[
            SMEM((2, 128), jnp.int32),
            SMEM((1, tile_count), jnp.float32),
            VMEM((slot_count * LENGTH, block_rows), jnp.float32),
            VMEM((peers * peer_targets * STEPS, block_rows), jnp.float32),
            pltpu.SemaphoreType.DMA((2,)),
        ],
        compiler_params=params(),
        name="tract_tiles",
    )(fracs, tiles, table, heads, weights, hist, *news)
    order = [*range(2, peers), 1, 0]
    arrived = [swap(shares[r], "narrow", r) if r else shares[r] for r in order]

    new_coefs, final_state = pl.pallas_call(
        functools.partial(
            window_kernel,
            peers=peers, own_blocks=own_blocks, peer_targets=peer_targets, coef_count=coef_count,
        ),
        out_shape=[
            jax.ShapeDtypeStruct(fresh_coefs.shape, jnp.bfloat16),
            jax.ShapeDtypeStruct(state.shape, jnp.float32),
        ],
        in_specs=[vmem_spec] * (peers + 2),
        out_specs=[hbm_spec] * 2,
        scratch_shapes=[
            VMEM((own_blocks * PITCH, block_rows), jnp.float32),
            VMEM((2, own_blocks, block_rows), jnp.float32),
            VMEM(fresh_coefs.shape, jnp.bfloat16),
            VMEM(state.shape, jnp.float32),
            pltpu.SemaphoreType.DMA((1 + own_blocks // GROUP // 2,)),
        ],
        compiler_params=params(),
        name="window_steps",
    )(*arrived, ready, jnp.asarray(fit_table(coef_count)))
    return new_coefs, final_state


def solution(mesh):
    in_specs = (
        P(("sweep", "wide", "narrow"), None, None),
        P(("sweep", "wide"), "narrow", None, None, None, None),
        P(None, ("sweep", "wide", "narrow")),
        P(("sweep", "wide", "narrow")),
        P("sweep"),
        P("sweep"),
        P("wide", "narrow", None, None),
        P("wide", "narrow", None),
        P("wide", "narrow", None),
        P("wide", "narrow", None),
        P("wide", "narrow", None),
        P("wide", "narrow", None, None, None),
    )
    out_specs = (P(("sweep", "wide", "narrow"), None, None), P(None, ("sweep", "wide", "narrow")))
    return jax.shard_map(local, mesh=mesh, in_specs=in_specs, out_specs=out_specs, check_vma=False)
```

```python
import functools
import math

import jax
import jax.numpy as jnp
import ml_dtypes
import numpy as np
from jax import lax
from jax.experimental import pallas as pl
from jax.experimental.pallas import tpu as pltpu
from jax.sharding import PartitionSpec as P

STEPS = 32
HSEG = 2
SEGS = HSEG + 1
LENGTH = SEGS * STEPS
GROUP = 4
HEAD = 16
PITCH = STEPS + 1
CHUNKS = 8
UNROLL = 4

excite_rate = 0.1
inhibit_rate = 0.05
excite_excite = 1.5
inhibit_excite = 2.0
excite_inhibit = 2.0
inhibit_inhibit = 0.5
excite_offset = 0.5
inhibit_offset = 0.5
tract_gain = 2.0

SMEM = pltpu.SMEM
VMEM = pltpu.VMEM
vmem_spec = pl.BlockSpec(memory_space=VMEM)
hbm_spec = pl.BlockSpec(memory_space=pltpu.HBM)


def basis_table(coef_count, step_count):
    order = np.arange(coef_count, dtype=np.float32)[:, None]
    places = np.arange(step_count, dtype=np.float32)[None, :]
    angles = np.float32(np.pi) * (step_count - places - np.float32(0.5)) / np.float32(step_count)
    return np.cos((order * angles).astype(np.float64)).astype(np.float32)


def expand_table(coef_count):
    basis = basis_table(coef_count, STEPS).astype(ml_dtypes.bfloat16)
    table = np.zeros((LENGTH, SEGS * coef_count), ml_dtypes.bfloat16)
    for seg in range(SEGS):
        table[seg * STEPS : (seg + 1) * STEPS, seg * coef_count : (seg + 1) * coef_count] = basis.T
    return table


def fit_table(coef_count):
    scales = np.where(np.arange(coef_count)[:, None] == 0, 1.0, 2.0) / STEPS
    fit = (basis_table(coef_count, STEPS) * scales).astype(np.float32)
    whole = np.zeros((GROUP * coef_count, GROUP * STEPS), np.float32)
    for g in range(GROUP):
        whole[g * coef_count : (g + 1) * coef_count, g * STEPS : (g + 1) * STEPS] = fit
    high = whole.astype(ml_dtypes.bfloat16)
    low = (whole - high.astype(np.float32)).astype(ml_dtypes.bfloat16)
    return np.concatenate([high, high, low], axis=1)


TOGETHER = 8


def lane_tables(peers, peer_targets, own_blocks):
    width = TOGETHER * peer_targets
    assert TOGETHER * own_blocks <= 256 and peers * width <= HEAD * 128
    lane = np.arange(HEAD * 128)
    used = lane < peers * width
    within = lane % width
    rank = np.where(used, within // TOGETHER, -5)
    offset = within % TOGETHER * own_blocks + 1
    place = np.where(used, lane // width, -5)
    return np.stack([rank, offset, place]).astype(np.float32).reshape(3, HEAD, 128)


def prepare_kernel(
    fresh_ref, reads_hbm, state_hbm, lesion_hbm, stim_hbm, wave_hbm, slot_hbm, target_hbm,
    delay_hbm, lanes_hbm, table_hbm, older_hbm, frac_hbm,
    ready_out, hist_out, tiles_out, fracs_out, head_out,
    reads, state, lesion, stim, wave, slot, target, delay, lanes, table, older, sems,
    *, peers, own_blocks, peer_targets, capacity,
):
    pairs = [
        (reads_hbm, reads), (target_hbm, target), (slot_hbm, slot),
        (delay_hbm, delay), (lanes_hbm, lanes), (table_hbm, table), (older_hbm, older),
        (state_hbm, state), (lesion_hbm, lesion), (stim_hbm, stim), (wave_hbm, wave),
        (frac_hbm, fracs_out),
    ]
    copies = [
        pltpu.make_async_copy(source, into, sems.at[i]) for i, (source, into) in enumerate(pairs)
    ]
    for copy in copies:
        copy.start()
    for copy in copies[1:5]:
        copy.wait()
    place = lax.axis_index("narrow")
    owner = lax.axis_index("wide")
    tile_count = target.shape[1]
    target_count = peers * own_blocks

    numbers = lax.broadcasted_iota(jnp.int32, (target_count, tile_count), 0)
    hits = jnp.where(numbers == target[...], 1.0, 0.0)
    held = jnp.dot(
        hits.astype(jnp.bfloat16), jnp.ones((tile_count, 128), jnp.bfloat16),
        preferred_element_type=jnp.float32,
    )
    held = jnp.minimum(held, 1.0)
    shape = (own_blocks, own_blocks)
    below = jnp.where(
        lax.broadcasted_iota(jnp.int32, shape, 0) > lax.broadcasted_iota(jnp.int32, shape, 1),
        1.0, 0.0,
    ).astype(jnp.bfloat16)
    block = lax.broadcasted_iota(jnp.int32, (own_blocks, 128), 0).astype(jnp.float32)
    ranks = jnp.zeros((1, tile_count), jnp.float32)
    head_rows = pl.cdiv(peers * TOGETHER * peer_targets, 128)
    for p in range(peers):
        part = slice(p * own_blocks, (p + 1) * own_blocks)
        rank = jnp.dot(below, held[part].astype(jnp.bfloat16), preferred_element_type=jnp.float32)
        ranks = ranks + jnp.sum(hits[part] * rank[:, :tile_count], axis=0, keepdims=True)
        rank = jnp.where(held[part] > 0.5, rank, -1.0)
        source = (place ^ p).astype(jnp.float32)
        rows = []
        for h in range(head_rows):
            match = rank == lanes[0, h : h + 1, :]
            ids = jnp.sum(jnp.where(match, block, 0.0), axis=0, keepdims=True)
            mine = lanes[2, h : h + 1, :] == source
            rows.append(jnp.where(mine, ids + lanes[1, h : h + 1, :], 0.0))
        rows.append(jnp.zeros((HEAD - head_rows, 128), jnp.float32))
        head_out[p] = jnp.concatenate(rows, axis=0).astype(jnp.bfloat16)

    across = jnp.zeros((1, tile_count), jnp.int32)
    for p in range(1, peers):
        across = across + jnp.where(target[...] >= p * own_blocks, 1, 0)
    tiles_out[0:1, :tile_count] = slot[...] * LENGTH + (LENGTH - 1) - delay[...]
    tiles_out[1:2, :tile_count] = (across * peer_targets + ranks.astype(jnp.int32)) * TOGETHER

    for copy in copies[5:7]:
        copy.wait()
    coef_count = older.shape[2]
    earlier = HSEG * STEPS
    for s in range(older.shape[0]):
        segments = [older[s, h] for h in range(HSEG - 1, -1, -1)]
        hist_out[s * LENGTH : s * LENGTH + earlier, :] = jnp.dot(
            table[:earlier, : HSEG * coef_count], jnp.concatenate(segments, axis=0),
            preferred_element_type=jnp.float32,
        )
        hist_out[s * LENGTH + earlier : (s + 1) * LENGTH, :] = jnp.zeros(
            (STEPS, hist_out.shape[1]), jnp.float32
        )
    copies[0].wait()
    for c in range(capacity):
        rows = pl.ds(pl.multiple_of((owner * capacity + c) * LENGTH + earlier, 8), STEPS)
        hist_out[rows, :] = jnp.dot(
            table[:STEPS, :coef_count], fresh_ref[jnp.maximum(reads[c, owner], 0)],
            preferred_element_type=jnp.float32,
        )

    for copy in copies[7:11]:
        copy.wait()
    block_rows = lesion.shape[1]
    for b in range(own_blocks):
        piece = state[:, b * block_rows : (b + 1) * block_rows]
        ready_out[b : b + 1, :] = piece[0:1, :]
        ready_out[own_blocks + b : own_blocks + b + 1, :] = piece[1:2, :]
    ready_out[2 * own_blocks : 3 * own_blocks, :] = tract_gain * (
        1.0 - lesion[...].astype(jnp.float32)
    )
    stim_count = stim.shape[1]
    nodes = stim[...] - (owner * peers + place) * (own_blocks * block_rows)
    blocks = lax.shift_right_arithmetic(nodes, block_rows.bit_length() - 1)
    offsets = nodes & (block_rows - 1)
    in_block = lax.broadcasted_iota(jnp.int32, (own_blocks, stim_count), 0) == blocks
    at_offset = lax.broadcasted_iota(jnp.int32, (block_rows, stim_count), 0) == offsets
    ready_out[3 * own_blocks : 4 * own_blocks, :] = lax.dot_general(
        jnp.where(in_block, 1.0, 0.0).astype(jnp.bfloat16),
        jnp.where(at_offset, 1.0, 0.0).astype(jnp.bfloat16),
        (((1,), (1,)), ((), ())),
        preferred_element_type=jnp.float32,
    )
    shape = (STEPS, STEPS)
    diagonal = lax.broadcasted_iota(jnp.int32, shape, 0) == lax.broadcasted_iota(jnp.int32, shape, 1)
    column = jnp.sum(jnp.where(diagonal, wave[...], 0.0), axis=1, keepdims=True)
    ready_out[4 * own_blocks :, :] = jnp.broadcast_to(column, (STEPS, block_rows))
    for copy in copies[11:]:
        copy.wait()


def near_kernel(fresh_hbm, weights_hbm, fresh_out, weights_out, sems):
    copies = [pltpu.make_async_copy(fresh_hbm, fresh_out, sems.at[CHUNKS])]
    part = weights_hbm.shape[0] // CHUNKS
    for i in range(CHUNKS):
        rows = pl.ds(i * part, part)
        copies.append(
            pltpu.make_async_copy(weights_hbm.at[rows], weights_out.at[rows], sems.at[i])
        )
    for copy in copies:
        copy.start()
    for copy in copies:
        copy.wait()


def pick_kernel(*refs, capacity, peers, ways):
    tables = refs[: peers - 1]
    fresh = refs[peers - 1]
    outs = refs[peers : 2 * peers - 1]
    asked, sems = refs[2 * peers - 1 :]
    place = lax.axis_index("wide")
    copies = [pltpu.make_async_copy(tables[r], asked.at[r], sems.at[r]) for r in range(peers - 1)]
    for copy in copies:
        copy.start()
    for i, r in enumerate(ways):
        copies[i].wait()
        for c in range(capacity):
            outs[r - 1][c] = fresh[jnp.maximum(asked[i, c, place], 0)]


def tract_kernel(
    fracs_ref, tiles_ref, table_ref, head_ref, weights, hist_ref, *refs,
    wide_peers, peers, capacity, peer_targets,
):
    news = refs[: wide_peers - 1]
    outs = refs[wide_peers - 1 : wide_peers - 1 + peers]
    tiles, frac, hist, total, sems = refs[wide_peers - 1 + peers :]
    place = lax.axis_index("narrow")
    owner = lax.axis_index("wide")
    copies = [
        pltpu.make_async_copy(tiles_ref, tiles, sems.at[0]),
        pltpu.make_async_copy(fracs_ref, frac, sems.at[1]),
    ]
    for copy in copies:
        copy.start()
    total[...] = jnp.zeros_like(total)
    hist[...] = hist_ref[...]
    for i, block in enumerate(news):
        table = table_ref[:STEPS, : block.shape[1]]
        for c in range(capacity):
            slot = (owner ^ (wide_peers - 1 - i)) * capacity + c
            rows = pl.ds(pl.multiple_of(slot * LENGTH + HSEG * STEPS, 8), STEPS)
            hist[rows, :] = jnp.dot(table, block[c], preferred_element_type=jnp.float32)
    for copy in copies:
        copy.wait()

    span = peer_targets * TOGETHER
    pitch = peers * span
    block_rows = weights.shape[2]
    for turn in range(0, weights.shape[0], UNROLL):
        rows = []
        for t in range(turn, turn + UNROLL):
            fraction = frac[0, t]
            start = tiles[0, t]
            earlier = hist[pl.ds(start, STEPS), :]
            later = hist[pl.ds(start + 1, STEPS), :]
            rows.append(((1.0 - fraction) * later + fraction * earlier).astype(jnp.bfloat16))
        none = jnp.zeros((2 * STEPS, block_rows), jnp.bfloat16)
        left = jnp.concatenate([*rows[:2], none], axis=0)
        right = jnp.concatenate([none, *rows[2:]], axis=0)
        product = lax.dot_general(
            jnp.concatenate([left, right], axis=1),
            jnp.concatenate(
                [
                    weights[t : t + 2].reshape(2 * block_rows, block_rows)
                    for t in (turn, turn + 2)
                ],
                axis=1,
            ),
            (((1,), (1,)), ((), ())),
            preferred_element_type=jnp.float32,
        )
        sums = [
            product[i * STEPS : (i + 1) * STEPS, i % 2 * block_rows : (i % 2 + 1) * block_rows]
            for i in range(UNROLL)
        ]
        for t in range(turn, turn + UNROLL):
            first = tiles[1, t]
            for g in range(STEPS // TOGETHER):
                rows = pl.ds(pl.multiple_of(first + g * pitch, 8), TOGETHER)
                total[rows, :] += sums[t - turn][g * TOGETHER : (g + 1) * TOGETHER]

    for r in range(peers):
        for g in range(STEPS // TOGETHER):
            first = pl.multiple_of(g * pitch + (place ^ r) * span, 8)
            outs[r][g * span : (g + 1) * span, :] = total[pl.ds(first, span), :].astype(
                jnp.bfloat16
            )
        outs[r][peer_targets * STEPS :, :] = head_ref[place ^ r]


def window_kernel(*refs, peers, own_blocks, peer_targets, coef_count):
    shares = dict(zip([*range(2, peers), 1, 0], refs))
    (
        ready_ref, fit_ref, coefs_hbm, state_hbm, samples, rates, coefs, state, sems,
    ) = refs[peers:]
    block_rows = ready_ref.shape[1]
    width = TOGETHER * peer_targets
    span = peer_targets * STEPS

    head = shares[0][span:, :].astype(jnp.float32)
    for r in range(1, peers):
        head = head + shares[r][span:, :].astype(jnp.float32)
    row = lax.broadcasted_iota(jnp.int32, (TOGETHER * own_blocks, 128), 0).astype(jnp.float32) + 1.0
    columns = peers * width
    scatter = jnp.concatenate(
        [
            jnp.where(row == head[h : h + 1, :], 1.0, 0.0).astype(jnp.bfloat16)
            for h in range(pl.cdiv(columns, 128))
        ],
        axis=1,
    )[:, :columns]

    excite, inhibit, gain, counts = [
        ready_ref[i * own_blocks : (i + 1) * own_blocks, :] for i in range(4)
    ]
    a = excite_excite / 2
    gain = 0.5 * gain
    counts = 0.5 * counts
    carried = a * excite
    for pair in range(0, STEPS // TOGETHER, 2):
        arrived = jnp.concatenate(
            [
                jnp.concatenate(
                    [shares[r][g * width : (g + 1) * width, :] for r in range(peers)], axis=0
                )
                for g in (pair, pair + 1)
            ],
            axis=1,
        )
        inflow = jnp.dot(scatter, arrived, preferred_element_type=jnp.float32)
        for jj in range(2 * TOGETHER):
            j = pair * TOGETHER + jj
            wave = ready_ref[4 * own_blocks + j : 4 * own_blocks + j + 1, :]
            first = jj % TOGETHER * own_blocks
            left = jj // TOGETHER * block_rows
            half_forcing = gain * inflow[
                first : first + own_blocks, left : left + block_rows
            ] + (wave * counts - excite_offset / 2)
            inhibit_drive = (inhibit_inhibit / 2) * inhibit + inhibit_offset / 2
            excite_turn = jnp.tanh(carried + (half_forcing - (inhibit_excite / 2) * inhibit))
            inhibit_turn = jnp.tanh((excite_inhibit / 2 / a) * carried - inhibit_drive)
            carried = ((1 - excite_rate) * carried + a * excite_rate / 2) + (
                a * excite_rate / 2
            ) * excite_turn
            inhibit = ((1 - inhibit_rate) * inhibit + inhibit_rate / 2) + (
                inhibit_rate / 2
            ) * inhibit_turn
            samples[pl.ds(j, own_blocks, stride=PITCH), :] = carried * (1 / a)
    rates[0] = carried * (1 / a)
    rates[1] = inhibit
    for b in range(own_blocks):
        where = slice(b * block_rows, (b + 1) * block_rows)
        state[0:1, where] = rates[0, b : b + 1, :]
        state[1:2, where] = rates[1, b : b + 1, :]
    copies = [pltpu.make_async_copy(state, state_hbm, sems.at[0])]
    copies[0].start()

    fit = fit_ref[...]
    for g in range(0, own_blocks // GROUP, 2):
        part = jnp.concatenate(
            [
                jnp.concatenate(
                    [
                        samples[b * PITCH : b * PITCH + STEPS, :]
                        for b in range((g + i) * GROUP, (g + i + 1) * GROUP)
                    ],
                    axis=0,
                )
                for i in range(2)
            ],
            axis=1,
        )
        part_high = part.astype(jnp.bfloat16)
        part_low = (part - part_high.astype(jnp.float32)).astype(jnp.bfloat16)
        fitted = jnp.dot(
            fit, jnp.concatenate([part_high, part_low, part_high], axis=0),
            preferred_element_type=jnp.float32,
        ).astype(jnp.bfloat16)
        for i in range(2):
            coefs[(g + i) * GROUP : (g + i + 1) * GROUP] = fitted[
                :, i * block_rows : (i + 1) * block_rows
            ].reshape(GROUP, coef_count, block_rows)
        where = pl.ds(g * GROUP, 2 * GROUP)
        copies.append(
            pltpu.make_async_copy(coefs.at[where], coefs_hbm.at[where], sems.at[1 + g // 2])
        )
        copies[-1].start()
    for copy in copies:
        copy.wait()


def far(x):
    return pltpu.with_memory_space_constraint(x, pltpu.HBM)


def params():
    return pltpu.CompilerParams(vmem_limit_bytes=20 << 20)


def local(
    fresh_coefs,
    older_coefs,
    state,
    lesion,
    stim_nodes,
    stim_wave,
    read_blocks,
    tract_slot,
    tract_target,
    tract_delay,
    tract_frac,
    tract_weights,
):
    wide_peers = lax.axis_size("wide")
    peers = lax.axis_size("narrow")
    own_blocks, coef_count, block_rows = fresh_coefs.shape
    capacity = read_blocks.shape[3]
    slot_count = wide_peers * capacity
    tile_count = tract_slot.shape[2]
    peer_targets = tile_count // (2 * peers)
    share_rows = peer_targets * STEPS + HEAD

    def swap(x, axis, r):
        return lax.ppermute(x, axis, [(i, i ^ r) for i in range(lax.axis_size(axis))])

    reads = read_blocks.reshape(wide_peers, capacity).T
    ways = [1, *range(wide_peers - 1, 1, -1)]
    asked = [swap(reads, "wide", r) for r in ways]

    vmem_inputs = [
        VMEM(state.shape, jnp.float32),
        VMEM((own_blocks, block_rows), jnp.int32),
        VMEM((1, stim_nodes.shape[0]), jnp.int32),
        VMEM((1, STEPS), jnp.float32),
        VMEM((1, tile_count), jnp.int32),
        VMEM((1, tile_count), jnp.int32),
        VMEM((1, tile_count), jnp.int32),
        VMEM((3, HEAD, 128), jnp.float32),
        VMEM((LENGTH, SEGS * coef_count), jnp.bfloat16),
        VMEM((slot_count, HSEG, coef_count, block_rows), jnp.bfloat16),
    ]
    table = far(jnp.asarray(expand_table(coef_count)))
    fresh, weights = pl.pallas_call(
        near_kernel,
        out_shape=[
            pltpu.VMEM(fresh_coefs.shape, jnp.bfloat16),
            pltpu.VMEM((tile_count, block_rows, block_rows), jnp.bfloat16),
        ],
        in_specs=[hbm_spec] * 2,
        out_specs=[vmem_spec] * 2,
        scratch_shapes=[pltpu.SemaphoreType.DMA((CHUNKS + 1,))],
        compiler_params=params(),
        name="near",
    )(far(fresh_coefs), far(tract_weights.reshape(tile_count, block_rows, block_rows)))
    ready, hist, tiles, fracs, heads = pl.pallas_call(
        functools.partial(
            prepare_kernel,
            peers=peers, own_blocks=own_blocks, peer_targets=peer_targets, capacity=capacity,
        ),
        out_shape=[
            pltpu.VMEM((4 * own_blocks + STEPS, block_rows), jnp.float32),
            pltpu.VMEM((slot_count * LENGTH, block_rows), jnp.float32),
            pltpu.VMEM((2, 128), jnp.int32),
            pltpu.VMEM((1, tile_count), jnp.float32),
            pltpu.VMEM((peers, HEAD, 128), jnp.bfloat16),
        ],
        in_specs=[vmem_spec] + [hbm_spec] * 12,
        out_specs=[vmem_spec] * 5,
        scratch_shapes=[
            SMEM((capacity, wide_peers), jnp.int32),
            *vmem_inputs,
            pltpu.SemaphoreType.DMA((12,)),
        ],
        compiler_params=params(),
        name="prepare",
    )(
        fresh,
        far(reads),
        far(state),
        far(lesion.reshape(own_blocks, block_rows)),
        far(stim_nodes.reshape(1, -1)),
        far(stim_wave.reshape(1, -1)),
        far(tract_slot.reshape(1, tile_count)),
        far(tract_target.reshape(1, tile_count)),
        far(tract_delay.reshape(1, tile_count)),
        far(jnp.asarray(lane_tables(peers, peer_targets, own_blocks))),
        table,
        far(older_coefs.reshape(slot_count, HSEG, coef_count, block_rows)),
        far(tract_frac.reshape(1, tile_count)),
    )

    picked = pl.pallas_call(
        functools.partial(pick_kernel, capacity=capacity, peers=wide_peers, ways=ways),
        out_shape=[pltpu.VMEM((capacity, coef_count, block_rows), jnp.bfloat16)]
        * (wide_peers - 1),
        in_specs=[vmem_spec] * wide_peers,
        out_specs=[vmem_spec] * (wide_peers - 1),
        scratch_shapes=[
            SMEM((wide_peers - 1, capacity, wide_peers), jnp.int32),
            pltpu.SemaphoreType.DMA((wide_peers - 1,)),
        ],
        compiler_params=params(),
        name="pick_blocks",
    )(*asked, fresh)
    news = [swap(picked[r - 1], "wide", r) for r in range(wide_peers - 1, 0, -1)]

    shares = pl.pallas_call(
        functools.partial(
            tract_kernel,
            wide_peers=wide_peers, peers=peers, capacity=capacity, peer_targets=peer_targets,
        ),
        out_shape=[pltpu.VMEM((share_rows, block_rows), jnp.bfloat16)] * peers,
        in_specs=[vmem_spec] * (5 + wide_peers),
        out_specs=[vmem_spec] * peers,
        scratch_shapes=[
            SMEM((2, 128), jnp.int32),
            SMEM((1, tile_count), jnp.float32),
            VMEM((slot_count * LENGTH, block_rows), jnp.float32),
            VMEM((peers * peer_targets * STEPS, block_rows), jnp.float32),
            pltpu.SemaphoreType.DMA((2,)),
        ],
        compiler_params=params(),
        name="tract_tiles",
    )(fracs, tiles, table, heads, weights, hist, *news)
    order = [*range(2, peers), 1, 0]
    arrived = [swap(shares[r], "narrow", r) if r else shares[r] for r in order]

    new_coefs, final_state = pl.pallas_call(
        functools.partial(
            window_kernel,
            peers=peers, own_blocks=own_blocks, peer_targets=peer_targets, coef_count=coef_count,
        ),
        out_shape=[
            jax.ShapeDtypeStruct(fresh_coefs.shape, jnp.bfloat16),
            jax.ShapeDtypeStruct(state.shape, jnp.float32),
        ],
        in_specs=[vmem_spec] * (peers + 2),
        out_specs=[hbm_spec] * 2,
        scratch_shapes=[
            VMEM((own_blocks * PITCH, block_rows), jnp.float32),
            VMEM((2, own_blocks, block_rows), jnp.float32),
            VMEM(fresh_coefs.shape, jnp.bfloat16),
            VMEM(state.shape, jnp.float32),
            pltpu.SemaphoreType.DMA((1 + own_blocks // GROUP // 2,)),
        ],
        compiler_params=params(),
        name="window_steps",
    )(*arrived, ready, jnp.asarray(fit_table(coef_count)))
    return new_coefs, final_state


def solution(mesh):
    in_specs = (
        P(("sweep", "wide", "narrow"), None, None),
        P(("sweep", "wide"), "narrow", None, None, None, None),
        P(None, ("sweep", "wide", "narrow")),
        P(("sweep", "wide", "narrow")),
        P("sweep"),
        P("sweep"),
        P("wide", "narrow", None, None),
        P("wide", "narrow", None),
        P("wide", "narrow", None),
        P("wide", "narrow", None),
        P("wide", "narrow", None),
        P("wide", "narrow", None, None, None),
    )
    out_specs = (P(("sweep", "wide", "narrow"), None, None), P(None, ("sweep", "wide", "narrow")))
    return jax.shard_map(local, mesh=mesh, in_specs=in_specs, out_specs=out_specs, check_vma=False)
```

```python
import functools
import math

import jax
import jax.numpy as jnp
import ml_dtypes
import numpy as np
from jax import lax
from jax.experimental import pallas as pl
from jax.experimental.pallas import tpu as pltpu
from jax.sharding import PartitionSpec as P

STEPS = 32
HSEG = 2
SEGS = HSEG + 1
LENGTH = SEGS * STEPS
GROUP = 4
HEAD = 16
PITCH = STEPS + 1
CHUNKS = 8
UNROLL = 4

excite_rate = 0.1
inhibit_rate = 0.05
excite_excite = 1.5
inhibit_excite = 2.0
excite_inhibit = 2.0
inhibit_inhibit = 0.5
excite_offset = 0.5
inhibit_offset = 0.5
tract_gain = 2.0

SMEM = pltpu.SMEM
VMEM = pltpu.VMEM
vmem_spec = pl.BlockSpec(memory_space=VMEM)
hbm_spec = pl.BlockSpec(memory_space=pltpu.HBM)


def basis_table(coef_count, step_count):
    order = np.arange(coef_count, dtype=np.float32)[:, None]
    places = np.arange(step_count, dtype=np.float32)[None, :]
    angles = np.float32(np.pi) * (step_count - places - np.float32(0.5)) / np.float32(step_count)
    return np.cos((order * angles).astype(np.float64)).astype(np.float32)


def expand_table(coef_count):
    basis = basis_table(coef_count, STEPS).astype(ml_dtypes.bfloat16)
    table = np.zeros((LENGTH, SEGS * coef_count), ml_dtypes.bfloat16)
    for seg in range(SEGS):
        table[seg * STEPS : (seg + 1) * STEPS, seg * coef_count : (seg + 1) * coef_count] = basis.T
    return table


def fit_table(coef_count):
    scales = np.where(np.arange(coef_count)[:, None] == 0, 1.0, 2.0) / STEPS
    fit = (basis_table(coef_count, STEPS) * scales).astype(np.float32)
    whole = np.zeros((GROUP * coef_count, GROUP * STEPS), np.float32)
    for g in range(GROUP):
        whole[g * coef_count : (g + 1) * coef_count, g * STEPS : (g + 1) * STEPS] = fit
    high = whole.astype(ml_dtypes.bfloat16)
    low = (whole - high.astype(np.float32)).astype(ml_dtypes.bfloat16)
    return np.concatenate([high, high, low], axis=1)


TOGETHER = 8


def lane_tables(peers, peer_targets, own_blocks):
    width = TOGETHER * peer_targets
    assert TOGETHER * own_blocks <= 256 and peers * width <= HEAD * 128
    lane = np.arange(HEAD * 128)
    used = lane < peers * width
    within = lane % width
    rank = np.where(used, within // TOGETHER, -5)
    offset = within % TOGETHER * own_blocks + 1
    place = np.where(used, lane // width, -5)
    return np.stack([rank, offset, place]).astype(np.float32).reshape(3, HEAD, 128)


def prepare_kernel(
    fresh_ref, reads_hbm, state_hbm, lesion_hbm, stim_hbm, wave_hbm, slot_hbm, target_hbm,
    delay_hbm, lanes_hbm, table_hbm, older_hbm, frac_hbm,
    ready_out, hist_out, tiles_out, fracs_out, head_out,
    reads, state, lesion, stim, wave, slot, target, delay, frac, lanes, table, older, sems,
    *, peers, own_blocks, peer_targets, capacity,
):
    pairs = [
        (reads_hbm, reads), (target_hbm, target), (slot_hbm, slot),
        (delay_hbm, delay), (lanes_hbm, lanes), (table_hbm, table), (older_hbm, older),
        (state_hbm, state), (lesion_hbm, lesion), (stim_hbm, stim), (wave_hbm, wave),
        (frac_hbm, frac),
    ]
    copies = [
        pltpu.make_async_copy(source, into, sems.at[i]) for i, (source, into) in enumerate(pairs)
    ]
    for copy in copies:
        copy.start()
    for copy in (*copies[1:5], copies[11]):
        copy.wait()
    place = lax.axis_index("narrow")
    owner = lax.axis_index("wide")
    tile_count = target.shape[1]
    target_count = peers * own_blocks

    numbers = lax.broadcasted_iota(jnp.int32, (target_count, tile_count), 0)
    hits = jnp.where(numbers == target[...], 1.0, 0.0)
    held = jnp.dot(
        hits.astype(jnp.bfloat16), jnp.ones((tile_count, 128), jnp.bfloat16),
        preferred_element_type=jnp.float32,
    )
    held = jnp.minimum(held, 1.0)
    shape = (own_blocks, own_blocks)
    below = jnp.where(
        lax.broadcasted_iota(jnp.int32, shape, 0) > lax.broadcasted_iota(jnp.int32, shape, 1),
        1.0, 0.0,
    ).astype(jnp.bfloat16)
    block = lax.broadcasted_iota(jnp.int32, (own_blocks, 128), 0).astype(jnp.float32)
    ranks = jnp.zeros((1, tile_count), jnp.float32)
    head_rows = pl.cdiv(peers * TOGETHER * peer_targets, 128)
    for p in range(peers):
        part = slice(p * own_blocks, (p + 1) * own_blocks)
        rank = jnp.dot(below, held[part].astype(jnp.bfloat16), preferred_element_type=jnp.float32)
        ranks = ranks + jnp.sum(hits[part] * rank[:, :tile_count], axis=0, keepdims=True)
        rank = jnp.where(held[part] > 0.5, rank, -1.0)
        source = (place ^ p).astype(jnp.float32)
        rows = []
        for h in range(head_rows):
            match = rank == lanes[0, h : h + 1, :]
            ids = jnp.sum(jnp.where(match, block, 0.0), axis=0, keepdims=True)
            mine = lanes[2, h : h + 1, :] == source
            rows.append(jnp.where(mine, ids + lanes[1, h : h + 1, :], 0.0))
        rows.append(jnp.zeros((HEAD - head_rows, 128), jnp.float32))
        head_out[p] = jnp.concatenate(rows, axis=0).astype(jnp.bfloat16)

    across = jnp.zeros((1, tile_count), jnp.int32)
    for p in range(1, peers):
        across = across + jnp.where(target[...] >= p * own_blocks, 1, 0)
    key_row = ((peers - 1) - (across ^ place)).astype(jnp.float32)
    shape = (tile_count, tile_count)
    down = lax.broadcasted_iota(jnp.int32, shape, 0)
    along = lax.broadcasted_iota(jnp.int32, shape, 1)
    key = jnp.sum(jnp.where(down == along, key_row, 0.0), axis=1, keepdims=True)
    ahead = (key_row < key) | ((key_row == key) & (along < down))
    position = jnp.sum(jnp.where(ahead, 1.0, 0.0), axis=1, keepdims=True)
    lane = lax.broadcasted_iota(jnp.int32, (tile_count, 128), 1).astype(jnp.float32)
    chosen = jnp.where(position == lane, 1.0, 0.0)
    starts = (slot[...] * LENGTH + (LENGTH - 1) - delay[...]).astype(jnp.float32)
    index = lax.broadcasted_iota(jnp.int32, (1, tile_count), 1).astype(jnp.float32)
    firsts = (key_row * float(peer_targets) + ranks) * float(TOGETHER)
    facts = jnp.concatenate(
        [index, starts, firsts, frac[...], jnp.zeros((4, tile_count), jnp.float32)], axis=0
    )
    ordered = jnp.dot(
        facts, chosen, precision=lax.Precision.HIGHEST, preferred_element_type=jnp.float32
    )
    fracs_out[...] = ordered[3:4, :]
    tiles_out[0:3, :] = (ordered[0:3, :] + 0.5).astype(jnp.int32)
    tiles_out[3:4, :] = jnp.sum(
        jnp.where(key < lane, 1.0, 0.0), axis=0, keepdims=True
    ).astype(jnp.int32)

    for copy in copies[5:7]:
        copy.wait()
    coef_count = older.shape[2]
    earlier = HSEG * STEPS
    for s in range(older.shape[0]):
        segments = [older[s, h] for h in range(HSEG - 1, -1, -1)]
        hist_out[s * LENGTH : s * LENGTH + earlier, :] = jnp.dot(
            table[:earlier, : HSEG * coef_count], jnp.concatenate(segments, axis=0),
            preferred_element_type=jnp.float32,
        )
        hist_out[s * LENGTH + earlier : (s + 1) * LENGTH, :] = jnp.zeros(
            (STEPS, hist_out.shape[1]), jnp.float32
        )
    copies[0].wait()
    for c in range(capacity):
        rows = pl.ds(pl.multiple_of((owner * capacity + c) * LENGTH + earlier, 8), STEPS)
        hist_out[rows, :] = jnp.dot(
            table[:STEPS, :coef_count], fresh_ref[jnp.maximum(reads[c, owner], 0)],
            preferred_element_type=jnp.float32,
        )

    for copy in copies[7:11]:
        copy.wait()
    block_rows = lesion.shape[1]
    for b in range(own_blocks):
        piece = state[:, b * block_rows : (b + 1) * block_rows]
        ready_out[b : b + 1, :] = piece[0:1, :]
        ready_out[own_blocks + b : own_blocks + b + 1, :] = piece[1:2, :]
    ready_out[2 * own_blocks : 3 * own_blocks, :] = tract_gain * (
        1.0 - lesion[...].astype(jnp.float32)
    )
    stim_count = stim.shape[1]
    nodes = stim[...] - (owner * peers + place) * (own_blocks * block_rows)
    blocks = lax.shift_right_arithmetic(nodes, block_rows.bit_length() - 1)
    offsets = nodes & (block_rows - 1)
    in_block = lax.broadcasted_iota(jnp.int32, (own_blocks, stim_count), 0) == blocks
    at_offset = lax.broadcasted_iota(jnp.int32, (block_rows, stim_count), 0) == offsets
    ready_out[3 * own_blocks : 4 * own_blocks, :] = lax.dot_general(
        jnp.where(in_block, 1.0, 0.0).astype(jnp.bfloat16),
        jnp.where(at_offset, 1.0, 0.0).astype(jnp.bfloat16),
        (((1,), (1,)), ((), ())),
        preferred_element_type=jnp.float32,
    )
    shape = (STEPS, STEPS)
    diagonal = lax.broadcasted_iota(jnp.int32, shape, 0) == lax.broadcasted_iota(jnp.int32, shape, 1)
    column = jnp.sum(jnp.where(diagonal, wave[...], 0.0), axis=1, keepdims=True)
    ready_out[4 * own_blocks :, :] = jnp.broadcast_to(column, (STEPS, block_rows))


def near_kernel(fresh_hbm, weights_hbm, fresh_out, weights_out, sems):
    copies = [pltpu.make_async_copy(fresh_hbm, fresh_out, sems.at[CHUNKS])]
    part = weights_hbm.shape[0] // CHUNKS
    for i in range(CHUNKS):
        rows = pl.ds(i * part, part)
        copies.append(
            pltpu.make_async_copy(weights_hbm.at[rows], weights_out.at[rows], sems.at[i])
        )
    for copy in copies:
        copy.start()
    for copy in copies:
        copy.wait()


def pick_kernel(*refs, capacity, peers, ways):
    tables = refs[: peers - 1]
    fresh = refs[peers - 1]
    outs = refs[peers : 2 * peers - 1]
    asked, sems = refs[2 * peers - 1 :]
    place = lax.axis_index("wide")
    copies = [pltpu.make_async_copy(tables[r], asked.at[r], sems.at[r]) for r in range(peers - 1)]
    for copy in copies:
        copy.start()
    for i, r in enumerate(ways):
        copies[i].wait()
        for c in range(capacity):
            outs[r - 1][c] = fresh[jnp.maximum(asked[i, c, place], 0)]


def add_tiles(tiles, frac, hist, weights, total, pitch, items):
    block_rows = weights.shape[2]
    rows = []
    for t, _ in items:
        fraction = frac[0, t]
        start = tiles[1, t]
        earlier = hist[pl.ds(start, STEPS), :]
        later = hist[pl.ds(start + 1, STEPS), :]
        rows.append(((1.0 - fraction) * later + fraction * earlier).astype(jnp.bfloat16))
    tile = [weights[tiles[0, t]] for t, _ in items]
    none = jnp.zeros((2 * STEPS, block_rows), jnp.bfloat16)
    product = lax.dot_general(
        jnp.concatenate(
            [
                jnp.concatenate([*rows[:2], none], axis=0),
                jnp.concatenate([none, *rows[2:]], axis=0),
            ],
            axis=1,
        ),
        jnp.concatenate(
            [jnp.concatenate(tile[:2], axis=0), jnp.concatenate(tile[2:], axis=0)], axis=1
        ),
        (((1,), (1,)), ((), ())),
        preferred_element_type=jnp.float32,
    )
    for i, (_, first) in enumerate(items):
        left = i % 2 * block_rows
        for g in range(STEPS // TOGETHER):
            where = pl.ds(pl.multiple_of(first + g * pitch, 8), TOGETHER)
            top = i * STEPS + g * TOGETHER
            total[where, :] += product[top : top + TOGETHER, left : left + block_rows]


def write_share(pieces, total, head, first, span, pitch):
    groups = STEPS // TOGETHER // len(pieces)
    for i, piece in enumerate(pieces):
        for g in range(groups):
            top = (i * groups + g) * pitch + first
            piece[g * span : (g + 1) * span, :] = total[top : top + span, :].astype(jnp.bfloat16)
    pieces[-1][groups * span :, :] = head


def far_kernel(
    fracs_ref, tiles_ref, table_ref, head_ref, weights, hist_ref, *refs,
    wide_peers, peers, capacity, peer_targets, fixed,
):
    news = refs[: wide_peers - 1]
    outs = refs[wide_peers - 1 : wide_peers + peers - 3]
    hist, total, tiles, frac, sems = refs[wide_peers + peers - 3 :]
    place = lax.axis_index("narrow")
    owner = lax.axis_index("wide")
    copies = [
        pltpu.make_async_copy(tiles_ref, tiles, sems.at[0]),
        pltpu.make_async_copy(fracs_ref, frac, sems.at[1]),
    ]
    for copy in copies:
        copy.start()
    total[...] = jnp.zeros_like(total)
    hist[...] = hist_ref[...]
    for i, block in enumerate(news):
        table = table_ref[:STEPS, : block.shape[1]]
        for c in range(capacity):
            slot = (owner ^ (wide_peers - 1 - i)) * capacity + c
            rows = pl.ds(pl.multiple_of(slot * LENGTH + HSEG * STEPS, 8), STEPS)
            hist[rows, :] = jnp.dot(table, block[c], preferred_element_type=jnp.float32)
    for copy in copies:
        copy.wait()

    span = peer_targets * TOGETHER
    spare = peers * span
    pitch = spare + TOGETHER
    for t in range(0, fixed, UNROLL):
        items = [(u, tiles[2, u]) for u in range(t, t + UNROLL)]
        add_tiles(tiles, frac, hist, weights, total, pitch, items)
    far_count = tiles[3, peers - 2]

    @pl.loop(0, lax.div(jnp.maximum(far_count - fixed, 0) + (UNROLL - 1), UNROLL))
    def _(turn):
        places = [fixed + turn * UNROLL + u for u in range(UNROLL)]
        items = [(t, jnp.where(t < far_count, tiles[2, t], spare)) for t in places]
        add_tiles(tiles, frac, hist, weights, total, pitch, items)

    for part, out in enumerate(outs):
        write_share([out], total, head_ref[place ^ (peers - 1 - part)], part * span, span, pitch)


def near_tiles_kernel(
    fracs_ref, tiles_ref, head_ref, weights, hist, total_ref, *refs,
    peers, peer_targets, fixed,
):
    *pair, own, tiles, frac, total, sems = refs
    place = lax.axis_index("narrow")
    copies = [
        pltpu.make_async_copy(tiles_ref, tiles, sems.at[0]),
        pltpu.make_async_copy(fracs_ref, frac, sems.at[1]),
    ]
    for copy in copies:
        copy.start()
    total[...] = total_ref[...]
    for copy in copies:
        copy.wait()
    span = peer_targets * TOGETHER
    spare = peers * span
    pitch = spare + TOGETHER
    far_count = tiles[3, peers - 2]
    for t in range(fixed, weights.shape[0], UNROLL):
        items = [
            (u, jnp.where(u < far_count, spare, tiles[2, u])) for u in range(t, t + UNROLL)
        ]
        add_tiles(tiles, frac, hist, weights, total, pitch, items)
    write_share(pair, total, head_ref[place ^ 1], (peers - 2) * span, span, pitch)
    write_share([own], total, head_ref[place], (peers - 1) * span, span, pitch)


def share_rows(pieces, group, width):
    groups = STEPS // TOGETHER // len(pieces)
    first = group % groups * width
    return pieces[group // groups][first : first + width, :]


def window_kernel(*refs, peers, own_blocks, peer_targets, coef_count):
    shares = {r: (ref,) for r, ref in zip(range(2, peers), refs)}
    shares |= {1: refs[peers - 2 : peers], 0: (refs[peers],)}
    (
        ready_ref, fit_ref, coefs_hbm, state_hbm, samples, rates, coefs, state, sems,
    ) = refs[peers + 1 :]
    block_rows = ready_ref.shape[1]
    width = TOGETHER * peer_targets

    head = sum(shares[r][-1][-HEAD:, :].astype(jnp.float32) for r in range(peers))
    row = lax.broadcasted_iota(jnp.int32, (TOGETHER * own_blocks, 128), 0).astype(jnp.float32) + 1.0
    columns = peers * width
    scatter = jnp.concatenate(
        [
            jnp.where(row == head[h : h + 1, :], 1.0, 0.0).astype(jnp.bfloat16)
            for h in range(pl.cdiv(columns, 128))
        ],
        axis=1,
    )[:, :columns]

    excite, inhibit, gain, counts = [
        ready_ref[i * own_blocks : (i + 1) * own_blocks, :] for i in range(4)
    ]
    a = excite_excite / 2
    gain = 0.5 * gain
    counts = 0.5 * counts
    carried = a * excite
    for pair in range(0, STEPS // TOGETHER, 2):
        arrived = jnp.concatenate(
            [
                jnp.concatenate(
                    [share_rows(shares[r], g, width) for r in range(peers)], axis=0
                )
                for g in (pair, pair + 1)
            ],
            axis=1,
        )
        inflow = jnp.dot(scatter, arrived, preferred_element_type=jnp.float32)
        for jj in range(2 * TOGETHER):
            j = pair * TOGETHER + jj
            wave = ready_ref[4 * own_blocks + j : 4 * own_blocks + j + 1, :]
            first = jj % TOGETHER * own_blocks
            left = jj // TOGETHER * block_rows
            half_forcing = gain * inflow[
                first : first + own_blocks, left : left + block_rows
            ] + (wave * counts - excite_offset / 2)
            inhibit_drive = (inhibit_inhibit / 2) * inhibit + inhibit_offset / 2
            excite_turn = jnp.tanh(carried + (half_forcing - (inhibit_excite / 2) * inhibit))
            inhibit_turn = jnp.tanh((excite_inhibit / 2 / a) * carried - inhibit_drive)
            carried = ((1 - excite_rate) * carried + a * excite_rate / 2) + (
                a * excite_rate / 2
            ) * excite_turn
            inhibit = ((1 - inhibit_rate) * inhibit + inhibit_rate / 2) + (
                inhibit_rate / 2
            ) * inhibit_turn
            samples[pl.ds(j, own_blocks, stride=PITCH), :] = carried * (1 / a)
    rates[0] = carried * (1 / a)
    rates[1] = inhibit
    for b in range(own_blocks):
        where = slice(b * block_rows, (b + 1) * block_rows)
        state[0:1, where] = rates[0, b : b + 1, :]
        state[1:2, where] = rates[1, b : b + 1, :]
    copies = [pltpu.make_async_copy(state, state_hbm, sems.at[0])]
    copies[0].start()

    fit = fit_ref[...]
    for g in range(0, own_blocks // GROUP, 2):
        part = jnp.concatenate(
            [
                jnp.concatenate(
                    [
                        samples[b * PITCH : b * PITCH + STEPS, :]
                        for b in range((g + i) * GROUP, (g + i + 1) * GROUP)
                    ],
                    axis=0,
                )
                for i in range(2)
            ],
            axis=1,
        )
        part_high = part.astype(jnp.bfloat16)
        part_low = (part - part_high.astype(jnp.float32)).astype(jnp.bfloat16)
        fitted = jnp.dot(
            fit, jnp.concatenate([part_high, part_low, part_high], axis=0),
            preferred_element_type=jnp.float32,
        ).astype(jnp.bfloat16)
        for i in range(2):
            coefs[(g + i) * GROUP : (g + i + 1) * GROUP] = fitted[
                :, i * block_rows : (i + 1) * block_rows
            ].reshape(GROUP, coef_count, block_rows)
        where = pl.ds(g * GROUP, 2 * GROUP)
        copies.append(
            pltpu.make_async_copy(coefs.at[where], coefs_hbm.at[where], sems.at[1 + g // 2])
        )
        copies[-1].start()
    for copy in copies:
        copy.wait()


def far(x):
    return pltpu.with_memory_space_constraint(x, pltpu.HBM)


def params():
    return pltpu.CompilerParams(vmem_limit_bytes=20 << 20)


def local(
    fresh_coefs,
    older_coefs,
    state,
    lesion,
    stim_nodes,
    stim_wave,
    read_blocks,
    tract_slot,
    tract_target,
    tract_delay,
    tract_frac,
    tract_weights,
):
    wide_peers = lax.axis_size("wide")
    peers = lax.axis_size("narrow")
    own_blocks, coef_count, block_rows = fresh_coefs.shape
    capacity = read_blocks.shape[3]
    slot_count = wide_peers * capacity
    tile_count = tract_slot.shape[2]
    peer_targets = tile_count // (2 * peers)
    share_rows = peer_targets * STEPS + HEAD

    def swap(x, axis, r):
        return lax.ppermute(x, axis, [(i, i ^ r) for i in range(lax.axis_size(axis))])

    reads = read_blocks.reshape(wide_peers, capacity).T
    ways = [1, *range(wide_peers - 1, 1, -1)]
    asked = [swap(reads, "wide", r) for r in ways]

    vmem_inputs = [
        VMEM(state.shape, jnp.float32),
        VMEM((own_blocks, block_rows), jnp.int32),
        VMEM((1, stim_nodes.shape[0]), jnp.int32),
        VMEM((1, STEPS), jnp.float32),
        VMEM((1, tile_count), jnp.int32),
        VMEM((1, tile_count), jnp.int32),
        VMEM((1, tile_count), jnp.int32),
        VMEM((1, tile_count), jnp.float32),
        VMEM((3, HEAD, 128), jnp.float32),
        VMEM((LENGTH, SEGS * coef_count), jnp.bfloat16),
        VMEM((slot_count, HSEG, coef_count, block_rows), jnp.bfloat16),
    ]
    table = far(jnp.asarray(expand_table(coef_count)))
    fresh, weights = pl.pallas_call(
        near_kernel,
        out_shape=[
            pltpu.VMEM(fresh_coefs.shape, jnp.bfloat16),
            pltpu.VMEM((tile_count, block_rows, block_rows), jnp.bfloat16),
        ],
        in_specs=[hbm_spec] * 2,
        out_specs=[vmem_spec] * 2,
        scratch_shapes=[pltpu.SemaphoreType.DMA((CHUNKS + 1,))],
        compiler_params=params(),
        name="near",
    )(far(fresh_coefs), far(tract_weights.reshape(tile_count, block_rows, block_rows)))
    ready, hist, tiles, fracs, heads = pl.pallas_call(
        functools.partial(
            prepare_kernel,
            peers=peers, own_blocks=own_blocks, peer_targets=peer_targets, capacity=capacity,
        ),
        out_shape=[
            pltpu.VMEM((4 * own_blocks + STEPS, block_rows), jnp.float32),
            pltpu.VMEM((slot_count * LENGTH, block_rows), jnp.float32),
            pltpu.VMEM((4, 128), jnp.int32),
            pltpu.VMEM((1, 128), jnp.float32),
            pltpu.VMEM((peers, HEAD, 128), jnp.bfloat16),
        ],
        in_specs=[vmem_spec] + [hbm_spec] * 12,
        out_specs=[vmem_spec] * 5,
        scratch_shapes=[
            SMEM((capacity, wide_peers), jnp.int32),
            *vmem_inputs,
            pltpu.SemaphoreType.DMA((12,)),
        ],
        compiler_params=params(),
        name="prepare",
    )(
        fresh,
        far(reads),
        far(state),
        far(lesion.reshape(own_blocks, block_rows)),
        far(stim_nodes.reshape(1, -1)),
        far(stim_wave.reshape(1, -1)),
        far(tract_slot.reshape(1, tile_count)),
        far(tract_target.reshape(1, tile_count)),
        far(tract_delay.reshape(1, tile_count)),
        far(jnp.asarray(lane_tables(peers, peer_targets, own_blocks))),
        table,
        far(older_coefs.reshape(slot_count, HSEG, coef_count, block_rows)),
        far(tract_frac.reshape(1, tile_count)),
    )

    picked = pl.pallas_call(
        functools.partial(pick_kernel, capacity=capacity, peers=wide_peers, ways=ways),
        out_shape=[pltpu.VMEM((capacity, coef_count, block_rows), jnp.bfloat16)]
        * (wide_peers - 1),
        in_specs=[vmem_spec] * wide_peers,
        out_specs=[vmem_spec] * (wide_peers - 1),
        scratch_shapes=[
            SMEM((wide_peers - 1, capacity, wide_peers), jnp.int32),
            pltpu.SemaphoreType.DMA((wide_peers - 1,)),
        ],
        compiler_params=params(),
        name="pick_blocks",
    )(*asked, fresh)
    news = [swap(picked[r - 1], "wide", r) for r in range(wide_peers - 1, 0, -1)]

    fixed = tile_count * (peers - 2) // peers + 2 * UNROLL
    fixed = min(tile_count, -(-fixed // UNROLL) * UNROLL)
    share = pltpu.VMEM((share_rows, block_rows), jnp.bfloat16)
    total = pltpu.VMEM(((peers * peer_targets + 1) * STEPS, block_rows), jnp.float32)
    scalars = [SMEM((4, 128), jnp.int32), SMEM((1, 128), jnp.float32)]
    *shares, hist, sums = pl.pallas_call(
        functools.partial(
            far_kernel,
            wide_peers=wide_peers, peers=peers, capacity=capacity, peer_targets=peer_targets,
            fixed=fixed,
        ),
        out_shape=[share] * (peers - 2) + [pltpu.VMEM(hist.shape, jnp.float32), total],
        in_specs=[vmem_spec] * (5 + wide_peers),
        out_specs=[vmem_spec] * peers,
        scratch_shapes=[*scalars, pltpu.SemaphoreType.DMA((2,))],
        compiler_params=params(),
        name="far_tiles",
    )(fracs, tiles, table, heads, weights, hist, *news)
    sent = {r: swap(shares[peers - 1 - r], "narrow", r) for r in range(2, peers)}

    half = peer_targets * STEPS // 2
    pieces = [
        pltpu.VMEM((rows, block_rows), jnp.bfloat16) for rows in (half, share_rows - half)
    ]
    *pair, own = pl.pallas_call(
        functools.partial(near_tiles_kernel, peers=peers, peer_targets=peer_targets, fixed=fixed),
        out_shape=[*pieces, share],
        in_specs=[vmem_spec] * 6,
        out_specs=[vmem_spec] * 3,
        scratch_shapes=[*scalars, VMEM(total.shape, jnp.float32), pltpu.SemaphoreType.DMA((2,))],
        compiler_params=params(),
        name="near_tiles",
    )(fracs, tiles, heads, weights, hist, sums)
    arrived = [sent[r] for r in range(2, peers)] + [swap(x, "narrow", 1) for x in pair] + [own]

    new_coefs, final_state = pl.pallas_call(
        functools.partial(
            window_kernel,
            peers=peers, own_blocks=own_blocks, peer_targets=peer_targets, coef_count=coef_count,
        ),
        out_shape=[
            jax.ShapeDtypeStruct(fresh_coefs.shape, jnp.bfloat16),
            jax.ShapeDtypeStruct(state.shape, jnp.float32),
        ],
        in_specs=[vmem_spec] * (peers + 3),
        out_specs=[hbm_spec] * 2,
        scratch_shapes=[
            VMEM((own_blocks * PITCH, block_rows), jnp.float32),
            VMEM((2, own_blocks, block_rows), jnp.float32),
            VMEM(fresh_coefs.shape, jnp.bfloat16),
            VMEM(state.shape, jnp.float32),
            pltpu.SemaphoreType.DMA((1 + own_blocks // GROUP // 2,)),
        ],
        compiler_params=params(),
        name="window_steps",
    )(*arrived, ready, jnp.asarray(fit_table(coef_count)))
    return new_coefs, final_state


def solution(mesh):
    in_specs = (
        P(("sweep", "wide", "narrow"), None, None),
        P(("sweep", "wide"), "narrow", None, None, None, None),
        P(None, ("sweep", "wide", "narrow")),
        P(("sweep", "wide", "narrow")),
        P("sweep"),
        P("sweep"),
        P("wide", "narrow", None, None),
        P("wide", "narrow", None),
        P("wide", "narrow", None),
        P("wide", "narrow", None),
        P("wide", "narrow", None),
        P("wide", "narrow", None, None, None),
    )
    out_specs = (P(("sweep", "wide", "narrow"), None, None), P(None, ("sweep", "wide", "narrow")))
    return jax.shard_map(local, mesh=mesh, in_specs=in_specs, out_specs=out_specs, check_vma=False)
```

```python
import functools
import math

import jax
import jax.numpy as jnp
import ml_dtypes
import numpy as np
from jax import lax
from jax.experimental import pallas as pl
from jax.experimental.pallas import tpu as pltpu
from jax.sharding import PartitionSpec as P

STEPS = 32
HSEG = 2
SEGS = HSEG + 1
LENGTH = SEGS * STEPS
GROUP = 4
HEAD = 16
PITCH = STEPS + 1
CHUNKS = 8
UNROLL = 4

excite_rate = 0.1
inhibit_rate = 0.05
excite_excite = 1.5
inhibit_excite = 2.0
excite_inhibit = 2.0
inhibit_inhibit = 0.5
excite_offset = 0.5
inhibit_offset = 0.5
tract_gain = 2.0

SMEM = pltpu.SMEM
VMEM = pltpu.VMEM
vmem_spec = pl.BlockSpec(memory_space=VMEM)
hbm_spec = pl.BlockSpec(memory_space=pltpu.HBM)


def basis_table(coef_count, step_count):
    order = np.arange(coef_count, dtype=np.float32)[:, None]
    places = np.arange(step_count, dtype=np.float32)[None, :]
    angles = np.float32(np.pi) * (step_count - places - np.float32(0.5)) / np.float32(step_count)
    return np.cos((order * angles).astype(np.float64)).astype(np.float32)


def expand_table(coef_count):
    basis = basis_table(coef_count, STEPS).astype(ml_dtypes.bfloat16)
    table = np.zeros((LENGTH, SEGS * coef_count), ml_dtypes.bfloat16)
    for seg in range(SEGS):
        table[seg * STEPS : (seg + 1) * STEPS, seg * coef_count : (seg + 1) * coef_count] = basis.T
    return table


def fit_table(coef_count):
    scales = np.where(np.arange(coef_count)[:, None] == 0, 1.0, 2.0) / STEPS
    fit = (basis_table(coef_count, STEPS) * scales).astype(np.float32)
    whole = np.zeros((GROUP * coef_count, GROUP * STEPS), np.float32)
    for g in range(GROUP):
        whole[g * coef_count : (g + 1) * coef_count, g * STEPS : (g + 1) * STEPS] = fit
    high = whole.astype(ml_dtypes.bfloat16)
    low = (whole - high.astype(np.float32)).astype(ml_dtypes.bfloat16)
    return np.concatenate([high, high, low], axis=1)


TOGETHER = 8


def lane_tables(peers, peer_targets, own_blocks):
    width = TOGETHER * peer_targets
    assert TOGETHER * own_blocks <= 256 and peers * width <= HEAD * 128
    lane = np.arange(HEAD * 128)
    used = lane < peers * width
    within = lane % width
    rank = np.where(used, within // TOGETHER, -5)
    offset = within % TOGETHER * own_blocks + 1
    place = np.where(used, lane // width, -5)
    return np.stack([rank, offset, place]).astype(np.float32).reshape(3, HEAD, 128)


def prepare_kernel(
    fresh_ref, reads_hbm, state_hbm, lesion_hbm, stim_hbm, wave_hbm, slot_hbm, target_hbm,
    delay_hbm, lanes_hbm, table_hbm, older_hbm, frac_hbm,
    ready_out, hist_out, tiles_out, fracs_out, head_out, table,
    reads, state, lesion, stim, wave, slot, target, delay, frac, lanes, older, sems,
    *, peers, own_blocks, peer_targets, capacity,
):
    pairs = [
        (reads_hbm, reads), (target_hbm, target), (slot_hbm, slot),
        (delay_hbm, delay), (lanes_hbm, lanes), (table_hbm, table), (older_hbm, older),
        (state_hbm, state), (lesion_hbm, lesion), (stim_hbm, stim), (wave_hbm, wave),
        (frac_hbm, frac),
    ]
    copies = [
        pltpu.make_async_copy(source, into, sems.at[i]) for i, (source, into) in enumerate(pairs)
    ]
    for copy in copies:
        copy.start()
    for copy in (*copies[1:5], copies[11]):
        copy.wait()
    place = lax.axis_index("narrow")
    owner = lax.axis_index("wide")
    tile_count = target.shape[1]
    target_count = peers * own_blocks

    numbers = lax.broadcasted_iota(jnp.int32, (target_count, tile_count), 0)
    hits = jnp.where(numbers == target[...], 1.0, 0.0)
    held = jnp.dot(
        hits.astype(jnp.bfloat16), jnp.ones((tile_count, 128), jnp.bfloat16),
        preferred_element_type=jnp.float32,
    )
    held = jnp.minimum(held, 1.0)
    shape = (own_blocks, own_blocks)
    below = jnp.where(
        lax.broadcasted_iota(jnp.int32, shape, 0) > lax.broadcasted_iota(jnp.int32, shape, 1),
        1.0, 0.0,
    ).astype(jnp.bfloat16)
    block = lax.broadcasted_iota(jnp.int32, (own_blocks, 128), 0).astype(jnp.float32)
    ranks = jnp.zeros((1, tile_count), jnp.float32)
    head_rows = pl.cdiv(peers * TOGETHER * peer_targets, 128)
    for p in range(peers):
        part = slice(p * own_blocks, (p + 1) * own_blocks)
        rank = jnp.dot(below, held[part].astype(jnp.bfloat16), preferred_element_type=jnp.float32)
        ranks = ranks + jnp.sum(hits[part] * rank[:, :tile_count], axis=0, keepdims=True)
        rank = jnp.where(held[part] > 0.5, rank, -1.0)
        source = ((peers - 1) - (place ^ p)).astype(jnp.float32)
        rows = []
        for h in range(head_rows):
            match = rank == lanes[0, h : h + 1, :]
            ids = jnp.sum(jnp.where(match, block, 0.0), axis=0, keepdims=True)
            mine = lanes[2, h : h + 1, :] == source
            rows.append(jnp.where(mine, ids + lanes[1, h : h + 1, :], 0.0))
        rows.append(jnp.zeros((HEAD - head_rows, 128), jnp.float32))
        head_out[p] = jnp.concatenate(rows, axis=0).astype(jnp.bfloat16)

    across = jnp.zeros((1, tile_count), jnp.int32)
    for p in range(1, peers):
        across = across + jnp.where(target[...] >= p * own_blocks, 1, 0)
    key_row = ((peers - 1) - (across ^ place)).astype(jnp.float32)
    shape = (tile_count, tile_count)
    down = lax.broadcasted_iota(jnp.int32, shape, 0)
    along = lax.broadcasted_iota(jnp.int32, shape, 1)
    key = jnp.sum(jnp.where(down == along, key_row, 0.0), axis=1, keepdims=True)
    ahead = (key_row < key) | ((key_row == key) & (along < down))
    position = jnp.sum(jnp.where(ahead, 1.0, 0.0), axis=1, keepdims=True)
    lane = lax.broadcasted_iota(jnp.int32, (tile_count, 128), 1).astype(jnp.float32)
    chosen = jnp.where(position == lane, 1.0, 0.0)
    starts = (slot[...] * LENGTH + (LENGTH - 1) - delay[...]).astype(jnp.float32)
    index = lax.broadcasted_iota(jnp.int32, (1, tile_count), 1).astype(jnp.float32)
    firsts = (key_row * float(peer_targets) + ranks) * float(TOGETHER)
    facts = jnp.concatenate(
        [index, starts, firsts, frac[...], jnp.zeros((4, tile_count), jnp.float32)], axis=0
    )
    ordered = jnp.dot(
        facts, chosen, precision=lax.Precision.HIGHEST, preferred_element_type=jnp.float32
    )
    fracs_out[...] = ordered[3:4, :]
    tiles_out[0:3, :] = (ordered[0:3, :] + 0.5).astype(jnp.int32)
    tiles_out[3:4, :] = jnp.sum(
        jnp.where(key < lane, 1.0, 0.0), axis=0, keepdims=True
    ).astype(jnp.int32)

    for copy in copies[5:7]:
        copy.wait()
    coef_count = older.shape[2]
    earlier = HSEG * STEPS
    for s in range(older.shape[0]):
        segments = [older[s, h] for h in range(HSEG - 1, -1, -1)]
        hist_out[s * LENGTH : s * LENGTH + earlier, :] = jnp.dot(
            table[:earlier, : HSEG * coef_count], jnp.concatenate(segments, axis=0),
            preferred_element_type=jnp.float32,
        )
        hist_out[s * LENGTH + earlier : (s + 1) * LENGTH, :] = jnp.zeros(
            (STEPS, hist_out.shape[1]), jnp.float32
        )
    copies[0].wait()
    for c in range(capacity):
        rows = pl.ds(pl.multiple_of((owner * capacity + c) * LENGTH + earlier, 8), STEPS)
        hist_out[rows, :] = jnp.dot(
            table[:STEPS, :coef_count], fresh_ref[jnp.maximum(reads[c, owner], 0)],
            preferred_element_type=jnp.float32,
        )

    for copy in copies[7:11]:
        copy.wait()
    block_rows = lesion.shape[1]
    for b in range(own_blocks):
        piece = state[:, b * block_rows : (b + 1) * block_rows]
        ready_out[b : b + 1, :] = piece[0:1, :]
        ready_out[own_blocks + b : own_blocks + b + 1, :] = piece[1:2, :]
    ready_out[2 * own_blocks : 3 * own_blocks, :] = tract_gain * (
        1.0 - lesion[...].astype(jnp.float32)
    )
    stim_count = stim.shape[1]
    nodes = stim[...] - (owner * peers + place) * (own_blocks * block_rows)
    blocks = lax.shift_right_arithmetic(nodes, block_rows.bit_length() - 1)
    offsets = nodes & (block_rows - 1)
    in_block = lax.broadcasted_iota(jnp.int32, (own_blocks, stim_count), 0) == blocks
    at_offset = lax.broadcasted_iota(jnp.int32, (block_rows, stim_count), 0) == offsets
    ready_out[3 * own_blocks : 4 * own_blocks, :] = lax.dot_general(
        jnp.where(in_block, 1.0, 0.0).astype(jnp.bfloat16),
        jnp.where(at_offset, 1.0, 0.0).astype(jnp.bfloat16),
        (((1,), (1,)), ((), ())),
        preferred_element_type=jnp.float32,
    )
    shape = (STEPS, STEPS)
    diagonal = lax.broadcasted_iota(jnp.int32, shape, 0) == lax.broadcasted_iota(jnp.int32, shape, 1)
    column = jnp.sum(jnp.where(diagonal, wave[...], 0.0), axis=1, keepdims=True)
    ready_out[4 * own_blocks :, :] = jnp.broadcast_to(column, (STEPS, block_rows))


def near_kernel(fresh_hbm, weights_hbm, fresh_out, weights_out, sems):
    copies = [pltpu.make_async_copy(fresh_hbm, fresh_out, sems.at[CHUNKS])]
    part = weights_hbm.shape[0] // CHUNKS
    for i in range(CHUNKS):
        rows = pl.ds(i * part, part)
        copies.append(
            pltpu.make_async_copy(weights_hbm.at[rows], weights_out.at[rows], sems.at[i])
        )
    for copy in copies:
        copy.start()
    for copy in copies:
        copy.wait()


def pick_kernel(*refs, capacity, peers, ways):
    tables = refs[: peers - 1]
    fresh = refs[peers - 1]
    outs = refs[peers : 2 * peers - 1]
    asked, sems = refs[2 * peers - 1 :]
    place = lax.axis_index("wide")
    copies = [pltpu.make_async_copy(tables[r], asked.at[r], sems.at[r]) for r in range(peers - 1)]
    for copy in copies:
        copy.start()
    for i, r in enumerate(ways):
        copies[i].wait()
        for c in range(capacity):
            outs[r - 1][c] = fresh[jnp.maximum(asked[i, c, place], 0)]


def add_tiles(tiles, frac, hist, weights, total, pitch, items):
    block_rows = weights.shape[2]
    rows = []
    for t, _ in items:
        fraction = frac[0, t]
        start = tiles[1, t]
        earlier = hist[pl.ds(start, STEPS), :]
        later = hist[pl.ds(start + 1, STEPS), :]
        rows.append(((1.0 - fraction) * later + fraction * earlier).astype(jnp.bfloat16))
    tile = [weights[tiles[0, t]] for t, _ in items]
    none = jnp.zeros((2 * STEPS, block_rows), jnp.bfloat16)
    product = lax.dot_general(
        jnp.concatenate(
            [
                jnp.concatenate([*rows[:2], none], axis=0),
                jnp.concatenate([none, *rows[2:]], axis=0),
            ],
            axis=1,
        ),
        jnp.concatenate(
            [jnp.concatenate(tile[:2], axis=0), jnp.concatenate(tile[2:], axis=0)], axis=1
        ),
        (((1,), (1,)), ((), ())),
        preferred_element_type=jnp.float32,
    )
    for i, (_, first) in enumerate(items):
        left = i % 2 * block_rows
        for g in range(STEPS // TOGETHER):
            where = pl.ds(pl.multiple_of(first + g * pitch, 8), TOGETHER)
            top = i * STEPS + g * TOGETHER
            total[where, :] += product[top : top + TOGETHER, left : left + block_rows]


def write_share(pieces, total, head, first, span, pitch):
    groups = STEPS // TOGETHER // len(pieces)
    for i, piece in enumerate(pieces):
        for g in range(groups):
            top = (i * groups + g) * pitch + first
            piece[g * span : (g + 1) * span, :] = total[top : top + span, :].astype(jnp.bfloat16)
    pieces[-1][groups * span :, :] = head


def far_kernel(
    fracs_ref, tiles_ref, table_ref, head_ref, weights, hist_ref, *refs,
    wide_peers, peers, capacity, peer_targets, fixed,
):
    news = refs[: wide_peers - 1]
    outs = refs[wide_peers - 1 : wide_peers + peers - 3]
    hist, total, tiles, frac, sems = refs[wide_peers + peers - 3 :]
    place = lax.axis_index("narrow")
    owner = lax.axis_index("wide")
    copies = [
        pltpu.make_async_copy(tiles_ref, tiles, sems.at[0]),
        pltpu.make_async_copy(fracs_ref, frac, sems.at[1]),
    ]
    for copy in copies:
        copy.start()
    total[...] = jnp.zeros_like(total)
    hist[...] = hist_ref[...]
    came = [(i, c) for i in range(len(news)) for c in range(capacity)]
    coef_count = news[0].shape[1]
    for first in range(0, len(came), SEGS):
        some = came[first : first + SEGS]
        values = jnp.dot(
            table_ref[: len(some) * STEPS, : len(some) * coef_count],
            jnp.concatenate([news[i][c] for i, c in some], axis=0),
            preferred_element_type=jnp.float32,
        )
        for place_here, (i, c) in enumerate(some):
            slot = (owner ^ (wide_peers - 1 - i)) * capacity + c
            rows = pl.ds(pl.multiple_of(slot * LENGTH + HSEG * STEPS, 8), STEPS)
            hist[rows, :] = values[place_here * STEPS : (place_here + 1) * STEPS]
    for copy in copies:
        copy.wait()

    span = peer_targets * TOGETHER
    spare = peers * span
    pitch = spare + TOGETHER
    for t in range(0, fixed, UNROLL):
        items = [(u, tiles[2, u]) for u in range(t, t + UNROLL)]
        add_tiles(tiles, frac, hist, weights, total, pitch, items)
    far_count = tiles[3, peers - 2]

    @pl.loop(0, lax.div(jnp.maximum(far_count - fixed, 0) + (UNROLL - 1), UNROLL))
    def _(turn):
        places = [fixed + turn * UNROLL + u for u in range(UNROLL)]
        items = [(t, jnp.where(t < far_count, tiles[2, t], spare)) for t in places]
        add_tiles(tiles, frac, hist, weights, total, pitch, items)

    for part, out in enumerate(outs):
        write_share([out], total, head_ref[place ^ (peers - 1 - part)], part * span, span, pitch)


def near_tiles_kernel(
    fracs_ref, tiles_ref, head_ref, weights, hist, total_ref, *refs,
    peers, peer_targets, fixed,
):
    *pair, own, tiles, frac, total, sems = refs
    place = lax.axis_index("narrow")
    copies = [
        pltpu.make_async_copy(tiles_ref, tiles, sems.at[0]),
        pltpu.make_async_copy(fracs_ref, frac, sems.at[1]),
    ]
    for copy in copies:
        copy.start()
    total[...] = total_ref[...]
    for copy in copies:
        copy.wait()
    span = peer_targets * TOGETHER
    spare = peers * span
    pitch = spare + TOGETHER
    far_count = tiles[3, peers - 2]
    for t in range(fixed, weights.shape[0], UNROLL):
        items = [
            (u, jnp.where(u < far_count, spare, tiles[2, u])) for u in range(t, t + UNROLL)
        ]
        add_tiles(tiles, frac, hist, weights, total, pitch, items)
    write_share(pair, total, head_ref[place ^ 1], (peers - 2) * span, span, pitch)
    write_share([own], total, head_ref[place], (peers - 1) * span, span, pitch)


def share_rows(pieces, group, width):
    groups = STEPS // TOGETHER // len(pieces)
    first = group % groups * width
    return pieces[group // groups][first : first + width, :]


def one_hot(head, rows, columns):
    row = lax.broadcasted_iota(jnp.int32, (rows, 128), 0).astype(jnp.float32) + 1.0
    parts = [
        jnp.where(row == head[h : h + 1, :], 1.0, 0.0).astype(jnp.bfloat16)
        for h in range(pl.cdiv(columns, 128))
    ]
    return jnp.concatenate(parts, axis=1)[:, :columns]


def two_groups(shares, pair, width):
    return jnp.concatenate(
        [
            jnp.concatenate([share_rows(share, g, width) for share in shares], axis=0)
            for g in (pair, pair + 1)
        ],
        axis=1,
    )


def forcing_kernel(*refs, peers, own_blocks, peer_targets):
    shares = {r: (ref,) for r, ref in zip(range(2, peers - 1), refs)}
    shares |= {1: refs[peers - 3 : peers - 1], 0: (refs[peers - 1],)}
    ready_ref, out_ref = refs[peers:]
    block_rows = ready_ref.shape[1]
    width = TOGETHER * peer_targets
    head = sum(share[-1][-HEAD:, :].astype(jnp.float32) for share in shares.values())
    scatter = one_hot(head, TOGETHER * own_blocks, peers * width)
    stack = [shares[r] for r in (peers - 2, *range(peers - 2, -1, -1))]
    gain, counts = [
        0.5 * ready_ref[i * own_blocks : (i + 1) * own_blocks, :] for i in (2, 3)
    ]
    for pair in range(0, STEPS // TOGETHER, 2):
        inflow = jnp.dot(
            scatter, two_groups(stack, pair, width), preferred_element_type=jnp.float32
        )
        for jj in range(2 * TOGETHER):
            j = pair * TOGETHER + jj
            wave = ready_ref[4 * own_blocks + j : 4 * own_blocks + j + 1, :]
            first = jj % TOGETHER * own_blocks
            left = jj // TOGETHER * block_rows
            out_ref[j * own_blocks : (j + 1) * own_blocks, :] = gain * inflow[
                first : first + own_blocks, left : left + block_rows
            ] + (wave * counts - excite_offset / 2)


def window_kernel(
    share_ref, forcing_ref, ready_ref, fit_ref, coefs_hbm, state_hbm,
    samples, rates, coefs, state, sems,
    *, own_blocks, peer_targets, coef_count,
):
    block_rows = ready_ref.shape[1]
    width = TOGETHER * peer_targets
    scatter = one_hot(
        share_ref[-HEAD:, :].astype(jnp.float32), TOGETHER * own_blocks, width
    )

    excite, inhibit, gain = [
        ready_ref[i * own_blocks : (i + 1) * own_blocks, :] for i in range(3)
    ]
    a = excite_excite / 2
    gain = 0.5 * gain
    carried = a * excite
    for pair in range(0, STEPS // TOGETHER, 2):
        inflow = jnp.dot(
            scatter, two_groups([(share_ref,)], pair, width), preferred_element_type=jnp.float32
        )
        for jj in range(2 * TOGETHER):
            j = pair * TOGETHER + jj
            first = jj % TOGETHER * own_blocks
            left = jj // TOGETHER * block_rows
            half_forcing = (
                forcing_ref[j * own_blocks : (j + 1) * own_blocks, :]
                + gain * inflow[first : first + own_blocks, left : left + block_rows]
            )
            inhibit_drive = (inhibit_inhibit / 2) * inhibit + inhibit_offset / 2
            excite_turn = jnp.tanh(carried + (half_forcing - (inhibit_excite / 2) * inhibit))
            inhibit_turn = jnp.tanh((excite_inhibit / 2 / a) * carried - inhibit_drive)
            carried = ((1 - excite_rate) * carried + a * excite_rate / 2) + (
                a * excite_rate / 2
            ) * excite_turn
            inhibit = ((1 - inhibit_rate) * inhibit + inhibit_rate / 2) + (
                inhibit_rate / 2
            ) * inhibit_turn
            samples[pl.ds(j, own_blocks, stride=PITCH), :] = carried * (1 / a)
    rates[0] = carried * (1 / a)
    rates[1] = inhibit
    for b in range(own_blocks):
        where = slice(b * block_rows, (b + 1) * block_rows)
        state[0:1, where] = rates[0, b : b + 1, :]
        state[1:2, where] = rates[1, b : b + 1, :]
    copies = [pltpu.make_async_copy(state, state_hbm, sems.at[0])]
    copies[0].start()

    fit = fit_ref[...]
    for g in range(0, own_blocks // GROUP, 2):
        part = jnp.concatenate(
            [
                jnp.concatenate(
                    [
                        samples[b * PITCH : b * PITCH + STEPS, :]
                        for b in range((g + i) * GROUP, (g + i + 1) * GROUP)
                    ],
                    axis=0,
                )
                for i in range(2)
            ],
            axis=1,
        )
        part_high = part.astype(jnp.bfloat16)
        part_low = (part - part_high.astype(jnp.float32)).astype(jnp.bfloat16)
        fitted = jnp.dot(
            fit, jnp.concatenate([part_high, part_low, part_high], axis=0),
            preferred_element_type=jnp.float32,
        ).astype(jnp.bfloat16)
        for i in range(2):
            coefs[(g + i) * GROUP : (g + i + 1) * GROUP] = fitted[
                :, i * block_rows : (i + 1) * block_rows
            ].reshape(GROUP, coef_count, block_rows)
        where = pl.ds(g * GROUP, 2 * GROUP)
        copies.append(
            pltpu.make_async_copy(coefs.at[where], coefs_hbm.at[where], sems.at[1 + g // 2])
        )
        copies[-1].start()
    for copy in copies:
        copy.wait()


def far(x):
    return pltpu.with_memory_space_constraint(x, pltpu.HBM)


def params():
    return pltpu.CompilerParams(vmem_limit_bytes=20 << 20)


def local(
    fresh_coefs,
    older_coefs,
    state,
    lesion,
    stim_nodes,
    stim_wave,
    read_blocks,
    tract_slot,
    tract_target,
    tract_delay,
    tract_frac,
    tract_weights,
):
    wide_peers = lax.axis_size("wide")
    peers = lax.axis_size("narrow")
    own_blocks, coef_count, block_rows = fresh_coefs.shape
    capacity = read_blocks.shape[3]
    slot_count = wide_peers * capacity
    tile_count = tract_slot.shape[2]
    peer_targets = tile_count // (2 * peers)
    share_rows = peer_targets * STEPS + HEAD

    def swap(x, axis, r):
        return lax.ppermute(x, axis, [(i, i ^ r) for i in range(lax.axis_size(axis))])

    reads = read_blocks.reshape(wide_peers, capacity).T
    ways = [1, *range(wide_peers - 1, 1, -1)]
    asked = [swap(reads, "wide", r) for r in ways]

    vmem_inputs = [
        VMEM(state.shape, jnp.float32),
        VMEM((own_blocks, block_rows), jnp.int32),
        VMEM((1, stim_nodes.shape[0]), jnp.int32),
        VMEM((1, STEPS), jnp.float32),
        VMEM((1, tile_count), jnp.int32),
        VMEM((1, tile_count), jnp.int32),
        VMEM((1, tile_count), jnp.int32),
        VMEM((1, tile_count), jnp.float32),
        VMEM((3, HEAD, 128), jnp.float32),
        VMEM((slot_count, HSEG, coef_count, block_rows), jnp.bfloat16),
    ]
    fresh, weights = pl.pallas_call(
        near_kernel,
        out_shape=[
            pltpu.VMEM(fresh_coefs.shape, jnp.bfloat16),
            pltpu.VMEM((tile_count, block_rows, block_rows), jnp.bfloat16),
        ],
        in_specs=[hbm_spec] * 2,
        out_specs=[vmem_spec] * 2,
        scratch_shapes=[pltpu.SemaphoreType.DMA((CHUNKS + 1,))],
        compiler_params=params(),
        name="near",
    )(far(fresh_coefs), far(tract_weights.reshape(tile_count, block_rows, block_rows)))
    ready, hist, tiles, fracs, heads, table = pl.pallas_call(
        functools.partial(
            prepare_kernel,
            peers=peers, own_blocks=own_blocks, peer_targets=peer_targets, capacity=capacity,
        ),
        out_shape=[
            pltpu.VMEM((4 * own_blocks + STEPS, block_rows), jnp.float32),
            pltpu.VMEM((slot_count * LENGTH, block_rows), jnp.float32),
            pltpu.VMEM((4, 128), jnp.int32),
            pltpu.VMEM((1, 128), jnp.float32),
            pltpu.VMEM((peers, HEAD, 128), jnp.bfloat16),
            pltpu.VMEM((LENGTH, SEGS * coef_count), jnp.bfloat16),
        ],
        in_specs=[vmem_spec] + [hbm_spec] * 12,
        out_specs=[vmem_spec] * 6,
        scratch_shapes=[
            SMEM((capacity, wide_peers), jnp.int32),
            *vmem_inputs,
            pltpu.SemaphoreType.DMA((12,)),
        ],
        compiler_params=params(),
        name="prepare",
    )(
        fresh,
        far(reads),
        far(state),
        far(lesion.reshape(own_blocks, block_rows)),
        far(stim_nodes.reshape(1, -1)),
        far(stim_wave.reshape(1, -1)),
        far(tract_slot.reshape(1, tile_count)),
        far(tract_target.reshape(1, tile_count)),
        far(tract_delay.reshape(1, tile_count)),
        far(jnp.asarray(lane_tables(peers, peer_targets, own_blocks))),
        far(jnp.asarray(expand_table(coef_count))),
        far(older_coefs.reshape(slot_count, HSEG, coef_count, block_rows)),
        far(tract_frac.reshape(1, tile_count)),
    )

    picked = pl.pallas_call(
        functools.partial(pick_kernel, capacity=capacity, peers=wide_peers, ways=ways),
        out_shape=[pltpu.VMEM((capacity, coef_count, block_rows), jnp.bfloat16)]
        * (wide_peers - 1),
        in_specs=[vmem_spec] * wide_peers,
        out_specs=[vmem_spec] * (wide_peers - 1),
        scratch_shapes=[
            SMEM((wide_peers - 1, capacity, wide_peers), jnp.int32),
            pltpu.SemaphoreType.DMA((wide_peers - 1,)),
        ],
        compiler_params=params(),
        name="pick_blocks",
    )(*asked, fresh)
    news = [swap(picked[r - 1], "wide", r) for r in range(wide_peers - 1, 0, -1)]

    fixed = tile_count * (peers - 2) // peers + 2 * UNROLL
    fixed = min(tile_count, -(-fixed // UNROLL) * UNROLL)
    share = pltpu.VMEM((share_rows, block_rows), jnp.bfloat16)
    total = pltpu.VMEM(((peers * peer_targets + 1) * STEPS, block_rows), jnp.float32)
    scalars = [SMEM((4, 128), jnp.int32), SMEM((1, 128), jnp.float32)]
    *shares, hist, sums = pl.pallas_call(
        functools.partial(
            far_kernel,
            wide_peers=wide_peers, peers=peers, capacity=capacity, peer_targets=peer_targets,
            fixed=fixed,
        ),
        out_shape=[share] * (peers - 2) + [pltpu.VMEM(hist.shape, jnp.float32), total],
        in_specs=[vmem_spec] * (5 + wide_peers),
        out_specs=[vmem_spec] * peers,
        scratch_shapes=[*scalars, pltpu.SemaphoreType.DMA((2,))],
        compiler_params=params(),
        name="far_tiles",
    )(fracs, tiles, table, heads, weights, hist, *news)
    sent = {r: swap(shares[peers - 1 - r], "narrow", r) for r in range(2, peers)}

    half = peer_targets * STEPS // 2
    pieces = [
        pltpu.VMEM((rows, block_rows), jnp.bfloat16) for rows in (half, share_rows - half)
    ]
    *pair, own = pl.pallas_call(
        functools.partial(near_tiles_kernel, peers=peers, peer_targets=peer_targets, fixed=fixed),
        out_shape=[*pieces, share],
        in_specs=[vmem_spec] * 6,
        out_specs=[vmem_spec] * 3,
        scratch_shapes=[*scalars, VMEM(total.shape, jnp.float32), pltpu.SemaphoreType.DMA((2,))],
        compiler_params=params(),
        name="near_tiles",
    )(fracs, tiles, heads, weights, hist, sums)
    pair = [swap(x, "narrow", 1) for x in pair]
    forcing = pl.pallas_call(
        functools.partial(
            forcing_kernel, peers=peers, own_blocks=own_blocks, peer_targets=peer_targets
        ),
        out_shape=pltpu.VMEM((STEPS * own_blocks, block_rows), jnp.float32),
        in_specs=[vmem_spec] * (peers + 1),
        out_specs=vmem_spec,
        compiler_params=params(),
        name="forcing",
    )(*[sent[r] for r in range(2, peers - 1)], *pair, own, ready)

    new_coefs, final_state = pl.pallas_call(
        functools.partial(
            window_kernel,
            own_blocks=own_blocks, peer_targets=peer_targets, coef_count=coef_count,
        ),
        out_shape=[
            jax.ShapeDtypeStruct(fresh_coefs.shape, jnp.bfloat16),
            jax.ShapeDtypeStruct(state.shape, jnp.float32),
        ],
        in_specs=[vmem_spec] * 4,
        out_specs=[hbm_spec] * 2,
        scratch_shapes=[
            VMEM((own_blocks * PITCH, block_rows), jnp.float32),
            VMEM((2, own_blocks, block_rows), jnp.float32),
            VMEM(fresh_coefs.shape, jnp.bfloat16),
            VMEM(state.shape, jnp.float32),
            pltpu.SemaphoreType.DMA((1 + own_blocks // GROUP // 2,)),
        ],
        compiler_params=params(),
        name="window_steps",
    )(sent[peers - 1], forcing, ready, jnp.asarray(fit_table(coef_count)))
    return new_coefs, final_state


def solution(mesh):
    in_specs = (
        P(("sweep", "wide", "narrow"), None, None),
        P(("sweep", "wide"), "narrow", None, None, None, None),
        P(None, ("sweep", "wide", "narrow")),
        P(("sweep", "wide", "narrow")),
        P("sweep"),
        P("sweep"),
        P("wide", "narrow", None, None),
        P("wide", "narrow", None),
        P("wide", "narrow", None),
        P("wide", "narrow", None),
        P("wide", "narrow", None),
        P("wide", "narrow", None, None, None),
    )
    out_specs = (P(("sweep", "wide", "narrow"), None, None), P(None, ("sweep", "wide", "narrow")))
    return jax.shard_map(local, mesh=mesh, in_specs=in_specs, out_specs=out_specs, check_vma=False)
```

```python
import functools
import math

import jax
import jax.numpy as jnp
import ml_dtypes
import numpy as np
from jax import lax
from jax.experimental import pallas as pl
from jax.experimental.pallas import tpu as pltpu
from jax.sharding import PartitionSpec as P

STEPS = 32
HSEG = 2
SEGS = HSEG + 1
LENGTH = SEGS * STEPS
GROUP = 4
HEAD = 16
PITCH = STEPS // 2 + 1
CHUNKS = 8
UNROLL = 4

excite_rate = 0.1
inhibit_rate = 0.05
excite_excite = 1.5
inhibit_excite = 2.0
excite_inhibit = 2.0
inhibit_inhibit = 0.5
excite_offset = 0.5
inhibit_offset = 0.5
tract_gain = 2.0

SMEM = pltpu.SMEM
VMEM = pltpu.VMEM
vmem_spec = pl.BlockSpec(memory_space=VMEM)
hbm_spec = pl.BlockSpec(memory_space=pltpu.HBM)


def basis_table(coef_count, step_count):
    order = np.arange(coef_count, dtype=np.float32)[:, None]
    places = np.arange(step_count, dtype=np.float32)[None, :]
    angles = np.float32(np.pi) * (step_count - places - np.float32(0.5)) / np.float32(step_count)
    return np.cos((order * angles).astype(np.float64)).astype(np.float32)


def expand_table(coef_count):
    basis = basis_table(coef_count, STEPS).astype(ml_dtypes.bfloat16)
    table = np.zeros((LENGTH, SEGS * coef_count), ml_dtypes.bfloat16)
    for seg in range(SEGS):
        table[seg * STEPS : (seg + 1) * STEPS, seg * coef_count : (seg + 1) * coef_count] = basis.T
    return table


def fit_table(coef_count):
    scales = np.where(np.arange(coef_count)[:, None] == 0, 1.0, 2.0) / STEPS
    fit = (basis_table(coef_count, STEPS) * scales).astype(np.float32)
    half = STEPS // 2
    tables = []
    for i in range(2):
        whole = np.zeros((GROUP * coef_count, GROUP * half), np.float32)
        for g in range(GROUP):
            whole[g * coef_count : (g + 1) * coef_count, g * half : (g + 1) * half] = fit[
                :, i * half : (i + 1) * half
            ]
        high = whole.astype(ml_dtypes.bfloat16)
        low = (whole - high.astype(np.float32)).astype(ml_dtypes.bfloat16)
        tables.append(np.concatenate([high, high, low], axis=1))
    return np.stack(tables)


TOGETHER = 8


def lane_tables(peers, peer_targets, own_blocks):
    width = TOGETHER * peer_targets
    assert TOGETHER * own_blocks <= 256 and peers * width <= HEAD * 128
    lane = np.arange(HEAD * 128)
    used = lane < peers * width
    within = lane % width
    rank = np.where(used, within // TOGETHER, -5)
    offset = within % TOGETHER * own_blocks + 1
    place = np.where(used, lane // width, -5)
    return np.stack([rank, offset, place]).astype(np.float32).reshape(3, HEAD, 128)


def prepare_kernel(
    fresh_ref, reads_hbm, state_hbm, lesion_hbm, stim_hbm, wave_hbm, slot_hbm, target_hbm,
    delay_hbm, lanes_hbm, table_hbm, older_hbm, frac_hbm,
    ready_out, hist_out, tiles_out, fracs_out, head_out, table,
    reads, state, lesion, stim, wave, slot, target, delay, frac, lanes, older, sems,
    *, peers, own_blocks, peer_targets, capacity,
):
    pairs = [
        (reads_hbm, reads), (target_hbm, target), (slot_hbm, slot),
        (delay_hbm, delay), (lanes_hbm, lanes), (table_hbm, table), (older_hbm, older),
        (state_hbm, state), (lesion_hbm, lesion), (stim_hbm, stim), (wave_hbm, wave),
        (frac_hbm, frac),
    ]
    copies = [
        pltpu.make_async_copy(source, into, sems.at[i]) for i, (source, into) in enumerate(pairs)
    ]
    for copy in copies:
        copy.start()
    for copy in (*copies[1:5], copies[11]):
        copy.wait()
    place = lax.axis_index("narrow")
    owner = lax.axis_index("wide")
    tile_count = target.shape[1]
    target_count = peers * own_blocks

    numbers = lax.broadcasted_iota(jnp.int32, (target_count, tile_count), 0)
    hits = jnp.where(numbers == target[...], 1.0, 0.0)
    held = jnp.dot(
        hits.astype(jnp.bfloat16), jnp.ones((tile_count, 128), jnp.bfloat16),
        preferred_element_type=jnp.float32,
    )
    held = jnp.minimum(held, 1.0)
    shape = (own_blocks, own_blocks)
    below = jnp.where(
        lax.broadcasted_iota(jnp.int32, shape, 0) > lax.broadcasted_iota(jnp.int32, shape, 1),
        1.0, 0.0,
    ).astype(jnp.bfloat16)
    block = lax.broadcasted_iota(jnp.int32, (own_blocks, 128), 0).astype(jnp.float32)
    ranks = jnp.zeros((1, tile_count), jnp.float32)
    head_rows = pl.cdiv(peers * TOGETHER * peer_targets, 128)
    for p in range(peers):
        part = slice(p * own_blocks, (p + 1) * own_blocks)
        rank = jnp.dot(below, held[part].astype(jnp.bfloat16), preferred_element_type=jnp.float32)
        ranks = ranks + jnp.sum(hits[part] * rank[:, :tile_count], axis=0, keepdims=True)
        rank = jnp.where(held[part] > 0.5, rank, -1.0)
        source = ((peers - 1) - (place ^ p)).astype(jnp.float32)
        rows = []
        for h in range(head_rows):
            match = rank == lanes[0, h : h + 1, :]
            ids = jnp.sum(jnp.where(match, block, 0.0), axis=0, keepdims=True)
            mine = lanes[2, h : h + 1, :] == source
            rows.append(jnp.where(mine, ids + lanes[1, h : h + 1, :], 0.0))
        rows.append(jnp.zeros((HEAD - head_rows, 128), jnp.float32))
        head_out[p] = jnp.concatenate(rows, axis=0).astype(jnp.bfloat16)

    across = jnp.zeros((1, tile_count), jnp.int32)
    for p in range(1, peers):
        across = across + jnp.where(target[...] >= p * own_blocks, 1, 0)
    key_row = ((peers - 1) - (across ^ place)).astype(jnp.float32)
    shape = (tile_count, tile_count)
    down = lax.broadcasted_iota(jnp.int32, shape, 0)
    along = lax.broadcasted_iota(jnp.int32, shape, 1)
    key = jnp.sum(jnp.where(down == along, key_row, 0.0), axis=1, keepdims=True)
    ahead = (key_row < key) | ((key_row == key) & (along < down))
    position = jnp.sum(jnp.where(ahead, 1.0, 0.0), axis=1, keepdims=True)
    lane = lax.broadcasted_iota(jnp.int32, (tile_count, 128), 1).astype(jnp.float32)
    chosen = jnp.where(position == lane, 1.0, 0.0)
    starts = (slot[...] * LENGTH + (LENGTH - 1) - delay[...]).astype(jnp.float32)
    index = lax.broadcasted_iota(jnp.int32, (1, tile_count), 1).astype(jnp.float32)
    firsts = (key_row * float(peer_targets) + ranks) * float(TOGETHER)
    facts = jnp.concatenate(
        [index, starts, firsts, frac[...], jnp.zeros((4, tile_count), jnp.float32)], axis=0
    )
    ordered = jnp.dot(
        facts, chosen, precision=lax.Precision.HIGHEST, preferred_element_type=jnp.float32
    )
    fracs_out[...] = ordered[3:4, :]
    tiles_out[0:3, :] = (ordered[0:3, :] + 0.5).astype(jnp.int32)
    tiles_out[3:4, :] = jnp.sum(
        jnp.where(key < lane, 1.0, 0.0), axis=0, keepdims=True
    ).astype(jnp.int32)

    for copy in copies[5:7]:
        copy.wait()
    coef_count = older.shape[2]
    earlier = HSEG * STEPS
    for s in range(older.shape[0]):
        segments = [older[s, h] for h in range(HSEG - 1, -1, -1)]
        hist_out[s * LENGTH : s * LENGTH + earlier, :] = jnp.dot(
            table[:earlier, : HSEG * coef_count], jnp.concatenate(segments, axis=0),
            preferred_element_type=jnp.float32,
        )
        hist_out[s * LENGTH + earlier : (s + 1) * LENGTH, :] = jnp.zeros(
            (STEPS, hist_out.shape[1]), jnp.float32
        )
    copies[0].wait()
    for c in range(capacity):
        rows = pl.ds(pl.multiple_of((owner * capacity + c) * LENGTH + earlier, 8), STEPS)
        hist_out[rows, :] = jnp.dot(
            table[:STEPS, :coef_count], fresh_ref[jnp.maximum(reads[c, owner], 0)],
            preferred_element_type=jnp.float32,
        )

    for copy in copies[7:11]:
        copy.wait()
    block_rows = lesion.shape[1]
    for b in range(own_blocks):
        piece = state[:, b * block_rows : (b + 1) * block_rows]
        ready_out[b : b + 1, :] = piece[0:1, :]
        ready_out[own_blocks + b : own_blocks + b + 1, :] = piece[1:2, :]
    ready_out[2 * own_blocks : 3 * own_blocks, :] = tract_gain * (
        1.0 - lesion[...].astype(jnp.float32)
    )
    stim_count = stim.shape[1]
    nodes = stim[...] - (owner * peers + place) * (own_blocks * block_rows)
    blocks = lax.shift_right_arithmetic(nodes, block_rows.bit_length() - 1)
    offsets = nodes & (block_rows - 1)
    in_block = lax.broadcasted_iota(jnp.int32, (own_blocks, stim_count), 0) == blocks
    at_offset = lax.broadcasted_iota(jnp.int32, (block_rows, stim_count), 0) == offsets
    ready_out[3 * own_blocks : 4 * own_blocks, :] = lax.dot_general(
        jnp.where(in_block, 1.0, 0.0).astype(jnp.bfloat16),
        jnp.where(at_offset, 1.0, 0.0).astype(jnp.bfloat16),
        (((1,), (1,)), ((), ())),
        preferred_element_type=jnp.float32,
    )
    shape = (STEPS, STEPS)
    diagonal = lax.broadcasted_iota(jnp.int32, shape, 0) == lax.broadcasted_iota(jnp.int32, shape, 1)
    column = jnp.sum(jnp.where(diagonal, wave[...], 0.0), axis=1, keepdims=True)
    ready_out[4 * own_blocks :, :] = jnp.broadcast_to(column, (STEPS, block_rows))


def near_kernel(fresh_hbm, weights_hbm, fresh_out, weights_out, sems):
    copies = [pltpu.make_async_copy(fresh_hbm, fresh_out, sems.at[CHUNKS])]
    part = weights_hbm.shape[0] // CHUNKS
    for i in range(CHUNKS):
        rows = pl.ds(i * part, part)
        copies.append(
            pltpu.make_async_copy(weights_hbm.at[rows], weights_out.at[rows], sems.at[i])
        )
    for copy in copies:
        copy.start()
    for copy in copies:
        copy.wait()


def pick_kernel(*refs, capacity, peers):
    tables = refs[: peers - 1][::-1]
    fresh = refs[peers - 1]
    outs = refs[peers : 2 * peers - 1]
    asked, sems = refs[2 * peers - 1 :]
    place = lax.axis_index("wide")
    copies = [pltpu.make_async_copy(tables[r], asked.at[r], sems.at[r]) for r in range(peers - 1)]
    for copy in copies:
        copy.start()

    def ring_place(i):
        return jnp.where(i % 2 == 1, (i + 1) // 2, (peers - i // 2) % peers)

    for copy in copies:
        copy.wait()
    for distance in range(1, peers):
        way = (ring_place(place) - ring_place(place ^ distance) + peers) % peers
        for c in range(capacity):
            block = jnp.maximum(asked[way - 1, c, place], 0)
            outs[distance - 1][c] = fresh[block]


def add_tiles(tiles, frac, hist, weights, total, pitch, items):
    block_rows = weights.shape[2]
    rows = []
    for t, _ in items:
        fraction = frac[0, t]
        start = tiles[1, t]
        earlier = hist[pl.ds(start, STEPS), :]
        later = hist[pl.ds(start + 1, STEPS), :]
        rows.append(((1.0 - fraction) * later + fraction * earlier).astype(jnp.bfloat16))
    tile = [weights[tiles[0, t]] for t, _ in items]
    none = jnp.zeros((2 * STEPS, block_rows), jnp.bfloat16)
    product = lax.dot_general(
        jnp.concatenate(
            [
                jnp.concatenate([*rows[:2], none], axis=0),
                jnp.concatenate([none, *rows[2:]], axis=0),
            ],
            axis=1,
        ),
        jnp.concatenate(
            [jnp.concatenate(tile[:2], axis=0), jnp.concatenate(tile[2:], axis=0)], axis=1
        ),
        (((1,), (1,)), ((), ())),
        preferred_element_type=jnp.float32,
    )
    for i, (_, first) in enumerate(items):
        left = i % 2 * block_rows
        for g in range(STEPS // TOGETHER):
            where = pl.ds(pl.multiple_of(first + g * pitch, 8), TOGETHER)
            top = i * STEPS + g * TOGETHER
            total[where, :] += product[top : top + TOGETHER, left : left + block_rows]


def write_share(pieces, total, head, first, span, pitch):
    groups = STEPS // TOGETHER // len(pieces)
    for i, piece in enumerate(pieces):
        for g in range(groups):
            top = (i * groups + g) * pitch + first
            piece[g * span : (g + 1) * span, :] = total[top : top + span, :].astype(jnp.bfloat16)
    pieces[-1][groups * span :, :] = head


def far_kernel(
    fracs_ref, tiles_ref, table_ref, head_ref, weights, hist_ref, *refs,
    wide_peers, peers, capacity, peer_targets, fixed,
):
    news = refs[: wide_peers - 1]
    outs = refs[wide_peers - 1 : wide_peers + peers - 3]
    hist, total, tiles, frac, sems = refs[wide_peers + peers - 3 :]
    place = lax.axis_index("narrow")
    owner = lax.axis_index("wide")
    copies = [
        pltpu.make_async_copy(tiles_ref, tiles, sems.at[0]),
        pltpu.make_async_copy(fracs_ref, frac, sems.at[1]),
    ]
    for copy in copies:
        copy.start()
    total[...] = jnp.zeros_like(total)
    hist[...] = hist_ref[...]
    came = [(i, c) for i in range(len(news)) for c in range(capacity)]
    coef_count = news[0].shape[1]
    for first in range(0, len(came), SEGS):
        some = came[first : first + SEGS]
        values = jnp.dot(
            table_ref[: len(some) * STEPS, : len(some) * coef_count],
            jnp.concatenate([news[i][c] for i, c in some], axis=0),
            preferred_element_type=jnp.float32,
        )
        for place_here, (i, c) in enumerate(some):
            slot = (owner ^ (wide_peers - 1 - i)) * capacity + c
            rows = pl.ds(pl.multiple_of(slot * LENGTH + HSEG * STEPS, 8), STEPS)
            hist[rows, :] = values[place_here * STEPS : (place_here + 1) * STEPS]
    for copy in copies:
        copy.wait()

    span = peer_targets * TOGETHER
    spare = peers * span
    pitch = spare + TOGETHER
    for t in range(0, fixed, UNROLL):
        items = [(u, tiles[2, u]) for u in range(t, t + UNROLL)]
        add_tiles(tiles, frac, hist, weights, total, pitch, items)
    far_count = tiles[3, peers - 2]

    @pl.loop(0, lax.div(jnp.maximum(far_count - fixed, 0) + (UNROLL - 1), UNROLL))
    def _(turn):
        places = [fixed + turn * UNROLL + u for u in range(UNROLL)]
        items = [(t, jnp.where(t < far_count, tiles[2, t], spare)) for t in places]
        add_tiles(tiles, frac, hist, weights, total, pitch, items)

    for part, out in enumerate(outs):
        write_share([out], total, head_ref[place ^ (peers - 1 - part)], part * span, span, pitch)


def near_tiles_kernel(
    fracs_ref, tiles_ref, head_ref, weights, hist, total_ref, *refs,
    peers, peer_targets, fixed,
):
    *pair, own, tiles, frac, total, sems = refs
    place = lax.axis_index("narrow")
    copies = [
        pltpu.make_async_copy(tiles_ref, tiles, sems.at[0]),
        pltpu.make_async_copy(fracs_ref, frac, sems.at[1]),
    ]
    for copy in copies:
        copy.start()
    total[...] = total_ref[...]
    for copy in copies:
        copy.wait()
    span = peer_targets * TOGETHER
    spare = peers * span
    pitch = spare + TOGETHER
    far_count = tiles[3, peers - 2]
    for t in range(fixed, weights.shape[0], UNROLL):
        items = [
            (u, jnp.where(u < far_count, spare, tiles[2, u])) for u in range(t, t + UNROLL)
        ]
        add_tiles(tiles, frac, hist, weights, total, pitch, items)
    write_share(pair, total, head_ref[place ^ 1], (peers - 2) * span, span, pitch)
    write_share([own], total, head_ref[place], (peers - 1) * span, span, pitch)


def share_rows(pieces, group, width):
    groups = STEPS // TOGETHER // len(pieces)
    first = group % groups * width
    return pieces[group // groups][first : first + width, :]


def one_hot(head, rows, columns):
    row = lax.broadcasted_iota(jnp.int32, (rows, 128), 0).astype(jnp.float32) + 1.0
    parts = [
        jnp.where(row == head[h : h + 1, :], 1.0, 0.0).astype(jnp.bfloat16)
        for h in range(pl.cdiv(columns, 128))
    ]
    return jnp.concatenate(parts, axis=1)[:, :columns]


def two_groups(shares, pair, width):
    return jnp.concatenate(
        [
            jnp.concatenate([share_rows(share, g, width) for share in shares], axis=0)
            for g in (pair, pair + 1)
        ],
        axis=1,
    )


def forcing_kernel(*refs, peers, own_blocks, peer_targets):
    shares = {r: (ref,) for r, ref in zip(range(2, peers - 1), refs)}
    shares |= {1: refs[peers - 3 : peers - 1], 0: (refs[peers - 1],)}
    ready_ref, out_ref = refs[peers:]
    block_rows = ready_ref.shape[1]
    width = TOGETHER * peer_targets
    head = sum(share[-1][-HEAD:, :].astype(jnp.float32) for share in shares.values())
    scatter = one_hot(head, TOGETHER * own_blocks, peers * width)
    stack = [shares[r] for r in (peers - 2, *range(peers - 2, -1, -1))]
    gain, counts = [
        0.5 * ready_ref[i * own_blocks : (i + 1) * own_blocks, :] for i in (2, 3)
    ]
    for pair in range(0, STEPS // TOGETHER, 2):
        inflow = jnp.dot(
            scatter, two_groups(stack, pair, width), preferred_element_type=jnp.float32
        )
        for jj in range(2 * TOGETHER):
            j = pair * TOGETHER + jj
            wave = ready_ref[4 * own_blocks + j : 4 * own_blocks + j + 1, :]
            first = jj % TOGETHER * own_blocks
            left = jj // TOGETHER * block_rows
            out_ref[j * own_blocks : (j + 1) * own_blocks, :] = gain * inflow[
                first : first + own_blocks, left : left + block_rows
            ] + (wave * counts - excite_offset / 2)


def window_kernel(
    share_ref, forcing_ref, ready_ref, fit_ref, coefs_hbm, state_hbm,
    early, late, rates, coefs, state, sems,
    *, own_blocks, peer_targets, coef_count,
):
    samples = (early, late)
    block_rows = ready_ref.shape[1]
    width = TOGETHER * peer_targets
    scatter = one_hot(
        share_ref[-HEAD:, :].astype(jnp.float32), TOGETHER * own_blocks, width
    )

    excite, inhibit, gain = [
        ready_ref[i * own_blocks : (i + 1) * own_blocks, :] for i in range(3)
    ]
    a = excite_excite / 2
    gain = 0.5 * gain
    carried = a * excite

    def fit_half(values, fit):
        products = []
        for g in range(0, own_blocks // GROUP, 2):
            part = jnp.concatenate(
                [
                    jnp.concatenate(
                        [
                            values[b * PITCH : b * PITCH + STEPS // 2, :]
                            for b in range((g + i) * GROUP, (g + i + 1) * GROUP)
                        ],
                        axis=0,
                    )
                    for i in range(2)
                ],
                axis=1,
            )
            high = part.astype(jnp.bfloat16)
            low = (part - high.astype(jnp.float32)).astype(jnp.bfloat16)
            products.append(
                jnp.dot(
                    fit, jnp.concatenate([high, low, high], axis=0),
                    preferred_element_type=jnp.float32,
                )
            )
        return products

    fitted = [None, None]
    for pair in range(0, STEPS // TOGETHER, 2):
        inflow = jnp.dot(
            scatter, two_groups([(share_ref,)], pair, width), preferred_element_type=jnp.float32
        )
        for jj in range(2 * TOGETHER):
            j = pair * TOGETHER + jj
            first = jj % TOGETHER * own_blocks
            left = jj // TOGETHER * block_rows
            half_forcing = (
                forcing_ref[j * own_blocks : (j + 1) * own_blocks, :]
                + gain * inflow[first : first + own_blocks, left : left + block_rows]
            )
            inhibit_drive = (inhibit_inhibit / 2) * inhibit + inhibit_offset / 2
            excite_turn = jnp.tanh(carried + (half_forcing - (inhibit_excite / 2) * inhibit))
            inhibit_turn = jnp.tanh((excite_inhibit / 2 / a) * carried - inhibit_drive)
            carried = ((1 - excite_rate) * carried + a * excite_rate / 2) + (
                a * excite_rate / 2
            ) * excite_turn
            inhibit = ((1 - inhibit_rate) * inhibit + inhibit_rate / 2) + (
                inhibit_rate / 2
            ) * inhibit_turn
            samples[pair // 2][pl.ds(jj, own_blocks, stride=PITCH), :] = carried * (1 / a)
        fitted[pair // 2] = fit_half(samples[pair // 2], fit_ref[pair // 2])
    rates[0] = carried * (1 / a)
    rates[1] = inhibit
    for b in range(own_blocks):
        where = slice(b * block_rows, (b + 1) * block_rows)
        state[0:1, where] = rates[0, b : b + 1, :]
        state[1:2, where] = rates[1, b : b + 1, :]
    copies = [pltpu.make_async_copy(state, state_hbm, sems.at[0])]
    copies[0].start()

    for g in range(0, own_blocks // GROUP, 2):
        both = (fitted[0][g // 2] + fitted[1][g // 2]).astype(jnp.bfloat16)
        for i in range(2):
            coefs[(g + i) * GROUP : (g + i + 1) * GROUP] = both[
                :, i * block_rows : (i + 1) * block_rows
            ].reshape(GROUP, coef_count, block_rows)
        where = pl.ds(g * GROUP, 2 * GROUP)
        copies.append(
            pltpu.make_async_copy(coefs.at[where], coefs_hbm.at[where], sems.at[1 + g // 2])
        )
        copies[-1].start()
    for copy in copies:
        copy.wait()


def far(x):
    return pltpu.with_memory_space_constraint(x, pltpu.HBM)


def params():
    return pltpu.CompilerParams(vmem_limit_bytes=20 << 20)


def local(
    fresh_coefs,
    older_coefs,
    state,
    lesion,
    stim_nodes,
    stim_wave,
    read_blocks,
    tract_slot,
    tract_target,
    tract_delay,
    tract_frac,
    tract_weights,
):
    wide_peers = lax.axis_size("wide")
    peers = lax.axis_size("narrow")
    own_blocks, coef_count, block_rows = fresh_coefs.shape
    capacity = read_blocks.shape[3]
    slot_count = wide_peers * capacity
    tile_count = tract_slot.shape[2]
    peer_targets = tile_count // (2 * peers)
    share_rows = peer_targets * STEPS + HEAD

    def swap(x, axis, r):
        return lax.ppermute(x, axis, [(i, i ^ r) for i in range(lax.axis_size(axis))])

    reads = read_blocks.reshape(wide_peers, capacity).T
    ring = [0, *range(1, wide_peers, 2), *reversed(range(2, wide_peers, 2))]
    asked = [
        lax.ppermute(
            reads, "wide", [(ring[k], ring[(k + r) % wide_peers]) for k in range(wide_peers)]
        )
        for r in range(1, wide_peers)
    ]

    vmem_inputs = [
        VMEM(state.shape, jnp.float32),
        VMEM((own_blocks, block_rows), jnp.int32),
        VMEM((1, stim_nodes.shape[0]), jnp.int32),
        VMEM((1, STEPS), jnp.float32),
        VMEM((1, tile_count), jnp.int32),
        VMEM((1, tile_count), jnp.int32),
        VMEM((1, tile_count), jnp.int32),
        VMEM((1, tile_count), jnp.float32),
        VMEM((3, HEAD, 128), jnp.float32),
        VMEM((slot_count, HSEG, coef_count, block_rows), jnp.bfloat16),
    ]
    fresh, weights = pl.pallas_call(
        near_kernel,
        out_shape=[
            pltpu.VMEM(fresh_coefs.shape, jnp.bfloat16),
            pltpu.VMEM((tile_count, block_rows, block_rows), jnp.bfloat16),
        ],
        in_specs=[hbm_spec] * 2,
        out_specs=[vmem_spec] * 2,
        scratch_shapes=[pltpu.SemaphoreType.DMA((CHUNKS + 1,))],
        compiler_params=params(),
        name="near",
    )(far(fresh_coefs), far(tract_weights.reshape(tile_count, block_rows, block_rows)))
    ready, hist, tiles, fracs, heads, table = pl.pallas_call(
        functools.partial(
            prepare_kernel,
            peers=peers, own_blocks=own_blocks, peer_targets=peer_targets, capacity=capacity,
        ),
        out_shape=[
            pltpu.VMEM((4 * own_blocks + STEPS, block_rows), jnp.float32),
            pltpu.VMEM((slot_count * LENGTH, block_rows), jnp.float32),
            pltpu.VMEM((4, 128), jnp.int32),
            pltpu.VMEM((1, 128), jnp.float32),
            pltpu.VMEM((peers, HEAD, 128), jnp.bfloat16),
            pltpu.VMEM((LENGTH, SEGS * coef_count), jnp.bfloat16),
        ],
        in_specs=[vmem_spec] + [hbm_spec] * 12,
        out_specs=[vmem_spec] * 6,
        scratch_shapes=[
            SMEM((capacity, wide_peers), jnp.int32),
            *vmem_inputs,
            pltpu.SemaphoreType.DMA((12,)),
        ],
        compiler_params=params(),
        name="prepare",
    )(
        fresh,
        far(reads),
        far(state),
        far(lesion.reshape(own_blocks, block_rows)),
        far(stim_nodes.reshape(1, -1)),
        far(stim_wave.reshape(1, -1)),
        far(tract_slot.reshape(1, tile_count)),
        far(tract_target.reshape(1, tile_count)),
        far(tract_delay.reshape(1, tile_count)),
        far(jnp.asarray(lane_tables(peers, peer_targets, own_blocks))),
        far(jnp.asarray(expand_table(coef_count))),
        far(older_coefs.reshape(slot_count, HSEG, coef_count, block_rows)),
        far(tract_frac.reshape(1, tile_count)),
    )

    picked = pl.pallas_call(
        functools.partial(pick_kernel, capacity=capacity, peers=wide_peers),
        out_shape=[pltpu.VMEM((capacity, coef_count, block_rows), jnp.bfloat16)]
        * (wide_peers - 1),
        in_specs=[vmem_spec] * wide_peers,
        out_specs=[vmem_spec] * (wide_peers - 1),
        scratch_shapes=[
            SMEM((wide_peers - 1, capacity, wide_peers), jnp.int32),
            pltpu.SemaphoreType.DMA((wide_peers - 1,)),
        ],
        compiler_params=params(),
        name="pick_blocks",
    )(*asked[::-1], fresh)
    news = [swap(picked[r - 1], "wide", r) for r in range(wide_peers - 1, 0, -1)]

    fixed = tile_count * (peers - 2) // peers + 2 * UNROLL
    fixed = min(tile_count, -(-fixed // UNROLL) * UNROLL)
    share = pltpu.VMEM((share_rows, block_rows), jnp.bfloat16)
    total = pltpu.VMEM(((peers * peer_targets + 1) * STEPS, block_rows), jnp.float32)
    scalars = [SMEM((4, 128), jnp.int32), SMEM((1, 128), jnp.float32)]
    *shares, hist, sums = pl.pallas_call(
        functools.partial(
            far_kernel,
            wide_peers=wide_peers, peers=peers, capacity=capacity, peer_targets=peer_targets,
            fixed=fixed,
        ),
        out_shape=[share] * (peers - 2) + [pltpu.VMEM(hist.shape, jnp.float32), total],
        in_specs=[vmem_spec] * (5 + wide_peers),
        out_specs=[vmem_spec] * peers,
        scratch_shapes=[*scalars, pltpu.SemaphoreType.DMA((2,))],
        compiler_params=params(),
        name="far_tiles",
    )(fracs, tiles, table, heads, weights, hist, *news)
    sent = {r: swap(shares[peers - 1 - r], "narrow", r) for r in range(2, peers)}

    half = peer_targets * STEPS // 2
    pieces = [
        pltpu.VMEM((rows, block_rows), jnp.bfloat16) for rows in (half, share_rows - half)
    ]
    *pair, own = pl.pallas_call(
        functools.partial(near_tiles_kernel, peers=peers, peer_targets=peer_targets, fixed=fixed),
        out_shape=[*pieces, share],
        in_specs=[vmem_spec] * 6,
        out_specs=[vmem_spec] * 3,
        scratch_shapes=[*scalars, VMEM(total.shape, jnp.float32), pltpu.SemaphoreType.DMA((2,))],
        compiler_params=params(),
        name="near_tiles",
    )(fracs, tiles, heads, weights, hist, sums)
    pair = [swap(x, "narrow", 1) for x in pair]
    forcing = pl.pallas_call(
        functools.partial(
            forcing_kernel, peers=peers, own_blocks=own_blocks, peer_targets=peer_targets
        ),
        out_shape=pltpu.VMEM((STEPS * own_blocks, block_rows), jnp.float32),
        in_specs=[vmem_spec] * (peers + 1),
        out_specs=vmem_spec,
        compiler_params=params(),
        name="forcing",
    )(*[sent[r] for r in range(2, peers - 1)], *pair, own, ready)

    new_coefs, final_state = pl.pallas_call(
        functools.partial(
            window_kernel,
            own_blocks=own_blocks, peer_targets=peer_targets, coef_count=coef_count,
        ),
        out_shape=[
            jax.ShapeDtypeStruct(fresh_coefs.shape, jnp.bfloat16),
            jax.ShapeDtypeStruct(state.shape, jnp.float32),
        ],
        in_specs=[vmem_spec] * 4,
        out_specs=[hbm_spec] * 2,
        scratch_shapes=[
            VMEM((own_blocks * PITCH, block_rows), jnp.float32),
            VMEM((own_blocks * PITCH, block_rows), jnp.float32),
            VMEM((2, own_blocks, block_rows), jnp.float32),
            VMEM(fresh_coefs.shape, jnp.bfloat16),
            VMEM(state.shape, jnp.float32),
            pltpu.SemaphoreType.DMA((1 + own_blocks // GROUP // 2,)),
        ],
        compiler_params=params(),
        name="window_steps",
    )(sent[peers - 1], forcing, ready, jnp.asarray(fit_table(coef_count)))
    return new_coefs, final_state


def solution(mesh):
    in_specs = (
        P(("sweep", "wide", "narrow"), None, None),
        P(("sweep", "wide"), "narrow", None, None, None, None),
        P(None, ("sweep", "wide", "narrow")),
        P(("sweep", "wide", "narrow")),
        P("sweep"),
        P("sweep"),
        P("wide", "narrow", None, None),
        P("wide", "narrow", None),
        P("wide", "narrow", None),
        P("wide", "narrow", None),
        P("wide", "narrow", None),
        P("wide", "narrow", None, None, None),
    )
    out_specs = (P(("sweep", "wide", "narrow"), None, None), P(None, ("sweep", "wide", "narrow")))
    return jax.shard_map(local, mesh=mesh, in_specs=in_specs, out_specs=out_specs, check_vma=False)
```

```python
import functools
import math

import jax
import jax.numpy as jnp
import ml_dtypes
import numpy as np
from jax import lax
from jax.experimental import pallas as pl
from jax.experimental.pallas import tpu as pltpu
from jax.sharding import PartitionSpec as P

STEPS = 32
HSEG = 2
SEGS = HSEG + 1
LENGTH = SEGS * STEPS
GROUP = 4
HEAD = 16
PITCH = STEPS // 2 + 1
CHUNKS = 8
UNROLL = 4

excite_rate = 0.1
inhibit_rate = 0.05
excite_excite = 1.5
inhibit_excite = 2.0
excite_inhibit = 2.0
inhibit_inhibit = 0.5
excite_offset = 0.5
inhibit_offset = 0.5
tract_gain = 2.0

SMEM = pltpu.SMEM
VMEM = pltpu.VMEM
vmem_spec = pl.BlockSpec(memory_space=VMEM)
hbm_spec = pl.BlockSpec(memory_space=pltpu.HBM)


def basis_table(coef_count, step_count):
    order = np.arange(coef_count, dtype=np.float32)[:, None]
    places = np.arange(step_count, dtype=np.float32)[None, :]
    angles = np.float32(np.pi) * (step_count - places - np.float32(0.5)) / np.float32(step_count)
    return np.cos((order * angles).astype(np.float64)).astype(np.float32)


def expand_table(coef_count):
    basis = basis_table(coef_count, STEPS).astype(ml_dtypes.bfloat16)
    table = np.zeros((LENGTH, SEGS * coef_count), ml_dtypes.bfloat16)
    for seg in range(SEGS):
        table[seg * STEPS : (seg + 1) * STEPS, seg * coef_count : (seg + 1) * coef_count] = basis.T
    return table


def fit_table(coef_count):
    scales = np.where(np.arange(coef_count)[:, None] == 0, 1.0, 2.0) / STEPS
    fit = (basis_table(coef_count, STEPS) * scales).astype(np.float32)
    half = STEPS // 2
    tables = []
    for i in range(2):
        whole = np.zeros((GROUP * coef_count, GROUP * half), np.float32)
        for g in range(GROUP):
            whole[g * coef_count : (g + 1) * coef_count, g * half : (g + 1) * half] = fit[
                :, i * half : (i + 1) * half
            ]
        high = whole.astype(ml_dtypes.bfloat16)
        low = (whole - high.astype(np.float32)).astype(ml_dtypes.bfloat16)
        tables.append(np.concatenate([high, high, low], axis=1))
    return np.stack(tables)


TOGETHER = 8


def lane_tables(peers, peer_targets, own_blocks):
    width = TOGETHER * peer_targets
    assert TOGETHER * own_blocks <= 256 and peers * width <= HEAD * 128
    lane = np.arange(HEAD * 128)
    used = lane < peers * width
    within = lane % width
    rank = np.where(used, within // TOGETHER, -5)
    offset = within % TOGETHER * own_blocks + 1
    place = np.where(used, lane // width, -5)
    return np.stack([rank, offset, place]).astype(np.float32).reshape(3, HEAD, 128)


def prepare_kernel(
    fresh_ref, reads_hbm, state_hbm, lesion_hbm, stim_hbm, wave_hbm, slot_hbm, target_hbm,
    delay_hbm, lanes_hbm, table_hbm, older_hbm, frac_hbm,
    ready_out, hist_out, tiles_out, fracs_out, head_out, table,
    reads, state, lesion, stim, wave, slot, target, delay, frac, lanes, older, sems,
    *, peers, own_blocks, peer_targets, capacity,
):
    pairs = [
        (reads_hbm, reads), (target_hbm, target), (slot_hbm, slot),
        (delay_hbm, delay), (lanes_hbm, lanes), (table_hbm, table), (older_hbm, older),
        (state_hbm, state), (lesion_hbm, lesion), (stim_hbm, stim), (wave_hbm, wave),
        (frac_hbm, frac),
    ]
    copies = [
        pltpu.make_async_copy(source, into, sems.at[i]) for i, (source, into) in enumerate(pairs)
    ]
    for copy in copies:
        copy.start()
    for copy in (*copies[1:5], copies[11]):
        copy.wait()
    place = lax.axis_index("narrow")
    owner = lax.axis_index("wide")
    tile_count = target.shape[1]
    target_count = peers * own_blocks

    numbers = lax.broadcasted_iota(jnp.int32, (target_count, tile_count), 0)
    hits = jnp.where(numbers == target[...], 1.0, 0.0)
    held = jnp.dot(
        hits.astype(jnp.bfloat16), jnp.ones((tile_count, 128), jnp.bfloat16),
        preferred_element_type=jnp.float32,
    )
    held = jnp.minimum(held, 1.0)
    shape = (own_blocks, own_blocks)
    below = jnp.where(
        lax.broadcasted_iota(jnp.int32, shape, 0) > lax.broadcasted_iota(jnp.int32, shape, 1),
        1.0, 0.0,
    ).astype(jnp.bfloat16)
    block = lax.broadcasted_iota(jnp.int32, (own_blocks, 128), 0).astype(jnp.float32)
    ranks = jnp.zeros((1, tile_count), jnp.float32)
    head_rows = pl.cdiv(peers * TOGETHER * peer_targets, 128)
    for p in range(peers):
        part = slice(p * own_blocks, (p + 1) * own_blocks)
        rank = jnp.dot(below, held[part].astype(jnp.bfloat16), preferred_element_type=jnp.float32)
        ranks = ranks + jnp.sum(hits[part] * rank[:, :tile_count], axis=0, keepdims=True)
        rank = jnp.where(held[part] > 0.5, rank, -1.0)
        source = ((peers - 1) - (place ^ p)).astype(jnp.float32)
        rows = []
        for h in range(head_rows):
            match = rank == lanes[0, h : h + 1, :]
            ids = jnp.sum(jnp.where(match, block, 0.0), axis=0, keepdims=True)
            mine = lanes[2, h : h + 1, :] == source
            rows.append(jnp.where(mine, ids + lanes[1, h : h + 1, :], 0.0))
        rows.append(jnp.zeros((HEAD - head_rows, 128), jnp.float32))
        head_out[p] = jnp.concatenate(rows, axis=0).astype(jnp.bfloat16)

    across = jnp.zeros((1, tile_count), jnp.int32)
    for p in range(1, peers):
        across = across + jnp.where(target[...] >= p * own_blocks, 1, 0)
    key_row = ((peers - 1) - (across ^ place)).astype(jnp.float32)
    shape = (tile_count, tile_count)
    down = lax.broadcasted_iota(jnp.int32, shape, 0)
    along = lax.broadcasted_iota(jnp.int32, shape, 1)
    key = jnp.sum(jnp.where(down == along, key_row, 0.0), axis=1, keepdims=True)
    ahead = (key_row < key) | ((key_row == key) & (along < down))
    position = jnp.sum(jnp.where(ahead, 1.0, 0.0), axis=1, keepdims=True)
    lane = lax.broadcasted_iota(jnp.int32, (tile_count, 128), 1).astype(jnp.float32)
    chosen = jnp.where(position == lane, 1.0, 0.0)
    starts = (slot[...] * LENGTH + (LENGTH - 1) - delay[...]).astype(jnp.float32)
    index = lax.broadcasted_iota(jnp.int32, (1, tile_count), 1).astype(jnp.float32)
    firsts = (key_row * float(peer_targets) + ranks) * float(TOGETHER)
    facts = jnp.concatenate(
        [index, starts, firsts, frac[...], jnp.zeros((4, tile_count), jnp.float32)], axis=0
    )
    ordered = jnp.dot(
        facts, chosen, precision=lax.Precision.HIGHEST, preferred_element_type=jnp.float32
    )
    fracs_out[...] = ordered[3:4, :]
    tiles_out[0:3, :] = (ordered[0:3, :] + 0.5).astype(jnp.int32)
    tiles_out[3:4, :] = jnp.sum(
        jnp.where(key < lane, 1.0, 0.0), axis=0, keepdims=True
    ).astype(jnp.int32)

    for copy in copies[5:7]:
        copy.wait()
    coef_count = older.shape[2]
    earlier = HSEG * STEPS
    for s in range(older.shape[0]):
        segments = [older[s, h] for h in range(HSEG - 1, -1, -1)]
        hist_out[s * LENGTH : s * LENGTH + earlier, :] = jnp.dot(
            table[:earlier, : HSEG * coef_count], jnp.concatenate(segments, axis=0),
            preferred_element_type=jnp.float32,
        )
        hist_out[s * LENGTH + earlier : (s + 1) * LENGTH, :] = jnp.zeros(
            (STEPS, hist_out.shape[1]), jnp.float32
        )
    copies[0].wait()
    for c in range(capacity):
        rows = pl.ds(pl.multiple_of((owner * capacity + c) * LENGTH + earlier, 8), STEPS)
        hist_out[rows, :] = jnp.dot(
            table[:STEPS, :coef_count], fresh_ref[jnp.maximum(reads[c, owner], 0)],
            preferred_element_type=jnp.float32,
        )

    for copy in copies[7:11]:
        copy.wait()
    block_rows = lesion.shape[1]
    for b in range(own_blocks):
        piece = state[:, b * block_rows : (b + 1) * block_rows]
        ready_out[b : b + 1, :] = piece[0:1, :]
        ready_out[own_blocks + b : own_blocks + b + 1, :] = piece[1:2, :]
    ready_out[2 * own_blocks : 3 * own_blocks, :] = tract_gain * (
        1.0 - lesion[...].astype(jnp.float32)
    )
    stim_count = stim.shape[1]
    nodes = stim[...] - (owner * peers + place) * (own_blocks * block_rows)
    blocks = lax.shift_right_arithmetic(nodes, block_rows.bit_length() - 1)
    offsets = nodes & (block_rows - 1)
    in_block = lax.broadcasted_iota(jnp.int32, (own_blocks, stim_count), 0) == blocks
    at_offset = lax.broadcasted_iota(jnp.int32, (block_rows, stim_count), 0) == offsets
    ready_out[3 * own_blocks : 4 * own_blocks, :] = lax.dot_general(
        jnp.where(in_block, 1.0, 0.0).astype(jnp.bfloat16),
        jnp.where(at_offset, 1.0, 0.0).astype(jnp.bfloat16),
        (((1,), (1,)), ((), ())),
        preferred_element_type=jnp.float32,
    )
    shape = (STEPS, STEPS)
    diagonal = lax.broadcasted_iota(jnp.int32, shape, 0) == lax.broadcasted_iota(jnp.int32, shape, 1)
    column = jnp.sum(jnp.where(diagonal, wave[...], 0.0), axis=1, keepdims=True)
    ready_out[4 * own_blocks :, :] = jnp.broadcast_to(column, (STEPS, block_rows))


def near_kernel(fresh_hbm, weights_hbm, fresh_out, weights_out, sems):
    copies = [pltpu.make_async_copy(fresh_hbm, fresh_out, sems.at[CHUNKS])]
    part = weights_hbm.shape[0] // CHUNKS
    for i in range(CHUNKS):
        rows = pl.ds(i * part, part)
        copies.append(
            pltpu.make_async_copy(weights_hbm.at[rows], weights_out.at[rows], sems.at[i])
        )
    for copy in copies:
        copy.start()
    for copy in copies:
        copy.wait()


def wide_plans(count):
    if count == 4:
        requests = [
            [(2, 1), (3, 0)],
            [(0, 1), (2, 0)],
            [(0, 2), (1, 0), (2, 3), (3, 1)],
            [(0, 3), (1, 2)],
            [(1, 3), (3, 2)],
        ]
        blocks = [
            [(2, 0)],
            [(1, 0), (3, 1)],
            [(0, 3), (1, 2), (2, 1), (3, 0)],
            [(0, 1), (1, 3), (3, 2)],
            [(0, 2), (2, 3)],
        ]
        return requests, blocks
    whole = [[(i, i ^ r) for i in range(count)] for r in range(1, count)]
    return whole, whole


def ways(plan, pairs):
    return [next((k for k, part in enumerate(plan) if pair in part), None) for pair in pairs]


def by_place(place, values):
    known = [v for v in values if v is not None]
    result = known[0]
    for i, value in enumerate(values):
        if value is not None and value != known[0]:
            result = jnp.where(place == i, value, result)
    return result


def pick_kernel(*refs, capacity, requests, blocks):
    tables = refs[: len(requests)][::-1]
    fresh = refs[len(requests)]
    outs = refs[len(requests) + 1 : len(requests) + 1 + len(blocks)]
    asked, sems = refs[len(requests) + 1 + len(blocks) :]
    place = lax.axis_index("wide")
    count = lax.axis_size("wide")
    copies = [
        pltpu.make_async_copy(table, asked.at[k], sems.at[k]) for k, table in enumerate(tables)
    ]
    for copy in copies:
        copy.start()
    for copy in copies:
        copy.wait()
    for out, part in zip(outs, blocks):
        target = dict(part)
        way = by_place(place, ways(requests, [(target.get(i), i) for i in range(count)]))
        for c in range(capacity):
            block = jnp.clip(asked[way, c, place], 0, fresh.shape[0] - 1)
            out[c] = fresh[block]


def add_tiles(tiles, frac, hist, weights, total, pitch, items):
    block_rows = weights.shape[2]
    rows = []
    for t, _ in items:
        fraction = frac[0, t]
        start = tiles[1, t]
        earlier = hist[pl.ds(start, STEPS), :]
        later = hist[pl.ds(start + 1, STEPS), :]
        rows.append(((1.0 - fraction) * later + fraction * earlier).astype(jnp.bfloat16))
    tile = [weights[tiles[0, t]] for t, _ in items]
    none = jnp.zeros((2 * STEPS, block_rows), jnp.bfloat16)
    product = lax.dot_general(
        jnp.concatenate(
            [
                jnp.concatenate([*rows[:2], none], axis=0),
                jnp.concatenate([none, *rows[2:]], axis=0),
            ],
            axis=1,
        ),
        jnp.concatenate(
            [jnp.concatenate(tile[:2], axis=0), jnp.concatenate(tile[2:], axis=0)], axis=1
        ),
        (((1,), (1,)), ((), ())),
        preferred_element_type=jnp.float32,
    )
    for i, (_, first) in enumerate(items):
        left = i % 2 * block_rows
        for g in range(STEPS // TOGETHER):
            where = pl.ds(pl.multiple_of(first + g * pitch, 8), TOGETHER)
            top = i * STEPS + g * TOGETHER
            total[where, :] += product[top : top + TOGETHER, left : left + block_rows]


def write_share(pieces, total, head, first, span, pitch):
    groups = STEPS // TOGETHER // len(pieces)
    for i, piece in enumerate(pieces):
        for g in range(groups):
            top = (i * groups + g) * pitch + first
            piece[g * span : (g + 1) * span, :] = total[top : top + span, :].astype(jnp.bfloat16)
    pieces[-1][groups * span :, :] = head


def far_kernel(
    fracs_ref, tiles_ref, table_ref, head_ref, weights, hist_ref, *refs,
    blocks, wide_peers, peers, capacity, peer_targets, fixed,
):
    news = refs[: len(blocks)]
    outs = refs[len(blocks) : len(blocks) + peers - 2]
    hist, total, tiles, frac, sems = refs[len(blocks) + peers - 2 :]
    place = lax.axis_index("narrow")
    owner = lax.axis_index("wide")
    copies = [
        pltpu.make_async_copy(tiles_ref, tiles, sems.at[0]),
        pltpu.make_async_copy(fracs_ref, frac, sems.at[1]),
    ]
    for copy in copies:
        copy.start()
    total[...] = jnp.zeros_like(total)
    hist[...] = hist_ref[...]
    came = []
    for r in range(1, wide_peers):
        possible = ways(blocks, [(i ^ r, i) for i in range(wide_peers)])
        way = by_place(owner, possible)
        for c in range(capacity):
            block = news[possible[0]][c]
            for k in sorted(set(possible) - {possible[0]}):
                block = jnp.where(way == k, news[k][c], block)
            came.append((r, c, block))
    coef_count = news[0].shape[1]
    for first in range(0, len(came), SEGS):
        some = came[first : first + SEGS]
        values = jnp.dot(
            table_ref[: len(some) * STEPS, : len(some) * coef_count],
            jnp.concatenate([block for _, _, block in some], axis=0),
            preferred_element_type=jnp.float32,
        )
        for place_here, (r, c, _) in enumerate(some):
            slot = (owner ^ r) * capacity + c
            rows = pl.ds(pl.multiple_of(slot * LENGTH + HSEG * STEPS, 8), STEPS)
            hist[rows, :] = values[place_here * STEPS : (place_here + 1) * STEPS]
    for copy in copies:
        copy.wait()

    span = peer_targets * TOGETHER
    spare = peers * span
    pitch = spare + TOGETHER
    for t in range(0, fixed, UNROLL):
        items = [(u, tiles[2, u]) for u in range(t, t + UNROLL)]
        add_tiles(tiles, frac, hist, weights, total, pitch, items)
    far_count = tiles[3, peers - 2]

    @pl.loop(0, lax.div(jnp.maximum(far_count - fixed, 0) + (UNROLL - 1), UNROLL))
    def _(turn):
        places = [fixed + turn * UNROLL + u for u in range(UNROLL)]
        items = [(t, jnp.where(t < far_count, tiles[2, t], spare)) for t in places]
        add_tiles(tiles, frac, hist, weights, total, pitch, items)

    for part, out in enumerate(outs):
        write_share([out], total, head_ref[place ^ (peers - 1 - part)], part * span, span, pitch)


def near_tiles_kernel(
    fracs_ref, tiles_ref, head_ref, weights, hist, total_ref, *refs,
    peers, peer_targets, fixed,
):
    *pair, own, tiles, frac, total, sems = refs
    place = lax.axis_index("narrow")
    copies = [
        pltpu.make_async_copy(tiles_ref, tiles, sems.at[0]),
        pltpu.make_async_copy(fracs_ref, frac, sems.at[1]),
    ]
    for copy in copies:
        copy.start()
    total[...] = total_ref[...]
    for copy in copies:
        copy.wait()
    span = peer_targets * TOGETHER
    spare = peers * span
    pitch = spare + TOGETHER
    far_count = tiles[3, peers - 2]
    for t in range(fixed, weights.shape[0], UNROLL):
        items = [
            (u, jnp.where(u < far_count, spare, tiles[2, u])) for u in range(t, t + UNROLL)
        ]
        add_tiles(tiles, frac, hist, weights, total, pitch, items)
    write_share(pair, total, head_ref[place ^ 1], (peers - 2) * span, span, pitch)
    write_share([own], total, head_ref[place], (peers - 1) * span, span, pitch)


def share_rows(pieces, group, width):
    groups = STEPS // TOGETHER // len(pieces)
    first = group % groups * width
    return pieces[group // groups][first : first + width, :]


def one_hot(head, rows, columns):
    row = lax.broadcasted_iota(jnp.int32, (rows, 128), 0).astype(jnp.float32) + 1.0
    parts = [
        jnp.where(row == head[h : h + 1, :], 1.0, 0.0).astype(jnp.bfloat16)
        for h in range(pl.cdiv(columns, 128))
    ]
    return jnp.concatenate(parts, axis=1)[:, :columns]


def two_groups(shares, pair, width):
    return jnp.concatenate(
        [
            jnp.concatenate([share_rows(share, g, width) for share in shares], axis=0)
            for g in (pair, pair + 1)
        ],
        axis=1,
    )


def forcing_kernel(*refs, peers, own_blocks, peer_targets):
    shares = {r: (ref,) for r, ref in zip(range(2, peers - 1), refs)}
    shares |= {1: refs[peers - 3 : peers - 1], 0: (refs[peers - 1],)}
    ready_ref, out_ref = refs[peers:]
    block_rows = ready_ref.shape[1]
    width = TOGETHER * peer_targets
    head = sum(share[-1][-HEAD:, :].astype(jnp.float32) for share in shares.values())
    scatter = one_hot(head, TOGETHER * own_blocks, peers * width)
    stack = [shares[r] for r in (peers - 2, *range(peers - 2, -1, -1))]
    gain, counts = [
        0.5 * ready_ref[i * own_blocks : (i + 1) * own_blocks, :] for i in (2, 3)
    ]
    for pair in range(0, STEPS // TOGETHER, 2):
        inflow = jnp.dot(
            scatter, two_groups(stack, pair, width), preferred_element_type=jnp.float32
        )
        for jj in range(2 * TOGETHER):
            j = pair * TOGETHER + jj
            wave = ready_ref[4 * own_blocks + j : 4 * own_blocks + j + 1, :]
            first = jj % TOGETHER * own_blocks
            left = jj // TOGETHER * block_rows
            out_ref[j * own_blocks : (j + 1) * own_blocks, :] = gain * inflow[
                first : first + own_blocks, left : left + block_rows
            ] + (wave * counts - excite_offset / 2)


def window_kernel(
    share_ref, forcing_ref, ready_ref, fit_ref, coefs_hbm, state_hbm,
    early, late, rates, coefs, state, sems,
    *, own_blocks, peer_targets, coef_count,
):
    samples = (early, late)
    block_rows = ready_ref.shape[1]
    width = TOGETHER * peer_targets
    scatter = one_hot(
        share_ref[-HEAD:, :].astype(jnp.float32), TOGETHER * own_blocks, width
    )

    excite, inhibit, gain = [
        ready_ref[i * own_blocks : (i + 1) * own_blocks, :] for i in range(3)
    ]
    a = excite_excite / 2
    gain = 0.5 * gain
    carried = a * excite

    def fit_half(values, fit):
        products = []
        for g in range(0, own_blocks // GROUP, 2):
            part = jnp.concatenate(
                [
                    jnp.concatenate(
                        [
                            values[b * PITCH : b * PITCH + STEPS // 2, :]
                            for b in range((g + i) * GROUP, (g + i + 1) * GROUP)
                        ],
                        axis=0,
                    )
                    for i in range(2)
                ],
                axis=1,
            )
            high = part.astype(jnp.bfloat16)
            low = (part - high.astype(jnp.float32)).astype(jnp.bfloat16)
            products.append(
                jnp.dot(
                    fit, jnp.concatenate([high, low, high], axis=0),
                    preferred_element_type=jnp.float32,
                )
            )
        return products

    fitted = [None, None]
    for pair in range(0, STEPS // TOGETHER, 2):
        inflow = jnp.dot(
            scatter, two_groups([(share_ref,)], pair, width), preferred_element_type=jnp.float32
        )
        for jj in range(2 * TOGETHER):
            j = pair * TOGETHER + jj
            first = jj % TOGETHER * own_blocks
            left = jj // TOGETHER * block_rows
            half_forcing = (
                forcing_ref[j * own_blocks : (j + 1) * own_blocks, :]
                + gain * inflow[first : first + own_blocks, left : left + block_rows]
            )
            inhibit_drive = (inhibit_inhibit / 2) * inhibit + inhibit_offset / 2
            excite_turn = jnp.tanh(carried + (half_forcing - (inhibit_excite / 2) * inhibit))
            inhibit_turn = jnp.tanh((excite_inhibit / 2 / a) * carried - inhibit_drive)
            carried = ((1 - excite_rate) * carried + a * excite_rate / 2) + (
                a * excite_rate / 2
            ) * excite_turn
            inhibit = ((1 - inhibit_rate) * inhibit + inhibit_rate / 2) + (
                inhibit_rate / 2
            ) * inhibit_turn
            samples[pair // 2][pl.ds(jj, own_blocks, stride=PITCH), :] = carried * (1 / a)
        fitted[pair // 2] = fit_half(samples[pair // 2], fit_ref[pair // 2])
    rates[0] = carried * (1 / a)
    rates[1] = inhibit
    for b in range(own_blocks):
        where = slice(b * block_rows, (b + 1) * block_rows)
        state[0:1, where] = rates[0, b : b + 1, :]
        state[1:2, where] = rates[1, b : b + 1, :]
    copies = [pltpu.make_async_copy(state, state_hbm, sems.at[0])]
    copies[0].start()

    for g in range(0, own_blocks // GROUP, 2):
        both = (fitted[0][g // 2] + fitted[1][g // 2]).astype(jnp.bfloat16)
        for i in range(2):
            coefs[(g + i) * GROUP : (g + i + 1) * GROUP] = both[
                :, i * block_rows : (i + 1) * block_rows
            ].reshape(GROUP, coef_count, block_rows)
        where = pl.ds(g * GROUP, 2 * GROUP)
        copies.append(
            pltpu.make_async_copy(coefs.at[where], coefs_hbm.at[where], sems.at[1 + g // 2])
        )
        copies[-1].start()
    for copy in copies:
        copy.wait()


def far(x):
    return pltpu.with_memory_space_constraint(x, pltpu.HBM)


def params():
    return pltpu.CompilerParams(vmem_limit_bytes=20 << 20)


def local(
    fresh_coefs,
    older_coefs,
    state,
    lesion,
    stim_nodes,
    stim_wave,
    read_blocks,
    tract_slot,
    tract_target,
    tract_delay,
    tract_frac,
    tract_weights,
):
    wide_peers = lax.axis_size("wide")
    peers = lax.axis_size("narrow")
    own_blocks, coef_count, block_rows = fresh_coefs.shape
    capacity = read_blocks.shape[3]
    slot_count = wide_peers * capacity
    tile_count = tract_slot.shape[2]
    peer_targets = tile_count // (2 * peers)
    share_rows = peer_targets * STEPS + HEAD

    def swap(x, axis, r):
        return lax.ppermute(x, axis, [(i, i ^ r) for i in range(lax.axis_size(axis))])

    reads = read_blocks.reshape(wide_peers, capacity).T
    requests, blocks = wide_plans(wide_peers)
    asked = [lax.ppermute(reads, "wide", part) for part in requests]

    vmem_inputs = [
        VMEM(state.shape, jnp.float32),
        VMEM((own_blocks, block_rows), jnp.int32),
        VMEM((1, stim_nodes.shape[0]), jnp.int32),
        VMEM((1, STEPS), jnp.float32),
        VMEM((1, tile_count), jnp.int32),
        VMEM((1, tile_count), jnp.int32),
        VMEM((1, tile_count), jnp.int32),
        VMEM((1, tile_count), jnp.float32),
        VMEM((3, HEAD, 128), jnp.float32),
        VMEM((slot_count, HSEG, coef_count, block_rows), jnp.bfloat16),
    ]
    fresh, weights = pl.pallas_call(
        near_kernel,
        out_shape=[
            pltpu.VMEM(fresh_coefs.shape, jnp.bfloat16),
            pltpu.VMEM((tile_count, block_rows, block_rows), jnp.bfloat16),
        ],
        in_specs=[hbm_spec] * 2,
        out_specs=[vmem_spec] * 2,
        scratch_shapes=[pltpu.SemaphoreType.DMA((CHUNKS + 1,))],
        compiler_params=params(),
        name="near",
    )(far(fresh_coefs), far(tract_weights.reshape(tile_count, block_rows, block_rows)))
    ready, hist, tiles, fracs, heads, table = pl.pallas_call(
        functools.partial(
            prepare_kernel,
            peers=peers, own_blocks=own_blocks, peer_targets=peer_targets, capacity=capacity,
        ),
        out_shape=[
            pltpu.VMEM((4 * own_blocks + STEPS, block_rows), jnp.float32),
            pltpu.VMEM((slot_count * LENGTH, block_rows), jnp.float32),
            pltpu.VMEM((4, 128), jnp.int32),
            pltpu.VMEM((1, 128), jnp.float32),
            pltpu.VMEM((peers, HEAD, 128), jnp.bfloat16),
            pltpu.VMEM((LENGTH, SEGS * coef_count), jnp.bfloat16),
        ],
        in_specs=[vmem_spec] + [hbm_spec] * 12,
        out_specs=[vmem_spec] * 6,
        scratch_shapes=[
            SMEM((capacity, wide_peers), jnp.int32),
            *vmem_inputs,
            pltpu.SemaphoreType.DMA((12,)),
        ],
        compiler_params=params(),
        name="prepare",
    )(
        fresh,
        far(reads),
        far(state),
        far(lesion.reshape(own_blocks, block_rows)),
        far(stim_nodes.reshape(1, -1)),
        far(stim_wave.reshape(1, -1)),
        far(tract_slot.reshape(1, tile_count)),
        far(tract_target.reshape(1, tile_count)),
        far(tract_delay.reshape(1, tile_count)),
        far(jnp.asarray(lane_tables(peers, peer_targets, own_blocks))),
        far(jnp.asarray(expand_table(coef_count))),
        far(older_coefs.reshape(slot_count, HSEG, coef_count, block_rows)),
        far(tract_frac.reshape(1, tile_count)),
    )

    picked = pl.pallas_call(
        functools.partial(
            pick_kernel, capacity=capacity, requests=requests, blocks=blocks
        ),
        out_shape=[pltpu.VMEM((capacity, coef_count, block_rows), jnp.bfloat16)] * len(blocks),
        in_specs=[vmem_spec] * (len(requests) + 1),
        out_specs=[vmem_spec] * len(blocks),
        scratch_shapes=[
            SMEM((len(requests), capacity, wide_peers), jnp.int32),
            pltpu.SemaphoreType.DMA((len(requests),)),
        ],
        compiler_params=params(),
        name="pick_blocks",
    )(*asked[::-1], fresh)
    news = [lax.ppermute(x, "wide", part) for x, part in zip(picked, blocks)]

    fixed = tile_count * (peers - 2) // peers + 2 * UNROLL
    fixed = min(tile_count, -(-fixed // UNROLL) * UNROLL)
    share = pltpu.VMEM((share_rows, block_rows), jnp.bfloat16)
    total = pltpu.VMEM(((peers * peer_targets + 1) * STEPS, block_rows), jnp.float32)
    scalars = [SMEM((4, 128), jnp.int32), SMEM((1, 128), jnp.float32)]
    *shares, hist, sums = pl.pallas_call(
        functools.partial(
            far_kernel,
            blocks=blocks, wide_peers=wide_peers, peers=peers, capacity=capacity, peer_targets=peer_targets,
            fixed=fixed,
        ),
        out_shape=[share] * (peers - 2) + [pltpu.VMEM(hist.shape, jnp.float32), total],
        in_specs=[vmem_spec] * (6 + len(blocks)),
        out_specs=[vmem_spec] * peers,
        scratch_shapes=[*scalars, pltpu.SemaphoreType.DMA((2,))],
        compiler_params=params(),
        name="far_tiles",
    )(fracs, tiles, table, heads, weights, hist, *news)
    sent = {r: swap(shares[peers - 1 - r], "narrow", r) for r in range(2, peers)}

    half = peer_targets * STEPS // 2
    pieces = [
        pltpu.VMEM((rows, block_rows), jnp.bfloat16) for rows in (half, share_rows - half)
    ]
    *pair, own = pl.pallas_call(
        functools.partial(near_tiles_kernel, peers=peers, peer_targets=peer_targets, fixed=fixed),
        out_shape=[*pieces, share],
        in_specs=[vmem_spec] * 6,
        out_specs=[vmem_spec] * 3,
        scratch_shapes=[*scalars, VMEM(total.shape, jnp.float32), pltpu.SemaphoreType.DMA((2,))],
        compiler_params=params(),
        name="near_tiles",
    )(fracs, tiles, heads, weights, hist, sums)
    pair = [swap(x, "narrow", 1) for x in pair]
    forcing = pl.pallas_call(
        functools.partial(
            forcing_kernel, peers=peers, own_blocks=own_blocks, peer_targets=peer_targets
        ),
        out_shape=pltpu.VMEM((STEPS * own_blocks, block_rows), jnp.float32),
        in_specs=[vmem_spec] * (peers + 1),
        out_specs=vmem_spec,
        compiler_params=params(),
        name="forcing",
    )(*[sent[r] for r in range(2, peers - 1)], *pair, own, ready)

    new_coefs, final_state = pl.pallas_call(
        functools.partial(
            window_kernel,
            own_blocks=own_blocks, peer_targets=peer_targets, coef_count=coef_count,
        ),
        out_shape=[
            jax.ShapeDtypeStruct(fresh_coefs.shape, jnp.bfloat16),
            jax.ShapeDtypeStruct(state.shape, jnp.float32),
        ],
        in_specs=[vmem_spec] * 4,
        out_specs=[hbm_spec] * 2,
        scratch_shapes=[
            VMEM((own_blocks * PITCH, block_rows), jnp.float32),
            VMEM((own_blocks * PITCH, block_rows), jnp.float32),
            VMEM((2, own_blocks, block_rows), jnp.float32),
            VMEM(fresh_coefs.shape, jnp.bfloat16),
            VMEM(state.shape, jnp.float32),
            pltpu.SemaphoreType.DMA((1 + own_blocks // GROUP // 2,)),
        ],
        compiler_params=params(),
        name="window_steps",
    )(sent[peers - 1], forcing, ready, jnp.asarray(fit_table(coef_count)))
    return new_coefs, final_state


def solution(mesh):
    in_specs = (
        P(("sweep", "wide", "narrow"), None, None),
        P(("sweep", "wide"), "narrow", None, None, None, None),
        P(None, ("sweep", "wide", "narrow")),
        P(("sweep", "wide", "narrow")),
        P("sweep"),
        P("sweep"),
        P("wide", "narrow", None, None),
        P("wide", "narrow", None),
        P("wide", "narrow", None),
        P("wide", "narrow", None),
        P("wide", "narrow", None),
        P("wide", "narrow", None, None, None),
    )
    out_specs = (P(("sweep", "wide", "narrow"), None, None), P(None, ("sweep", "wide", "narrow")))
    return jax.shard_map(local, mesh=mesh, in_specs=in_specs, out_specs=out_specs, check_vma=False)
```

```python
import functools
import math

import jax
import jax.numpy as jnp
import ml_dtypes
import numpy as np
from jax import lax
from jax.experimental import pallas as pl
from jax.experimental.pallas import tpu as pltpu
from jax.sharding import PartitionSpec as P

STEPS = 32
HSEG = 2
SEGS = HSEG + 1
LENGTH = SEGS * STEPS
GROUP = 4
HEAD = 16
LAST = 2
PITCH = STEPS // 2 + 1
CHUNKS = 8
UNROLL = 4

excite_rate = 0.1
inhibit_rate = 0.05
excite_excite = 1.5
inhibit_excite = 2.0
excite_inhibit = 2.0
inhibit_inhibit = 0.5
excite_offset = 0.5
inhibit_offset = 0.5
tract_gain = 2.0

SMEM = pltpu.SMEM
VMEM = pltpu.VMEM
vmem_spec = pl.BlockSpec(memory_space=VMEM)
hbm_spec = pl.BlockSpec(memory_space=pltpu.HBM)


def basis_table(coef_count, step_count):
    order = np.arange(coef_count, dtype=np.float32)[:, None]
    places = np.arange(step_count, dtype=np.float32)[None, :]
    angles = np.float32(np.pi) * (step_count - places - np.float32(0.5)) / np.float32(step_count)
    return np.cos((order * angles).astype(np.float64)).astype(np.float32)


def expand_table(coef_count):
    basis = basis_table(coef_count, STEPS).astype(ml_dtypes.bfloat16)
    table = np.zeros((LENGTH, SEGS * coef_count), ml_dtypes.bfloat16)
    for seg in range(SEGS):
        table[seg * STEPS : (seg + 1) * STEPS, seg * coef_count : (seg + 1) * coef_count] = basis.T
    return table


def fit_table(coef_count):
    scales = np.where(np.arange(coef_count)[:, None] == 0, 1.0, 2.0) / STEPS
    fit = (basis_table(coef_count, STEPS) * scales).astype(np.float32)
    half = STEPS // 2
    tables = []
    for i in range(2):
        whole = np.zeros((GROUP * coef_count, GROUP * half), np.float32)
        for g in range(GROUP):
            whole[g * coef_count : (g + 1) * coef_count, g * half : (g + 1) * half] = fit[
                :, i * half : (i + 1) * half
            ]
        high = whole.astype(ml_dtypes.bfloat16)
        low = (whole - high.astype(np.float32)).astype(ml_dtypes.bfloat16)
        tables.append(np.concatenate([high, high, low], axis=1))
    return np.stack(tables)


TOGETHER = 8


def lane_tables(peers, peer_targets, own_blocks):
    width = TOGETHER * peer_targets
    assert TOGETHER * own_blocks <= 256 and peers * width <= HEAD * 128
    lane = np.arange(HEAD * 128)
    used = lane < peers * width
    within = lane % width
    rank = np.where(used, within // TOGETHER, -5)
    offset = within % TOGETHER * own_blocks + 1
    place = np.where(used, lane // width, -5)
    return np.stack([rank, offset, place]).astype(np.float32).reshape(3, HEAD, 128)


def prepare_kernel(
    fresh_ref, reads_hbm, state_hbm, lesion_hbm, stim_hbm, wave_hbm, slot_hbm, target_hbm,
    delay_hbm, lanes_hbm, table_hbm, older_hbm, frac_hbm,
    ready_out, hist_out, tiles_out, fracs_out, head_out, table,
    reads, state, lesion, stim, wave, slot, target, delay, frac, lanes, older, sems,
    *, peers, own_blocks, peer_targets, capacity,
):
    pairs = [
        (reads_hbm, reads), (target_hbm, target), (slot_hbm, slot),
        (delay_hbm, delay), (lanes_hbm, lanes), (table_hbm, table), (older_hbm, older),
        (state_hbm, state), (lesion_hbm, lesion), (stim_hbm, stim), (wave_hbm, wave),
        (frac_hbm, frac),
    ]
    copies = [
        pltpu.make_async_copy(source, into, sems.at[i]) for i, (source, into) in enumerate(pairs)
    ]
    for copy in copies:
        copy.start()
    for copy in (*copies[1:5], copies[11]):
        copy.wait()
    place = lax.axis_index("narrow")
    owner = lax.axis_index("wide")
    tile_count = target.shape[1]
    target_count = peers * own_blocks

    numbers = lax.broadcasted_iota(jnp.int32, (target_count, tile_count), 0)
    hits = jnp.where(numbers == target[...], 1.0, 0.0)
    held = jnp.dot(
        hits.astype(jnp.bfloat16), jnp.ones((tile_count, 128), jnp.bfloat16),
        preferred_element_type=jnp.float32,
    )
    held = jnp.minimum(held, 1.0)
    shape = (own_blocks, own_blocks)
    below = jnp.where(
        lax.broadcasted_iota(jnp.int32, shape, 0) > lax.broadcasted_iota(jnp.int32, shape, 1),
        1.0, 0.0,
    ).astype(jnp.bfloat16)
    block = lax.broadcasted_iota(jnp.int32, (own_blocks, 128), 0).astype(jnp.float32)
    ranks = jnp.zeros((1, tile_count), jnp.float32)
    head_rows = pl.cdiv(peers * TOGETHER * peer_targets, 128)
    for p in range(peers):
        part = slice(p * own_blocks, (p + 1) * own_blocks)
        rank = jnp.dot(below, held[part].astype(jnp.bfloat16), preferred_element_type=jnp.float32)
        ranks = ranks + jnp.sum(hits[part] * rank[:, :tile_count], axis=0, keepdims=True)
        rank = jnp.where(held[part] > 0.5, rank, -1.0)
        source = place ^ p
        source = jnp.where(
            source == LAST, 0, (peers - 1) - source + jnp.where(source > LAST, 1, 0)
        ).astype(jnp.float32)
        rows = []
        for h in range(head_rows):
            match = rank == lanes[0, h : h + 1, :]
            ids = jnp.sum(jnp.where(match, block, 0.0), axis=0, keepdims=True)
            mine = lanes[2, h : h + 1, :] == source
            rows.append(jnp.where(mine, ids + lanes[1, h : h + 1, :], 0.0))
        rows.append(jnp.zeros((HEAD - head_rows, 128), jnp.float32))
        head_out[p] = jnp.concatenate(rows, axis=0).astype(jnp.bfloat16)

    across = jnp.zeros((1, tile_count), jnp.int32)
    for p in range(1, peers):
        across = across + jnp.where(target[...] >= p * own_blocks, 1, 0)
    key_row = ((peers - 1) - (across ^ place)).astype(jnp.float32)
    shape = (tile_count, tile_count)
    down = lax.broadcasted_iota(jnp.int32, shape, 0)
    along = lax.broadcasted_iota(jnp.int32, shape, 1)
    key = jnp.sum(jnp.where(down == along, key_row, 0.0), axis=1, keepdims=True)
    ahead = (key_row < key) | ((key_row == key) & (along < down))
    position = jnp.sum(jnp.where(ahead, 1.0, 0.0), axis=1, keepdims=True)
    lane = lax.broadcasted_iota(jnp.int32, (tile_count, 128), 1).astype(jnp.float32)
    chosen = jnp.where(position == lane, 1.0, 0.0)
    starts = (slot[...] * LENGTH + (LENGTH - 1) - delay[...]).astype(jnp.float32)
    index = lax.broadcasted_iota(jnp.int32, (1, tile_count), 1).astype(jnp.float32)
    firsts = (key_row * float(peer_targets) + ranks) * float(TOGETHER)
    facts = jnp.concatenate(
        [index, starts, firsts, frac[...], jnp.zeros((4, tile_count), jnp.float32)], axis=0
    )
    ordered = jnp.dot(
        facts, chosen, precision=lax.Precision.HIGHEST, preferred_element_type=jnp.float32
    )
    fracs_out[...] = ordered[3:4, :]
    tiles_out[0:3, :] = (ordered[0:3, :] + 0.5).astype(jnp.int32)
    tiles_out[3:4, :] = jnp.sum(
        jnp.where(key < lane, 1.0, 0.0), axis=0, keepdims=True
    ).astype(jnp.int32)

    for copy in copies[5:7]:
        copy.wait()
    coef_count = older.shape[2]
    earlier = HSEG * STEPS
    for s in range(older.shape[0]):
        segments = [older[s, h] for h in range(HSEG - 1, -1, -1)]
        hist_out[s * LENGTH : s * LENGTH + earlier, :] = jnp.dot(
            table[:earlier, : HSEG * coef_count], jnp.concatenate(segments, axis=0),
            preferred_element_type=jnp.float32,
        )
        hist_out[s * LENGTH + earlier : (s + 1) * LENGTH, :] = jnp.zeros(
            (STEPS, hist_out.shape[1]), jnp.float32
        )
    copies[0].wait()
    for c in range(capacity):
        rows = pl.ds(pl.multiple_of((owner * capacity + c) * LENGTH + earlier, 8), STEPS)
        hist_out[rows, :] = jnp.dot(
            table[:STEPS, :coef_count], fresh_ref[jnp.maximum(reads[c, owner], 0)],
            preferred_element_type=jnp.float32,
        )

    for copy in copies[7:11]:
        copy.wait()
    block_rows = lesion.shape[1]
    for b in range(own_blocks):
        piece = state[:, b * block_rows : (b + 1) * block_rows]
        ready_out[b : b + 1, :] = piece[0:1, :]
        ready_out[own_blocks + b : own_blocks + b + 1, :] = piece[1:2, :]
    ready_out[2 * own_blocks : 3 * own_blocks, :] = tract_gain * (
        1.0 - lesion[...].astype(jnp.float32)
    )
    stim_count = stim.shape[1]
    nodes = stim[...] - (owner * peers + place) * (own_blocks * block_rows)
    blocks = lax.shift_right_arithmetic(nodes, block_rows.bit_length() - 1)
    offsets = nodes & (block_rows - 1)
    in_block = lax.broadcasted_iota(jnp.int32, (own_blocks, stim_count), 0) == blocks
    at_offset = lax.broadcasted_iota(jnp.int32, (block_rows, stim_count), 0) == offsets
    ready_out[3 * own_blocks : 4 * own_blocks, :] = lax.dot_general(
        jnp.where(in_block, 1.0, 0.0).astype(jnp.bfloat16),
        jnp.where(at_offset, 1.0, 0.0).astype(jnp.bfloat16),
        (((1,), (1,)), ((), ())),
        preferred_element_type=jnp.float32,
    )
    shape = (STEPS, STEPS)
    diagonal = lax.broadcasted_iota(jnp.int32, shape, 0) == lax.broadcasted_iota(jnp.int32, shape, 1)
    column = jnp.sum(jnp.where(diagonal, wave[...], 0.0), axis=1, keepdims=True)
    ready_out[4 * own_blocks :, :] = jnp.broadcast_to(column, (STEPS, block_rows))


def near_kernel(fresh_hbm, weights_hbm, fresh_out, weights_out, sems):
    copies = [pltpu.make_async_copy(fresh_hbm, fresh_out, sems.at[CHUNKS])]
    part = weights_hbm.shape[0] // CHUNKS
    for i in range(CHUNKS):
        rows = pl.ds(i * part, part)
        copies.append(
            pltpu.make_async_copy(weights_hbm.at[rows], weights_out.at[rows], sems.at[i])
        )
    for copy in copies:
        copy.start()
    for copy in copies:
        copy.wait()


def folded_ring(count):
    return [0, *range(1, count, 2), *reversed(range(2, count, 2))]


def pick_kernel(*refs, capacity, peers):
    tables = refs[: peers - 1][::-1]
    fresh = refs[peers - 1]
    outs = refs[peers : 2 * peers - 1]
    asked, sems = refs[2 * peers - 1 :]
    place = lax.axis_index("wide")
    copies = [pltpu.make_async_copy(tables[r], asked.at[r], sems.at[r]) for r in range(peers - 1)]
    for copy in copies:
        copy.start()

    for copy in copies:
        copy.wait()
    ring = folded_ring(peers)
    for distance in range(1, peers):
        turns = [(ring.index(i) - ring.index(i ^ distance)) % peers for i in range(peers)]
        way = turns[0]
        for i in range(1, peers):
            if turns[i] != turns[0]:
                way = jnp.where(place == i, turns[i], way)
        for c in range(capacity):
            block = jnp.maximum(asked[way - 1, c, place], 0)
            outs[distance - 1][c] = fresh[block]


def add_tiles(tiles, frac, hist, weights, total, pitch, items):
    block_rows = weights.shape[2]
    rows = []
    for t, _ in items:
        fraction = frac[0, t]
        start = tiles[1, t]
        earlier = hist[pl.ds(start, STEPS), :]
        later = hist[pl.ds(start + 1, STEPS), :]
        rows.append(((1.0 - fraction) * later + fraction * earlier).astype(jnp.bfloat16))
    tile = [weights[tiles[0, t]] for t, _ in items]
    none = jnp.zeros((2 * STEPS, block_rows), jnp.bfloat16)
    product = lax.dot_general(
        jnp.concatenate(
            [
                jnp.concatenate([*rows[:2], none], axis=0),
                jnp.concatenate([none, *rows[2:]], axis=0),
            ],
            axis=1,
        ),
        jnp.concatenate(
            [jnp.concatenate(tile[:2], axis=0), jnp.concatenate(tile[2:], axis=0)], axis=1
        ),
        (((1,), (1,)), ((), ())),
        preferred_element_type=jnp.float32,
    )
    for i, (_, first) in enumerate(items):
        left = i % 2 * block_rows
        for g in range(STEPS // TOGETHER):
            where = pl.ds(pl.multiple_of(first + g * pitch, 8), TOGETHER)
            top = i * STEPS + g * TOGETHER
            total[where, :] += product[top : top + TOGETHER, left : left + block_rows]


def write_share(pieces, total, head, first, span, pitch):
    groups = STEPS // TOGETHER // len(pieces)
    for i, piece in enumerate(pieces):
        for g in range(groups):
            top = (i * groups + g) * pitch + first
            piece[g * span : (g + 1) * span, :] = total[top : top + span, :].astype(jnp.bfloat16)
    pieces[-1][groups * span :, :] = head


def far_kernel(
    fracs_ref, tiles_ref, table_ref, head_ref, weights, hist_ref, *refs,
    wide_peers, peers, capacity, peer_targets, fixed,
):
    news = refs[: wide_peers - 1]
    outs = refs[wide_peers - 1 : wide_peers + peers - 3]
    hist, total, tiles, frac, sems = refs[wide_peers + peers - 3 :]
    place = lax.axis_index("narrow")
    owner = lax.axis_index("wide")
    copies = [
        pltpu.make_async_copy(tiles_ref, tiles, sems.at[0]),
        pltpu.make_async_copy(fracs_ref, frac, sems.at[1]),
    ]
    for copy in copies:
        copy.start()
    total[...] = jnp.zeros_like(total)
    hist[...] = hist_ref[...]
    came = [(i, c) for i in range(len(news)) for c in range(capacity)]
    coef_count = news[0].shape[1]
    for first in range(0, len(came), SEGS):
        some = came[first : first + SEGS]
        values = jnp.dot(
            table_ref[: len(some) * STEPS, : len(some) * coef_count],
            jnp.concatenate([news[i][c] for i, c in some], axis=0),
            preferred_element_type=jnp.float32,
        )
        for place_here, (i, c) in enumerate(some):
            slot = (owner ^ (wide_peers - 1 - i)) * capacity + c
            rows = pl.ds(pl.multiple_of(slot * LENGTH + HSEG * STEPS, 8), STEPS)
            hist[rows, :] = values[place_here * STEPS : (place_here + 1) * STEPS]
    for copy in copies:
        copy.wait()

    span = peer_targets * TOGETHER
    spare = peers * span
    pitch = spare + TOGETHER
    for t in range(0, fixed, UNROLL):
        items = [(u, tiles[2, u]) for u in range(t, t + UNROLL)]
        add_tiles(tiles, frac, hist, weights, total, pitch, items)
    far_count = tiles[3, peers - 2]

    @pl.loop(0, lax.div(jnp.maximum(far_count - fixed, 0) + (UNROLL - 1), UNROLL))
    def _(turn):
        places = [fixed + turn * UNROLL + u for u in range(UNROLL)]
        items = [(t, jnp.where(t < far_count, tiles[2, t], spare)) for t in places]
        add_tiles(tiles, frac, hist, weights, total, pitch, items)

    for part, out in enumerate(outs):
        write_share([out], total, head_ref[place ^ (peers - 1 - part)], part * span, span, pitch)


def near_tiles_kernel(
    fracs_ref, tiles_ref, head_ref, weights, hist, total_ref, *refs,
    peers, peer_targets, fixed,
):
    *pair, own, tiles, frac, total, sems = refs
    place = lax.axis_index("narrow")
    copies = [
        pltpu.make_async_copy(tiles_ref, tiles, sems.at[0]),
        pltpu.make_async_copy(fracs_ref, frac, sems.at[1]),
    ]
    for copy in copies:
        copy.start()
    total[...] = total_ref[...]
    for copy in copies:
        copy.wait()
    span = peer_targets * TOGETHER
    spare = peers * span
    pitch = spare + TOGETHER
    far_count = tiles[3, peers - 2]
    for t in range(fixed, weights.shape[0], UNROLL):
        items = [
            (u, jnp.where(u < far_count, spare, tiles[2, u])) for u in range(t, t + UNROLL)
        ]
        add_tiles(tiles, frac, hist, weights, total, pitch, items)
    write_share(pair, total, head_ref[place ^ 1], (peers - 2) * span, span, pitch)
    write_share([own], total, head_ref[place], (peers - 1) * span, span, pitch)


def share_rows(pieces, group, width):
    groups = STEPS // TOGETHER // len(pieces)
    first = group % groups * width
    return pieces[group // groups][first : first + width, :]


def one_hot(head, rows, columns):
    row = lax.broadcasted_iota(jnp.int32, (rows, 128), 0).astype(jnp.float32) + 1.0
    parts = [
        jnp.where(row == head[h : h + 1, :], 1.0, 0.0).astype(jnp.bfloat16)
        for h in range(pl.cdiv(columns, 128))
    ]
    return jnp.concatenate(parts, axis=1)[:, :columns]


def two_groups(shares, pair, width):
    return jnp.concatenate(
        [
            jnp.concatenate([share_rows(share, g, width) for share in shares], axis=0)
            for g in (pair, pair + 1)
        ],
        axis=1,
    )


def forcing_kernel(*refs, peers, own_blocks, peer_targets):
    shares = {r: (ref,) for r, ref in zip(range(LAST + 1, peers), refs)}
    shares |= {1: refs[peers - 3 : peers - 1], 0: (refs[peers - 1],)}
    ready_ref, out_ref = refs[peers:]
    block_rows = ready_ref.shape[1]
    width = TOGETHER * peer_targets
    head = sum(share[-1][-HEAD:, :].astype(jnp.float32) for share in shares.values())
    scatter = one_hot(head, TOGETHER * own_blocks, peers * width)
    stack = [shares[r] for r in (0, *range(peers - 1, LAST, -1), *range(LAST - 1, -1, -1))]
    gain, counts = [
        0.5 * ready_ref[i * own_blocks : (i + 1) * own_blocks, :] for i in (2, 3)
    ]
    for pair in range(0, STEPS // TOGETHER, 2):
        inflow = jnp.dot(
            scatter, two_groups(stack, pair, width), preferred_element_type=jnp.float32
        )
        for jj in range(2 * TOGETHER):
            j = pair * TOGETHER + jj
            wave = ready_ref[4 * own_blocks + j : 4 * own_blocks + j + 1, :]
            first = jj % TOGETHER * own_blocks
            left = jj // TOGETHER * block_rows
            out_ref[j * own_blocks : (j + 1) * own_blocks, :] = gain * inflow[
                first : first + own_blocks, left : left + block_rows
            ] + (wave * counts - excite_offset / 2)


def window_kernel(
    share_ref, forcing_ref, ready_ref, fit_ref, coefs_hbm, state_hbm,
    early, late, rates, coefs, state, sems,
    *, own_blocks, peer_targets, coef_count,
):
    samples = (early, late)
    block_rows = ready_ref.shape[1]
    width = TOGETHER * peer_targets
    scatter = one_hot(
        share_ref[-HEAD:, :].astype(jnp.float32), TOGETHER * own_blocks, width
    )

    excite, inhibit, gain = [
        ready_ref[i * own_blocks : (i + 1) * own_blocks, :] for i in range(3)
    ]
    a = excite_excite / 2
    gain = 0.5 * gain
    carried = a * excite

    def fit_half(values, fit):
        products = []
        for g in range(0, own_blocks // GROUP, 2):
            part = jnp.concatenate(
                [
                    jnp.concatenate(
                        [
                            values[b * PITCH : b * PITCH + STEPS // 2, :]
                            for b in range((g + i) * GROUP, (g + i + 1) * GROUP)
                        ],
                        axis=0,
                    )
                    for i in range(2)
                ],
                axis=1,
            )
            high = part.astype(jnp.bfloat16)
            low = (part - high.astype(jnp.float32)).astype(jnp.bfloat16)
            products.append(
                jnp.dot(
                    fit, jnp.concatenate([high, low, high], axis=0),
                    preferred_element_type=jnp.float32,
                )
            )
        return products

    fitted = [None, None]
    for pair in range(0, STEPS // TOGETHER, 2):
        inflow = jnp.dot(
            scatter, two_groups([(share_ref,)], pair, width), preferred_element_type=jnp.float32
        )
        for jj in range(2 * TOGETHER):
            j = pair * TOGETHER + jj
            first = jj % TOGETHER * own_blocks
            left = jj // TOGETHER * block_rows
            half_forcing = (
                forcing_ref[j * own_blocks : (j + 1) * own_blocks, :]
                + gain * inflow[first : first + own_blocks, left : left + block_rows]
            )
            inhibit_drive = (inhibit_inhibit / 2) * inhibit + inhibit_offset / 2
            excite_turn = jnp.tanh(carried + (half_forcing - (inhibit_excite / 2) * inhibit))
            inhibit_turn = jnp.tanh((excite_inhibit / 2 / a) * carried - inhibit_drive)
            carried = ((1 - excite_rate) * carried + a * excite_rate / 2) + (
                a * excite_rate / 2
            ) * excite_turn
            inhibit = ((1 - inhibit_rate) * inhibit + inhibit_rate / 2) + (
                inhibit_rate / 2
            ) * inhibit_turn
            samples[pair // 2][pl.ds(jj, own_blocks, stride=PITCH), :] = carried * (1 / a)
        fitted[pair // 2] = fit_half(samples[pair // 2], fit_ref[pair // 2])
    rates[0] = carried * (1 / a)
    rates[1] = inhibit
    for b in range(own_blocks):
        where = slice(b * block_rows, (b + 1) * block_rows)
        state[0:1, where] = rates[0, b : b + 1, :]
        state[1:2, where] = rates[1, b : b + 1, :]
    copies = [pltpu.make_async_copy(state, state_hbm, sems.at[0])]
    copies[0].start()

    for g in range(0, own_blocks // GROUP, 2):
        both = (fitted[0][g // 2] + fitted[1][g // 2]).astype(jnp.bfloat16)
        for i in range(2):
            coefs[(g + i) * GROUP : (g + i + 1) * GROUP] = both[
                :, i * block_rows : (i + 1) * block_rows
            ].reshape(GROUP, coef_count, block_rows)
        where = pl.ds(g * GROUP, 2 * GROUP)
        copies.append(
            pltpu.make_async_copy(coefs.at[where], coefs_hbm.at[where], sems.at[1 + g // 2])
        )
        copies[-1].start()
    for copy in copies:
        copy.wait()


def far(x):
    return pltpu.with_memory_space_constraint(x, pltpu.HBM)


def params():
    return pltpu.CompilerParams(vmem_limit_bytes=20 << 20)


def local(
    fresh_coefs,
    older_coefs,
    state,
    lesion,
    stim_nodes,
    stim_wave,
    read_blocks,
    tract_slot,
    tract_target,
    tract_delay,
    tract_frac,
    tract_weights,
):
    wide_peers = lax.axis_size("wide")
    peers = lax.axis_size("narrow")
    own_blocks, coef_count, block_rows = fresh_coefs.shape
    capacity = read_blocks.shape[3]
    slot_count = wide_peers * capacity
    tile_count = tract_slot.shape[2]
    peer_targets = tile_count // (2 * peers)
    share_rows = peer_targets * STEPS + HEAD

    def swap(x, axis, r):
        return lax.ppermute(x, axis, [(i, i ^ r) for i in range(lax.axis_size(axis))])

    reads = read_blocks.reshape(wide_peers, capacity).T
    ring = folded_ring(wide_peers)
    asked = [
        lax.ppermute(
            reads, "wide", [(ring[k], ring[(k + r) % wide_peers]) for k in range(wide_peers)]
        )
        for r in range(1, wide_peers)
    ]

    vmem_inputs = [
        VMEM(state.shape, jnp.float32),
        VMEM((own_blocks, block_rows), jnp.int32),
        VMEM((1, stim_nodes.shape[0]), jnp.int32),
        VMEM((1, STEPS), jnp.float32),
        VMEM((1, tile_count), jnp.int32),
        VMEM((1, tile_count), jnp.int32),
        VMEM((1, tile_count), jnp.int32),
        VMEM((1, tile_count), jnp.float32),
        VMEM((3, HEAD, 128), jnp.float32),
        VMEM((slot_count, HSEG, coef_count, block_rows), jnp.bfloat16),
    ]
    fresh, weights = pl.pallas_call(
        near_kernel,
        out_shape=[
            pltpu.VMEM(fresh_coefs.shape, jnp.bfloat16),
            pltpu.VMEM((tile_count, block_rows, block_rows), jnp.bfloat16),
        ],
        in_specs=[hbm_spec] * 2,
        out_specs=[vmem_spec] * 2,
        scratch_shapes=[pltpu.SemaphoreType.DMA((CHUNKS + 1,))],
        compiler_params=params(),
        name="near",
    )(far(fresh_coefs), far(tract_weights.reshape(tile_count, block_rows, block_rows)))
    ready, hist, tiles, fracs, heads, table = pl.pallas_call(
        functools.partial(
            prepare_kernel,
            peers=peers, own_blocks=own_blocks, peer_targets=peer_targets, capacity=capacity,
        ),
        out_shape=[
            pltpu.VMEM((4 * own_blocks + STEPS, block_rows), jnp.float32),
            pltpu.VMEM((slot_count * LENGTH, block_rows), jnp.float32),
            pltpu.VMEM((4, 128), jnp.int32),
            pltpu.VMEM((1, 128), jnp.float32),
            pltpu.VMEM((peers, HEAD, 128), jnp.bfloat16),
            pltpu.VMEM((LENGTH, SEGS * coef_count), jnp.bfloat16),
        ],
        in_specs=[vmem_spec] + [hbm_spec] * 12,
        out_specs=[vmem_spec] * 6,
        scratch_shapes=[
            SMEM((capacity, wide_peers), jnp.int32),
            *vmem_inputs,
            pltpu.SemaphoreType.DMA((12,)),
        ],
        compiler_params=params(),
        name="prepare",
    )(
        fresh,
        far(reads),
        far(state),
        far(lesion.reshape(own_blocks, block_rows)),
        far(stim_nodes.reshape(1, -1)),
        far(stim_wave.reshape(1, -1)),
        far(tract_slot.reshape(1, tile_count)),
        far(tract_target.reshape(1, tile_count)),
        far(tract_delay.reshape(1, tile_count)),
        far(jnp.asarray(lane_tables(peers, peer_targets, own_blocks))),
        far(jnp.asarray(expand_table(coef_count))),
        far(older_coefs.reshape(slot_count, HSEG, coef_count, block_rows)),
        far(tract_frac.reshape(1, tile_count)),
    )

    picked = pl.pallas_call(
        functools.partial(pick_kernel, capacity=capacity, peers=wide_peers),
        out_shape=[pltpu.VMEM((capacity, coef_count, block_rows), jnp.bfloat16)]
        * (wide_peers - 1),
        in_specs=[vmem_spec] * wide_peers,
        out_specs=[vmem_spec] * (wide_peers - 1),
        scratch_shapes=[
            SMEM((wide_peers - 1, capacity, wide_peers), jnp.int32),
            pltpu.SemaphoreType.DMA((wide_peers - 1,)),
        ],
        compiler_params=params(),
        name="pick_blocks",
    )(*asked[::-1], fresh)
    news = [swap(picked[r - 1], "wide", r) for r in range(wide_peers - 1, 0, -1)]

    fixed = tile_count * (peers - 2) // peers + 2 * UNROLL
    fixed = min(tile_count, -(-fixed // UNROLL) * UNROLL)
    share = pltpu.VMEM((share_rows, block_rows), jnp.bfloat16)
    total = pltpu.VMEM(((peers * peer_targets + 1) * STEPS, block_rows), jnp.float32)
    scalars = [SMEM((4, 128), jnp.int32), SMEM((1, 128), jnp.float32)]
    *shares, hist, sums = pl.pallas_call(
        functools.partial(
            far_kernel,
            wide_peers=wide_peers, peers=peers, capacity=capacity, peer_targets=peer_targets,
            fixed=fixed,
        ),
        out_shape=[share] * (peers - 2) + [pltpu.VMEM(hist.shape, jnp.float32), total],
        in_specs=[vmem_spec] * (5 + wide_peers),
        out_specs=[vmem_spec] * peers,
        scratch_shapes=[*scalars, pltpu.SemaphoreType.DMA((2,))],
        compiler_params=params(),
        name="far_tiles",
    )(fracs, tiles, table, heads, weights, hist, *news)
    sent = {r: swap(shares[peers - 1 - r], "narrow", r) for r in range(2, peers)}

    half = peer_targets * STEPS // 2
    pieces = [
        pltpu.VMEM((rows, block_rows), jnp.bfloat16) for rows in (half, share_rows - half)
    ]
    *pair, own = pl.pallas_call(
        functools.partial(near_tiles_kernel, peers=peers, peer_targets=peer_targets, fixed=fixed),
        out_shape=[*pieces, share],
        in_specs=[vmem_spec] * 6,
        out_specs=[vmem_spec] * 3,
        scratch_shapes=[*scalars, VMEM(total.shape, jnp.float32), pltpu.SemaphoreType.DMA((2,))],
        compiler_params=params(),
        name="near_tiles",
    )(fracs, tiles, heads, weights, hist, sums)
    pair = [swap(x, "narrow", 1) for x in pair]
    forcing = pl.pallas_call(
        functools.partial(
            forcing_kernel, peers=peers, own_blocks=own_blocks, peer_targets=peer_targets
        ),
        out_shape=pltpu.VMEM((STEPS * own_blocks, block_rows), jnp.float32),
        in_specs=[vmem_spec] * (peers + 1),
        out_specs=vmem_spec,
        compiler_params=params(),
        name="forcing",
    )(*[sent[r] for r in range(LAST + 1, peers)], *pair, own, ready)

    new_coefs, final_state = pl.pallas_call(
        functools.partial(
            window_kernel,
            own_blocks=own_blocks, peer_targets=peer_targets, coef_count=coef_count,
        ),
        out_shape=[
            jax.ShapeDtypeStruct(fresh_coefs.shape, jnp.bfloat16),
            jax.ShapeDtypeStruct(state.shape, jnp.float32),
        ],
        in_specs=[vmem_spec] * 4,
        out_specs=[hbm_spec] * 2,
        scratch_shapes=[
            VMEM((own_blocks * PITCH, block_rows), jnp.float32),
            VMEM((own_blocks * PITCH, block_rows), jnp.float32),
            VMEM((2, own_blocks, block_rows), jnp.float32),
            VMEM(fresh_coefs.shape, jnp.bfloat16),
            VMEM(state.shape, jnp.float32),
            pltpu.SemaphoreType.DMA((1 + own_blocks // GROUP // 2,)),
        ],
        compiler_params=params(),
        name="window_steps",
    )(sent[LAST], forcing, ready, jnp.asarray(fit_table(coef_count)))
    return new_coefs, final_state


def solution(mesh):
    in_specs = (
        P(("sweep", "wide", "narrow"), None, None),
        P(("sweep", "wide"), "narrow", None, None, None, None),
        P(None, ("sweep", "wide", "narrow")),
        P(("sweep", "wide", "narrow")),
        P("sweep"),
        P("sweep"),
        P("wide", "narrow", None, None),
        P("wide", "narrow", None),
        P("wide", "narrow", None),
        P("wide", "narrow", None),
        P("wide", "narrow", None),
        P("wide", "narrow", None, None, None),
    )
    out_specs = (P(("sweep", "wide", "narrow"), None, None), P(None, ("sweep", "wide", "narrow")))
    return jax.shard_map(local, mesh=mesh, in_specs=in_specs, out_specs=out_specs, check_vma=False)
```

```python
import functools
import math

import jax
import jax.numpy as jnp
import ml_dtypes
import numpy as np
from jax import lax
from jax.experimental import pallas as pl
from jax.experimental.pallas import tpu as pltpu
from jax.sharding import PartitionSpec as P

STEPS = 32
HSEG = 2
SEGS = HSEG + 1
LENGTH = SEGS * STEPS
GROUP = 4
HEAD = 16
PITCH = STEPS // 2 + 1
CHUNKS = 8
UNROLL = 4

excite_rate = 0.1
inhibit_rate = 0.05
excite_excite = 1.5
inhibit_excite = 2.0
excite_inhibit = 2.0
inhibit_inhibit = 0.5
excite_offset = 0.5
inhibit_offset = 0.5
tract_gain = 2.0

SMEM = pltpu.SMEM
VMEM = pltpu.VMEM
vmem_spec = pl.BlockSpec(memory_space=VMEM)
hbm_spec = pl.BlockSpec(memory_space=pltpu.HBM)


def basis_table(coef_count, step_count):
    order = np.arange(coef_count, dtype=np.float32)[:, None]
    places = np.arange(step_count, dtype=np.float32)[None, :]
    angles = np.float32(np.pi) * (step_count - places - np.float32(0.5)) / np.float32(step_count)
    return np.cos((order * angles).astype(np.float64)).astype(np.float32)


def expand_table(coef_count):
    basis = basis_table(coef_count, STEPS).astype(ml_dtypes.bfloat16)
    table = np.zeros((LENGTH, SEGS * coef_count), ml_dtypes.bfloat16)
    for seg in range(SEGS):
        table[seg * STEPS : (seg + 1) * STEPS, seg * coef_count : (seg + 1) * coef_count] = basis.T
    return table


def fit_table(coef_count):
    scales = np.where(np.arange(coef_count)[:, None] == 0, 1.0, 2.0) / STEPS
    fit = (basis_table(coef_count, STEPS) * scales / (excite_excite / 2)).astype(np.float32)
    half = STEPS // 2
    tables = []
    for i in range(2):
        whole = np.zeros((GROUP * coef_count, GROUP * half), np.float32)
        for g in range(GROUP):
            whole[g * coef_count : (g + 1) * coef_count, g * half : (g + 1) * half] = fit[
                :, i * half : (i + 1) * half
            ]
        high = whole.astype(ml_dtypes.bfloat16)
        low = (whole - high.astype(np.float32)).astype(ml_dtypes.bfloat16)
        tables.append(np.concatenate([high, high, low], axis=1))
    return np.stack(tables)


TOGETHER = 8


def lane_tables(peers, peer_targets, own_blocks):
    width = TOGETHER * peer_targets
    assert TOGETHER * own_blocks <= 256 and peers * width <= HEAD * 128
    lane = np.arange(HEAD * 128)
    used = lane < peers * width
    within = lane % width
    rank = np.where(used, within // TOGETHER, -5)
    offset = within % TOGETHER * own_blocks + 1
    place = np.where(used, lane // width, -5)
    return np.stack([rank, offset, place]).astype(np.float32).reshape(3, HEAD, 128)


def prepare_kernel(
    fresh_ref, reads_hbm, state_hbm, lesion_hbm, stim_hbm, wave_hbm, slot_hbm, target_hbm,
    delay_hbm, lanes_hbm, table_hbm, older_hbm, frac_hbm,
    ready_out, hist_out, tiles_out, fracs_out, head_out, table,
    reads, state, lesion, stim, wave, slot, target, delay, frac, lanes, older, sems,
    *, peers, own_blocks, peer_targets, capacity,
):
    pairs = [
        (reads_hbm, reads), (target_hbm, target), (slot_hbm, slot),
        (delay_hbm, delay), (lanes_hbm, lanes), (table_hbm, table), (older_hbm, older),
        (state_hbm, state), (lesion_hbm, lesion), (stim_hbm, stim), (wave_hbm, wave),
        (frac_hbm, frac),
    ]
    copies = [
        pltpu.make_async_copy(source, into, sems.at[i]) for i, (source, into) in enumerate(pairs)
    ]
    for copy in copies:
        copy.start()
    for copy in (*copies[1:5], copies[11]):
        copy.wait()
    place = lax.axis_index("narrow")
    owner = lax.axis_index("wide")
    tile_count = target.shape[1]
    target_count = peers * own_blocks

    numbers = lax.broadcasted_iota(jnp.int32, (target_count, tile_count), 0)
    hits = jnp.where(numbers == target[...], 1.0, 0.0)
    held = jnp.dot(
        hits.astype(jnp.bfloat16), jnp.ones((tile_count, 128), jnp.bfloat16),
        preferred_element_type=jnp.float32,
    )
    held = jnp.minimum(held, 1.0)
    shape = (own_blocks, own_blocks)
    below = jnp.where(
        lax.broadcasted_iota(jnp.int32, shape, 0) > lax.broadcasted_iota(jnp.int32, shape, 1),
        1.0, 0.0,
    ).astype(jnp.bfloat16)
    block = lax.broadcasted_iota(jnp.int32, (own_blocks, 128), 0).astype(jnp.float32)
    ranks = jnp.zeros((1, tile_count), jnp.float32)
    head_rows = pl.cdiv(peers * TOGETHER * peer_targets, 128)
    for p in range(peers):
        part = slice(p * own_blocks, (p + 1) * own_blocks)
        rank = jnp.dot(below, held[part].astype(jnp.bfloat16), preferred_element_type=jnp.float32)
        ranks = ranks + jnp.sum(hits[part] * rank[:, :tile_count], axis=0, keepdims=True)
        rank = jnp.where(held[part] > 0.5, rank, -1.0)
        source = ((peers - 1) - (place ^ p)).astype(jnp.float32)
        rows = []
        for h in range(head_rows):
            match = rank == lanes[0, h : h + 1, :]
            ids = jnp.sum(jnp.where(match, block, 0.0), axis=0, keepdims=True)
            mine = lanes[2, h : h + 1, :] == source
            rows.append(jnp.where(mine, ids + lanes[1, h : h + 1, :], 0.0))
        rows.append(jnp.zeros((HEAD - head_rows, 128), jnp.float32))
        head_out[p] = jnp.concatenate(rows, axis=0).astype(jnp.bfloat16)

    across = jnp.zeros((1, tile_count), jnp.int32)
    for p in range(1, peers):
        across = across + jnp.where(target[...] >= p * own_blocks, 1, 0)
    key_row = ((peers - 1) - (across ^ place)).astype(jnp.float32)
    shape = (tile_count, tile_count)
    down = lax.broadcasted_iota(jnp.int32, shape, 0)
    along = lax.broadcasted_iota(jnp.int32, shape, 1)
    key = jnp.sum(jnp.where(down == along, key_row, 0.0), axis=1, keepdims=True)
    ahead = (key_row < key) | ((key_row == key) & (along < down))
    position = jnp.sum(jnp.where(ahead, 1.0, 0.0), axis=1, keepdims=True)
    lane = lax.broadcasted_iota(jnp.int32, (tile_count, 128), 1).astype(jnp.float32)
    chosen = jnp.where(position == lane, 1.0, 0.0)
    starts = (slot[...] * LENGTH + (LENGTH - 1) - delay[...]).astype(jnp.float32)
    index = lax.broadcasted_iota(jnp.int32, (1, tile_count), 1).astype(jnp.float32)
    firsts = (key_row * float(peer_targets) + ranks) * float(TOGETHER)
    facts = jnp.concatenate(
        [index, starts, firsts, frac[...], jnp.zeros((4, tile_count), jnp.float32)], axis=0
    )
    ordered = jnp.dot(
        facts, chosen, precision=lax.Precision.HIGHEST, preferred_element_type=jnp.float32
    )
    fracs_out[...] = ordered[3:4, :]
    tiles_out[0:3, :] = (ordered[0:3, :] + 0.5).astype(jnp.int32)
    tiles_out[3:4, :] = jnp.sum(
        jnp.where(key < lane, 1.0, 0.0), axis=0, keepdims=True
    ).astype(jnp.int32)

    for copy in copies[5:7]:
        copy.wait()
    coef_count = older.shape[2]
    earlier = HSEG * STEPS
    for s in range(older.shape[0]):
        segments = [older[s, h] for h in range(HSEG - 1, -1, -1)]
        hist_out[s * LENGTH : s * LENGTH + earlier, :] = jnp.dot(
            table[:earlier, : HSEG * coef_count], jnp.concatenate(segments, axis=0),
            preferred_element_type=jnp.float32,
        )
        hist_out[s * LENGTH + earlier : (s + 1) * LENGTH, :] = jnp.zeros(
            (STEPS, hist_out.shape[1]), jnp.float32
        )
    copies[0].wait()
    for c in range(capacity):
        rows = pl.ds(pl.multiple_of((owner * capacity + c) * LENGTH + earlier, 8), STEPS)
        hist_out[rows, :] = jnp.dot(
            table[:STEPS, :coef_count], fresh_ref[jnp.maximum(reads[c, owner], 0)],
            preferred_element_type=jnp.float32,
        )

    for copy in copies[7:11]:
        copy.wait()
    block_rows = lesion.shape[1]
    for b in range(own_blocks):
        piece = state[:, b * block_rows : (b + 1) * block_rows]
        ready_out[b : b + 1, :] = piece[0:1, :]
        ready_out[own_blocks + b : own_blocks + b + 1, :] = piece[1:2, :]
    ready_out[2 * own_blocks : 3 * own_blocks, :] = tract_gain * (
        1.0 - lesion[...].astype(jnp.float32)
    )
    stim_count = stim.shape[1]
    nodes = stim[...] - (owner * peers + place) * (own_blocks * block_rows)
    blocks = lax.shift_right_arithmetic(nodes, block_rows.bit_length() - 1)
    offsets = nodes & (block_rows - 1)
    in_block = lax.broadcasted_iota(jnp.int32, (own_blocks, stim_count), 0) == blocks
    at_offset = lax.broadcasted_iota(jnp.int32, (block_rows, stim_count), 0) == offsets
    ready_out[3 * own_blocks : 4 * own_blocks, :] = lax.dot_general(
        jnp.where(in_block, 1.0, 0.0).astype(jnp.bfloat16),
        jnp.where(at_offset, 1.0, 0.0).astype(jnp.bfloat16),
        (((1,), (1,)), ((), ())),
        preferred_element_type=jnp.float32,
    )
    shape = (STEPS, STEPS)
    diagonal = lax.broadcasted_iota(jnp.int32, shape, 0) == lax.broadcasted_iota(jnp.int32, shape, 1)
    column = jnp.sum(jnp.where(diagonal, wave[...], 0.0), axis=1, keepdims=True)
    ready_out[4 * own_blocks :, :] = jnp.broadcast_to(column, (STEPS, block_rows))


def near_kernel(fresh_hbm, weights_hbm, fresh_out, weights_out, sems):
    copies = [pltpu.make_async_copy(fresh_hbm, fresh_out, sems.at[CHUNKS])]
    part = weights_hbm.shape[0] // CHUNKS
    for i in range(CHUNKS):
        rows = pl.ds(i * part, part)
        copies.append(
            pltpu.make_async_copy(weights_hbm.at[rows], weights_out.at[rows], sems.at[i])
        )
    for copy in copies:
        copy.start()
    for copy in copies:
        copy.wait()


def folded_ring(count):
    return [0, *range(1, count, 2), *reversed(range(2, count, 2))]


def pick_kernel(*refs, capacity, peers):
    tables = refs[: peers - 1][::-1]
    fresh = refs[peers - 1]
    outs = refs[peers : 2 * peers - 1]
    asked, sems = refs[2 * peers - 1 :]
    place = lax.axis_index("wide")
    copies = [pltpu.make_async_copy(tables[r], asked.at[r], sems.at[r]) for r in range(peers - 1)]
    for copy in copies:
        copy.start()

    for copy in copies:
        copy.wait()
    ring = folded_ring(peers)
    for distance in range(1, peers):
        turns = [(ring.index(i) - ring.index(i ^ distance)) % peers for i in range(peers)]
        way = turns[0]
        for i in range(1, peers):
            if turns[i] != turns[0]:
                way = jnp.where(place == i, turns[i], way)
        for c in range(capacity):
            block = jnp.maximum(asked[way - 1, c, place], 0)
            outs[distance - 1][c] = fresh[block]


def add_tiles(tiles, frac, hist, weights, total, pitch, items):
    block_rows = weights.shape[2]
    rows = []
    for t, _ in items:
        fraction = frac[0, t]
        start = tiles[1, t]
        earlier = hist[pl.ds(start, STEPS), :]
        later = hist[pl.ds(start + 1, STEPS), :]
        rows.append(((1.0 - fraction) * later + fraction * earlier).astype(jnp.bfloat16))
    tile = [weights[tiles[0, t]] for t, _ in items]
    none = jnp.zeros((2 * STEPS, block_rows), jnp.bfloat16)
    product = lax.dot_general(
        jnp.concatenate(
            [
                jnp.concatenate([*rows[:2], none], axis=0),
                jnp.concatenate([none, *rows[2:]], axis=0),
            ],
            axis=1,
        ),
        jnp.concatenate(
            [jnp.concatenate(tile[:2], axis=0), jnp.concatenate(tile[2:], axis=0)], axis=1
        ),
        (((1,), (1,)), ((), ())),
        preferred_element_type=jnp.float32,
    )
    for i, (_, first) in enumerate(items):
        left = i % 2 * block_rows
        for g in range(STEPS // TOGETHER):
            where = pl.ds(pl.multiple_of(first + g * pitch, 8), TOGETHER)
            top = i * STEPS + g * TOGETHER
            total[where, :] += product[top : top + TOGETHER, left : left + block_rows]


def write_share(pieces, total, head, first, span, pitch):
    groups = STEPS // TOGETHER // len(pieces)
    for i, piece in enumerate(pieces):
        for g in range(groups):
            top = (i * groups + g) * pitch + first
            piece[g * span : (g + 1) * span, :] = total[top : top + span, :].astype(jnp.bfloat16)
    pieces[-1][groups * span :, :] = head


def far_kernel(
    fracs_ref, tiles_ref, table_ref, head_ref, weights, hist_ref, *refs,
    wide_peers, peers, capacity, peer_targets, fixed,
):
    news = refs[: wide_peers - 1]
    outs = refs[wide_peers - 1 : wide_peers + peers - 3]
    hist, total, tiles, frac, sems = refs[wide_peers + peers - 3 :]
    place = lax.axis_index("narrow")
    owner = lax.axis_index("wide")
    copies = [
        pltpu.make_async_copy(tiles_ref, tiles, sems.at[0]),
        pltpu.make_async_copy(fracs_ref, frac, sems.at[1]),
    ]
    for copy in copies:
        copy.start()
    total[...] = jnp.zeros_like(total)
    hist[...] = hist_ref[...]
    came = [(i, c) for i in range(len(news)) for c in range(capacity)]
    coef_count = news[0].shape[1]
    for first in range(0, len(came), SEGS):
        some = came[first : first + SEGS]
        values = jnp.dot(
            table_ref[: len(some) * STEPS, : len(some) * coef_count],
            jnp.concatenate([news[i][c] for i, c in some], axis=0),
            preferred_element_type=jnp.float32,
        )
        for place_here, (i, c) in enumerate(some):
            slot = (owner ^ (wide_peers - 1 - i)) * capacity + c
            rows = pl.ds(pl.multiple_of(slot * LENGTH + HSEG * STEPS, 8), STEPS)
            hist[rows, :] = values[place_here * STEPS : (place_here + 1) * STEPS]
    for copy in copies:
        copy.wait()

    span = peer_targets * TOGETHER
    spare = peers * span
    pitch = spare + TOGETHER
    for t in range(0, fixed, UNROLL):
        items = [(u, tiles[2, u]) for u in range(t, t + UNROLL)]
        add_tiles(tiles, frac, hist, weights, total, pitch, items)
    far_count = tiles[3, peers - 2]

    @pl.loop(0, lax.div(jnp.maximum(far_count - fixed, 0) + (UNROLL - 1), UNROLL))
    def _(turn):
        places = [fixed + turn * UNROLL + u for u in range(UNROLL)]
        items = [(t, jnp.where(t < far_count, tiles[2, t], spare)) for t in places]
        add_tiles(tiles, frac, hist, weights, total, pitch, items)

    for part, out in enumerate(outs):
        write_share([out], total, head_ref[place ^ (peers - 1 - part)], part * span, span, pitch)


def near_tiles_kernel(
    fracs_ref, tiles_ref, head_ref, weights, hist, total_ref, *refs,
    peers, peer_targets, fixed,
):
    *pair, own, tiles, frac, total, sems = refs
    place = lax.axis_index("narrow")
    copies = [
        pltpu.make_async_copy(tiles_ref, tiles, sems.at[0]),
        pltpu.make_async_copy(fracs_ref, frac, sems.at[1]),
    ]
    for copy in copies:
        copy.start()
    total[...] = total_ref[...]
    for copy in copies:
        copy.wait()
    span = peer_targets * TOGETHER
    spare = peers * span
    pitch = spare + TOGETHER
    far_count = tiles[3, peers - 2]
    for t in range(fixed, weights.shape[0], UNROLL):
        items = [
            (u, jnp.where(u < far_count, spare, tiles[2, u])) for u in range(t, t + UNROLL)
        ]
        add_tiles(tiles, frac, hist, weights, total, pitch, items)
    write_share(pair, total, head_ref[place ^ 1], (peers - 2) * span, span, pitch)
    write_share([own], total, head_ref[place], (peers - 1) * span, span, pitch)


def share_rows(pieces, group, width):
    groups = STEPS // TOGETHER // len(pieces)
    first = group % groups * width
    return pieces[group // groups][first : first + width, :]


def one_hot(head, rows, columns):
    row = lax.broadcasted_iota(jnp.int32, (rows, 128), 0).astype(jnp.float32) + 1.0
    parts = [
        jnp.where(row == head[h : h + 1, :], 1.0, 0.0).astype(jnp.bfloat16)
        for h in range(pl.cdiv(columns, 128))
    ]
    return jnp.concatenate(parts, axis=1)[:, :columns]


def two_groups(shares, pair, width):
    return jnp.concatenate(
        [
            jnp.concatenate([share_rows(share, g, width) for share in shares], axis=0)
            for g in (pair, pair + 1)
        ],
        axis=1,
    )


def forcing_kernel(*refs, peers, own_blocks, peer_targets):
    shares = {r: (ref,) for r, ref in zip(range(2, peers - 1), refs)}
    shares |= {1: refs[peers - 3 : peers - 1], 0: (refs[peers - 1],)}
    ready_ref, out_ref = refs[peers:]
    block_rows = ready_ref.shape[1]
    width = TOGETHER * peer_targets
    head = sum(share[-1][-HEAD:, :].astype(jnp.float32) for share in shares.values())
    scatter = one_hot(head, TOGETHER * own_blocks, peers * width)
    stack = [shares[r] for r in (0, *range(peers - 2, -1, -1))]
    gain, counts = [
        0.5 * ready_ref[i * own_blocks : (i + 1) * own_blocks, :] for i in (2, 3)
    ]
    for pair in range(0, STEPS // TOGETHER, 2):
        inflow = jnp.dot(
            scatter, two_groups(stack, pair, width), preferred_element_type=jnp.float32
        )
        for jj in range(2 * TOGETHER):
            j = pair * TOGETHER + jj
            wave = ready_ref[4 * own_blocks + j : 4 * own_blocks + j + 1, :]
            first = jj % TOGETHER * own_blocks
            left = jj // TOGETHER * block_rows
            out_ref[j * own_blocks : (j + 1) * own_blocks, :] = gain * inflow[
                first : first + own_blocks, left : left + block_rows
            ] + (wave * counts - excite_offset / 2)


def window_kernel(
    share_ref, forcing_ref, ready_ref, fit_ref, coefs_hbm, state_hbm,
    early, late, rates, coefs, state, sems,
    *, own_blocks, peer_targets, coef_count,
):
    samples = (early, late)
    block_rows = ready_ref.shape[1]
    width = TOGETHER * peer_targets
    scatter = one_hot(
        share_ref[-HEAD:, :].astype(jnp.float32), TOGETHER * own_blocks, width
    )

    excite, inhibit, gain = [
        ready_ref[i * own_blocks : (i + 1) * own_blocks, :] for i in range(3)
    ]
    a = excite_excite / 2
    gain = 0.5 * gain
    carried = a * excite

    def fit_half(values, fit):
        products = []
        for g in range(0, own_blocks // GROUP, 2):
            part = jnp.concatenate(
                [
                    jnp.concatenate(
                        [
                            values[b * PITCH : b * PITCH + STEPS // 2, :]
                            for b in range((g + i) * GROUP, (g + i + 1) * GROUP)
                        ],
                        axis=0,
                    )
                    for i in range(2)
                ],
                axis=1,
            )
            high = part.astype(jnp.bfloat16)
            low = (part - high.astype(jnp.float32)).astype(jnp.bfloat16)
            products.append(
                jnp.dot(
                    fit, jnp.concatenate([high, low, high], axis=0),
                    preferred_element_type=jnp.float32,
                )
            )
        return products

    fitted = [None, None]
    for pair in range(0, STEPS // TOGETHER, 2):
        inflow = jnp.dot(
            scatter, two_groups([(share_ref,)], pair, width), preferred_element_type=jnp.float32
        )
        for jj in range(2 * TOGETHER):
            j = pair * TOGETHER + jj
            first = jj % TOGETHER * own_blocks
            left = jj // TOGETHER * block_rows
            half_forcing = (
                forcing_ref[j * own_blocks : (j + 1) * own_blocks, :]
                + gain * inflow[first : first + own_blocks, left : left + block_rows]
            )
            inhibit_drive = (inhibit_inhibit / 2) * inhibit + inhibit_offset / 2
            excite_turn = jnp.tanh(carried + (half_forcing - (inhibit_excite / 2) * inhibit))
            inhibit_turn = jnp.tanh((excite_inhibit / 2 / a) * carried - inhibit_drive)
            carried = ((1 - excite_rate) * carried + a * excite_rate / 2) + (
                a * excite_rate / 2
            ) * excite_turn
            inhibit = ((1 - inhibit_rate) * inhibit + inhibit_rate / 2) + (
                inhibit_rate / 2
            ) * inhibit_turn
            samples[pair // 2][pl.ds(jj, own_blocks, stride=PITCH), :] = carried
        fitted[pair // 2] = fit_half(samples[pair // 2], fit_ref[pair // 2])
    rates[0] = carried * (1 / a)
    rates[1] = inhibit
    for b in range(own_blocks):
        where = slice(b * block_rows, (b + 1) * block_rows)
        state[0:1, where] = rates[0, b : b + 1, :]
        state[1:2, where] = rates[1, b : b + 1, :]
    copies = [pltpu.make_async_copy(state, state_hbm, sems.at[0])]
    copies[0].start()

    for g in range(0, own_blocks // GROUP, 2):
        both = (fitted[0][g // 2] + fitted[1][g // 2]).astype(jnp.bfloat16)
        for i in range(2):
            coefs[(g + i) * GROUP : (g + i + 1) * GROUP] = both[
                :, i * block_rows : (i + 1) * block_rows
            ].reshape(GROUP, coef_count, block_rows)
        where = pl.ds(g * GROUP, 2 * GROUP)
        copies.append(
            pltpu.make_async_copy(coefs.at[where], coefs_hbm.at[where], sems.at[1 + g // 2])
        )
        copies[-1].start()
    for copy in copies:
        copy.wait()


def far(x):
    return pltpu.with_memory_space_constraint(x, pltpu.HBM)


def params():
    return pltpu.CompilerParams(vmem_limit_bytes=20 << 20)


def local(
    fresh_coefs,
    older_coefs,
    state,
    lesion,
    stim_nodes,
    stim_wave,
    read_blocks,
    tract_slot,
    tract_target,
    tract_delay,
    tract_frac,
    tract_weights,
):
    wide_peers = lax.axis_size("wide")
    peers = lax.axis_size("narrow")
    own_blocks, coef_count, block_rows = fresh_coefs.shape
    capacity = read_blocks.shape[3]
    slot_count = wide_peers * capacity
    tile_count = tract_slot.shape[2]
    peer_targets = tile_count // (2 * peers)
    share_rows = peer_targets * STEPS + HEAD

    def swap(x, axis, r):
        return lax.ppermute(x, axis, [(i, i ^ r) for i in range(lax.axis_size(axis))])

    reads = read_blocks.reshape(wide_peers, capacity).T
    ring = folded_ring(wide_peers)
    asked = [
        lax.ppermute(
            reads, "wide", [(ring[k], ring[(k + r) % wide_peers]) for k in range(wide_peers)]
        )
        for r in range(1, wide_peers)
    ]

    vmem_inputs = [
        VMEM(state.shape, jnp.float32),
        VMEM((own_blocks, block_rows), jnp.int32),
        VMEM((1, stim_nodes.shape[0]), jnp.int32),
        VMEM((1, STEPS), jnp.float32),
        VMEM((1, tile_count), jnp.int32),
        VMEM((1, tile_count), jnp.int32),
        VMEM((1, tile_count), jnp.int32),
        VMEM((1, tile_count), jnp.float32),
        VMEM((3, HEAD, 128), jnp.float32),
        VMEM((slot_count, HSEG, coef_count, block_rows), jnp.bfloat16),
    ]
    fresh, weights = pl.pallas_call(
        near_kernel,
        out_shape=[
            pltpu.VMEM(fresh_coefs.shape, jnp.bfloat16),
            pltpu.VMEM((tile_count, block_rows, block_rows), jnp.bfloat16),
        ],
        in_specs=[hbm_spec] * 2,
        out_specs=[vmem_spec] * 2,
        scratch_shapes=[pltpu.SemaphoreType.DMA((CHUNKS + 1,))],
        compiler_params=params(),
        name="near",
    )(far(fresh_coefs), far(tract_weights.reshape(tile_count, block_rows, block_rows)))
    ready, hist, tiles, fracs, heads, table = pl.pallas_call(
        functools.partial(
            prepare_kernel,
            peers=peers, own_blocks=own_blocks, peer_targets=peer_targets, capacity=capacity,
        ),
        out_shape=[
            pltpu.VMEM((4 * own_blocks + STEPS, block_rows), jnp.float32),
            pltpu.VMEM((slot_count * LENGTH, block_rows), jnp.float32),
            pltpu.VMEM((4, 128), jnp.int32),
            pltpu.VMEM((1, 128), jnp.float32),
            pltpu.VMEM((peers, HEAD, 128), jnp.bfloat16),
            pltpu.VMEM((LENGTH, SEGS * coef_count), jnp.bfloat16),
        ],
        in_specs=[vmem_spec] + [hbm_spec] * 12,
        out_specs=[vmem_spec] * 6,
        scratch_shapes=[
            SMEM((capacity, wide_peers), jnp.int32),
            *vmem_inputs,
            pltpu.SemaphoreType.DMA((12,)),
        ],
        compiler_params=params(),
        name="prepare",
    )(
        fresh,
        far(reads),
        far(state),
        far(lesion.reshape(own_blocks, block_rows)),
        far(stim_nodes.reshape(1, -1)),
        far(stim_wave.reshape(1, -1)),
        far(tract_slot.reshape(1, tile_count)),
        far(tract_target.reshape(1, tile_count)),
        far(tract_delay.reshape(1, tile_count)),
        far(jnp.asarray(lane_tables(peers, peer_targets, own_blocks))),
        far(jnp.asarray(expand_table(coef_count))),
        far(older_coefs.reshape(slot_count, HSEG, coef_count, block_rows)),
        far(tract_frac.reshape(1, tile_count)),
    )

    picked = pl.pallas_call(
        functools.partial(pick_kernel, capacity=capacity, peers=wide_peers),
        out_shape=[pltpu.VMEM((capacity, coef_count, block_rows), jnp.bfloat16)]
        * (wide_peers - 1),
        in_specs=[vmem_spec] * wide_peers,
        out_specs=[vmem_spec] * (wide_peers - 1),
        scratch_shapes=[
            SMEM((wide_peers - 1, capacity, wide_peers), jnp.int32),
            pltpu.SemaphoreType.DMA((wide_peers - 1,)),
        ],
        compiler_params=params(),
        name="pick_blocks",
    )(*asked[::-1], fresh)
    news = [swap(picked[r - 1], "wide", r) for r in range(wide_peers - 1, 0, -1)]

    fixed = tile_count * (peers - 2) // peers + 2 * UNROLL
    fixed = min(tile_count, -(-fixed // UNROLL) * UNROLL)
    share = pltpu.VMEM((share_rows, block_rows), jnp.bfloat16)
    total = pltpu.VMEM(((peers * peer_targets + 1) * STEPS, block_rows), jnp.float32)
    scalars = [SMEM((4, 128), jnp.int32), SMEM((1, 128), jnp.float32)]
    *shares, hist, sums = pl.pallas_call(
        functools.partial(
            far_kernel,
            wide_peers=wide_peers, peers=peers, capacity=capacity, peer_targets=peer_targets,
            fixed=fixed,
        ),
        out_shape=[share] * (peers - 2) + [pltpu.VMEM(hist.shape, jnp.float32), total],
        in_specs=[vmem_spec] * (5 + wide_peers),
        out_specs=[vmem_spec] * peers,
        scratch_shapes=[*scalars, pltpu.SemaphoreType.DMA((2,))],
        compiler_params=params(),
        name="far_tiles",
    )(fracs, tiles, table, heads, weights, hist, *news)
    sent = {r: swap(shares[peers - 1 - r], "narrow", r) for r in range(2, peers)}

    half = peer_targets * STEPS // 2
    pieces = [
        pltpu.VMEM((rows, block_rows), jnp.bfloat16) for rows in (half, share_rows - half)
    ]
    *pair, own = pl.pallas_call(
        functools.partial(near_tiles_kernel, peers=peers, peer_targets=peer_targets, fixed=fixed),
        out_shape=[*pieces, share],
        in_specs=[vmem_spec] * 6,
        out_specs=[vmem_spec] * 3,
        scratch_shapes=[*scalars, VMEM(total.shape, jnp.float32), pltpu.SemaphoreType.DMA((2,))],
        compiler_params=params(),
        name="near_tiles",
    )(fracs, tiles, heads, weights, hist, sums)
    pair = [swap(x, "narrow", 1) for x in pair]
    forcing = pl.pallas_call(
        functools.partial(
            forcing_kernel, peers=peers, own_blocks=own_blocks, peer_targets=peer_targets
        ),
        out_shape=pltpu.VMEM((STEPS * own_blocks, block_rows), jnp.float32),
        in_specs=[vmem_spec] * (peers + 1),
        out_specs=vmem_spec,
        compiler_params=params(),
        name="forcing",
    )(*[sent[r] for r in range(2, peers - 1)], *pair, own, ready)

    new_coefs, final_state = pl.pallas_call(
        functools.partial(
            window_kernel,
            own_blocks=own_blocks, peer_targets=peer_targets, coef_count=coef_count,
        ),
        out_shape=[
            jax.ShapeDtypeStruct(fresh_coefs.shape, jnp.bfloat16),
            jax.ShapeDtypeStruct(state.shape, jnp.float32),
        ],
        in_specs=[vmem_spec] * 4,
        out_specs=[hbm_spec] * 2,
        scratch_shapes=[
            VMEM((own_blocks * PITCH, block_rows), jnp.float32),
            VMEM((own_blocks * PITCH, block_rows), jnp.float32),
            VMEM((2, own_blocks, block_rows), jnp.float32),
            VMEM(fresh_coefs.shape, jnp.bfloat16),
            VMEM(state.shape, jnp.float32),
            pltpu.SemaphoreType.DMA((1 + own_blocks // GROUP // 2,)),
        ],
        compiler_params=params(),
        name="window_steps",
    )(sent[peers - 1], forcing, ready, jnp.asarray(fit_table(coef_count)))
    return new_coefs, final_state


def solution(mesh):
    in_specs = (
        P(("sweep", "wide", "narrow"), None, None),
        P(("sweep", "wide"), "narrow", None, None, None, None),
        P(None, ("sweep", "wide", "narrow")),
        P(("sweep", "wide", "narrow")),
        P("sweep"),
        P("sweep"),
        P("wide", "narrow", None, None),
        P("wide", "narrow", None),
        P("wide", "narrow", None),
        P("wide", "narrow", None),
        P("wide", "narrow", None),
        P("wide", "narrow", None, None, None),
    )
    out_specs = (P(("sweep", "wide", "narrow"), None, None), P(None, ("sweep", "wide", "narrow")))
    return jax.shard_map(local, mesh=mesh, in_specs=in_specs, out_specs=out_specs, check_vma=False)
```

```python
import functools
import math

import jax
import jax.numpy as jnp
import ml_dtypes
import numpy as np
from jax import lax
from jax.experimental import pallas as pl
from jax.experimental.pallas import tpu as pltpu
from jax.sharding import PartitionSpec as P

STEPS = 32
HSEG = 2
SEGS = HSEG + 1
LENGTH = SEGS * STEPS
GROUP = 4
HEAD = 16
PITCH = STEPS // 2 + 1
CHUNKS = 8
UNROLL = 4

excite_rate = 0.1
inhibit_rate = 0.05
excite_excite = 1.5
inhibit_excite = 2.0
excite_inhibit = 2.0
inhibit_inhibit = 0.5
excite_offset = 0.5
inhibit_offset = 0.5
tract_gain = 2.0

SMEM = pltpu.SMEM
VMEM = pltpu.VMEM
vmem_spec = pl.BlockSpec(memory_space=VMEM)
hbm_spec = pl.BlockSpec(memory_space=pltpu.HBM)


def basis_table(coef_count, step_count):
    order = np.arange(coef_count, dtype=np.float32)[:, None]
    places = np.arange(step_count, dtype=np.float32)[None, :]
    angles = np.float32(np.pi) * (step_count - places - np.float32(0.5)) / np.float32(step_count)
    return np.cos((order * angles).astype(np.float64)).astype(np.float32)


def expand_table(coef_count):
    basis = basis_table(coef_count, STEPS).astype(ml_dtypes.bfloat16)
    table = np.zeros((LENGTH, SEGS * coef_count), ml_dtypes.bfloat16)
    for seg in range(SEGS):
        table[seg * STEPS : (seg + 1) * STEPS, seg * coef_count : (seg + 1) * coef_count] = basis.T
    return table


def fit_table(coef_count):
    scales = np.where(np.arange(coef_count)[:, None] == 0, 1.0, 2.0) / STEPS
    fit = (basis_table(coef_count, STEPS) * scales / (excite_excite / 2)).astype(np.float32)
    half = STEPS // 2
    tables = []
    for i in range(2):
        whole = np.zeros((GROUP * coef_count, GROUP * half), np.float32)
        for g in range(GROUP):
            whole[g * coef_count : (g + 1) * coef_count, g * half : (g + 1) * half] = fit[
                :, i * half : (i + 1) * half
            ]
        high = whole.astype(ml_dtypes.bfloat16)
        low = (whole - high.astype(np.float32)).astype(ml_dtypes.bfloat16)
        tables.append(np.concatenate([high, high, low], axis=1))
    return np.stack(tables)


TOGETHER = 8


def lane_tables(peers, peer_targets, own_blocks):
    width = TOGETHER * peer_targets
    assert TOGETHER * own_blocks <= 256 and peers * width <= HEAD * 128
    lane = np.arange(HEAD * 128)
    used = lane < peers * width
    within = lane % width
    rank = np.where(used, within // TOGETHER, -5)
    offset = within % TOGETHER * own_blocks + 1
    place = np.where(used, lane // width, -5)
    return np.stack([rank, offset, place]).astype(np.float32).reshape(3, HEAD, 128)


def prepare_kernel(
    fresh_ref, reads_hbm, state_hbm, lesion_hbm, stim_hbm, wave_hbm, slot_hbm, target_hbm,
    delay_hbm, lanes_hbm, table_hbm, older_hbm, frac_hbm,
    ready_out, hist_out, tiles_out, fracs_out, head_out, table,
    reads, state, lesion, stim, wave, slot, target, delay, frac, lanes, older, sems,
    *, peers, own_blocks, peer_targets, capacity,
):
    pairs = [
        (reads_hbm, reads), (target_hbm, target), (slot_hbm, slot),
        (delay_hbm, delay), (lanes_hbm, lanes), (table_hbm, table), (older_hbm, older),
        (state_hbm, state), (lesion_hbm, lesion), (stim_hbm, stim), (wave_hbm, wave),
        (frac_hbm, frac),
    ]
    copies = [
        pltpu.make_async_copy(source, into, sems.at[i]) for i, (source, into) in enumerate(pairs)
    ]
    for copy in copies:
        copy.start()
    for copy in (*copies[1:5], copies[11]):
        copy.wait()
    place = lax.axis_index("narrow")
    owner = lax.axis_index("wide")
    tile_count = target.shape[1]
    target_count = peers * own_blocks

    numbers = lax.broadcasted_iota(jnp.int32, (target_count, tile_count), 0)
    hits = jnp.where(numbers == target[...], 1.0, 0.0)
    held = jnp.dot(
        hits.astype(jnp.bfloat16), jnp.ones((tile_count, 128), jnp.bfloat16),
        preferred_element_type=jnp.float32,
    )
    held = jnp.minimum(held, 1.0)
    shape = (own_blocks, own_blocks)
    below = jnp.where(
        lax.broadcasted_iota(jnp.int32, shape, 0) > lax.broadcasted_iota(jnp.int32, shape, 1),
        1.0, 0.0,
    ).astype(jnp.bfloat16)
    block = lax.broadcasted_iota(jnp.int32, (own_blocks, 128), 0).astype(jnp.float32)
    ranks = jnp.zeros((1, tile_count), jnp.float32)
    head_rows = pl.cdiv(peers * TOGETHER * peer_targets, 128)
    for p in range(peers):
        part = slice(p * own_blocks, (p + 1) * own_blocks)
        rank = jnp.dot(below, held[part].astype(jnp.bfloat16), preferred_element_type=jnp.float32)
        ranks = ranks + jnp.sum(hits[part] * rank[:, :tile_count], axis=0, keepdims=True)
        rank = jnp.where(held[part] > 0.5, rank, -1.0)
        source = ((peers - 1) - (place ^ p)).astype(jnp.float32)
        rows = []
        for h in range(head_rows):
            match = rank == lanes[0, h : h + 1, :]
            ids = jnp.sum(jnp.where(match, block, 0.0), axis=0, keepdims=True)
            mine = lanes[2, h : h + 1, :] == source
            rows.append(jnp.where(mine, ids + lanes[1, h : h + 1, :], 0.0))
        rows.append(jnp.zeros((HEAD - head_rows, 128), jnp.float32))
        head_out[p] = jnp.concatenate(rows, axis=0).astype(jnp.bfloat16)

    across = jnp.zeros((1, tile_count), jnp.int32)
    for p in range(1, peers):
        across = across + jnp.where(target[...] >= p * own_blocks, 1, 0)
    key_row = ((peers - 1) - (across ^ place)).astype(jnp.float32)
    shape = (tile_count, tile_count)
    down = lax.broadcasted_iota(jnp.int32, shape, 0)
    along = lax.broadcasted_iota(jnp.int32, shape, 1)
    key = jnp.sum(jnp.where(down == along, key_row, 0.0), axis=1, keepdims=True)
    ahead = (key_row < key) | ((key_row == key) & (along < down))
    position = jnp.sum(jnp.where(ahead, 1.0, 0.0), axis=1, keepdims=True)
    lane = lax.broadcasted_iota(jnp.int32, (tile_count, 128), 1).astype(jnp.float32)
    chosen = jnp.where(position == lane, 1.0, 0.0)
    starts = (slot[...] * LENGTH + (LENGTH - 1) - delay[...]).astype(jnp.float32)
    index = lax.broadcasted_iota(jnp.int32, (1, tile_count), 1).astype(jnp.float32)
    firsts = key_row * float(peer_targets) + ranks
    facts = jnp.concatenate(
        [index, starts, firsts, frac[...], jnp.zeros((4, tile_count), jnp.float32)], axis=0
    )
    ordered = jnp.dot(
        facts, chosen, precision=lax.Precision.HIGHEST, preferred_element_type=jnp.float32
    )
    fracs_out[...] = ordered[3:4, :]
    ints = (ordered + 0.5).astype(jnp.int32)
    packed = ints[1:2, :] * (1 << 16) + ints[0:1, :] * (1 << 8) + ints[2:3, :]
    before = jnp.sum(jnp.where(key < lane - float(tile_count), 1.0, 0.0), axis=0, keepdims=True)
    tiles_out[...] = jnp.where(lane[0:1, :] < tile_count, packed, before.astype(jnp.int32))

    for copy in copies[5:7]:
        copy.wait()
    coef_count = older.shape[2]
    earlier = HSEG * STEPS
    for s in range(older.shape[0]):
        segments = [older[s, h] for h in range(HSEG - 1, -1, -1)]
        hist_out[s * LENGTH : s * LENGTH + earlier, :] = jnp.dot(
            table[:earlier, : HSEG * coef_count], jnp.concatenate(segments, axis=0),
            preferred_element_type=jnp.float32,
        )
        hist_out[s * LENGTH + earlier : (s + 1) * LENGTH, :] = jnp.zeros(
            (STEPS, hist_out.shape[1]), jnp.float32
        )
    copies[0].wait()
    for c in range(capacity):
        rows = pl.ds(pl.multiple_of((owner * capacity + c) * LENGTH + earlier, 8), STEPS)
        hist_out[rows, :] = jnp.dot(
            table[:STEPS, :coef_count], fresh_ref[jnp.maximum(reads[c, owner], 0)],
            preferred_element_type=jnp.float32,
        )

    for copy in copies[7:11]:
        copy.wait()
    block_rows = lesion.shape[1]
    for b in range(own_blocks):
        piece = state[:, b * block_rows : (b + 1) * block_rows]
        ready_out[b : b + 1, :] = piece[0:1, :]
        ready_out[own_blocks + b : own_blocks + b + 1, :] = piece[1:2, :]
    ready_out[2 * own_blocks : 3 * own_blocks, :] = tract_gain * (
        1.0 - lesion[...].astype(jnp.float32)
    )
    stim_count = stim.shape[1]
    nodes = stim[...] - (owner * peers + place) * (own_blocks * block_rows)
    blocks = lax.shift_right_arithmetic(nodes, block_rows.bit_length() - 1)
    offsets = nodes & (block_rows - 1)
    in_block = lax.broadcasted_iota(jnp.int32, (own_blocks, stim_count), 0) == blocks
    at_offset = lax.broadcasted_iota(jnp.int32, (block_rows, stim_count), 0) == offsets
    ready_out[3 * own_blocks : 4 * own_blocks, :] = lax.dot_general(
        jnp.where(in_block, 1.0, 0.0).astype(jnp.bfloat16),
        jnp.where(at_offset, 1.0, 0.0).astype(jnp.bfloat16),
        (((1,), (1,)), ((), ())),
        preferred_element_type=jnp.float32,
    )
    shape = (STEPS, STEPS)
    diagonal = lax.broadcasted_iota(jnp.int32, shape, 0) == lax.broadcasted_iota(jnp.int32, shape, 1)
    column = jnp.sum(jnp.where(diagonal, wave[...], 0.0), axis=1, keepdims=True)
    ready_out[4 * own_blocks :, :] = jnp.broadcast_to(column, (STEPS, block_rows))


def near_kernel(fresh_hbm, weights_hbm, fresh_out, weights_out, sems):
    copies = [pltpu.make_async_copy(fresh_hbm, fresh_out, sems.at[CHUNKS])]
    part = weights_hbm.shape[0] // CHUNKS
    for i in range(CHUNKS):
        rows = pl.ds(i * part, part)
        copies.append(
            pltpu.make_async_copy(weights_hbm.at[rows], weights_out.at[rows], sems.at[i])
        )
    for copy in copies:
        copy.start()
    for copy in copies:
        copy.wait()


def folded_ring(count):
    return [0, *range(1, count, 2), *reversed(range(2, count, 2))]


def pick_kernel(*refs, capacity, peers):
    tables = refs[: peers - 1][::-1]
    fresh = refs[peers - 1]
    outs = refs[peers : 2 * peers - 1]
    asked, sems = refs[2 * peers - 1 :]
    place = lax.axis_index("wide")
    copies = [pltpu.make_async_copy(tables[r], asked.at[r], sems.at[r]) for r in range(peers - 1)]
    for copy in copies:
        copy.start()

    for copy in copies:
        copy.wait()
    ring = folded_ring(peers)
    for distance in range(1, peers):
        turns = [(ring.index(i) - ring.index(i ^ distance)) % peers for i in range(peers)]
        way = turns[0]
        for i in range(1, peers):
            if turns[i] != turns[0]:
                way = jnp.where(place == i, turns[i], way)
        for c in range(capacity):
            block = jnp.maximum(asked[way - 1, c, place], 0)
            outs[distance - 1][c] = fresh[block]


def row_of(tiles, t):
    return (tiles[0, t] & 255) * TOGETHER


def add_tiles(tiles, frac, hist, weights, total, pitch, items):
    block_rows = weights.shape[2]
    rows = []
    for t, _ in items:
        fraction = frac[0, t]
        start = lax.shift_right_logical(tiles[0, t], 16)
        earlier = hist[pl.ds(start, STEPS), :]
        later = hist[pl.ds(start + 1, STEPS), :]
        rows.append(((1.0 - fraction) * later + fraction * earlier).astype(jnp.bfloat16))
    tile = [weights[lax.shift_right_logical(tiles[0, t], 8) & 255] for t, _ in items]
    none = jnp.zeros((2 * STEPS, block_rows), jnp.bfloat16)
    product = lax.dot_general(
        jnp.concatenate(
            [
                jnp.concatenate([*rows[:2], none], axis=0),
                jnp.concatenate([none, *rows[2:]], axis=0),
            ],
            axis=1,
        ),
        jnp.concatenate(
            [jnp.concatenate(tile[:2], axis=0), jnp.concatenate(tile[2:], axis=0)], axis=1
        ),
        (((1,), (1,)), ((), ())),
        preferred_element_type=jnp.float32,
    )
    for i, (_, first) in enumerate(items):
        left = i % 2 * block_rows
        for g in range(STEPS // TOGETHER):
            where = pl.ds(pl.multiple_of(first + g * pitch, 8), TOGETHER)
            top = i * STEPS + g * TOGETHER
            total[where, :] += product[top : top + TOGETHER, left : left + block_rows]


def write_share(pieces, total, head, first, span, pitch):
    groups = STEPS // TOGETHER // len(pieces)
    for i, piece in enumerate(pieces):
        for g in range(groups):
            top = (i * groups + g) * pitch + first
            piece[g * span : (g + 1) * span, :] = total[top : top + span, :].astype(jnp.bfloat16)
    pieces[-1][groups * span :, :] = head


def far_kernel(
    fracs_ref, tiles_ref, table_ref, head_ref, weights, hist_ref, *refs,
    wide_peers, peers, capacity, peer_targets, fixed,
):
    news = refs[: wide_peers - 1]
    outs = refs[wide_peers - 1 : wide_peers + peers - 3]
    hist, total, tiles, frac, sems = refs[wide_peers + peers - 3 :]
    place = lax.axis_index("narrow")
    owner = lax.axis_index("wide")
    copies = [
        pltpu.make_async_copy(tiles_ref, tiles, sems.at[0]),
        pltpu.make_async_copy(fracs_ref, frac, sems.at[1]),
    ]
    for copy in copies:
        copy.start()
    total[...] = jnp.zeros_like(total)
    hist[...] = hist_ref[...]
    came = [(i, c) for i in range(len(news)) for c in range(capacity)]
    coef_count = news[0].shape[1]
    for first in range(0, len(came), SEGS):
        some = came[first : first + SEGS]
        values = jnp.dot(
            table_ref[: len(some) * STEPS, : len(some) * coef_count],
            jnp.concatenate([news[i][c] for i, c in some], axis=0),
            preferred_element_type=jnp.float32,
        )
        for place_here, (i, c) in enumerate(some):
            slot = (owner ^ (wide_peers - 1 - i)) * capacity + c
            rows = pl.ds(pl.multiple_of(slot * LENGTH + HSEG * STEPS, 8), STEPS)
            hist[rows, :] = values[place_here * STEPS : (place_here + 1) * STEPS]
    for copy in copies:
        copy.wait()

    span = peer_targets * TOGETHER
    spare = peers * span
    pitch = spare + TOGETHER
    for t in range(0, fixed, UNROLL):
        items = [(u, row_of(tiles, u)) for u in range(t, t + UNROLL)]
        add_tiles(tiles, frac, hist, weights, total, pitch, items)
    far_count = tiles[0, weights.shape[0] + peers - 2]

    @pl.loop(0, lax.div(jnp.maximum(far_count - fixed, 0) + (UNROLL - 1), UNROLL))
    def _(turn):
        places = [fixed + turn * UNROLL + u for u in range(UNROLL)]
        items = [(t, jnp.where(t < far_count, row_of(tiles, t), spare)) for t in places]
        add_tiles(tiles, frac, hist, weights, total, pitch, items)

    for part, out in enumerate(outs):
        write_share([out], total, head_ref[place ^ (peers - 1 - part)], part * span, span, pitch)


def near_tiles_kernel(
    fracs_ref, tiles_ref, head_ref, weights, hist, total_ref, *refs,
    peers, peer_targets, fixed,
):
    *pair, own, tiles, frac, total, sems = refs
    place = lax.axis_index("narrow")
    copies = [
        pltpu.make_async_copy(tiles_ref, tiles, sems.at[0]),
        pltpu.make_async_copy(fracs_ref, frac, sems.at[1]),
    ]
    for copy in copies:
        copy.start()
    total[...] = total_ref[...]
    for copy in copies:
        copy.wait()
    span = peer_targets * TOGETHER
    spare = peers * span
    pitch = spare + TOGETHER
    far_count = tiles[0, weights.shape[0] + peers - 2]
    for t in range(fixed, weights.shape[0], UNROLL):
        items = [
            (u, jnp.where(u < far_count, spare, row_of(tiles, u))) for u in range(t, t + UNROLL)
        ]
        add_tiles(tiles, frac, hist, weights, total, pitch, items)
    write_share(pair, total, head_ref[place ^ 1], (peers - 2) * span, span, pitch)
    write_share([own], total, head_ref[place], (peers - 1) * span, span, pitch)


def share_rows(pieces, group, width):
    groups = STEPS // TOGETHER // len(pieces)
    first = group % groups * width
    return pieces[group // groups][first : first + width, :]


def one_hot(head, rows, columns):
    row = lax.broadcasted_iota(jnp.int32, (rows, 128), 0).astype(jnp.float32) + 1.0
    parts = [
        jnp.where(row == head[h : h + 1, :], 1.0, 0.0).astype(jnp.bfloat16)
        for h in range(pl.cdiv(columns, 128))
    ]
    return jnp.concatenate(parts, axis=1)[:, :columns]


def two_groups(shares, pair, width):
    return jnp.concatenate(
        [
            jnp.concatenate([share_rows(share, g, width) for share in shares], axis=0)
            for g in (pair, pair + 1)
        ],
        axis=1,
    )


def forcing_kernel(*refs, peers, own_blocks, peer_targets):
    shares = {r: (ref,) for r, ref in zip(range(2, peers - 1), refs)}
    shares |= {1: refs[peers - 3 : peers - 1], 0: (refs[peers - 1],)}
    ready_ref, out_ref = refs[peers:]
    block_rows = ready_ref.shape[1]
    width = TOGETHER * peer_targets
    head = sum(share[-1][-HEAD:, :].astype(jnp.float32) for share in shares.values())
    scatter = one_hot(head, TOGETHER * own_blocks, peers * width)
    stack = [shares[r] for r in (0, *range(peers - 2, -1, -1))]
    gain, counts = [
        0.5 * ready_ref[i * own_blocks : (i + 1) * own_blocks, :] for i in (2, 3)
    ]
    for pair in range(0, STEPS // TOGETHER, 2):
        inflow = jnp.dot(
            scatter, two_groups(stack, pair, width), preferred_element_type=jnp.float32
        )
        for jj in range(2 * TOGETHER):
            j = pair * TOGETHER + jj
            wave = ready_ref[4 * own_blocks + j : 4 * own_blocks + j + 1, :]
            first = jj % TOGETHER * own_blocks
            left = jj // TOGETHER * block_rows
            out_ref[j * own_blocks : (j + 1) * own_blocks, :] = gain * inflow[
                first : first + own_blocks, left : left + block_rows
            ] + (wave * counts - excite_offset / 2)


def window_kernel(
    share_ref, forcing_ref, ready_ref, fit_ref, coefs_hbm, state_hbm,
    early, late, rates, coefs, state, sems,
    *, own_blocks, peer_targets, coef_count,
):
    samples = (early, late)
    block_rows = ready_ref.shape[1]
    width = TOGETHER * peer_targets
    scatter = one_hot(
        share_ref[-HEAD:, :].astype(jnp.float32), TOGETHER * own_blocks, width
    )

    excite, inhibit, gain = [
        ready_ref[i * own_blocks : (i + 1) * own_blocks, :] for i in range(3)
    ]
    a = excite_excite / 2
    gain = 0.5 * gain
    carried = a * excite

    def fit_half(values, fit):
        products = []
        for g in range(0, own_blocks // GROUP, 2):
            part = jnp.concatenate(
                [
                    jnp.concatenate(
                        [
                            values[b * PITCH : b * PITCH + STEPS // 2, :]
                            for b in range((g + i) * GROUP, (g + i + 1) * GROUP)
                        ],
                        axis=0,
                    )
                    for i in range(2)
                ],
                axis=1,
            )
            high = part.astype(jnp.bfloat16)
            low = (part - high.astype(jnp.float32)).astype(jnp.bfloat16)
            products.append(
                jnp.dot(
                    fit, jnp.concatenate([high, low, high], axis=0),
                    preferred_element_type=jnp.float32,
                )
            )
        return products

    fitted = [None, None]
    for pair in range(0, STEPS // TOGETHER, 2):
        inflow = jnp.dot(
            scatter, two_groups([(share_ref,)], pair, width), preferred_element_type=jnp.float32
        )
        for jj in range(2 * TOGETHER):
            j = pair * TOGETHER + jj
            first = jj % TOGETHER * own_blocks
            left = jj // TOGETHER * block_rows
            half_forcing = (
                forcing_ref[j * own_blocks : (j + 1) * own_blocks, :]
                + gain * inflow[first : first + own_blocks, left : left + block_rows]
            )
            inhibit_drive = (inhibit_inhibit / 2) * inhibit + inhibit_offset / 2
            excite_turn = jnp.tanh(carried + (half_forcing - (inhibit_excite / 2) * inhibit))
            inhibit_turn = jnp.tanh((excite_inhibit / 2 / a) * carried - inhibit_drive)
            carried = ((1 - excite_rate) * carried + a * excite_rate / 2) + (
                a * excite_rate / 2
            ) * excite_turn
            inhibit = ((1 - inhibit_rate) * inhibit + inhibit_rate / 2) + (
                inhibit_rate / 2
            ) * inhibit_turn
            samples[pair // 2][pl.ds(jj, own_blocks, stride=PITCH), :] = carried
        fitted[pair // 2] = fit_half(samples[pair // 2], fit_ref[pair // 2])
    rates[0] = carried * (1 / a)
    rates[1] = inhibit
    for b in range(own_blocks):
        where = slice(b * block_rows, (b + 1) * block_rows)
        state[0:1, where] = rates[0, b : b + 1, :]
        state[1:2, where] = rates[1, b : b + 1, :]
    copies = [pltpu.make_async_copy(state, state_hbm, sems.at[0])]
    copies[0].start()

    for g in range(0, own_blocks // GROUP, 2):
        both = (fitted[0][g // 2] + fitted[1][g // 2]).astype(jnp.bfloat16)
        for i in range(2):
            coefs[(g + i) * GROUP : (g + i + 1) * GROUP] = both[
                :, i * block_rows : (i + 1) * block_rows
            ].reshape(GROUP, coef_count, block_rows)
        where = pl.ds(g * GROUP, 2 * GROUP)
        copies.append(
            pltpu.make_async_copy(coefs.at[where], coefs_hbm.at[where], sems.at[1 + g // 2])
        )
        copies[-1].start()
    for copy in copies:
        copy.wait()


def far(x):
    return pltpu.with_memory_space_constraint(x, pltpu.HBM)


def params():
    return pltpu.CompilerParams(vmem_limit_bytes=20 << 20)


def local(
    fresh_coefs,
    older_coefs,
    state,
    lesion,
    stim_nodes,
    stim_wave,
    read_blocks,
    tract_slot,
    tract_target,
    tract_delay,
    tract_frac,
    tract_weights,
):
    wide_peers = lax.axis_size("wide")
    peers = lax.axis_size("narrow")
    own_blocks, coef_count, block_rows = fresh_coefs.shape
    capacity = read_blocks.shape[3]
    slot_count = wide_peers * capacity
    tile_count = tract_slot.shape[2]
    peer_targets = tile_count // (2 * peers)
    share_rows = peer_targets * STEPS + HEAD

    def swap(x, axis, r):
        return lax.ppermute(x, axis, [(i, i ^ r) for i in range(lax.axis_size(axis))])

    reads = read_blocks.reshape(wide_peers, capacity).T
    ring = folded_ring(wide_peers)
    asked = [
        lax.ppermute(
            reads, "wide", [(ring[k], ring[(k + r) % wide_peers]) for k in range(wide_peers)]
        )
        for r in range(1, wide_peers)
    ]

    vmem_inputs = [
        VMEM(state.shape, jnp.float32),
        VMEM((own_blocks, block_rows), jnp.int32),
        VMEM((1, stim_nodes.shape[0]), jnp.int32),
        VMEM((1, STEPS), jnp.float32),
        VMEM((1, tile_count), jnp.int32),
        VMEM((1, tile_count), jnp.int32),
        VMEM((1, tile_count), jnp.int32),
        VMEM((1, tile_count), jnp.float32),
        VMEM((3, HEAD, 128), jnp.float32),
        VMEM((slot_count, HSEG, coef_count, block_rows), jnp.bfloat16),
    ]
    fresh, weights = pl.pallas_call(
        near_kernel,
        out_shape=[
            pltpu.VMEM(fresh_coefs.shape, jnp.bfloat16),
            pltpu.VMEM((tile_count, block_rows, block_rows), jnp.bfloat16),
        ],
        in_specs=[hbm_spec] * 2,
        out_specs=[vmem_spec] * 2,
        scratch_shapes=[pltpu.SemaphoreType.DMA((CHUNKS + 1,))],
        compiler_params=params(),
        name="near",
    )(far(fresh_coefs), far(tract_weights.reshape(tile_count, block_rows, block_rows)))
    ready, hist, tiles, fracs, heads, table = pl.pallas_call(
        functools.partial(
            prepare_kernel,
            peers=peers, own_blocks=own_blocks, peer_targets=peer_targets, capacity=capacity,
        ),
        out_shape=[
            pltpu.VMEM((4 * own_blocks + STEPS, block_rows), jnp.float32),
            pltpu.VMEM((slot_count * LENGTH, block_rows), jnp.float32),
            pltpu.VMEM((1, 128), jnp.int32),
            pltpu.VMEM((1, 128), jnp.float32),
            pltpu.VMEM((peers, HEAD, 128), jnp.bfloat16),
            pltpu.VMEM((LENGTH, SEGS * coef_count), jnp.bfloat16),
        ],
        in_specs=[vmem_spec] + [hbm_spec] * 12,
        out_specs=[vmem_spec] * 6,
        scratch_shapes=[
            SMEM((capacity, wide_peers), jnp.int32),
            *vmem_inputs,
            pltpu.SemaphoreType.DMA((12,)),
        ],
        compiler_params=params(),
        name="prepare",
    )(
        fresh,
        far(reads),
        far(state),
        far(lesion.reshape(own_blocks, block_rows)),
        far(stim_nodes.reshape(1, -1)),
        far(stim_wave.reshape(1, -1)),
        far(tract_slot.reshape(1, tile_count)),
        far(tract_target.reshape(1, tile_count)),
        far(tract_delay.reshape(1, tile_count)),
        far(jnp.asarray(lane_tables(peers, peer_targets, own_blocks))),
        far(jnp.asarray(expand_table(coef_count))),
        far(older_coefs.reshape(slot_count, HSEG, coef_count, block_rows)),
        far(tract_frac.reshape(1, tile_count)),
    )

    picked = pl.pallas_call(
        functools.partial(pick_kernel, capacity=capacity, peers=wide_peers),
        out_shape=[pltpu.VMEM((capacity, coef_count, block_rows), jnp.bfloat16)]
        * (wide_peers - 1),
        in_specs=[vmem_spec] * wide_peers,
        out_specs=[vmem_spec] * (wide_peers - 1),
        scratch_shapes=[
            SMEM((wide_peers - 1, capacity, wide_peers), jnp.int32),
            pltpu.SemaphoreType.DMA((wide_peers - 1,)),
        ],
        compiler_params=params(),
        name="pick_blocks",
    )(*asked[::-1], fresh)
    news = [swap(picked[r - 1], "wide", r) for r in range(wide_peers - 1, 0, -1)]

    fixed = tile_count * (peers - 2) // peers + 2 * UNROLL
    fixed = min(tile_count, -(-fixed // UNROLL) * UNROLL)
    share = pltpu.VMEM((share_rows, block_rows), jnp.bfloat16)
    total = pltpu.VMEM(((peers * peer_targets + 1) * STEPS, block_rows), jnp.float32)
    scalars = [SMEM((1, 128), jnp.int32), SMEM((1, 128), jnp.float32)]
    *shares, hist, sums = pl.pallas_call(
        functools.partial(
            far_kernel,
            wide_peers=wide_peers, peers=peers, capacity=capacity, peer_targets=peer_targets,
            fixed=fixed,
        ),
        out_shape=[share] * (peers - 2) + [pltpu.VMEM(hist.shape, jnp.float32), total],
        in_specs=[vmem_spec] * (5 + wide_peers),
        out_specs=[vmem_spec] * peers,
        scratch_shapes=[*scalars, pltpu.SemaphoreType.DMA((2,))],
        compiler_params=params(),
        name="far_tiles",
    )(fracs, tiles, table, heads, weights, hist, *news)
    sent = {r: swap(shares[peers - 1 - r], "narrow", r) for r in range(2, peers)}

    half = peer_targets * STEPS // 2
    pieces = [
        pltpu.VMEM((rows, block_rows), jnp.bfloat16) for rows in (half, share_rows - half)
    ]
    *pair, own = pl.pallas_call(
        functools.partial(near_tiles_kernel, peers=peers, peer_targets=peer_targets, fixed=fixed),
        out_shape=[*pieces, share],
        in_specs=[vmem_spec] * 6,
        out_specs=[vmem_spec] * 3,
        scratch_shapes=[*scalars, VMEM(total.shape, jnp.float32), pltpu.SemaphoreType.DMA((2,))],
        compiler_params=params(),
        name="near_tiles",
    )(fracs, tiles, heads, weights, hist, sums)
    pair = [swap(x, "narrow", 1) for x in pair]
    forcing = pl.pallas_call(
        functools.partial(
            forcing_kernel, peers=peers, own_blocks=own_blocks, peer_targets=peer_targets
        ),
        out_shape=pltpu.VMEM((STEPS * own_blocks, block_rows), jnp.float32),
        in_specs=[vmem_spec] * (peers + 1),
        out_specs=vmem_spec,
        compiler_params=params(),
        name="forcing",
    )(*[sent[r] for r in range(2, peers - 1)], *pair, own, ready)

    new_coefs, final_state = pl.pallas_call(
        functools.partial(
            window_kernel,
            own_blocks=own_blocks, peer_targets=peer_targets, coef_count=coef_count,
        ),
        out_shape=[
            jax.ShapeDtypeStruct(fresh_coefs.shape, jnp.bfloat16),
            jax.ShapeDtypeStruct(state.shape, jnp.float32),
        ],
        in_specs=[vmem_spec] * 4,
        out_specs=[hbm_spec] * 2,
        scratch_shapes=[
            VMEM(((own_blocks + 1) * PITCH, block_rows), jnp.float32),
            VMEM(((own_blocks + 1) * PITCH, block_rows), jnp.float32),
            VMEM((2, own_blocks, block_rows), jnp.float32),
            VMEM(fresh_coefs.shape, jnp.bfloat16),
            VMEM(state.shape, jnp.float32),
            pltpu.SemaphoreType.DMA((1 + own_blocks // GROUP // 2,)),
        ],
        compiler_params=params(),
        name="window_steps",
    )(sent[peers - 1], forcing, ready, jnp.asarray(fit_table(coef_count)))
    return new_coefs, final_state


def solution(mesh):
    in_specs = (
        P(("sweep", "wide", "narrow"), None, None),
        P(("sweep", "wide"), "narrow", None, None, None, None),
        P(None, ("sweep", "wide", "narrow")),
        P(("sweep", "wide", "narrow")),
        P("sweep"),
        P("sweep"),
        P("wide", "narrow", None, None),
        P("wide", "narrow", None),
        P("wide", "narrow", None),
        P("wide", "narrow", None),
        P("wide", "narrow", None),
        P("wide", "narrow", None, None, None),
    )
    out_specs = (P(("sweep", "wide", "narrow"), None, None), P(None, ("sweep", "wide", "narrow")))
    return jax.shard_map(local, mesh=mesh, in_specs=in_specs, out_specs=out_specs, check_vma=False)
```
